32 devices in a mesh: dp: 8 (over z, y), ctx: 2 (over x), tp: 2 (over core).
Axes of the slice: x: 2, y: 2, z: 4, core: 2. Of those that a mesh axis runs over, the one named last changes fastest.
Arguments:
- tokens_in: bfloat16 [8, 1032, 1024], P('dp', 'ctx'), may hold values from -6 to 6
- cotangent: bfloat16 [8, 1032, 1024], P('dp', 'ctx'), may hold values from -6 to 6
- key_mask: int32 [8, 1032], P('dp', 'ctx'), may hold values from 0 to 1, as said below
- grid_pos: int32 [2, 8, 1032], P(None, 'dp', 'ctx'), may hold values from 0 to 31, as said below
- class_index: int32 [8], P('dp'), may hold values from 0 to 1031, as said below
- input_weight: bfloat16 [2, 1024, 3, 1024], P(None, ('dp', 'ctx'), None, 'tp'), may hold values from -0.1875 to 0.1875
- output_weight: bfloat16 [2, 1024, 1024], P(None, ('dp', 'ctx'), 'tp'), may hold values from -0.1875 to 0.1875
- gate_up_weight: bfloat16 [2, 1024, 2, 2730], P(None, ('dp', 'ctx'), None, 'tp'), may hold values from -0.1875 to 0.1875
- down_weight: bfloat16 [2, 1024, 2730], P(None, ('dp', 'ctx'), 'tp'), may hold values from -0.109375 to 0.109375
- norm_gains: bfloat16 [2, 2, 1024], replicated, may hold values from 0.099609375 to 1.8984375
- norm_biases: bfloat16 [2, 4, 1024], replicated, may hold values from -3 to 3
- head_gains: bfloat16 [2, 1024], P(None, 'tp'), may hold values from 0.099609375 to 1.8984375
- head_biases: bfloat16 [2, 3, 1024], P(None, None, 'tp'), may hold values from -3 to 3
- hidden_gains: bfloat16 [2, 2730], P(None, 'tp'), may hold values from 0.099609375 to 1.8984375
- hidden_biases: bfloat16 [2, 3, 2730], P(None, None, 'tp'), may hold values from -3 to 3
Outputs:
- activations: bfloat16 [8, 1032, 1024], P('dp', 'ctx')
- input_grad: float32 [8, 1032, 1024], P('dp', 'ctx')
- grad_input_weight: float32 [2, 1024, 3, 1024], P(None, ('dp', 'ctx'), None, 'tp')
- grad_output_weight: float32 [2, 1024, 1024], P(None, ('dp', 'ctx'), 'tp')
- grad_gate_up_weight: float32 [2, 1024, 2, 2730], P(None, ('dp', 'ctx'), None, 'tp')
- grad_down_weight: float32 [2, 1024, 2730], P(None, ('dp', 'ctx'), 'tp')
- grad_norm_gains: float32 [2, 2, 1024], replicated
- grad_norm_biases: float32 [2, 4, 1024], replicated
- grad_head_gains: float32 [2, 1024], P(None, 'tp')
- grad_head_biases: float32 [2, 3, 1024], P(None, None, 'tp')
- grad_hidden_gains: float32 [2, 2730], P(None, 'tp')
- grad_hidden_biases: float32 [2, 3, 2730], P(None, None, 'tp')
The draws below stay inside these ranges and needn't reach their ends.
Inputs may be any that keep to these rules, and one draw needn't show every extreme that they name: `key_mask`: exactly one image, drawn from the seed, is all zeros; every other image has 1 on exactly 1025 rows, among them its first and its last row, the others at drawn places, and 0 on the rest. `grid_pos`: in each image the rows where a nonempty image's key_mask would be 1, other than the class token, hold every patch of the 32 x 32 grid once, in a drawn order; the class token and pad rows hold 0. `class_index`: the class token lies on one of an image's real rows.
All inputs are finite; a program needn't handle non-finite values.
Results may differ from the reference program's by a relative error of at most 0.018.
Values may be sent and summed in bfloat16 or wider, within the bound.
A program may use at most 256 MiB of HBM per device.

```python
import jax
import jax.numpy as jnp
from jax import lax

D = 1024
HEADS = 16
FF = 2730
HEAD_DIM = 64
GRID = 32
SEQ = 1032
LAYERS = 2
IMAGES = 8


def token_layout(key):
    image_keys = jax.random.split(jax.random.fold_in(key, 11), IMAGES)
    real_count = GRID * GRID + 1

    def one_image(image_key):
        inner_order = jax.random.permutation(jax.random.fold_in(image_key, 7), SEQ - 2).astype(jnp.int32)
        inner_real = inner_order < real_count - 2
        edge = jnp.ones((1,), dtype=bool)
        real_rows = jnp.concatenate([edge, inner_real, edge])
        ordinal = jnp.cumsum(real_rows.astype(jnp.int32)) - 1
        order = jax.random.permutation(jax.random.fold_in(image_key, 1), GRID * GRID).astype(jnp.int32)
        class_place = jax.random.randint(jax.random.fold_in(image_key, 3), (), 0, real_count).astype(jnp.int32)
        places = jnp.arange(SEQ, dtype=jnp.int32)
        is_class = real_rows & (ordinal == class_place)
        class_row = jnp.sum(jnp.where(is_class, places, 0)).astype(jnp.int32)
        slot_index = jnp.where(ordinal < class_place, ordinal, ordinal - 1)
        slot_index = jnp.clip(slot_index, 0, GRID * GRID - 1)
        patch = order[slot_index]
        used = real_rows & jnp.logical_not(is_class)
        patch = jnp.where(used, patch, 0).astype(jnp.int32)
        return (real_rows, class_row, patch)
    real_rows, class_rows, patches = jax.vmap(one_image)(image_keys)
    empty_image = jax.random.randint(jax.random.fold_in(key, 5), (), 0, IMAGES)
    return (real_rows, class_rows, patches, empty_image)


def draw_key_mask(key, part):
    real_rows, class_rows, patches, empty_image = token_layout(key)
    real_images = jnp.arange(IMAGES, dtype=jnp.int32)[:, None] != empty_image
    return (real_rows & real_images).astype(jnp.int32)


def draw_class_index(key, part):
    real_rows, class_rows, patches, empty_image = token_layout(key)
    return class_rows.astype(jnp.int32)


def draw_grid_pos(key, part):
    real_rows, class_rows, patches, empty_image = token_layout(key)
    return jnp.stack([patches // GRID, patches % GRID]).astype(jnp.int32)


def levels(stream_key, shape, shards, smallest, largest):
    level, own = 1.0, jax.random.fold_in(stream_key, 6)
    for dim, shards_of in shards:
        draws = jnp.exp(jax.random.uniform(jax.random.fold_in(own, dim), (shards_of,), jnp.float32, smallest / len(shards), largest / len(shards)))
        level = level * jnp.repeat(draws, shape[dim] // shards_of).reshape([-1 if axis == dim else 1 for axis in range(len(shape))])
    return level


def scatter_about(stream_key, dims, scale, reach, cuts=(), kind=jnp.bfloat16):
    level = levels(stream_key, dims, cuts, -0.22, 0.18) if cuts else 1.0
    values = jax.random.normal(stream_key, dims, jnp.float32) * scale * level
    return jnp.minimum(jnp.maximum(values, -reach), reach).astype(kind)


def setup_inputs(seed: int = 0) -> dict:
    seeds = jax.random.split(jax.random.key(seed), 16)
    tokens_in = scatter_about(seeds[0], (IMAGES, SEQ, D), 1.0, 6.0, ((0, 8), (1, 2)))
    cotangent = scatter_about(seeds[1], (IMAGES, SEQ, D), 1.0, 6.0, ((0, 8), (1, 2)))
    key_mask = draw_key_mask(jax.random.fold_in(seeds[15], 71), 0)
    grid_pos = draw_grid_pos(jax.random.fold_in(seeds[15], 71), 0)
    class_index = draw_class_index(jax.random.fold_in(seeds[15], 71), 0)
    input_weight = scatter_about(seeds[5], (LAYERS, D, 3, D), D ** -0.5, 0.1875, ((1, 16), (3, 2)))
    output_weight = scatter_about(seeds[6], (LAYERS, D, D), D ** -0.5, 0.1875, ((1, 16), (2, 2)))
    gate_up_weight = scatter_about(seeds[7], (LAYERS, D, 2, FF), D ** -0.5, 0.1875, ((1, 16), (3, 2)))
    down_weight = scatter_about(seeds[8], (LAYERS, D, FF), FF ** -0.5, 0.109375, ((1, 16), (2, 2)))
    norm_gains = jnp.clip(1.0 + 0.18 * jax.random.normal(seeds[9], (LAYERS, 2, D), jnp.float32), 0.099609375, 1.8984375).astype(jnp.bfloat16)
    norm_biases = scatter_about(seeds[10], (LAYERS, 4, D), 0.5, 3.0)
    head_gains = jnp.clip(1.0 + 0.18 * jax.random.normal(seeds[11], (LAYERS, D), jnp.float32), 0.099609375, 1.8984375).astype(jnp.bfloat16)
    head_biases = scatter_about(seeds[12], (LAYERS, 3, D), 0.5, 3.0, ((2, 2),))
    hidden_gains = jnp.clip(1.0 + 0.18 * jax.random.normal(seeds[13], (LAYERS, FF), jnp.float32), 0.099609375, 1.8984375).astype(jnp.bfloat16)
    hidden_biases = scatter_about(seeds[14], (LAYERS, 3, FF), 0.5, 3.0, ((2, 2),))
    return {"tokens_in": tokens_in, "cotangent": cotangent, "key_mask": key_mask, "grid_pos": grid_pos, "class_index": class_index, "input_weight": input_weight, "output_weight": output_weight, "gate_up_weight": gate_up_weight, "down_weight": down_weight, "norm_gains": norm_gains, "norm_biases": norm_biases, "head_gains": head_gains, "head_biases": head_biases, "hidden_gains": hidden_gains, "hidden_biases": hidden_biases}


highest = lax.Precision.HIGHEST
norm_epsilon = 1e-06
rotary_base = 10000.0
masked_score = -10000.0

@jax.custom_vjp
def low(v):
    return lax.optimization_barrier(v.astype(jnp.bfloat16)).astype(jnp.float32)

@jax.custom_vjp
def low_back(v):
    return v

def low_keep(v):
    return (low(v), None)

def low_pass(kept, grad):
    return (grad,)

def back_keep(v):
    return (v, None)

def back_low(kept, grad):
    return (low(grad),)
low.defvjp(low_keep, low_pass)
low_back.defvjp(back_keep, back_low)

def layer_norm(values, gain_vec, shift_vec):
    center = values - lax.optimization_barrier(jnp.mean(values, axis=-1, keepdims=True))
    spread = lax.optimization_barrier(jnp.mean(center * center, axis=-1, keepdims=True))
    return center * lax.rsqrt(spread + norm_epsilon) * gain_vec + shift_vec

def rotary_tables(positions, not_class):
    quarter = HEAD_DIM // 4
    frequency = rotary_base ** (-jnp.arange(quarter, dtype=jnp.float32) / quarter)
    angles = jnp.transpose(positions).astype(jnp.float32)[:, :, None] * frequency * not_class[:, None, None]
    return (jnp.cos(angles), jnp.sin(angles))

def rotate(values, cosine, sine, direction):
    row_count, head_count, head_dim = values.shape
    paired = values.reshape(row_count, head_count, 2, 2, head_dim // 4)
    first_half = paired[:, :, :, 0]
    second_half = paired[:, :, :, 1]
    cos_rows = cosine[:, None]
    sin_rows = sine[:, None] * direction
    turned = jnp.stack([first_half * cos_rows - second_half * sin_rows, second_half * cos_rows + first_half * sin_rows], axis=3)
    return turned.reshape(row_count, head_count, head_dim)

def forward_image(image_x, weights, row_keep, cosine, sine):
    input_weight, output_weight, gate_up_weight, down_weight, norm_gains, norm_biases, head_gains, head_biases, hidden_gains, hidden_biases = weights
    keep_col = row_keep[:, None]
    valid = row_keep > 0.5
    hidden_state = image_x * keep_col
    for layer_index in range(LAYERS):
        normed = low(layer_norm(hidden_state, norm_gains[layer_index, 0], norm_biases[layer_index, 0]))
        projected = low_back(jnp.einsum('sd,dke->ske', normed, input_weight[layer_index], precision=highest))
        queries = projected[:, 0] + head_biases[layer_index, 0]
        keys_proj = projected[:, 1]
        values_proj = projected[:, 2] + head_biases[layer_index, 1]
        queries = low(rotate(queries.reshape(SEQ, HEADS, HEAD_DIM), cosine, sine, 1.0))
        keys_proj = low(rotate(keys_proj.reshape(SEQ, HEADS, HEAD_DIM), cosine, sine, 1.0))
        values_proj = low(values_proj.reshape(SEQ, HEADS, HEAD_DIM))
        raw_scores = low_back(jnp.einsum('qhe,khe->hqk', queries, keys_proj, precision=highest))
        scores = jnp.where(valid[None, None, :], raw_scores * HEAD_DIM ** (-0.5), masked_score)
        attn_probs = low(jax.nn.softmax(scores, axis=-1))
        attended = low_back(jnp.einsum('hqk,khe->qhe', attn_probs, values_proj, precision=highest)).reshape(SEQ, D)
        head_normed = low(layer_norm(attended, head_gains[layer_index], head_biases[layer_index, 2]))
        branch = low_back(jnp.einsum('sc,dc->sd', head_normed, output_weight[layer_index], precision=highest))
        hidden_state = hidden_state + keep_col * (branch + norm_biases[layer_index, 2])
        normed_two = low(layer_norm(hidden_state, norm_gains[layer_index, 1], norm_biases[layer_index, 1]))
        gate_up = low_back(jnp.einsum('sd,dkf->skf', normed_two, gate_up_weight[layer_index], precision=highest))
        gate_pre = gate_up[:, 0] + hidden_biases[layer_index, 0]
        up_pre = gate_up[:, 1] + hidden_biases[layer_index, 1]
        inner_act = jax.nn.silu(gate_pre) * up_pre
        inner_normed = low(layer_norm(inner_act, hidden_gains[layer_index], hidden_biases[layer_index, 2]))
        down_out = low_back(jnp.einsum('sf,df->sd', inner_normed, down_weight[layer_index], precision=highest))
        hidden_state = hidden_state + keep_col * (down_out + norm_biases[layer_index, 3])
    return hidden_state

def reference(tokens_in, cotangent, key_mask, grid_pos, class_index, input_weight, output_weight, gate_up_weight, down_weight, norm_gains, norm_biases, head_gains, head_biases, hidden_gains, hidden_biases):
    params = tuple((array.astype(jnp.float32) for array in (input_weight, output_weight, gate_up_weight, down_weight, norm_gains, norm_biases, head_gains, head_biases, hidden_gains, hidden_biases)))
    zero_grads = tuple((jnp.zeros_like(array) for array in params))
    places = jnp.arange(SEQ, dtype=jnp.int32)

    def one_image(totals, image_items):
        image_x, image_cot, image_mask, image_pos, image_class = image_items
        row_keep = image_mask.astype(jnp.float32)
        not_class = (places != image_class.astype(jnp.int32)).astype(jnp.float32)
        cosine, sine = rotary_tables(image_pos, not_class)

        def run_layers(inputs, weights):
            return forward_image(inputs, weights, row_keep, cosine, sine)
        result, pullback = jax.vjp(run_layers, image_x.astype(jnp.float32), params)
        image_grad, weight_grads = pullback(image_cot.astype(jnp.float32))
        totals = tuple((first + second for first, second in zip(totals, weight_grads)))
        return (totals, (result.astype(jnp.bfloat16), image_grad))
    totals, (activations, input_grad) = lax.scan(one_image, zero_grads, (tokens_in, cotangent, key_mask, jnp.transpose(grid_pos, (1, 0, 2)), class_index))
    return (activations, input_grad, totals[0], totals[1], totals[2], totals[3], totals[4], totals[5], totals[6], totals[7], totals[8], totals[9])
```

```python
import functools

import jax
import jax.numpy as jnp
from jax import lax
from jax.experimental import pallas as pl
from jax.experimental.pallas import tpu as pltpu
from jax.sharding import PartitionSpec as P

FF = 2730
HEAD_DIM = 64


norm_epsilon = 1e-06
rotary_base = 10000.0
masked_score = -10000.0


def rotary_tables(positions, not_class):
    quarter = HEAD_DIM // 4
    frequency = rotary_base ** (-jnp.arange(quarter, dtype=jnp.float32) / quarter)
    angles = (
        jnp.transpose(positions).astype(jnp.float32)[:, :, None]
        * frequency
        * not_class[:, None, None]
    )
    return (jnp.cos(angles), jnp.sin(angles))


def rotate(values, cosine, sine, direction):
    row_count, head_count, head_dim = values.shape
    paired = values.reshape(row_count, head_count, 2, 2, head_dim // 4)
    first_half = paired[:, :, :, 0]
    second_half = paired[:, :, :, 1]
    cos_rows = cosine[:, None]
    sin_rows = sine[:, None] * direction
    turned = jnp.stack(
        [
            first_half * cos_rows - second_half * sin_rows,
            second_half * cos_rows + first_half * sin_rows,
        ],
        axis=3,
    )
    return turned.reshape(row_count, head_count, head_dim)


def local_norm(values, gain_vec, shift_vec):
    center = values - jnp.mean(values, axis=-1, keepdims=True)
    spread = jnp.mean(center * center, axis=-1, keepdims=True)
    inv_spread = lax.rsqrt(spread + norm_epsilon)
    unit_rows = center * inv_spread
    return (unit_rows * gain_vec + shift_vec, unit_rows, inv_spread)


def local_norm_back(upstream, unit_rows, inv_spread, gain_vec):
    weighted = upstream * gain_vec
    return inv_spread * (
        weighted
        - jnp.mean(weighted, axis=-1, keepdims=True)
        - unit_rows * jnp.mean(weighted * unit_rows, axis=-1, keepdims=True)
    )


def row_totals(first_part, second_part):
    return lax.psum(
        (jnp.sum(first_part, axis=-1, keepdims=True), jnp.sum(second_part, axis=-1, keepdims=True)),
        "tp",
    )


def split_norm(values, gain_vec, shift_vec, full_width):
    sum_first, sum_second = row_totals(values, values * values)
    row_mean = sum_first / full_width
    inv_spread = lax.rsqrt(sum_second / full_width - row_mean * row_mean + norm_epsilon)
    unit_rows = (values - row_mean) * inv_spread
    return (unit_rows * gain_vec + shift_vec, unit_rows, inv_spread)


def split_norm_back(upstream, unit_rows, inv_spread, gain_vec, full_width):
    weighted = upstream * gain_vec
    sum_first, sum_second = row_totals(weighted, weighted * unit_rows)
    return inv_spread * (weighted - sum_first / full_width - unit_rows * (sum_second / full_width))


def tensor_sum(partial_value):
    return lax.psum(partial_value.astype(jnp.bfloat16), "tp").astype(jnp.float32)


def tensor_back(partial_value):
    return lax.psum(partial_value.astype(jnp.bfloat16), "tp").astype(jnp.float32)


def fetch_weights(layer_index, input_weight, output_weight, gate_up_weight, down_weight):
    return (
        lax.all_gather(input_weight[layer_index], ("dp", "ctx"), axis=0, tiled=True),
        lax.all_gather(output_weight[layer_index], ("dp", "ctx"), axis=0, tiled=True),
        lax.all_gather(gate_up_weight[layer_index], ("dp", "ctx"), axis=0, tiled=True),
        lax.all_gather(down_weight[layer_index], ("dp", "ctx"), axis=0, tiled=True),
    )


def masked_scores(queries, key_heads, valid_keys):
    raw_scores = jnp.einsum("qhe,khe->hqk", queries, key_heads, preferred_element_type=jnp.float32)
    return jnp.where(valid_keys[None, None, :] > 0, raw_scores * HEAD_DIM ** (-0.5), masked_score)


def attend_forward(block_items):
    queries, keys_all, values_all, valid_keys = block_items
    key_count = keys_all.shape[0]
    head_count = queries.shape[1]
    key_heads = keys_all.reshape(key_count, head_count, HEAD_DIM)
    value_heads = values_all.reshape(key_count, head_count, HEAD_DIM)
    scores = masked_scores(queries, key_heads, valid_keys)
    row_max = jnp.max(scores, axis=-1, keepdims=True)
    exp_scores = jnp.exp(scores - row_max)
    row_total = jnp.sum(exp_scores, axis=-1, keepdims=True)
    attn_probs = (exp_scores / row_total).astype(jnp.bfloat16)
    attended = jnp.einsum(
        "hqk,khe->qhe", attn_probs, value_heads, preferred_element_type=jnp.float32
    )
    return (
        attended.reshape(queries.shape[0], head_count * HEAD_DIM),
        (row_max + jnp.log(row_total))[:, :, 0],
    )


def attend_backward(block_items):
    queries, keys_all, values_all, valid_keys, log_total, grad_out = block_items
    key_count = keys_all.shape[0]
    head_count = queries.shape[1]
    key_heads = keys_all.reshape(key_count, head_count, HEAD_DIM)
    value_heads = values_all.reshape(key_count, head_count, HEAD_DIM)
    scores = masked_scores(queries, key_heads, valid_keys)
    probs_full = jnp.exp(scores - log_total[:, :, None])
    probs_low = probs_full.astype(jnp.bfloat16)
    grad_probs = jnp.einsum(
        "qhe,khe->hqk", grad_out, value_heads, preferred_element_type=jnp.float32
    )
    row_dot = jnp.sum(probs_full * grad_probs, axis=-1, keepdims=True)
    grad_raw = jnp.where(
        valid_keys[None, None, :] > 0, HEAD_DIM ** (-0.5) * probs_full * (grad_probs - row_dot), 0.0
    ).astype(jnp.bfloat16)
    grad_queries = jnp.einsum(
        "hqk,khe->qhe", grad_raw, key_heads, preferred_element_type=jnp.float32
    )
    grad_keys = jnp.einsum("hqk,qhe->khe", grad_raw, queries, preferred_element_type=jnp.float32)
    grad_values = jnp.einsum(
        "hqk,qhe->khe", probs_low, grad_out, preferred_element_type=jnp.float32
    )
    local_rows = queries.shape[0]
    return (
        grad_queries.reshape(local_rows, head_count * HEAD_DIM),
        grad_keys.reshape(key_count, head_count * HEAD_DIM),
        grad_values.reshape(key_count, head_count * HEAD_DIM),
    )


def contract_rows(left, right):
    return lax.dot_general(
        left, right, (((0,), (0,)), ((), ())), preferred_element_type=jnp.float32
    )


def contract_cols(left, right):
    return lax.dot_general(
        left, right, (((1,), (1,)), ((), ())), preferred_element_type=jnp.float32
    )


def on_device(
    tokens_in,
    cotangent,
    key_mask,
    grid_pos,
    class_index,
    input_weight,
    output_weight,
    gate_up_weight,
    down_weight,
    norm_gains,
    norm_biases,
    head_gains,
    head_biases,
    hidden_gains,
    hidden_biases,
):
    images, rows_dev, model_width = tokens_in.shape
    row_count = images * rows_dev
    dim_local = head_gains.shape[1]
    heads_local = dim_local // HEAD_DIM
    hidden_local = hidden_gains.shape[1]
    layer_count = input_weight.shape[0]
    first_row = lax.axis_index("ctx") * rows_dev
    places = first_row + jnp.arange(rows_dev, dtype=jnp.int32)
    not_class = (places[None, :] != class_index[:, None]).astype(jnp.float32).reshape(row_count)
    cosine, sine = rotary_tables(grid_pos.reshape(2, row_count), not_class)
    row_keep = key_mask.astype(jnp.float32).reshape(row_count, 1)
    key_keep = key_mask.astype(jnp.bfloat16)
    gains_norm = norm_gains.astype(jnp.float32)
    biases_norm = norm_biases.astype(jnp.float32)
    gains_head = head_gains.astype(jnp.float32)
    biases_head = head_biases.astype(jnp.float32)
    gains_hidden = hidden_gains.astype(jnp.float32)
    biases_hidden = hidden_biases.astype(jnp.float32)
    hidden_state = tokens_in.astype(jnp.float32).reshape(row_count, model_width) * row_keep
    saved_layers = []
    for layer_index in range(layer_count):
        layer_mats = fetch_weights(
            layer_index, input_weight, output_weight, gate_up_weight, down_weight
        )
        mat_in, mat_out, mat_gate_up, mat_down = layer_mats
        normed, unit_one, spread_one = local_norm(
            hidden_state, gains_norm[layer_index, 0], biases_norm[layer_index, 0]
        )
        normed_low = normed.astype(jnp.bfloat16)
        projected = jnp.dot(
            normed_low,
            mat_in.reshape(model_width, 3 * dim_local),
            preferred_element_type=jnp.float32,
        ).reshape(row_count, 3, dim_local)
        queries = projected[:, 0] + biases_head[layer_index, 0]
        keys_proj = projected[:, 1]
        values_proj = projected[:, 2] + biases_head[layer_index, 1]
        query_low = rotate(
            queries.reshape(row_count, heads_local, HEAD_DIM), cosine, sine, 1.0
        ).astype(jnp.bfloat16)
        key_low = rotate(
            keys_proj.reshape(row_count, heads_local, HEAD_DIM), cosine, sine, 1.0
        ).astype(jnp.bfloat16)
        value_low = values_proj.astype(jnp.bfloat16)
        keys_all, values_all, valid_all = (
            lax.all_gather(key_low.reshape(images, rows_dev, dim_local), "ctx", axis=1, tiled=True),
            lax.all_gather(
                value_low.reshape(images, rows_dev, dim_local), "ctx", axis=1, tiled=True
            ),
            lax.all_gather(key_keep, "ctx", axis=1, tiled=True),
        )
        query_blocks = query_low.reshape(images, rows_dev, heads_local, HEAD_DIM)
        attended, log_total = lax.map(
            attend_forward, (query_blocks, keys_all, values_all, valid_all)
        )
        attended = attended.reshape(row_count, dim_local)
        head_normed, unit_two, spread_two = split_norm(
            attended, gains_head[layer_index], biases_head[layer_index, 2], model_width
        )
        head_low = head_normed.astype(jnp.bfloat16)
        branch = tensor_sum(contract_cols(head_low, mat_out))
        hidden_mid = hidden_state + row_keep * (branch + biases_norm[layer_index, 2])
        normed_two, unit_three, spread_three = local_norm(
            hidden_mid, gains_norm[layer_index, 1], biases_norm[layer_index, 1]
        )
        normed_two_low = normed_two.astype(jnp.bfloat16)
        gate_up = jnp.dot(
            normed_two_low,
            mat_gate_up.reshape(model_width, 2 * hidden_local),
            preferred_element_type=jnp.float32,
        ).reshape(row_count, 2, hidden_local)
        gate_pre = gate_up[:, 0] + biases_hidden[layer_index, 0]
        up_pre = gate_up[:, 1] + biases_hidden[layer_index, 1]
        inner_act = jax.nn.silu(gate_pre) * up_pre
        inner_normed, unit_four, spread_four = split_norm(
            inner_act, gains_hidden[layer_index], biases_hidden[layer_index, 2], FF
        )
        inner_low = inner_normed.astype(jnp.bfloat16)
        down_out = tensor_sum(contract_cols(inner_low, mat_down))
        hidden_state = hidden_mid + row_keep * (down_out + biases_norm[layer_index, 3])
        held_mats = None
        saved_layers.append(
            (
                held_mats,
                normed_low,
                unit_one,
                spread_one,
                query_blocks,
                keys_all,
                values_all,
                valid_all,
                log_total,
                unit_two,
                spread_two,
                head_low,
                unit_three,
                spread_three,
                normed_two_low,
                gate_pre,
                up_pre,
                unit_four,
                spread_four,
                inner_low,
            )
        )
    activations = hidden_state.reshape(images, rows_dev, model_width).astype(jnp.bfloat16)
    upstream = cotangent.astype(jnp.float32).reshape(row_count, model_width)
    mat_grads = [None] * layer_count
    vector_parts = [None] * layer_count
    for layer_index in reversed(range(layer_count)):
        (
            held_mats,
            normed_low,
            unit_one,
            spread_one,
            query_blocks,
            keys_all,
            values_all,
            valid_all,
            log_total,
            unit_two,
            spread_two,
            head_low,
            unit_three,
            spread_three,
            normed_two_low,
            gate_pre,
            up_pre,
            unit_four,
            spread_four,
            inner_low,
        ) = saved_layers[layer_index]
        mat_in, mat_out, mat_gate_up, mat_down = fetch_weights(
            layer_index, input_weight, output_weight, gate_up_weight, down_weight
        )
        grad_down = row_keep * upstream
        grad_bias_down = jnp.sum(grad_down, axis=0)
        grad_down_low = grad_down.astype(jnp.bfloat16)
        grad_mat_down = contract_rows(grad_down_low, inner_low)
        grad_inner_normed = jnp.dot(grad_down_low, mat_down, preferred_element_type=jnp.float32)
        grad_gain_hidden = jnp.sum(grad_inner_normed * unit_four, axis=0)
        grad_shift_hidden = jnp.sum(grad_inner_normed, axis=0)
        grad_inner = split_norm_back(
            grad_inner_normed, unit_four, spread_four, gains_hidden[layer_index], FF
        )
        sigmoid_gate = jax.nn.sigmoid(gate_pre)
        grad_up = grad_inner * gate_pre * sigmoid_gate
        grad_gate = grad_inner * up_pre * sigmoid_gate * (1.0 + gate_pre * (1.0 - sigmoid_gate))
        grad_gate_up_low = (
            jnp.stack([grad_gate, grad_up], axis=1)
            .astype(jnp.bfloat16)
            .reshape(row_count, 2 * hidden_local)
        )
        grad_mat_gate_up = contract_rows(normed_two_low, grad_gate_up_low).reshape(
            model_width, 2, hidden_local
        )
        grad_normed_two = tensor_back(
            contract_cols(grad_gate_up_low, mat_gate_up.reshape(model_width, 2 * hidden_local))
        )
        grad_gain_two = jnp.sum(grad_normed_two * unit_three, axis=0)
        grad_shift_two = jnp.sum(grad_normed_two, axis=0)
        upstream = upstream + local_norm_back(
            grad_normed_two, unit_three, spread_three, gains_norm[layer_index, 1]
        )
        grad_branch = row_keep * upstream
        grad_bias_out = jnp.sum(grad_branch, axis=0)
        grad_branch_low = grad_branch.astype(jnp.bfloat16)
        grad_mat_out = contract_rows(grad_branch_low, head_low)
        grad_head = jnp.dot(grad_branch_low, mat_out, preferred_element_type=jnp.float32)
        grad_gain_head = jnp.sum(grad_head * unit_two, axis=0)
        grad_shift_head = jnp.sum(grad_head, axis=0)
        grad_attended = split_norm_back(
            grad_head, unit_two, spread_two, gains_head[layer_index], model_width
        )
        grad_att_low = grad_attended.astype(jnp.bfloat16).reshape(
            images, rows_dev, heads_local, HEAD_DIM
        )
        grad_query_rot, grad_keys_all, grad_values_all = lax.map(
            attend_backward,
            (query_blocks, keys_all, values_all, valid_all, log_total, grad_att_low),
        )
        grad_keys_rot, grad_values = (
            lax.psum_scatter(
                grad_keys_all.astype(jnp.bfloat16), "ctx", scatter_dimension=1, tiled=True
            ).astype(jnp.float32),
            lax.psum_scatter(
                grad_values_all.astype(jnp.bfloat16), "ctx", scatter_dimension=1, tiled=True
            ).astype(jnp.float32),
        )
        grad_queries = rotate(
            grad_query_rot.reshape(row_count, heads_local, HEAD_DIM), cosine, sine, -1.0
        ).reshape(row_count, dim_local)
        grad_keys = rotate(
            grad_keys_rot.reshape(row_count, heads_local, HEAD_DIM), cosine, sine, -1.0
        ).reshape(row_count, dim_local)
        grad_values = grad_values.reshape(row_count, dim_local)
        grad_proj_low = (
            jnp.stack([grad_queries, grad_keys, grad_values], axis=1)
            .astype(jnp.bfloat16)
            .reshape(row_count, 3 * dim_local)
        )
        grad_mat_in = contract_rows(normed_low, grad_proj_low).reshape(model_width, 3, dim_local)
        grad_normed_one = tensor_back(
            contract_cols(grad_proj_low, mat_in.reshape(model_width, 3 * dim_local))
        )
        grad_gain_one = jnp.sum(grad_normed_one * unit_one, axis=0)
        grad_shift_one = jnp.sum(grad_normed_one, axis=0)
        upstream = upstream + local_norm_back(
            grad_normed_one, unit_one, spread_one, gains_norm[layer_index, 0]
        )
        mat_grads[layer_index] = (
            lax.psum_scatter(grad_mat_in, ("dp", "ctx"), scatter_dimension=0, tiled=True),
            lax.psum_scatter(grad_mat_out, ("dp", "ctx"), scatter_dimension=0, tiled=True),
            lax.psum_scatter(grad_mat_gate_up, ("dp", "ctx"), scatter_dimension=0, tiled=True),
            lax.psum_scatter(grad_mat_down, ("dp", "ctx"), scatter_dimension=0, tiled=True),
        )
        vector_parts[layer_index] = (
            jnp.stack([grad_gain_one, grad_gain_two]),
            jnp.stack([grad_shift_one, grad_shift_two, grad_bias_out, grad_bias_down]),
            grad_gain_head,
            jnp.stack(
                [jnp.sum(grad_queries, axis=0), jnp.sum(grad_values, axis=0), grad_shift_head]
            ),
            grad_gain_hidden,
            jnp.stack([jnp.sum(grad_gate, axis=0), jnp.sum(grad_up, axis=0), grad_shift_hidden]),
        )
    input_grad = (row_keep * upstream).reshape(images, rows_dev, model_width)
    stacked_vectors = tuple(
        (
            jnp.stack([vector_parts[index][member] for index in range(layer_count)])
            for member in range(6)
        )
    )
    summed_vectors = lax.psum(
        (
            stacked_vectors[0],
            stacked_vectors[1],
            stacked_vectors[2],
            stacked_vectors[3],
            stacked_vectors[4],
            stacked_vectors[5],
        ),
        ("dp", "ctx"),
    )
    grad_input_weight = jnp.stack([mat_grads[index][0] for index in range(layer_count)])
    grad_output_weight = jnp.stack([mat_grads[index][1] for index in range(layer_count)])
    grad_gate_up_weight = jnp.stack([mat_grads[index][2] for index in range(layer_count)])
    grad_down_weight = jnp.stack([mat_grads[index][3] for index in range(layer_count)])
    return (
        activations,
        input_grad,
        grad_input_weight,
        grad_output_weight,
        grad_gate_up_weight,
        grad_down_weight,
        summed_vectors[0],
        summed_vectors[1],
        summed_vectors[2],
        summed_vectors[3],
        summed_vectors[4],
        summed_vectors[5],
    )


MESH=pl.DeviceIdType.MESH
RB=64

class Where:
    def __init__(self):
        self.dp=lax.axis_index("dp"); self.x=lax.axis_index("ctx"); self.c=lax.axis_index("tp")
        self.z=self.dp//2; self.y=self.dp%2
    def nx(self): return (self.dp,1-self.x,self.c)
    def ny(self): return (self.z*2+1-self.y,self.x,self.c)
    def up(self): return ((self.z+1)*2+self.y,self.x,self.c)
    def dn(self): return ((self.z-1)*2+self.y,self.x,self.c)

def greet(w):
    bar=pltpu.get_barrier_semaphore()
    def sig(dev): pl.semaphore_signal(bar,inc=1,device_id=dev,device_id_type=MESH)
    sig(w.nx()); sig(w.ny())
    @pl.when(w.z<3)
    def _(): sig(w.up())
    @pl.when(w.z>0)
    def _(): sig(w.dn())
    pl.semaphore_wait(bar,2+(w.z<3).astype(jnp.int32)+(w.z>0).astype(jnp.int32))

class Gather:
    def __init__(self,w,order,src,out,r0,nr,ssem,rsem,own_sem):
        self.w,self.order,self.src,self.out,self.r0,self.nr=w,order,src,out,r0,nr
        self.ssem,self.rsem=ssem,rsem
        self.pending=[]
    def rows(self,zz,yy,xx):
        return pl.ds(pl.multiple_of(((zz*2+yy)*2+xx)*RB+self.r0,16),self.nr)
    def here(self,zz,yy,xx,own=False):
        return self.src.at[pl.ds(self.r0,self.nr)] if own else self.out.at[self.rows(zz,yy,xx)]
    def copy(self,zz,yy,xx,dev,s,r,own=False):
        return pltpu.make_async_remote_copy(src_ref=self.here(zz,yy,xx,own),dst_ref=self.out.at[self.rows(zz,yy,xx)],
            send_sem=self.ssem.at[s],recv_sem=self.rsem.at[r],device_id=dev,device_id_type=MESH)
    def send(self,cond,*a,**k):
        self.pending.append((cond,a,k))
        if cond is None: self.copy(*a,**k).start()
        else:
            @pl.when(cond)
            def _(): self.copy(*a,**k).start()
    def finish_sends(self):
        for cond,a,k in self.pending:
            if cond is None: self.copy(*a,**k).wait_send()
            else:
                @pl.when(cond)
                def _(a=a,k=k): self.copy(*a,**k).wait_send()
    def arrived(self,zz,yy,xx,r):
        self.copy(zz,yy,xx,self.w.nx(),0,r).wait_recv()

class GatherZ(Gather):
    def pq(self,zz,pself):
        w=self.w
        if self.order=="zyx": return (zz,w.y if pself else 1-w.y,w.x)
        return (zz,w.y,w.x if pself else 1-w.x)
    def pdev(self): return self.w.ny() if self.order=="zyx" else self.w.nx()
    def qdev(self): return self.w.nx() if self.order=="zyx" else self.w.ny()
    def qcoord(self,zz,pself):
        w=self.w
        if self.order=="zyx": return (zz,w.y if pself else 1-w.y,1-w.x)
        return (zz,1-w.y,w.x if pself else 1-w.x)
    def emit(self,cond,zz,k,own=False):
        b=self.pq(zz,True)
        w=self.w
        if k<4:
            c=(w.z<3) if cond is None else jnp.logical_and(cond,w.z<3)
            self.send(c,*b,w.up(),k,zz,own=own)
        if k==0 or k>=4:
            c=(w.z>0) if cond is None else jnp.logical_and(cond,w.z>0)
            self.send(c,*b,w.dn(),7+(k if k==0 else k-3),zz,own=own)
        self.send(cond,*b,self.pdev(),11+k,4+zz,own=own)
        self.send(cond,*b,self.qdev(),18+k,8+zz*2,own=own)
    def rounds(self):
        w=self.w
        self.emit(None,w.z,0,own=True)
        yield
        for k in (1,2,3,4):
            if k<4:
                for kk,zz,cond in ((k,w.z-k,w.z>=k),(k+3,w.z+k,w.z+k<=3)):
                    @pl.when(cond)
                    def _(zz=zz): self.arrived(*self.pq(zz,True),zz)
                    self.emit(cond,zz,kk)
            for kk,zz,cond in (((0,w.z,None),) if k==1 else ((k-1,w.z-k+1,w.z>=k-1),(k+2,w.z+k-1,w.z+k-1<=3))):
                b=self.pq(zz,False)
                def go(zz=zz,b=b): self.arrived(*b,4+zz)
                if cond is None: go()
                else: pl.when(cond)(go)
                self.send(cond,*b,self.qdev(),25+kk,8+zz*2+1)
            yield
    def finish(self):
        for zz in range(4):
            for pself in (True,False):
                self.arrived(*self.qcoord(zz,pself),8+zz*2+(0 if pself else 1))
        self.finish_sends()
    NS,NR=32,16

class GatherX(Gather):
    NS,NR=3+4*7,19
    def blk(self,zz,j):
        w=self.w
        return (zz,w.y if j<2 else 1-w.y,w.x if j%2==0 else 1-w.x)
    def vert(self,cond,zz,j,k,own=False):
        w=self.w; b=self.blk(zz,j)
        if k<4:
            c=(w.z<3) if cond is None else jnp.logical_and(cond,w.z<3)
            self.send(c,*b,w.up(),3+j*7+k if k else 3+j*7,3+zz*4+j,own=own)
        if k==0 or k>=4:
            c=(w.z>0) if cond is None else jnp.logical_and(cond,w.z>0)
            self.send(c,*b,w.dn(),3+j*7+(k if k>=4 else 3),3+zz*4+j,own=own)
    def rounds(self):
        w=self.w
        self.send(None,*self.blk(w.z,0),w.nx(),0,0,own=True)
        self.send(None,*self.blk(w.z,0),w.ny(),1,1,own=True)
        self.vert(None,w.z,0,0,own=True)
        yield
        b=self.blk(w.z,1); self.arrived(*b,0)
        self.send(None,*b,w.ny(),2,2)
        self.vert(None,w.z,1,0)
        self.arrived(*self.blk(w.z,2),1)
        self.vert(None,w.z,2,0)
        yield
        self.arrived(*self.blk(w.z,3),2)
        self.vert(None,w.z,3,0)
        yield
        for k in (1,2,3):
            for j in range(4):
                for kk,zz,cond in ((k,w.z-k,w.z>=k),(k+3,w.z+k,w.z+k<=3)):
                    @pl.when(cond)
                    def _(zz=zz,j=j): self.arrived(*self.blk(zz,j),3+zz*4+j)
                    if k<3: self.vert(cond,zz,j,kk)
                if j%2==1: yield
    def finish(self):
        self.finish_sends()

def interleave(gens):
    gens=list(gens)
    while gens:
        for g in list(gens):
            try: next(g)
            except StopIteration: gens.remove(g)

def ag_kernel(nz,nx,*refs):
    n=nz+nx
    srcs,outs=refs[:n],refs[n:2*n]; sems=refs[2*n:]
    w=Where()
    greet(w)
    parts=[];i=0
    me=(w.dp*2+w.x)*RB
    locs=[]
    for a in range(n):
        lc=pltpu.make_async_copy(srcs[a],outs[a].at[pl.ds(pl.multiple_of(me,16),RB)],sems[-1].at[a]); lc.start(); locs.append(lc)
        if a<nz:
            parts.append(GatherZ(w,"zyx",srcs[a],outs[a],0,32,sems[i],sems[i+1],None)); i+=2
            parts.append(GatherZ(w,"zxy",srcs[a],outs[a],32,32,sems[i],sems[i+1],None)); i+=2
        else:
            parts.append(GatherX(w,"xyz",srcs[a],outs[a],0,64,sems[i],sems[i+1],None)); i+=2
    interleave([p.rounds() for p in parts])
    for p in parts: p.finish()
    for lc in locs: lc.wait()

def all_gather(zs,xs,cid):
    arrs=list(zs)+list(xs)
    sems=[]
    for a in range(len(arrs)):
        if a<len(zs): sems+=[pltpu.SemaphoreType.DMA((GatherZ.NS,)),pltpu.SemaphoreType.DMA((GatherZ.NR,))]*2
        else: sems+=[pltpu.SemaphoreType.DMA((GatherX.NS,)),pltpu.SemaphoreType.DMA((GatherX.NR,))]
    sems.append(pltpu.SemaphoreType.DMA((len(arrs),)))
    return pl.pallas_call(functools.partial(ag_kernel,len(zs),len(xs)),
        out_shape=[jax.ShapeDtypeStruct((16*RB,a.shape[1]),a.dtype) for a in arrs],
        in_specs=[pl.BlockSpec(memory_space=pl.ANY)]*len(arrs),
        out_specs=[pl.BlockSpec(memory_space=pl.ANY)]*len(arrs),
        scratch_shapes=sems,
        compiler_params=pltpu.CompilerParams(collective_id=cid,has_side_effects=True),name=f"gather{cid}")(*arrs)


ZORD=(3,0,2,1)
class Scatter:
    def __init__(self,w,order,src,out,r0,nr,ssem,rsem,lsem,own,bufs):
        self.w,self.order,self.src,self.out,self.r0,self.nr=w,order,src,out,r0,nr
        self.ssem,self.rsem,self.lsem,self.own=ssem,rsem,lsem,own
        self.bufs=bufs
        self.pending=[]
    def rows(self,zz,yy,xx):
        return pl.ds(pl.multiple_of(((zz*2+yy)*2+xx)*RB+self.r0,16),self.nr)
    def send(self,cond,src,dst,dev,s,r):
        mk=lambda: pltpu.make_async_remote_copy(src_ref=src,dst_ref=dst,send_sem=self.ssem.at[s],recv_sem=self.rsem.at[r],device_id=dev,device_id_type=MESH)
        self.pending.append((cond,mk))
        if cond is None: mk().start()
        else: pl.when(cond)(lambda: mk().start())
    def wait(self,cond,dst,r):
        def go(): pltpu.make_async_remote_copy(src_ref=dst,dst_ref=dst,send_sem=self.ssem.at[0],recv_sem=self.rsem.at[r],device_id=self.w.nx(),device_id_type=MESH).wait_recv()
        if cond is None: go()
        else: pl.when(cond)(go)
    def finish(self):
        for cond,mk in self.pending:
            if cond is None: mk().wait_send()
            else: pl.when(cond)(lambda mk=mk: mk().wait_send())
    def total(self,dst,terms,extra=()):
        def strip(i,_):
            s=pl.ds(pl.multiple_of(i*16,16),16)
            t=terms[0][s].astype(jnp.float32)
            for r in terms[1:]: t=t+r[s].astype(jnp.float32)
            dst[s]=t.astype(dst.dtype)
            return 0
        lax.fori_loop(0,self.nr//16,strip,0)

class ScatterZ(Scatter):
    NS,NR=16,20
    def mine(self,zz,pself):
        w=self.w
        if self.order=="zyx": return (zz,w.y if pself else 1-w.y,w.x)
        return (zz,w.y,w.x if pself else 1-w.x)
    def theirs(self,zz,pself):
        w=self.w
        if self.order=="zyx": return (zz,w.y if pself else 1-w.y,1-w.x)
        return (zz,1-w.y,w.x if pself else 1-w.x)
    def rounds(self):
        w=self.w; rq,rp,ru,rd=self.bufs
        pdev=w.ny() if self.order=="zyx" else w.nx()
        qdev=w.nx() if self.order=="zyx" else w.ny()
        self.loc=[]
        for zz in ZORD:
            for k in (1,0):
                self.send(None,self.src.at[self.rows(*self.theirs(zz,k==0))],rq.at[zz*2+k],qdev,zz*2+k,zz*2+k)
            for k in (1,0):
                c=pltpu.make_async_copy(self.src.at[self.rows(*self.mine(zz,k==0))],self.own.at[zz*2+k],self.lsem.at[zz*2+k]); c.start(); self.loc.append((zz*2+k,c))
        loc=dict(self.loc)
        yield
        for zz in ZORD:
            i=zz*2+1
            loc[i].wait(); self.wait(None,rq.at[i],i)
            self.total(rq.at[i],[self.own.at[i],rq.at[i]])
            self.send(None,rq.at[i],rp.at[zz],pdev,8+zz,8+zz)
            yield
        for zz in ZORD:
            i=zz*2
            loc[i].wait(); self.wait(None,rq.at[i],i)
            self.wait(None,rp.at[zz],8+zz)
            base=[self.own.at[i],rq.at[i],rp.at[zz]]
            if zz>0:
                @pl.when(w.z==0)
                def _(): self.total(rp.at[zz],base)
                @pl.when(jnp.logical_and(w.z>0,w.z<zz))
                def _():
                    self.wait(None,ru.at[zz],12+zz)
                    self.total(rp.at[zz],base+[ru.at[zz]])
                self.send(w.z<zz,rp.at[zz],ru.at[zz],w.up(),12+zz,12+zz)
            if zz<3:
                @pl.when(w.z==3)
                def _(): self.total(rp.at[zz],base)
                @pl.when(jnp.logical_and(w.z<3,w.z>zz))
                def _():
                    self.wait(None,rd.at[zz],16+zz)
                    self.total(rp.at[zz],base+[rd.at[zz]])
                self.send(w.z>zz,rp.at[zz],rd.at[zz],w.dn(),12+zz,16+zz)
            yield
        o=self.out.at[pl.ds(self.r0,self.nr)]
        for zz in range(4):
            base=[self.own.at[zz*2],rq.at[zz*2],rp.at[zz]]
            if zz>0: base=base+[ru.at[zz]]
            if zz<3: base=base+[rd.at[zz]]
            @pl.when(w.z==zz)
            def _():
                if zz>0: self.wait(None,ru.at[zz],12+zz)
                if zz<3: self.wait(None,rd.at[zz],16+zz)
                self.total(o,base)
        yield

class ScatterX(Scatter):
    NS,NR=19,35
    def blk(self,zz,j):
        w=self.w
        return (zz,w.y if j<2 else 1-w.y,w.x if j%2==0 else 1-w.x)
    def rounds(self):
        w=self.w; ru,rd,ry,rx=self.bufs
        loc={}
        for zz in ZORD:
            for j in (3,2,1,0):
                i=zz*4+j
                c=pltpu.make_async_copy(self.src.at[self.rows(*self.blk(zz,j))],self.own.at[i],self.lsem.at[i]); c.start(); loc[i]=c
        for j in (3,2,1,0):
            for zz in ZORD:
                i=zz*4+j
                if zz>0: self.send(w.z==0,self.src.at[self.rows(*self.blk(zz,j))],ru.at[i],w.up(),i,i)
                if zz<3: self.send(w.z==3,self.src.at[self.rows(*self.blk(zz,j))],rd.at[i],w.dn(),i,16+i)
        for i in loc: loc[i].wait()
        yield
        for j in (3,2,1,0):
            for zz in ZORD:
                i=zz*4+j
                if zz>1:
                    cu=jnp.logical_and(w.z>0,w.z<zz)
                    @pl.when(cu)
                    def _():
                        self.wait(None,ru.at[i],i)
                        self.total(ru.at[i],[self.own.at[i],ru.at[i]])
                    self.send(cu,ru.at[i],ru.at[i],w.up(),i,i)
                if zz<2:
                    cd=jnp.logical_and(w.z<3,w.z>zz)
                    @pl.when(cd)
                    def _():
                        self.wait(None,rd.at[i],16+i)
                        self.total(rd.at[i],[self.own.at[i],rd.at[i]])
                    self.send(cd,rd.at[i],rd.at[i],w.dn(),i,16+i)
            yield
        def zsum(j,dst,extra):
            for zz in range(4):
                i=zz*4+j
                t=[self.own.at[i]]
                if zz>0: t.append(ru.at[i])
                if zz<3: t.append(rd.at[i])
                @pl.when(w.z==zz)
                def _():
                    if zz>0: self.wait(None,ru.at[i],i)
                    if zz<3: self.wait(None,rd.at[i],16+i)
                    self.total(dst,t+extra)
        sy=self.bufs_stage
        for j in (3,2):
            k=j-2
            zsum(j,sy.at[k],[])
            self.send(None,sy.at[k],ry.at[k],w.ny(),16+k,32+k)
        yield
        self.wait(None,ry.at[1],33)
        zsum(1,sy.at[2],[ry.at[1]])
        self.send(None,sy.at[2],rx.at[0],w.nx(),18,34)
        yield
        self.wait(None,ry.at[0],32)
        self.wait(None,rx.at[0],34)
        zsum(0,self.out.at[pl.ds(self.r0,self.nr)],[ry.at[0],rx.at[0]])
        yield

def rs_kernel(nz,nx,*refs):
    n=nz+nx
    srcs,outs=refs[:n],refs[n:2*n]; sc=list(refs[2*n:])
    w=Where(); greet(w)
    parts=[]
    for a in range(n):
        if a<nz:
            for h,o in ((0,"zyx"),(1,"zxy")):
                ss,rs,ls,own,rq,rp,ru,rd=[sc.pop(0) for _ in range(8)]
                parts.append(ScatterZ(w,o,srcs[a],outs[a],h*32,32,ss,rs,ls,own,(rq,rp,ru,rd)))
        else:
            ss,rs,ls,own,ru,rd,ry,rx,st=[sc.pop(0) for _ in range(9)]
            p=ScatterX(w,"xyz",srcs[a],outs[a],0,64,ss,rs,ls,own,(ru,rd,ry,rx)); p.bufs_stage=st
            parts.append(p)
    interleave([p.rounds() for p in parts])
    for p in parts: p.finish()

def reduce_scatter(zs,xs,cid):
    arrs=list(zs)+list(xs); sc=[]
    D=pltpu.SemaphoreType.DMA; V=lambda *s: pltpu.VMEM(s,jnp.bfloat16)
    for a,v in enumerate(arrs):
        C=v.shape[1]
        if a<len(zs):
            for _ in range(2): sc+=[D((ScatterZ.NS,)),D((ScatterZ.NR,)),D((8,)),V(8,32,C),V(8,32,C),V(4,32,C),V(4,32,C),V(4,32,C)]
        else: sc+=[D((ScatterX.NS,)),D((ScatterX.NR,)),D((16,)),V(16,64,C),V(16,64,C),V(16,64,C),V(2,64,C),V(1,64,C),V(3,64,C)]
    return pl.pallas_call(functools.partial(rs_kernel,len(zs),len(xs)),
        out_shape=[jax.ShapeDtypeStruct((RB,v.shape[1]),jnp.float32) for v in arrs],
        in_specs=[pl.BlockSpec(memory_space=pl.ANY)]*len(arrs),
        out_specs=[pl.BlockSpec(memory_space=pltpu.VMEM)]*len(arrs),
        scratch_shapes=sc,
        compiler_params=pltpu.CompilerParams(collective_id=cid,has_side_effects=True,vmem_limit_bytes=56*2**20),name=f"scatter{cid}")(*arrs)


HP = 1408
XPERM = [(0, 1), (1, 0)]


def swap_tp(v):
    return lax.ppermute(v, "tp", XPERM)


def swap_ctx(v):
    return lax.ppermute(v, "ctx", XPERM)


def pair_sum(partial):
    low = partial.astype(jnp.bfloat16)
    return low.astype(jnp.float32) + swap_tp(low).astype(jnp.float32)


def pair_totals(first, second):
    both = jnp.stack([jnp.sum(first, axis=-1), jnp.sum(second, axis=-1)])
    both = both + swap_tp(both)
    return both[0][:, None], both[1][:, None]


def cut_norm(values, gain_vec, shift_vec, full_width):
    s1, s2 = pair_totals(values, values * values)
    mean = s1 / full_width
    inv = lax.rsqrt(s2 / full_width - mean * mean + norm_epsilon)
    unit = (values - mean) * inv
    return unit * gain_vec + shift_vec, unit, inv


def cut_norm_back(upstream, unit, inv, gain_vec, full_width):
    weighted = upstream * gain_vec
    s1, s2 = pair_totals(weighted, weighted * unit)
    return inv * (weighted - s1 / full_width - unit * (s2 / full_width))


def fast_device(
    tokens_in,
    cotangent,
    key_mask,
    grid_pos,
    class_index,
    input_weight,
    output_weight,
    gate_up_weight,
    down_weight,
    norm_gains,
    norm_biases,
    head_gains,
    head_biases,
    hidden_gains,
    hidden_biases,
):
    _, rows, model_width = tokens_in.shape
    dim = head_gains.shape[1]
    heads = dim // HEAD_DIM
    hidden = hidden_gains.shape[1]
    layers = input_weight.shape[0]
    pad = HP - hidden
    f32 = jnp.float32
    bf = jnp.bfloat16
    places = lax.axis_index("ctx") * rows + jnp.arange(rows, dtype=jnp.int32)
    not_class = (places != class_index[0]).astype(f32)
    cosine, sine = rotary_tables(grid_pos.reshape(2, rows), not_class)
    keep = key_mask.astype(f32).reshape(rows, 1)
    keep_low = key_mask.astype(bf).reshape(rows)
    valid_all = jnp.concatenate([keep_low, swap_ctx(keep_low)])
    gn = norm_gains.astype(f32)
    bn = norm_biases.astype(f32)
    gh = head_gains.astype(f32)
    bh = head_biases.astype(f32)
    gf = jnp.pad(hidden_gains.astype(f32), ((0, 0), (0, pad)))
    bfb = jnp.pad(hidden_biases.astype(f32), ((0, 0), (0, 0), (0, pad)))
    gu = jnp.pad(gate_up_weight, ((0, 0), (0, 0), (0, 0), (0, pad)))
    first = jnp.concatenate(
        [
            input_weight.reshape(layers, RB, 3 * dim),
            output_weight,
            gu.reshape(layers, RB, 2 * HP),
        ],
        axis=2,
    )
    second = jnp.pad(down_weight, ((0, 0), (0, 0), (0, pad)))
    mats = []
    for l in range(layers):
        big, small = all_gather([first[l]], [second[l]], l)
        mats.append((big[:, : 3 * dim], big[:, 3 * dim : 4 * dim], big[:, 4 * dim :], small))
    h = tokens_in.astype(f32).reshape(rows, model_width) * keep
    saved = []
    for l in range(layers):
        w_in, w_out, w_gu, w_dn = mats[l]
        n1, unit1, inv1 = local_norm(h, gn[l, 0], bn[l, 0])
        n1 = n1.astype(bf)
        proj = jnp.dot(n1, w_in, preferred_element_type=f32)
        q = rotate((proj[:, :dim] + bh[l, 0]).reshape(rows, heads, HEAD_DIM), cosine, sine, 1.0)
        k = rotate(proj[:, dim : 2 * dim].reshape(rows, heads, HEAD_DIM), cosine, sine, 1.0)
        q = q.astype(bf)
        k = k.astype(bf).reshape(rows, dim)
        v = (proj[:, 2 * dim :] + bh[l, 1]).astype(bf)
        k_all = jnp.concatenate([k, swap_ctx(k)])
        v_all = jnp.concatenate([v, swap_ctx(v)])
        att, log_total = attend_forward((q, k_all, v_all, valid_all))
        u, unit2, inv2 = cut_norm(att, gh[l], bh[l, 2], model_width)
        u = u.astype(bf)
        branch = pair_sum(contract_cols(u, w_out))
        h = h + keep * (branch + bn[l, 2])
        n2, unit3, inv3 = local_norm(h, gn[l, 1], bn[l, 1])
        n2 = n2.astype(bf)
        both = jnp.dot(n2, w_gu, preferred_element_type=f32)
        gate = both[:, :HP] + bfb[l, 0]
        up = both[:, HP:] + bfb[l, 1]
        zn, unit4, inv4 = cut_norm(jax.nn.silu(gate) * up, gf[l], bfb[l, 2], FF)
        zn = zn.astype(bf)
        h = h + keep * (pair_sum(contract_cols(zn, w_dn)) + bn[l, 3])
        saved.append(
            (n1, unit1, inv1, q, k_all, v_all, log_total, unit2, inv2, u, unit3, inv3, n2, gate, up, unit4, inv4, zn)
        )
    activations = h.astype(bf).reshape(1, rows, model_width)
    g = cotangent.astype(f32).reshape(rows, model_width)
    mat_grads = [None] * layers
    vectors = [None] * layers
    for l in reversed(range(layers)):
        (n1, unit1, inv1, q, k_all, v_all, log_total, unit2, inv2, u, unit3, inv3, n2, gate, up, unit4, inv4, zn) = saved[l]
        w_in, w_out, w_gu, w_dn = mats[l]
        e = keep * g
        d_bias_down = jnp.sum(e, axis=0)
        el = e.astype(bf)
        d_down = contract_rows(el, zn).astype(bf)
        ezn = jnp.dot(el, w_dn, preferred_element_type=f32)
        d_gain_hidden = jnp.sum(ezn * unit4, axis=0)
        d_shift_hidden = jnp.sum(ezn, axis=0)
        ez = cut_norm_back(ezn, unit4, inv4, gf[l], FF)
        sg = jax.nn.sigmoid(gate)
        eu = ez * gate * sg
        eg = ez * up * sg * (1.0 + gate * (1.0 - sg))
        egu = jnp.concatenate([eg.astype(bf), eu.astype(bf)], axis=1)
        d_gu = contract_rows(n2, egu).astype(bf)
        en2 = pair_sum(contract_cols(egu, w_gu))
        d_gain2 = jnp.sum(en2 * unit3, axis=0)
        d_shift2 = jnp.sum(en2, axis=0)
        g = g + local_norm_back(en2, unit3, inv3, gn[l, 1])
        e = keep * g
        d_bias_out = jnp.sum(e, axis=0)
        el = e.astype(bf)
        d_out = contract_rows(el, u).astype(bf)
        ehead = jnp.dot(el, w_out, preferred_element_type=f32)
        d_gain_head = jnp.sum(ehead * unit2, axis=0)
        d_shift_head = jnp.sum(ehead, axis=0)
        eo = cut_norm_back(ehead, unit2, inv2, gh[l], model_width)
        eo = eo.astype(bf).reshape(rows, heads, HEAD_DIM)
        dq, dk_all, dv_all = attend_backward((q, k_all, v_all, valid_all, log_total, eo))
        dk = dk_all[:rows] + swap_ctx(dk_all[rows:].astype(bf)).astype(f32)
        dv = dv_all[:rows] + swap_ctx(dv_all[rows:].astype(bf)).astype(f32)
        dq = rotate(dq.reshape(rows, heads, HEAD_DIM), cosine, sine, -1.0).reshape(rows, dim)
        dk = rotate(dk.reshape(rows, heads, HEAD_DIM), cosine, sine, -1.0).reshape(rows, dim)
        ep = jnp.concatenate([dq.astype(bf), dk.astype(bf), dv.astype(bf)], axis=1)
        d_in = contract_rows(n1, ep).astype(bf)
        en1 = pair_sum(contract_cols(ep, w_in))
        d_gain1 = jnp.sum(en1 * unit1, axis=0)
        d_shift1 = jnp.sum(en1, axis=0)
        g = g + local_norm_back(en1, unit1, inv1, gn[l, 0])
        mat_grads[l] = reduce_scatter([jnp.concatenate([d_in, d_out, d_gu], axis=1)], [d_down], 2 + l)
        vectors[l] = (
            jnp.stack([d_gain1, d_gain2]),
            jnp.stack([d_shift1, d_shift2, d_bias_out, d_bias_down]),
            d_gain_head,
            jnp.stack([jnp.sum(dq, axis=0), jnp.sum(dv, axis=0), d_shift_head]),
            d_gain_hidden[:hidden],
            jnp.stack([jnp.sum(eg, axis=0), jnp.sum(eu, axis=0), d_shift_hidden])[:, :hidden],
        )
    input_grad = (keep * g).reshape(1, rows, model_width)
    stacked = tuple(jnp.stack([vectors[l][i] for l in range(layers)]) for i in range(6))
    summed = lax.psum(stacked, ("dp", "ctx"))
    bigs = [mat_grads[l][0] for l in range(layers)]
    g_in = jnp.stack([b[:, : 3 * dim].reshape(RB, 3, dim) for b in bigs])
    g_out = jnp.stack([b[:, 3 * dim : 4 * dim] for b in bigs])
    g_gu = jnp.stack([b[:, 4 * dim :].reshape(RB, 2, HP)[:, :, :hidden] for b in bigs])
    g_dn = jnp.stack([mat_grads[l][1][:, :hidden] for l in range(layers)])
    return (activations, input_grad, g_in, g_out, g_gu, g_dn) + summed


def solution(mesh):
    sizes = dict(mesh.shape)
    fits = sizes == {"dp": 8, "ctx": 2, "tp": 2}
    return jax.shard_map(
        fast_device if fits else on_device,
        mesh=mesh,
        in_specs=(
            P("dp", "ctx", None),
            P("dp", "ctx", None),
            P("dp", "ctx"),
            P(None, "dp", "ctx"),
            P("dp"),
            P(None, ("dp", "ctx"), None, "tp"),
            P(None, ("dp", "ctx"), "tp"),
            P(None, ("dp", "ctx"), None, "tp"),
            P(None, ("dp", "ctx"), "tp"),
            P(),
            P(),
            P(None, "tp"),
            P(None, None, "tp"),
            P(None, "tp"),
            P(None, None, "tp"),
        ),
        out_specs=(
            P("dp", "ctx", None),
            P("dp", "ctx", None),
            P(None, ("dp", "ctx"), None, "tp"),
            P(None, ("dp", "ctx"), "tp"),
            P(None, ("dp", "ctx"), None, "tp"),
            P(None, ("dp", "ctx"), "tp"),
            P(),
            P(),
            P(None, "tp"),
            P(None, None, "tp"),
            P(None, "tp"),
            P(None, None, "tp"),
        ),
        check_vma=False,
    )
```

```python
import functools

import jax
import jax.numpy as jnp
from jax import lax
from jax.experimental import pallas as pl
from jax.experimental.pallas import tpu as pltpu
from jax.sharding import PartitionSpec as P

FF = 2730
HEAD_DIM = 64


norm_epsilon = 1e-06
rotary_base = 10000.0
masked_score = -10000.0


def rotary_tables(positions, not_class):
    quarter = HEAD_DIM // 4
    frequency = rotary_base ** (-jnp.arange(quarter, dtype=jnp.float32) / quarter)
    angles = (
        jnp.transpose(positions).astype(jnp.float32)[:, :, None]
        * frequency
        * not_class[:, None, None]
    )
    return (jnp.cos(angles), jnp.sin(angles))


def rotate(values, cosine, sine, direction):
    row_count, head_count, head_dim = values.shape
    paired = values.reshape(row_count, head_count, 2, 2, head_dim // 4)
    first_half = paired[:, :, :, 0]
    second_half = paired[:, :, :, 1]
    cos_rows = cosine[:, None]
    sin_rows = sine[:, None] * direction
    turned = jnp.stack(
        [
            first_half * cos_rows - second_half * sin_rows,
            second_half * cos_rows + first_half * sin_rows,
        ],
        axis=3,
    )
    return turned.reshape(row_count, head_count, head_dim)


def local_norm(values, gain_vec, shift_vec):
    center = values - jnp.mean(values, axis=-1, keepdims=True)
    spread = jnp.mean(center * center, axis=-1, keepdims=True)
    inv_spread = lax.rsqrt(spread + norm_epsilon)
    unit_rows = center * inv_spread
    return (unit_rows * gain_vec + shift_vec, unit_rows, inv_spread)


def local_norm_back(upstream, unit_rows, inv_spread, gain_vec):
    weighted = upstream * gain_vec
    return inv_spread * (
        weighted
        - jnp.mean(weighted, axis=-1, keepdims=True)
        - unit_rows * jnp.mean(weighted * unit_rows, axis=-1, keepdims=True)
    )


def row_totals(first_part, second_part):
    return lax.psum(
        (jnp.sum(first_part, axis=-1, keepdims=True), jnp.sum(second_part, axis=-1, keepdims=True)),
        "tp",
    )


def split_norm(values, gain_vec, shift_vec, full_width):
    sum_first, sum_second = row_totals(values, values * values)
    row_mean = sum_first / full_width
    inv_spread = lax.rsqrt(sum_second / full_width - row_mean * row_mean + norm_epsilon)
    unit_rows = (values - row_mean) * inv_spread
    return (unit_rows * gain_vec + shift_vec, unit_rows, inv_spread)


def split_norm_back(upstream, unit_rows, inv_spread, gain_vec, full_width):
    weighted = upstream * gain_vec
    sum_first, sum_second = row_totals(weighted, weighted * unit_rows)
    return inv_spread * (weighted - sum_first / full_width - unit_rows * (sum_second / full_width))


def tensor_sum(partial_value):
    return lax.psum(partial_value.astype(jnp.bfloat16), "tp").astype(jnp.float32)


def tensor_back(partial_value):
    return lax.psum(partial_value.astype(jnp.bfloat16), "tp").astype(jnp.float32)


def fetch_weights(layer_index, input_weight, output_weight, gate_up_weight, down_weight):
    return (
        lax.all_gather(input_weight[layer_index], ("dp", "ctx"), axis=0, tiled=True),
        lax.all_gather(output_weight[layer_index], ("dp", "ctx"), axis=0, tiled=True),
        lax.all_gather(gate_up_weight[layer_index], ("dp", "ctx"), axis=0, tiled=True),
        lax.all_gather(down_weight[layer_index], ("dp", "ctx"), axis=0, tiled=True),
    )


def masked_scores(queries, key_heads, valid_keys):
    raw_scores = jnp.einsum("qhe,khe->hqk", queries, key_heads, preferred_element_type=jnp.float32)
    return jnp.where(valid_keys[None, None, :] > 0, raw_scores * HEAD_DIM ** (-0.5), masked_score)


def attend_forward(block_items):
    queries, keys_all, values_all, valid_keys = block_items
    key_count = keys_all.shape[0]
    head_count = queries.shape[1]
    key_heads = keys_all.reshape(key_count, head_count, HEAD_DIM)
    value_heads = values_all.reshape(key_count, head_count, HEAD_DIM)
    scores = masked_scores(queries, key_heads, valid_keys)
    row_max = jnp.max(scores, axis=-1, keepdims=True)
    exp_scores = jnp.exp(scores - row_max)
    row_total = jnp.sum(exp_scores, axis=-1, keepdims=True)
    attn_probs = (exp_scores / row_total).astype(jnp.bfloat16)
    attended = jnp.einsum(
        "hqk,khe->qhe", attn_probs, value_heads, preferred_element_type=jnp.float32
    )
    return (
        attended.reshape(queries.shape[0], head_count * HEAD_DIM),
        (row_max + jnp.log(row_total))[:, :, 0],
    )


def attend_backward(block_items):
    queries, keys_all, values_all, valid_keys, log_total, grad_out = block_items
    key_count = keys_all.shape[0]
    head_count = queries.shape[1]
    key_heads = keys_all.reshape(key_count, head_count, HEAD_DIM)
    value_heads = values_all.reshape(key_count, head_count, HEAD_DIM)
    scores = masked_scores(queries, key_heads, valid_keys)
    probs_full = jnp.exp(scores - log_total[:, :, None])
    probs_low = probs_full.astype(jnp.bfloat16)
    grad_probs = jnp.einsum(
        "qhe,khe->hqk", grad_out, value_heads, preferred_element_type=jnp.float32
    )
    row_dot = jnp.sum(probs_full * grad_probs, axis=-1, keepdims=True)
    grad_raw = jnp.where(
        valid_keys[None, None, :] > 0, HEAD_DIM ** (-0.5) * probs_full * (grad_probs - row_dot), 0.0
    ).astype(jnp.bfloat16)
    grad_queries = jnp.einsum(
        "hqk,khe->qhe", grad_raw, key_heads, preferred_element_type=jnp.float32
    )
    grad_keys = jnp.einsum("hqk,qhe->khe", grad_raw, queries, preferred_element_type=jnp.float32)
    grad_values = jnp.einsum(
        "hqk,qhe->khe", probs_low, grad_out, preferred_element_type=jnp.float32
    )
    local_rows = queries.shape[0]
    return (
        grad_queries.reshape(local_rows, head_count * HEAD_DIM),
        grad_keys.reshape(key_count, head_count * HEAD_DIM),
        grad_values.reshape(key_count, head_count * HEAD_DIM),
    )


def contract_rows(left, right):
    return lax.dot_general(
        left, right, (((0,), (0,)), ((), ())), preferred_element_type=jnp.float32
    )


def contract_cols(left, right):
    return lax.dot_general(
        left, right, (((1,), (1,)), ((), ())), preferred_element_type=jnp.float32
    )


def on_device(
    tokens_in,
    cotangent,
    key_mask,
    grid_pos,
    class_index,
    input_weight,
    output_weight,
    gate_up_weight,
    down_weight,
    norm_gains,
    norm_biases,
    head_gains,
    head_biases,
    hidden_gains,
    hidden_biases,
):
    images, rows_dev, model_width = tokens_in.shape
    row_count = images * rows_dev
    dim_local = head_gains.shape[1]
    heads_local = dim_local // HEAD_DIM
    hidden_local = hidden_gains.shape[1]
    layer_count = input_weight.shape[0]
    first_row = lax.axis_index("ctx") * rows_dev
    places = first_row + jnp.arange(rows_dev, dtype=jnp.int32)
    not_class = (places[None, :] != class_index[:, None]).astype(jnp.float32).reshape(row_count)
    cosine, sine = rotary_tables(grid_pos.reshape(2, row_count), not_class)
    row_keep = key_mask.astype(jnp.float32).reshape(row_count, 1)
    key_keep = key_mask.astype(jnp.bfloat16)
    gains_norm = norm_gains.astype(jnp.float32)
    biases_norm = norm_biases.astype(jnp.float32)
    gains_head = head_gains.astype(jnp.float32)
    biases_head = head_biases.astype(jnp.float32)
    gains_hidden = hidden_gains.astype(jnp.float32)
    biases_hidden = hidden_biases.astype(jnp.float32)
    hidden_state = tokens_in.astype(jnp.float32).reshape(row_count, model_width) * row_keep
    saved_layers = []
    for layer_index in range(layer_count):
        layer_mats = fetch_weights(
            layer_index, input_weight, output_weight, gate_up_weight, down_weight
        )
        mat_in, mat_out, mat_gate_up, mat_down = layer_mats
        normed, unit_one, spread_one = local_norm(
            hidden_state, gains_norm[layer_index, 0], biases_norm[layer_index, 0]
        )
        normed_low = normed.astype(jnp.bfloat16)
        projected = jnp.dot(
            normed_low,
            mat_in.reshape(model_width, 3 * dim_local),
            preferred_element_type=jnp.float32,
        ).reshape(row_count, 3, dim_local)
        queries = projected[:, 0] + biases_head[layer_index, 0]
        keys_proj = projected[:, 1]
        values_proj = projected[:, 2] + biases_head[layer_index, 1]
        query_low = rotate(
            queries.reshape(row_count, heads_local, HEAD_DIM), cosine, sine, 1.0
        ).astype(jnp.bfloat16)
        key_low = rotate(
            keys_proj.reshape(row_count, heads_local, HEAD_DIM), cosine, sine, 1.0
        ).astype(jnp.bfloat16)
        value_low = values_proj.astype(jnp.bfloat16)
        keys_all, values_all, valid_all = (
            lax.all_gather(key_low.reshape(images, rows_dev, dim_local), "ctx", axis=1, tiled=True),
            lax.all_gather(
                value_low.reshape(images, rows_dev, dim_local), "ctx", axis=1, tiled=True
            ),
            lax.all_gather(key_keep, "ctx", axis=1, tiled=True),
        )
        query_blocks = query_low.reshape(images, rows_dev, heads_local, HEAD_DIM)
        attended, log_total = lax.map(
            attend_forward, (query_blocks, keys_all, values_all, valid_all)
        )
        attended = attended.reshape(row_count, dim_local)
        head_normed, unit_two, spread_two = split_norm(
            attended, gains_head[layer_index], biases_head[layer_index, 2], model_width
        )
        head_low = head_normed.astype(jnp.bfloat16)
        branch = tensor_sum(contract_cols(head_low, mat_out))
        hidden_mid = hidden_state + row_keep * (branch + biases_norm[layer_index, 2])
        normed_two, unit_three, spread_three = local_norm(
            hidden_mid, gains_norm[layer_index, 1], biases_norm[layer_index, 1]
        )
        normed_two_low = normed_two.astype(jnp.bfloat16)
        gate_up = jnp.dot(
            normed_two_low,
            mat_gate_up.reshape(model_width, 2 * hidden_local),
            preferred_element_type=jnp.float32,
        ).reshape(row_count, 2, hidden_local)
        gate_pre = gate_up[:, 0] + biases_hidden[layer_index, 0]
        up_pre = gate_up[:, 1] + biases_hidden[layer_index, 1]
        inner_act = jax.nn.silu(gate_pre) * up_pre
        inner_normed, unit_four, spread_four = split_norm(
            inner_act, gains_hidden[layer_index], biases_hidden[layer_index, 2], FF
        )
        inner_low = inner_normed.astype(jnp.bfloat16)
        down_out = tensor_sum(contract_cols(inner_low, mat_down))
        hidden_state = hidden_mid + row_keep * (down_out + biases_norm[layer_index, 3])
        held_mats = None
        saved_layers.append(
            (
                held_mats,
                normed_low,
                unit_one,
                spread_one,
                query_blocks,
                keys_all,
                values_all,
                valid_all,
                log_total,
                unit_two,
                spread_two,
                head_low,
                unit_three,
                spread_three,
                normed_two_low,
                gate_pre,
                up_pre,
                unit_four,
                spread_four,
                inner_low,
            )
        )
    activations = hidden_state.reshape(images, rows_dev, model_width).astype(jnp.bfloat16)
    upstream = cotangent.astype(jnp.float32).reshape(row_count, model_width)
    mat_grads = [None] * layer_count
    vector_parts = [None] * layer_count
    for layer_index in reversed(range(layer_count)):
        (
            held_mats,
            normed_low,
            unit_one,
            spread_one,
            query_blocks,
            keys_all,
            values_all,
            valid_all,
            log_total,
            unit_two,
            spread_two,
            head_low,
            unit_three,
            spread_three,
            normed_two_low,
            gate_pre,
            up_pre,
            unit_four,
            spread_four,
            inner_low,
        ) = saved_layers[layer_index]
        mat_in, mat_out, mat_gate_up, mat_down = fetch_weights(
            layer_index, input_weight, output_weight, gate_up_weight, down_weight
        )
        grad_down = row_keep * upstream
        grad_bias_down = jnp.sum(grad_down, axis=0)
        grad_down_low = grad_down.astype(jnp.bfloat16)
        grad_mat_down = contract_rows(grad_down_low, inner_low)
        grad_inner_normed = jnp.dot(grad_down_low, mat_down, preferred_element_type=jnp.float32)
        grad_gain_hidden = jnp.sum(grad_inner_normed * unit_four, axis=0)
        grad_shift_hidden = jnp.sum(grad_inner_normed, axis=0)
        grad_inner = split_norm_back(
            grad_inner_normed, unit_four, spread_four, gains_hidden[layer_index], FF
        )
        sigmoid_gate = jax.nn.sigmoid(gate_pre)
        grad_up = grad_inner * gate_pre * sigmoid_gate
        grad_gate = grad_inner * up_pre * sigmoid_gate * (1.0 + gate_pre * (1.0 - sigmoid_gate))
        grad_gate_up_low = (
            jnp.stack([grad_gate, grad_up], axis=1)
            .astype(jnp.bfloat16)
            .reshape(row_count, 2 * hidden_local)
        )
        grad_mat_gate_up = contract_rows(normed_two_low, grad_gate_up_low).reshape(
            model_width, 2, hidden_local
        )
        grad_normed_two = tensor_back(
            contract_cols(grad_gate_up_low, mat_gate_up.reshape(model_width, 2 * hidden_local))
        )
        grad_gain_two = jnp.sum(grad_normed_two * unit_three, axis=0)
        grad_shift_two = jnp.sum(grad_normed_two, axis=0)
        upstream = upstream + local_norm_back(
            grad_normed_two, unit_three, spread_three, gains_norm[layer_index, 1]
        )
        grad_branch = row_keep * upstream
        grad_bias_out = jnp.sum(grad_branch, axis=0)
        grad_branch_low = grad_branch.astype(jnp.bfloat16)
        grad_mat_out = contract_rows(grad_branch_low, head_low)
        grad_head = jnp.dot(grad_branch_low, mat_out, preferred_element_type=jnp.float32)
        grad_gain_head = jnp.sum(grad_head * unit_two, axis=0)
        grad_shift_head = jnp.sum(grad_head, axis=0)
        grad_attended = split_norm_back(
            grad_head, unit_two, spread_two, gains_head[layer_index], model_width
        )
        grad_att_low = grad_attended.astype(jnp.bfloat16).reshape(
            images, rows_dev, heads_local, HEAD_DIM
        )
        grad_query_rot, grad_keys_all, grad_values_all = lax.map(
            attend_backward,
            (query_blocks, keys_all, values_all, valid_all, log_total, grad_att_low),
        )
        grad_keys_rot, grad_values = (
            lax.psum_scatter(
                grad_keys_all.astype(jnp.bfloat16), "ctx", scatter_dimension=1, tiled=True
            ).astype(jnp.float32),
            lax.psum_scatter(
                grad_values_all.astype(jnp.bfloat16), "ctx", scatter_dimension=1, tiled=True
            ).astype(jnp.float32),
        )
        grad_queries = rotate(
            grad_query_rot.reshape(row_count, heads_local, HEAD_DIM), cosine, sine, -1.0
        ).reshape(row_count, dim_local)
        grad_keys = rotate(
            grad_keys_rot.reshape(row_count, heads_local, HEAD_DIM), cosine, sine, -1.0
        ).reshape(row_count, dim_local)
        grad_values = grad_values.reshape(row_count, dim_local)
        grad_proj_low = (
            jnp.stack([grad_queries, grad_keys, grad_values], axis=1)
            .astype(jnp.bfloat16)
            .reshape(row_count, 3 * dim_local)
        )
        grad_mat_in = contract_rows(normed_low, grad_proj_low).reshape(model_width, 3, dim_local)
        grad_normed_one = tensor_back(
            contract_cols(grad_proj_low, mat_in.reshape(model_width, 3 * dim_local))
        )
        grad_gain_one = jnp.sum(grad_normed_one * unit_one, axis=0)
        grad_shift_one = jnp.sum(grad_normed_one, axis=0)
        upstream = upstream + local_norm_back(
            grad_normed_one, unit_one, spread_one, gains_norm[layer_index, 0]
        )
        mat_grads[layer_index] = (
            lax.psum_scatter(grad_mat_in, ("dp", "ctx"), scatter_dimension=0, tiled=True),
            lax.psum_scatter(grad_mat_out, ("dp", "ctx"), scatter_dimension=0, tiled=True),
            lax.psum_scatter(grad_mat_gate_up, ("dp", "ctx"), scatter_dimension=0, tiled=True),
            lax.psum_scatter(grad_mat_down, ("dp", "ctx"), scatter_dimension=0, tiled=True),
        )
        vector_parts[layer_index] = (
            jnp.stack([grad_gain_one, grad_gain_two]),
            jnp.stack([grad_shift_one, grad_shift_two, grad_bias_out, grad_bias_down]),
            grad_gain_head,
            jnp.stack(
                [jnp.sum(grad_queries, axis=0), jnp.sum(grad_values, axis=0), grad_shift_head]
            ),
            grad_gain_hidden,
            jnp.stack([jnp.sum(grad_gate, axis=0), jnp.sum(grad_up, axis=0), grad_shift_hidden]),
        )
    input_grad = (row_keep * upstream).reshape(images, rows_dev, model_width)
    stacked_vectors = tuple(
        (
            jnp.stack([vector_parts[index][member] for index in range(layer_count)])
            for member in range(6)
        )
    )
    summed_vectors = lax.psum(
        (
            stacked_vectors[0],
            stacked_vectors[1],
            stacked_vectors[2],
            stacked_vectors[3],
            stacked_vectors[4],
            stacked_vectors[5],
        ),
        ("dp", "ctx"),
    )
    grad_input_weight = jnp.stack([mat_grads[index][0] for index in range(layer_count)])
    grad_output_weight = jnp.stack([mat_grads[index][1] for index in range(layer_count)])
    grad_gate_up_weight = jnp.stack([mat_grads[index][2] for index in range(layer_count)])
    grad_down_weight = jnp.stack([mat_grads[index][3] for index in range(layer_count)])
    return (
        activations,
        input_grad,
        grad_input_weight,
        grad_output_weight,
        grad_gate_up_weight,
        grad_down_weight,
        summed_vectors[0],
        summed_vectors[1],
        summed_vectors[2],
        summed_vectors[3],
        summed_vectors[4],
        summed_vectors[5],
    )


MESH = pl.DeviceIdType.MESH

RB=64

class Where:
    def __init__(self):
        self.dp=lax.axis_index("dp"); self.x=lax.axis_index("ctx"); self.c=lax.axis_index("tp")
        self.z=self.dp//2; self.y=self.dp%2
    def nx(self): return (self.dp,1-self.x,self.c)
    def ny(self): return (self.z*2+1-self.y,self.x,self.c)
    def up(self): return ((self.z+1)*2+self.y,self.x,self.c)
    def dn(self): return ((self.z-1)*2+self.y,self.x,self.c)

def greet(w):
    bar=pltpu.get_barrier_semaphore()
    def sig(dev): pl.semaphore_signal(bar,inc=1,device_id=dev,device_id_type=MESH)
    sig(w.nx()); sig(w.ny())
    @pl.when(w.z<3)
    def _(): sig(w.up())
    @pl.when(w.z>0)
    def _(): sig(w.dn())
    pl.semaphore_wait(bar,2+(w.z<3).astype(jnp.int32)+(w.z>0).astype(jnp.int32))

class Gather:
    def __init__(self,w,order,src,out,r0,nr,ssem,rsem,own_sem):
        self.w,self.order,self.src,self.out,self.r0,self.nr=w,order,src,out,r0,nr
        self.ssem,self.rsem=ssem,rsem
        self.pending=[]
    def rows(self,zz,yy,xx):
        return pl.ds(pl.multiple_of(((zz*2+yy)*2+xx)*RB+self.r0,16),self.nr)
    def here(self,zz,yy,xx,own=False):
        return self.src.at[pl.ds(self.r0,self.nr)] if own else self.out.at[self.rows(zz,yy,xx)]
    def copy(self,zz,yy,xx,dev,s,r,own=False):
        return pltpu.make_async_remote_copy(src_ref=self.here(zz,yy,xx,own),dst_ref=self.out.at[self.rows(zz,yy,xx)],
            send_sem=self.ssem.at[s],recv_sem=self.rsem.at[r],device_id=dev,device_id_type=MESH)
    def send(self,cond,*a,**k):
        self.pending.append((cond,a,k))
        if cond is None: self.copy(*a,**k).start()
        else:
            @pl.when(cond)
            def _(): self.copy(*a,**k).start()
    def finish_sends(self):
        for cond,a,k in self.pending:
            if cond is None: self.copy(*a,**k).wait_send()
            else:
                @pl.when(cond)
                def _(a=a,k=k): self.copy(*a,**k).wait_send()
    def arrived(self,zz,yy,xx,r):
        self.copy(zz,yy,xx,self.w.nx(),0,r).wait_recv()

class GatherZ(Gather):
    def pq(self,zz,pself):
        w=self.w
        if self.order=="zyx": return (zz,w.y if pself else 1-w.y,w.x)
        return (zz,w.y,w.x if pself else 1-w.x)
    def pdev(self): return self.w.ny() if self.order=="zyx" else self.w.nx()
    def qdev(self): return self.w.nx() if self.order=="zyx" else self.w.ny()
    def qcoord(self,zz,pself):
        w=self.w
        if self.order=="zyx": return (zz,w.y if pself else 1-w.y,1-w.x)
        return (zz,1-w.y,w.x if pself else 1-w.x)
    def emit(self,cond,zz,k,own=False):
        b=self.pq(zz,True)
        w=self.w
        if k<4:
            c=(w.z<3) if cond is None else jnp.logical_and(cond,w.z<3)
            self.send(c,*b,w.up(),k,zz,own=own)
        if k==0 or k>=4:
            c=(w.z>0) if cond is None else jnp.logical_and(cond,w.z>0)
            self.send(c,*b,w.dn(),7+(k if k==0 else k-3),zz,own=own)
        self.send(cond,*b,self.pdev(),11+k,4+zz,own=own)
        self.send(cond,*b,self.qdev(),18+k,8+zz*2,own=own)
    def rounds(self):
        w=self.w
        self.emit(None,w.z,0,own=True)
        yield
        for k in (1,2,3,4):
            if k<4:
                for kk,zz,cond in ((k,w.z-k,w.z>=k),(k+3,w.z+k,w.z+k<=3)):
                    @pl.when(cond)
                    def _(zz=zz): self.arrived(*self.pq(zz,True),zz)
                    self.emit(cond,zz,kk)
            for kk,zz,cond in (((0,w.z,None),) if k==1 else ((k-1,w.z-k+1,w.z>=k-1),(k+2,w.z+k-1,w.z+k-1<=3))):
                b=self.pq(zz,False)
                def go(zz=zz,b=b): self.arrived(*b,4+zz)
                if cond is None: go()
                else: pl.when(cond)(go)
                self.send(cond,*b,self.qdev(),25+kk,8+zz*2+1)
            yield
    def finish(self):
        for zz in range(4):
            for pself in (True,False):
                self.arrived(*self.qcoord(zz,pself),8+zz*2+(0 if pself else 1))
        self.finish_sends()
    NS,NR=32,16

class GatherX(Gather):
    NS,NR=3+4*7,19
    def blk(self,zz,j):
        w=self.w
        return (zz,w.y if j<2 else 1-w.y,w.x if j%2==0 else 1-w.x)
    def vert(self,cond,zz,j,k,own=False):
        w=self.w; b=self.blk(zz,j)
        if k<4:
            c=(w.z<3) if cond is None else jnp.logical_and(cond,w.z<3)
            self.send(c,*b,w.up(),3+j*7+k if k else 3+j*7,3+zz*4+j,own=own)
        if k==0 or k>=4:
            c=(w.z>0) if cond is None else jnp.logical_and(cond,w.z>0)
            self.send(c,*b,w.dn(),3+j*7+(k if k>=4 else 3),3+zz*4+j,own=own)
    def rounds(self):
        w=self.w
        self.send(None,*self.blk(w.z,0),w.nx(),0,0,own=True)
        self.send(None,*self.blk(w.z,0),w.ny(),1,1,own=True)
        self.vert(None,w.z,0,0,own=True)
        yield
        b=self.blk(w.z,1); self.arrived(*b,0)
        self.send(None,*b,w.ny(),2,2)
        self.vert(None,w.z,1,0)
        self.arrived(*self.blk(w.z,2),1)
        self.vert(None,w.z,2,0)
        yield
        self.arrived(*self.blk(w.z,3),2)
        self.vert(None,w.z,3,0)
        yield
        for k in (1,2,3):
            for j in range(4):
                for kk,zz,cond in ((k,w.z-k,w.z>=k),(k+3,w.z+k,w.z+k<=3)):
                    @pl.when(cond)
                    def _(zz=zz,j=j): self.arrived(*self.blk(zz,j),3+zz*4+j)
                    if k<3: self.vert(cond,zz,j,kk)
                if j%2==1: yield
    def finish(self):
        self.finish_sends()


ZORD=(3,0,2,1)
class Scatter:
    def __init__(self,w,order,src,out,r0,nr,ssem,rsem,lsem,own,bufs):
        self.w,self.order,self.src,self.out,self.r0,self.nr=w,order,src,out,r0,nr
        self.ssem,self.rsem,self.lsem,self.own=ssem,rsem,lsem,own
        self.bufs=bufs
        self.pending=[]
    def rows(self,zz,yy,xx):
        return pl.ds(pl.multiple_of(((zz*2+yy)*2+xx)*RB+self.r0,16),self.nr)
    def send(self,cond,src,dst,dev,s,r):
        mk=lambda: pltpu.make_async_remote_copy(src_ref=src,dst_ref=dst,send_sem=self.ssem.at[s],recv_sem=self.rsem.at[r],device_id=dev,device_id_type=MESH)
        self.pending.append((cond,mk))
        if cond is None: mk().start()
        else: pl.when(cond)(lambda: mk().start())
    def wait(self,cond,dst,r):
        def go(): pltpu.make_async_remote_copy(src_ref=dst,dst_ref=dst,send_sem=self.ssem.at[0],recv_sem=self.rsem.at[r],device_id=self.w.nx(),device_id_type=MESH).wait_recv()
        if cond is None: go()
        else: pl.when(cond)(go)
    def finish(self):
        for cond,mk in self.pending:
            if cond is None: mk().wait_send()
            else: pl.when(cond)(lambda mk=mk: mk().wait_send())
    def total(self,dst,terms,extra=()):
        def strip(i,_):
            s=pl.ds(pl.multiple_of(i*16,16),16)
            t=terms[0][s].astype(jnp.float32)
            for r in terms[1:]: t=t+r[s].astype(jnp.float32)
            dst[s]=t.astype(dst.dtype)
            return 0
        lax.fori_loop(0,self.nr//16,strip,0)

class ScatterZ(Scatter):
    NS,NR=16,17
    def mine(self,zz,pself):
        w=self.w
        if self.order=="zyx": return (zz,w.y if pself else 1-w.y,w.x)
        return (zz,w.y,w.x if pself else 1-w.x)
    def theirs(self,zz,pself):
        w=self.w
        if self.order=="zyx": return (zz,w.y if pself else 1-w.y,1-w.x)
        return (zz,1-w.y,w.x if pself else 1-w.x)
    def rounds(self):
        w=self.w; rq,rp,ru=self.bufs
        pdev=w.ny() if self.order=="zyx" else w.nx()
        qdev=w.nx() if self.order=="zyx" else w.ny()
        self.loc=[]
        for zz in ZORD:
            for k in (1,0):
                self.send(None,self.src.at[self.rows(*self.theirs(zz,k==0))],rq.at[zz*2+k],qdev,zz*2+k,zz*2+k)
            for k in (1,0):
                c=pltpu.make_async_copy(self.src.at[self.rows(*self.mine(zz,k==0))],self.own.at[zz*2+k],self.lsem.at[zz*2+k]); c.start(); self.loc.append((zz*2+k,c))
        loc=dict(self.loc)
        yield
        for zz in ZORD:
            i=zz*2+1
            loc[i].wait(); self.wait(None,rq.at[i],i)
            self.total(rq.at[i],[self.own.at[i],rq.at[i]])
            self.send(None,rq.at[i],rp.at[zz],pdev,8+zz,8+zz)
            yield
        for zz in ZORD:
            i=zz*2
            loc[i].wait(); self.wait(None,rq.at[i],i)
            self.wait(None,rp.at[zz],8+zz)
            base=[self.own.at[i],rq.at[i],rp.at[zz]]
            if zz>0:
                @pl.when(w.z==0)
                def _(): self.total(rp.at[zz],base)
                @pl.when(jnp.logical_and(w.z>0,w.z<zz))
                def _():
                    self.wait(None,ru.at[zz],12+zz)
                    self.total(rp.at[zz],base+[ru.at[zz]])
                self.send(w.z<zz,rp.at[zz],ru.at[zz],w.up(),12+zz,12+zz)
            if zz<3:
                @pl.when(w.z==3)
                def _(): self.total(rp.at[zz],base)
                @pl.when(jnp.logical_and(w.z<3,w.z>zz))
                def _():
                    self.wait(None,ru.at[zz],12+zz)
                    self.total(rp.at[zz],base+[ru.at[zz]])
                to=jnp.where(w.z-1==zz,4,zz)
                self.send(w.z>zz,rp.at[zz],ru.at[to],w.dn(),12+zz,12+to)
            yield
        o=self.out.at[pl.ds(self.r0,self.nr)]
        for zz in range(4):
            base=[self.own.at[zz*2],rq.at[zz*2],rp.at[zz]]
            if zz>0: base=base+[ru.at[zz]]
            if zz<3: base=base+[ru.at[4]]
            @pl.when(w.z==zz)
            def _():
                if zz>0: self.wait(None,ru.at[zz],12+zz)
                if zz<3: self.wait(None,ru.at[4],16)
                self.total(o,base)
        yield

class ScatterX(Scatter):
    NS,NR=19,23
    def blk(self,zz,j):
        w=self.w
        return (zz,w.y if j<2 else 1-w.y,w.x if j%2==0 else 1-w.x)
    def rounds(self):
        w=self.w; ru,ry,rx=self.bufs
        down=lambda zz,j: jnp.where(w.z-1==zz,16+j,zz*4+j)
        loc={}
        for zz in ZORD:
            for j in (3,2,1,0):
                i=zz*4+j
                c=pltpu.make_async_copy(self.src.at[self.rows(*self.blk(zz,j))],self.own.at[i],self.lsem.at[i]); c.start(); loc[i]=c
        for j in (3,2,1,0):
            for zz in ZORD:
                i=zz*4+j
                if zz>0: self.send(w.z==0,self.src.at[self.rows(*self.blk(zz,j))],ru.at[i],w.up(),i,i)
                if zz<3: self.send(w.z==3,self.src.at[self.rows(*self.blk(zz,j))],ru.at[down(zz,j)],w.dn(),i,down(zz,j))
        for i in loc: loc[i].wait()
        yield
        for j in (3,2,1,0):
            for zz in ZORD:
                i=zz*4+j
                if zz>1:
                    cu=jnp.logical_and(w.z>0,w.z<zz)
                    @pl.when(cu)
                    def _():
                        self.wait(None,ru.at[i],i)
                        self.total(ru.at[i],[self.own.at[i],ru.at[i]])
                    self.send(cu,ru.at[i],ru.at[i],w.up(),i,i)
                if zz<2:
                    cd=jnp.logical_and(w.z<3,w.z>zz)
                    @pl.when(cd)
                    def _():
                        self.wait(None,ru.at[i],i)
                        self.total(ru.at[i],[self.own.at[i],ru.at[i]])
                    self.send(cd,ru.at[i],ru.at[down(zz,j)],w.dn(),i,down(zz,j))
            yield
        def zsum(j,dst,extra):
            for zz in range(4):
                i=zz*4+j
                t=[self.own.at[i]]
                if zz>0: t.append(ru.at[i])
                if zz<3: t.append(ru.at[16+j])
                @pl.when(w.z==zz)
                def _():
                    if zz>0: self.wait(None,ru.at[i],i)
                    if zz<3: self.wait(None,ru.at[16+j],16+j)
                    self.total(dst,t+extra)
        sy=self.bufs_stage
        for j in (3,2):
            k=j-2
            zsum(j,sy.at[k],[])
            self.send(None,sy.at[k],ry.at[k],w.ny(),16+k,20+k)
        yield
        self.wait(None,ry.at[1],21)
        zsum(1,sy.at[2],[ry.at[1]])
        self.send(None,sy.at[2],rx.at[0],w.nx(),18,22)
        yield
        self.wait(None,ry.at[0],20)
        self.wait(None,rx.at[0],22)
        zsum(0,self.out.at[pl.ds(self.r0,self.nr)],[ry.at[0],rx.at[0]])
        yield


F32 = jnp.float32
BF = jnp.bfloat16
DMA = pltpu.SemaphoreType.DMA
EPS = 1e-06


class Bag:
    pass


def step_all(gens):
    gens = list(gens)
    while gens:
        for g in list(gens):
            try:
                next(g)
            except StopIteration:
                gens.remove(g)
                continue
            yield


def drive(compute, comm, ratio):
    comm_live = True
    for _ in compute:
        for _ in range(ratio):
            if comm_live:
                try:
                    next(comm)
                except StopIteration:
                    comm_live = False
    for _ in comm:
        pass


class GatherSet:
    def __init__(self, parts, names):
        self.parts, self.names = parts, names

    def scratch(self):
        out = []
        for name, cols, kind in self.parts:
            if kind == "z":
                out += [DMA((GatherZ.NS,)), DMA((GatherZ.NR,))] * 2
            else:
                out += [DMA((GatherX.NS,)), DMA((GatherX.NR,))]
        return out + [DMA((len(self.names),))]

    def start(self, w, srcs, outs, sems):
        sems = list(sems)
        me = pl.multiple_of((w.dp * 2 + w.x) * RB, 16)
        self.locs = []
        for i, name in enumerate(self.names):
            c = pltpu.make_async_copy(srcs[name], outs[name].at[pl.ds(me, RB)], sems[-1].at[i])
            c.start()
            self.locs.append(c)
        self.live = []
        for name, cols, kind in self.parts:
            s, o = srcs[name], outs[name]
            if cols is not None:
                s, o = s.at[:, cols[0] : cols[1]], o.at[:, cols[0] : cols[1]]
            if kind == "z":
                for r0, order in ((0, "zyx"), (32, "zxy")):
                    self.live.append(GatherZ(w, order, s, o, r0, 32, sems.pop(0), sems.pop(0), None))
            else:
                self.live.append(GatherX(w, "xyz", s, o, 0, 64, sems.pop(0), sems.pop(0), None))
        return step_all([p.rounds() for p in self.live])

    def finish(self):
        for p in self.live:
            p.finish()
        for c in self.locs:
            c.wait()


class VecSum:
    def __init__(self, w, src, out, st, rv, ss, rs):
        self.w, self.src, self.out, self.st, self.rv, self.ss, self.rs = w, src, out, st, rv, ss, rs

    def mk(self, src, k, dev, send):
        return pltpu.make_async_remote_copy(
            src_ref=src, dst_ref=self.rv.at[k], send_sem=self.ss.at[send], recv_sem=self.rs.at[k],
            device_id=dev, device_id_type=MESH)

    def rounds(self):
        w = self.w
        st, rv = self.st, self.rv
        even = w.z % 2 == 0
        odd = w.z % 2 == 1
        mid = jnp.logical_and(w.z > 0, w.z < 3)
        self.mk(self.src, 0, w.nx(), 0).start()
        yield
        self.mk(self.src, 0, w.nx(), 0).wait_recv()
        st[0] = self.src[...] + rv[0]
        self.mk(st.at[0], 1, w.ny(), 1).start()
        yield
        self.mk(self.src, 1, w.ny(), 1).wait_recv()
        st[1] = st[0] + rv[1]
        pl.when(even)(lambda: self.mk(st.at[1], 2, w.up(), 2).start())
        pl.when(odd)(lambda: self.mk(st.at[1], 2, w.dn(), 2).start())
        yield
        self.mk(self.src, 2, w.nx(), 2).wait_recv()
        st[2] = st[1] + rv[2]
        pl.when(w.z == 1)(lambda: self.mk(st.at[2], 3, w.up(), 3).start())
        pl.when(w.z == 2)(lambda: self.mk(st.at[2], 3, w.dn(), 3).start())
        yield

        @pl.when(mid)
        def _():
            self.mk(self.src, 3, w.nx(), 3).wait_recv()
            st[3] = st[2] + rv[3]
            self.out[...] = st[3]

        pl.when(w.z == 1)(lambda: self.mk(st.at[3], 4, w.dn(), 4).start())
        pl.when(w.z == 2)(lambda: self.mk(st.at[3], 4, w.up(), 4).start())
        yield

        @pl.when(jnp.logical_not(mid))
        def _():
            self.mk(self.src, 4, w.nx(), 4).wait_recv()
            self.out[...] = rv[4]

        yield

    def finish(self):
        w = self.w
        self.mk(self.src, 0, w.nx(), 0).wait_send()
        self.mk(self.src, 0, w.nx(), 1).wait_send()
        self.mk(self.src, 0, w.nx(), 2).wait_send()

        @pl.when(jnp.logical_and(w.z > 0, w.z < 3))
        def _():
            self.mk(self.src, 0, w.nx(), 3).wait_send()
            self.mk(self.src, 0, w.nx(), 4).wait_send()


class ScatterSet:
    def __init__(self, parts, names, widths):
        self.parts, self.names, self.widths = parts, names, widths

    def scratch(self):
        V = lambda *s: pltpu.VMEM(s, BF)
        sc = []
        for name, cols, kind in self.parts:
            C = self.widths[name] if cols is None else cols[1] - cols[0]
            if kind == "z":
                for _ in range(2):
                    sc += [DMA((ScatterZ.NS,)), DMA((ScatterZ.NR,)), DMA((8,))]
                    sc += [V(8, 32, C), V(8, 32, C), V(4, 32, C), V(5, 32, C)]
            else:
                sc += [DMA((ScatterX.NS,)), DMA((ScatterX.NR,)), DMA((16,))]
                sc += [V(16, 64, C), V(20, 64, C), V(2, 64, C), V(1, 64, C), V(3, 64, C)]
        sc += [pltpu.VMEM((4, 8, HP), F32), pltpu.VMEM((5, 8, HP), F32), DMA((5,)), DMA((5,))]
        return sc

    def start(self, w, srcs, outs, vec, vec_out, sc):
        sc = list(sc)
        self.live = []
        for name, cols, kind in self.parts:
            s, o = srcs[name], outs[name]
            if cols is not None:
                s, o = s.at[:, cols[0] : cols[1]], o.at[:, cols[0] : cols[1]]
            if kind == "z":
                for r0, order in ((0, "zyx"), (32, "zxy")):
                    ss, rs, ls, own, rq, rp, ru = [sc.pop(0) for _ in range(7)]
                    self.live.append(ScatterZ(w, order, s, o, r0, 32, ss, rs, ls, own, (rq, rp, ru)))
            else:
                ss, rs, ls, own, ru, ry, rx, st = [sc.pop(0) for _ in range(8)]
                p = ScatterX(w, "xyz", s, o, 0, 64, ss, rs, ls, own, (ru, ry, rx))
                p.bufs_stage = st
                self.live.append(p)
        st, rv, ss, rs = sc
        self.live.append(VecSum(w, vec, vec_out, st, rv, ss, rs))
        return step_all([p.rounds() for p in self.live])

    def finish(self):
        for p in self.live:
            p.finish()


AT_G = GatherSet([("in", None, "z"), ("out", None, "x")], ["in", "out"])
FF_G = GatherSet([("gu", None, "z"), ("dn", (0, 512), "z"), ("dn", (512, 1408), "x")], ["gu", "dn"])


def at_scatter():
    return ScatterSet([("in", None, "z"), ("out", None, "x")], ["in", "out"], {"in": 1536, "out": 512})


def ff_scatter():
    return ScatterSet(
        [("gu", None, "z"), ("dn", (0, 512), "z"), ("dn", (512, 1408), "x")], ["gu", "dn"], {"gu": 2816, "dn": 1408}
    )


def rows16(n, fn, step=176):
    def body(i, _):
        fn(pl.ds(pl.multiple_of(i * step, 16), step))
        return 0

    lax.fori_loop(0, n // step, body, 0)


def unit_of(x, width):
    mean = jnp.sum(x, axis=-1, keepdims=True) / width
    c = x - mean
    inv = lax.rsqrt(jnp.sum(c * c, axis=-1, keepdims=True) / width + EPS)
    return c * inv, inv


def dot_nn(a, b):
    return jnp.dot(a, b, preferred_element_type=F32)


def dot_nt(a, b):
    return lax.dot_general(a, b, (((1,), (1,)), ((), ())), preferred_element_type=F32)


def dot_tn(a, b):
    return lax.dot_general(a, b, (((0,), (0,)), ((), ())), preferred_element_type=F32)


def tiles(n, size=256):
    return [(a, min(size, n - a)) for a in range(0, n, size)]


def fold8(x):
    return jnp.sum(x.reshape(x.shape[0] // 8, 8, x.shape[1]), axis=0)


def wide(x, n):
    return jnp.concatenate([x] * (-(-n // 128)), axis=1)[:, :n]


def two_cols(a, b):
    lane = lax.broadcasted_iota(jnp.int32, (a.shape[0], 128), 1)
    return jnp.where(lane == 0, a, jnp.where(lane == 1, b, 0.0))


def turn(x, cos, sin):
    lane = lax.broadcasted_iota(jnp.int32, x.shape, 1)
    other = jnp.where((lane // 16) % 2 == 0, pltpu.roll(x, 112, 1), pltpu.roll(x, 16, 1))
    return x * cos + other * sin


def head_lanes(x, t):
    lane = lax.broadcasted_iota(jnp.int32, x.shape, 1)
    return jnp.where(lane // 64 == t, x, jnp.zeros_like(x))


class Peer:
    def __init__(self, dev, ss, rs):
        self.dev, self.ss, self.rs, self.open = dev, ss, rs, []

    def mk(self, src, dst, k):
        return pltpu.make_async_remote_copy(
            src_ref=src, dst_ref=dst, send_sem=self.ss.at[k], recv_sem=self.rs.at[k], device_id=self.dev, device_id_type=MESH)

    def send(self, src, dst, k):
        c = self.mk(src, dst, k)
        c.start()
        self.open.append(c)

    def recv(self, dst, k):
        self.mk(dst, dst, k).wait_recv()

    def finish(self):
        for c in self.open:
            c.wait_send()


def greet_all(w, links):
    bar = pltpu.get_barrier_semaphore()

    def sig(dev):
        pl.semaphore_signal(bar, inc=1, device_id=dev, device_id_type=MESH)

    sig((w.dp, w.x, 1 - w.c))
    n = jnp.int32(1)
    if links != "core":
        sig(w.nx())
        n = n + 1
    if links == "all":
        sig(w.ny())
        pl.when(w.z < 3)(lambda: sig(w.up()))
        pl.when(w.z > 0)(lambda: sig(w.dn()))
        n = n + 1 + (w.z < 3).astype(jnp.int32) + (w.z > 0).astype(jnp.int32)
    pl.semaphore_wait(bar, n)


def run_kernel(body, name, cid, ins, outs, scratch, extra=()):
    iname, oname, sname = list(ins), list(outs), list(scratch)

    def kernel(*refs):
        b = Bag()
        ni, no, ns = len(iname), len(oname), len(sname)
        for n, r in zip(iname + oname + sname, refs):
            setattr(b, n, r)
        b.extra = refs[ni + no + ns :]
        body(b)

    res = pl.pallas_call(
        kernel,
        out_shape=[jax.ShapeDtypeStruct(outs[n][0], outs[n][1]) for n in oname],
        in_specs=[pl.BlockSpec(memory_space=ins[n][1]) for n in iname],
        out_specs=[pl.BlockSpec(memory_space=outs[n][2]) for n in oname],
        scratch_shapes=[scratch[n] for n in sname] + list(extra),
        compiler_params=pltpu.CompilerParams(collective_id=cid, has_side_effects=True, vmem_limit_bytes=62 * 2**20),
        name=name,
    )(*[ins[n][0] for n in iname])
    return dict(zip(oname, res))


VM = pltpu.VMEM
ANY = pl.ANY


def gather_first(srcs, gset, cid):
    names = gset.names

    def body(b):
        w = Where()
        greet(w)
        g = gset.start(w, {n: getattr(b, "s_" + n) for n in names}, {n: getattr(b, "w_" + n) for n in names}, b.extra)
        for _ in g:
            pass
        gset.finish()

    return run_kernel(
        body, "gather", cid,
        {"s_" + n: (srcs[n], ANY) for n in names},
        {"w_" + n: ((16 * RB, srcs[n].shape[1]), BF, ANY) for n in names},
        {}, gset.scratch())


def attend_body(b, w, R, core, side):
    hp = b.h.shape[1]
    rows16(R, lambda s: norm_store(b.n, s, b.h[s], b.vn[0:1, :], b.vn[1:2, :]))
    yield
    D = 512
    for j in range(2):
        kt = dot_nn(b.n[...], b.w_in[:, D + 256 * j : D + 256 * j + 256])
        for hf in range(2):
            l = slice(256 * j + 128 * hf, 256 * j + 128 * hf + 128)
            b.k[0:R, l] = (turn(kt[:, 128 * hf : 128 * hf + 128], b.cos[...], b.sin[...]) * b.keep[...]).astype(BF)
        l = slice(256 * j, 256 * j + 256)
        side.send(b.k.at[pl.ds(0, R), l], b.k.at[pl.ds(R, R), l], 2 * j)
        vt = dot_nn(b.n[...], b.w_in[:, 2 * D + 256 * j : 2 * D + 256 * j + 256]) + b.vh[2:3, l]
        b.v[0:R, l] = vt.astype(BF)
        side.send(b.v.at[pl.ds(0, R), l], b.v.at[pl.ds(R, R), l], 2 * j + 1)
        yield
    for j in range(2):
        qt = dot_nn(b.n[...], b.w_in[:, 256 * j : 256 * j + 256]) + b.vh[1:2, 256 * j : 256 * j + 256]
        for hf in range(2):
            l = slice(256 * j + 128 * hf, 256 * j + 128 * hf + 128)
            b.q[:, l] = (turn(qt[:, 128 * hf : 128 * hf + 128], b.cos[...], b.sin[...]) * 0.125).astype(BF)
    yield
    S = 176
    for p in range(4):
        l = slice(128 * p, 128 * p + 128)
        if p % 2 == 0:
            j = p // 2
            lj = slice(256 * j, 256 * j + 256)
            side.recv(b.k.at[pl.ds(R, R), lj], 2 * j)
            side.recv(b.v.at[pl.ds(R, R), lj], 2 * j + 1)
        kp = b.k[:, l]
        vT = b.v[:, l].T
        halves = []
        for t in range(2):
            b.s[...] = dot_nt(kp, head_lanes(b.q[:, l], t))

            def top(i, m):
                r = pl.ds(pl.multiple_of(i * S, 16), S)
                x = b.s[r] + wide(b.fill[r], R)
                return jnp.maximum(m, jnp.max(x.reshape(S // 8, 8, R), axis=0))

            m = lax.fori_loop(0, 2 * R // S, top, jnp.full((8, R), -3.0e38, F32))
            m = jnp.max(m, axis=0, keepdims=True)

            def expo(i, acc):
                r = pl.ds(pl.multiple_of(i * S, 16), S)
                x = jnp.exp(b.s[r] + wide(b.fill[r], R) - m)
                b.p[r] = x.astype(BF)
                return acc + jnp.sum(x.reshape(S // 8, 8, R), axis=0)

            tot = lax.fori_loop(0, 2 * R // S, expo, jnp.zeros((8, R), F32))
            tot = jnp.sum(tot, axis=0, keepdims=True)
            halves.append(dot_nn(vT[64 * t : 64 * t + 64], b.p[...]) / tot)
            b.lse[2 * p + t : 2 * p + t + 1, :] = m + jnp.log(tot)
            yield
        b.o[:, l] = jnp.concatenate(halves, axis=0).T

    def stats(s):
        x = b.o[s]
        b.stat[s] = two_cols(jnp.sum(x, axis=-1, keepdims=True), jnp.sum(x * x, axis=-1, keepdims=True))

    rows16(R, stats)
    core.send(b.stat, b.rstat, 0)
    core.recv(b.rstat, 0)

    def unit(s):
        t = b.stat[s] + b.rstat[s]
        mean = t[:, 0:1] / hp
        inv = lax.rsqrt(t[:, 1:2] / hp - mean * mean + EPS)
        b.st[s] = two_cols(mean, inv)
        b.u[s] = ((b.o[s] - mean) * inv * b.vh[0:1, :] + b.vh[3:4, :]).astype(BF)

    rows16(R, unit)
    yield
    for d in range(4):
        l = slice(256 * d, 256 * d + 256)
        b.part[:, l] = dot_nt(b.u[...], b.w_out[256 * d : 256 * d + 256, :]).astype(BF)
        core.send(b.part.at[:, l], b.rpart.at[:, l], 1 + d)
        if d % 2 == 1:
            yield
    for d in range(4):
        l = slice(256 * d, 256 * d + 256)
        core.recv(b.rpart.at[:, l], 1 + d)

    def close(s):
        x = b.part[s].astype(F32) + b.rpart[s].astype(F32) + b.vn[4:5, :]
        b.hm[s] = b.h[s] + wide(b.keep[s], x.shape[1]) * x

    rows16(R, close)
    yield


def norm_store(dst, s, x, gain, bias):
    dst[s] = (unit_of(x, x.shape[1])[0] * gain + bias).astype(BF)


def forward_attend(h, tabs, wts, vn, vh, srcs, gset, cid):
    R, D = h.shape

    def body(b):
        w = Where()
        greet_all(w, "all")
        names = gset.names
        comm = gset.start(w, {n: getattr(b, "s_" + n) for n in names}, {n: getattr(b, "g_" + n) for n in names}, b.extra)
        core = Peer((w.dp, w.x, 1 - w.c), b.cs, b.cr)
        side = Peer(w.nx(), b.xs, b.xr)
        next(comm)
        drive(attend_body(b, w, R, core, side), comm, 2)
        gset.finish()
        core.finish()
        side.finish()

    ins = {"h": (h, VM), "keep": (tabs["keep"], VM), "fill": (tabs["fill"], VM), "cos": (tabs["cos"], VM),
           "sin": (tabs["sin"], VM), "w_in": (wts["in"], VM), "w_out": (wts["out"], VM), "vn": (vn, VM), "vh": (vh, VM)}
    ins.update({"s_" + n: (srcs[n], ANY) for n in gset.names})
    outs = {"hm": ((R, D), F32, VM), "q": ((R, 512), BF, VM), "k": ((2 * R, 512), BF, VM), "v": ((2 * R, 512), BF, VM),
            "lse": ((8, R), F32, VM), "o": ((R, 512), F32, VM), "st": ((R, 128), F32, VM)}
    outs.update({"g_" + n: ((16 * RB, srcs[n].shape[1]), BF, ANY) for n in gset.names})
    scratch = {"n": pltpu.VMEM((R, D), BF), "s": pltpu.VMEM((2 * R, R), F32), "p": pltpu.VMEM((2 * R, R), BF),
               "u": pltpu.VMEM((R, 512), BF), "part": pltpu.VMEM((R, D), BF), "rpart": pltpu.VMEM((R, D), BF),
               "stat": pltpu.VMEM((R, 128), F32), "rstat": pltpu.VMEM((R, 128), F32),
               "cs": DMA((5,)), "cr": DMA((5,)), "xs": DMA((4,)), "xr": DMA((4,))}
    return run_kernel(body, "attend", cid, ins, outs, scratch, gset.scratch())


def hidden_body(b, w, R, core):
    rows16(R, lambda s: norm_store(b.n, s, b.hm[s], b.vn[2:3, :], b.vn[3:4, :]))
    yield
    for i, (a, n) in enumerate(tiles(HP)):
        b.gate[:, a : a + n] = dot_nn(b.n[...], b.w_gu[:, a : a + n]) + b.vf[1:2, a : a + n]
        b.up[:, a : a + n] = dot_nn(b.n[...], b.w_gu[:, HP + a : HP + a + n]) + b.vf[2:3, a : a + n]
        if i % 2 == 1:
            yield

    def stats(s):
        g = b.gate[s]
        z = g * jax.nn.sigmoid(g) * b.up[s]
        b.z[s] = z
        b.stat[s] = two_cols(jnp.sum(z, axis=-1, keepdims=True), jnp.sum(z * z, axis=-1, keepdims=True))

    rows16(R, stats)
    core.send(b.stat, b.rstat, 0)
    core.recv(b.rstat, 0)
    yield

    def unit(s):
        t = b.stat[s] + b.rstat[s]
        mean = t[:, 0:1] / FF
        inv = lax.rsqrt(t[:, 1:2] / FF - mean * mean + EPS)
        b.st[s] = two_cols(mean, inv)
        b.zn[s] = ((b.z[s] - mean) * inv * b.vf[0:1, :] + b.vf[3:4, :]).astype(BF)

    rows16(R, unit)
    yield
    for d in range(4):
        l = slice(256 * d, 256 * d + 256)
        b.part[:, l] = dot_nt(b.zn[...], b.w_dn[256 * d : 256 * d + 256, :]).astype(BF)
        core.send(b.part.at[:, l], b.rpart.at[:, l], 1 + d)
        if d % 2 == 1:
            yield
    for d in range(4):
        l = slice(256 * d, 256 * d + 256)
        core.recv(b.rpart.at[:, l], 1 + d)

    def close(s):
        x = b.part[s].astype(F32) + b.rpart[s].astype(F32) + b.vn[5:6, :]
        b.ho[s] = b.hm[s] + wide(b.keep[s], x.shape[1]) * x

    rows16(R, close)
    yield


def forward_hidden(hm, tabs, wts, vn, vf, srcs, gset, cid):
    R, D = hm.shape

    def body(b):
        w = Where()
        greet_all(w, "all" if gset else "core")
        core = Peer((w.dp, w.x, 1 - w.c), b.cs, b.cr)
        comp = hidden_body(b, w, R, core)
        if gset:
            names = gset.names
            comm = gset.start(w, {n: getattr(b, "s_" + n) for n in names}, {n: getattr(b, "g_" + n) for n in names}, b.extra)
            next(comm)
            drive(comp, comm, 2)
            gset.finish()
        else:
            for _ in comp:
                pass
        core.finish()

    ins = {"hm": (hm, VM), "keep": (tabs["keep"], VM), "w_gu": (wts["gu"], VM), "w_dn": (wts["dn"], VM), "vn": (vn, VM), "vf": (vf, VM)}
    outs = {"ho": ((R, D), F32, VM), "gate": ((R, HP), F32, VM), "up": ((R, HP), F32, VM), "st": ((R, 128), F32, VM)}
    if gset:
        ins.update({"s_" + n: (srcs[n], ANY) for n in gset.names})
        outs.update({"g_" + n: ((16 * RB, srcs[n].shape[1]), BF, ANY) for n in gset.names})
    scratch = {"n": pltpu.VMEM((R, D), BF), "z": pltpu.VMEM((R, HP), F32), "zn": pltpu.VMEM((R, HP), BF),
               "part": pltpu.VMEM((R, D), BF), "rpart": pltpu.VMEM((R, D), BF),
               "stat": pltpu.VMEM((R, 128), F32), "rstat": pltpu.VMEM((R, 128), F32), "cs": DMA((5,)), "cr": DMA((5,))}
    return run_kernel(body, "hidden", cid, ins, outs, scratch, gset.scratch() if gset else ())


def add8(acc, x):
    acc[...] = acc[...] + fold8(x)


def put_vec(b, row, acc, n):
    b.vec[row : row + 1, 0:n] = jnp.sum(acc[...], axis=0, keepdims=True)


def close_back(b, s, x, gain, acc_gain, acc_shift):
    e = b.part[s].astype(F32) + b.rpart[s].astype(F32)
    unit, inv = unit_of(x, x.shape[1])
    add8(acc_gain, e * unit)
    add8(acc_shift, e)
    wt = e * gain
    n = x.shape[1]
    m1 = jnp.sum(wt, axis=-1, keepdims=True) / n
    m2 = jnp.sum(wt * unit, axis=-1, keepdims=True) / n
    b.go[s] = b.g[s] + inv * (wt - m1 - unit * m2)


def hidden_back_body(b, w, R, core):
    D = b.g.shape[1]
    for a in (b.a0, b.a1, b.a2, b.a3, b.a4, b.a5, b.a6, b.vec):
        a[...] = jnp.zeros_like(a)

    def unit4(s):
        g = b.gate[s]
        sg = jax.nn.sigmoid(g)
        return (g * sg * b.up[s] - b.st[s, 0:1]) * b.st[s, 1:2], g, sg

    def first(s):
        e = wide(b.keep[s], D) * b.g[s]
        b.el[s] = e.astype(BF)
        add8(b.a2, e)
        norm_store(b.n, s, b.go[s], b.vn[2:3, :], b.vn[3:4, :])
        b.zn[s] = (unit4(s)[0] * b.vf[0:1, :] + b.vf[3:4, :]).astype(BF)

    rows16(R, first)
    yield
    for i, (a, n) in enumerate(tiles(HP)):
        b.ez[:, a : a + n] = dot_nn(b.el[...], b.w_dn[:, a : a + n])
        if i % 3 == 2:
            yield

    def second(s):
        u = unit4(s)[0]
        e = b.ez[s]
        wt = e * b.vf[0:1, :]
        add8(b.a3, e * u)
        add8(b.a6, e)
        b.stat[s] = two_cols(jnp.sum(wt, axis=-1, keepdims=True), jnp.sum(wt * u, axis=-1, keepdims=True))

    rows16(R, second)
    core.send(b.stat, b.rstat, 0)
    b.xT[...] = b.el[...].T
    yield
    for i, (a, n) in enumerate(tiles(HP)):
        b.d_dn[:, a : a + n] = dot_nn(b.xT[...], b.zn[:, a : a + n]).astype(BF)
        if i % 3 == 2:
            yield
    core.recv(b.rstat, 0)

    def third(s):
        u, g, sg = unit4(s)
        t = (b.stat[s] + b.rstat[s]) / FF
        ez = b.st[s, 1:2] * (b.ez[s] * b.vf[0:1, :] - t[:, 0:1] - u * t[:, 1:2])
        eg = ez * b.up[s] * sg * (1.0 + g * (1.0 - sg))
        eu = ez * g * sg
        add8(b.a4, eg)
        add8(b.a5, eu)
        b.egu[s, 0:HP] = eg.astype(BF)
        b.egu[s, HP : 2 * HP] = eu.astype(BF)

    rows16(R, third, 48)
    yield
    for d in range(4):
        l = slice(256 * d, 256 * d + 256)
        b.part[:, l] = dot_nt(b.egu[...], b.w_gu[256 * d : 256 * d + 256, :]).astype(BF)
        core.send(b.part.at[:, l], b.rpart.at[:, l], 1 + d)
        yield
    b.xT[...] = b.n[...].T
    for i, (a, n) in enumerate(tiles(2 * HP)):
        b.d_gu[:, a : a + n] = dot_nn(b.xT[...], b.egu[:, a : a + n]).astype(BF)
        if i % 3 == 2:
            yield
    for d in range(4):
        l = slice(256 * d, 256 * d + 256)
        core.recv(b.rpart.at[:, l], 1 + d)
    rows16(R, lambda s: close_back(b, s, b.go[s], b.vn[2:3, :], b.a0, b.a1))
    for row, acc, n in ((0, b.a0, D), (1, b.a1, D), (2, b.a2, D), (3, b.a3, HP), (4, b.a4, HP), (5, b.a5, HP), (6, b.a6, HP)):
        put_vec(b, row, acc, n)
    yield


def attend_back_body(b, w, R, core, side):
    D = b.g.shape[1]
    hp = D
    for a in (b.a0, b.a1, b.a2, b.a3, b.a4, b.a5, b.a6, b.vec):
        a[...] = jnp.zeros_like(a)

    def first(s):
        e = wide(b.keep[s], D) * b.g[s]
        b.el[s] = e.astype(BF)
        add8(b.a2, e)
        norm_store(b.n, s, b.go[s], b.vn[0:1, :], b.vn[1:2, :])
        u = (b.o[s] - b.st[s, 0:1]) * b.st[s, 1:2]
        b.u[s] = (u * b.vh[0:1, :] + b.vh[3:4, :]).astype(BF)

    rows16(R, first)
    yield
    for a, n in tiles(512):
        b.dq[:, a : a + n] = dot_nn(b.el[...], b.w_out[:, a : a + n])

    def second(s):
        u = (b.o[s] - b.st[s, 0:1]) * b.st[s, 1:2]
        e = b.dq[s]
        wt = e * b.vh[0:1, :]
        add8(b.a3, e * u)
        add8(b.a6, e)
        b.stat[s] = two_cols(jnp.sum(wt, axis=-1, keepdims=True), jnp.sum(wt * u, axis=-1, keepdims=True))

    rows16(R, second)
    core.send(b.stat, b.rstat, 0)
    b.xT[...] = b.el[...].T
    yield
    for a, n in tiles(512):
        b.d_out[:, a : a + n] = dot_nn(b.xT[...], b.u[:, a : a + n]).astype(BF)
    yield
    core.recv(b.rstat, 0)

    def third(s):
        u = (b.o[s] - b.st[s, 0:1]) * b.st[s, 1:2]
        t = (b.stat[s] + b.rstat[s]) / hp
        b.eo[s] = (b.st[s, 1:2] * (b.dq[s] * b.vh[0:1, :] - t[:, 0:1] - u * t[:, 1:2])).astype(BF)

    rows16(R, third, 48)
    yield
    S = 176
    for p in range(4):
        l = slice(128 * p, 128 * p + 128)
        kp = b.k[:, l]
        vp = b.v[:, l]
        kT = kp.T
        dk, dv, dqs = None, None, []
        for t in range(2):
            qt = head_lanes(b.q[:, l], t)
            ot = head_lanes(b.eo[:, l], t)
            b.s[...] = dot_nt(kp, qt)
            b.dp[...] = dot_nt(vp, ot)
            lse = b.lse[2 * p + t : 2 * p + t + 1, :]

            def expo(i, acc):
                r = pl.ds(pl.multiple_of(i * S, 16), S)
                x = jnp.exp(b.s[r] + wide(b.fill[r], R) - lse)
                b.s[r] = x
                b.p[r] = x.astype(BF)
                return acc + jnp.sum((x * b.dp[r]).reshape(S // 8, 8, R), axis=0)

            tot = lax.fori_loop(0, 2 * R // S, expo, jnp.zeros((8, R), F32))
            tot = jnp.sum(tot, axis=0, keepdims=True)

            def grad(i, _):
                r = pl.ds(pl.multiple_of(i * S, 16), S)
                b.ds[r] = (b.s[r] * (b.dp[r] - tot)).astype(BF)
                return 0

            lax.fori_loop(0, 2 * R // S, grad, 0)
            yield
            v1 = dot_nn(b.p[...], ot)
            k1 = dot_nn(b.ds[...], qt)
            dqs.append(dot_nn(kT[64 * t : 64 * t + 64], b.ds[...]))
            dv = v1 if t == 0 else dv + v1
            dk = k1 if t == 0 else dk + k1
            yield
        dk = jnp.where(b.fill[:, 0:1] == 0.0, dk, 0.0)
        b.dq[:, l] = jnp.concatenate(dqs, axis=0).T * 0.125
        b.dk[:, l] = dk[:R]
        b.dv[:, l] = dv[:R]
        l2 = slice(512 + 128 * p, 640 + 128 * p)
        b.ep[:, l] = dk[R:].astype(BF)
        b.ep[:, l2] = dv[R:].astype(BF)
        side.send(b.ep.at[:, l], b.rk.at[:, l], 2 * p)
        side.send(b.ep.at[:, l2], b.rv.at[:, l], 2 * p + 1)
    yield
    side.finish()
    for p in range(4):
        l = slice(128 * p, 128 * p + 128)
        side.recv(b.rk.at[:, l], 2 * p)
        side.recv(b.rv.at[:, l], 2 * p + 1)

        def last(s):
            cos, sin = b.cos[s], -b.sin[s]
            eq = turn(b.dq[s, l], cos, sin)
            ek = turn(b.dk[s, l] + b.rk[s, l].astype(F32), cos, sin)
            ev = b.dv[s, l] + b.rv[s, l].astype(F32)
            b.a4[:, l] = b.a4[:, l] + fold8(eq)
            b.a5[:, l] = b.a5[:, l] + fold8(ev)
            b.ep[s, l] = eq.astype(BF)
            b.ep[s, 512 + 128 * p : 640 + 128 * p] = ek.astype(BF)
            b.ep[s, 1024 + 128 * p : 1152 + 128 * p] = ev.astype(BF)

        rows16(R, last)
    yield
    for d in range(4):
        l = slice(256 * d, 256 * d + 256)
        b.part[:, l] = dot_nt(b.ep[...], b.w_in[256 * d : 256 * d + 256, :]).astype(BF)
        core.send(b.part.at[:, l], b.rpart.at[:, l], 1 + d)
        if d % 2 == 1:
            yield
    b.xT[...] = b.n[...].T
    for i, (a, n) in enumerate(tiles(1536)):
        b.d_in[:, a : a + n] = dot_nn(b.xT[...], b.ep[:, a : a + n]).astype(BF)
        if i % 3 == 2:
            yield
    for d in range(4):
        l = slice(256 * d, 256 * d + 256)
        core.recv(b.rpart.at[:, l], 1 + d)
    rows16(R, lambda s: close_back(b, s, b.go[s], b.vn[0:1, :], b.a0, b.a1))
    for row, acc, n in ((0, b.a0, D), (1, b.a1, D), (2, b.a2, D), (3, b.a3, 512), (4, b.a4, 512), (5, b.a5, 512), (6, b.a6, 512)):
        put_vec(b, row, acc, n)
    yield


def scatter_args(sset, grads, vec):
    ins = {"s_" + n: (grads[n], ANY) for n in sset.names}
    ins["s_vec"] = (vec, VM)
    outs = {"r_" + n: ((RB, grads[n].shape[1]), F32, VM) for n in sset.names}
    outs["r_vec"] = ((8, HP), F32, VM)
    return ins, outs


def scatter_start(sset, w, b):
    n = sset.names
    return sset.start(w, {i: getattr(b, "s_" + i) for i in n}, {i: getattr(b, "r_" + i) for i in n}, b.s_vec, b.r_vec, b.extra)


def backward_hidden(g, fw, hm, tabs, wts, vn, vf, sset, grads, vec, cid):
    R, D = g.shape

    def body(b):
        w = Where()
        greet_all(w, "all" if sset else "core")
        core = Peer((w.dp, w.x, 1 - w.c), b.cs, b.cr)
        load = pltpu.make_async_copy(b.hm, b.go, b.ls.at[0])
        load.start()
        comp = hidden_back_body(b, w, R, core)
        if sset:
            comm = scatter_start(sset, w, b)
            for _ in sset.live:
                next(comm)
            load.wait()
            drive(comp, comm, 2)
            sset.finish()
        else:
            load.wait()
            for _ in comp:
                pass
        core.finish()

    ins = {"g": (g, VM), "keep": (tabs["keep"], VM), "hm": (hm, ANY), "gate": (fw["gate"], VM), "up": (fw["up"], VM), "st": (fw["st"], VM),
           "w_gu": (wts["gu"], VM), "w_dn": (wts["dn"], VM), "vn": (vn, VM), "vf": (vf, VM)}
    outs = {"go": ((R, D), F32, VM), "d_gu": ((D, 2 * HP), BF, VM), "d_dn": ((D, HP), BF, VM), "vec": ((8, HP), F32, VM)}
    extra = ()
    if sset:
        i2, o2 = scatter_args(sset, grads, vec)
        ins.update(i2)
        outs.update(o2)
        extra = sset.scratch()
    acc = lambda n: pltpu.VMEM((8, n), F32)
    scratch = {"el": pltpu.VMEM((R, D), BF), "xT": pltpu.VMEM((D, R), BF), "n": pltpu.VMEM((R, D), BF), "ez": pltpu.VMEM((R, HP), F32),
               "zn": pltpu.VMEM((R, HP), BF), "egu": pltpu.VMEM((R, 2 * HP), BF), "part": pltpu.VMEM((R, D), BF), "rpart": pltpu.VMEM((R, D), BF),
               "stat": pltpu.VMEM((R, 128), F32), "rstat": pltpu.VMEM((R, 128), F32), "cs": DMA((5,)), "cr": DMA((5,)), "ls": DMA((1,)),
               "a0": acc(D), "a1": acc(D), "a2": acc(D), "a3": acc(HP), "a4": acc(HP), "a5": acc(HP), "a6": acc(HP)}
    return run_kernel(body, "hidden_back", cid, ins, outs, scratch, extra)


def backward_attend(g, fw, h, tabs, wts, vn, vh, sset, grads, vec, cid):
    R, D = g.shape

    def body(b):
        w = Where()
        greet_all(w, "all")
        core = Peer((w.dp, w.x, 1 - w.c), b.cs, b.cr)
        side = Peer(w.nx(), b.xs, b.xr)
        load = pltpu.make_async_copy(b.h, b.go, b.ls.at[0])
        load.start()
        comm = scatter_start(sset, w, b)
        for _ in sset.live:
            next(comm)
        load.wait()
        drive(attend_back_body(b, w, R, core, side), comm, 2)
        sset.finish()
        core.finish()

    ins = {"g": (g, VM), "keep": (tabs["keep"], VM), "h": (h, ANY), "fill": (tabs["fill"], VM), "cos": (tabs["cos"], VM), "sin": (tabs["sin"], VM),
           "o": (fw["o"], VM), "st": (fw["st"], VM), "q": (fw["q"], VM), "k": (fw["k"], VM), "v": (fw["v"], VM), "lse": (fw["lse"], VM),
           "w_in": (wts["in"], VM), "w_out": (wts["out"], VM), "vn": (vn, VM), "vh": (vh, VM)}
    outs = {"go": ((R, D), F32, VM), "d_in": ((D, 1536), BF, VM), "d_out": ((D, 512), BF, VM), "vec": ((8, HP), F32, VM)}
    i2, o2 = scatter_args(sset, grads, vec)
    ins.update(i2)
    outs.update(o2)
    acc = lambda n: pltpu.VMEM((8, n), F32)
    B = lambda *s: pltpu.VMEM(s, BF)
    F = lambda *s: pltpu.VMEM(s, F32)
    scratch = {"el": B(R, D), "xT": B(D, R), "n": B(R, D), "u": B(R, 512), "eo": B(R, 512), "s": F(2 * R, R), "dp": F(2 * R, R),
               "p": B(2 * R, R), "ds": B(2 * R, R), "dq": F(R, 512), "dk": F(R, 512), "dv": F(R, 512),
               "rk": B(R, 512), "rv": B(R, 512), "ep": B(R, 1536), "part": B(R, D), "rpart": B(R, D), "stat": F(R, 128), "rstat": F(R, 128),
               "cs": DMA((5,)), "cr": DMA((5,)), "ls": DMA((1,)), "xs": DMA((8,)), "xr": DMA((8,)),
               "a0": acc(D), "a1": acc(D), "a2": acc(D), "a3": acc(512), "a4": acc(512), "a5": acc(512), "a6": acc(512)}
    return run_kernel(body, "attend_back", cid, ins, outs, scratch, sset.scratch())


def scatter_last(sset, grads, vec, cid):
    def body(b):
        w = Where()
        greet(w)
        for _ in scatter_start(sset, w, b):
            pass
        sset.finish()

    ins, outs = scatter_args(sset, grads, vec)
    return run_kernel(body, "scatter", cid, ins, outs, {}, sset.scratch())


HP = 1408


def fast_device(
    tokens_in,
    cotangent,
    key_mask,
    grid_pos,
    class_index,
    input_weight,
    output_weight,
    gate_up_weight,
    down_weight,
    norm_gains,
    norm_biases,
    head_gains,
    head_biases,
    hidden_gains,
    hidden_biases,
):
    _, rows, width = tokens_in.shape
    dim = head_gains.shape[1]
    hidden = hidden_gains.shape[1]
    layers = input_weight.shape[0]
    pad = HP - hidden
    R = -(-rows // 16) * 16
    more = R - rows
    places = lax.axis_index("ctx") * rows + jnp.arange(rows, dtype=jnp.int32)
    not_class = (places != class_index[0]).astype(F32)
    cosine, sine = rotary_tables(grid_pos.reshape(2, rows), not_class)
    c0, c1, s0, s1 = cosine[:, 0], cosine[:, 1], sine[:, 0], sine[:, 1]
    low = lambda a: jnp.pad(a, ((0, more), (0, 0)))
    keep = low(key_mask.astype(F32).reshape(rows, 1))
    fill = jnp.where(jnp.arange(R)[:, None] < rows, (keep - 1.0) * 10000.0, -1.0e30)
    other = lax.ppermute(fill[:, 0], "ctx", [(0, 1), (1, 0)])[:, None]
    tabs = {
        "keep": jnp.broadcast_to(keep, (R, 128)),
        "fill": jnp.broadcast_to(jnp.concatenate([fill, other]), (2 * R, 128)),
        "cos": low(jnp.concatenate([c0, c0, c1, c1] * 2, axis=1)),
        "sin": low(jnp.concatenate([-s0, s0, -s1, s1] * 2, axis=1)),
    }
    gn = norm_gains.astype(F32)
    bn = norm_biases.astype(F32)
    gh = head_gains.astype(F32)[:, None]
    bh = head_biases.astype(F32)
    vh = jnp.pad(jnp.concatenate([gh, bh], axis=1), ((0, 0), (0, 4), (0, 0)))
    vn = jnp.stack([gn[:, 0], bn[:, 0], gn[:, 1], bn[:, 1], bn[:, 2], bn[:, 3]], axis=1)
    vn = jnp.pad(vn, ((0, 0), (0, 2), (0, 0)))
    vf = jnp.concatenate([hidden_gains.astype(F32)[:, None], hidden_biases.astype(F32)], axis=1)
    vf = jnp.pad(vf, ((0, 0), (0, 4), (0, pad)))
    gu = jnp.pad(gate_up_weight, ((0, 0), (0, 0), (0, 0), (0, pad)))
    dn = jnp.pad(down_weight, ((0, 0), (0, 0), (0, pad)))
    at_src = [{"in": input_weight[l].reshape(RB, 3 * dim), "out": output_weight[l]} for l in range(layers)]
    ff_src = [{"gu": gu[l].reshape(RB, 2 * HP), "dn": dn[l]} for l in range(layers)]
    grab = lambda d, names: {n: d["g_" + n] for n in names}
    h = low(tokens_in.astype(F32).reshape(rows, width)) * keep
    first = gather_first(at_src[0], AT_G, 0)
    at_w = {0: {n: first["w_" + n] for n in AT_G.names}}
    ff_w, hs, hms, at_f, ff_f = {}, {}, {}, {}, {}
    for l in range(layers):
        hs[l] = h
        at_f[l] = forward_attend(h, tabs, at_w[l], vn[l], vh[l], ff_src[l], FF_G, 1 + 2 * l)
        ff_w[l] = grab(at_f[l], FF_G.names)
        hms[l] = at_f[l]["hm"]
        nxt = l + 1 < layers
        ff_f[l] = forward_hidden(hms[l], tabs, ff_w[l], vn[l], vf[l], at_src[l + 1] if nxt else None, AT_G if nxt else None, 2 + 2 * l)
        if nxt:
            at_w[l + 1] = grab(ff_f[l], AT_G.names)
        h = ff_f[l]["ho"]
    activations = h[:rows].astype(BF).reshape(1, rows, width)
    g = low(cotangent.astype(F32).reshape(rows, width))
    got = {}
    grads, vec, cid = None, None, 2 * layers + 1
    for l in reversed(range(layers)):
        sset = at_scatter() if grads else None
        r = backward_hidden(g, ff_f[l], hms[l], tabs, ff_w[l], vn[l], vf[l], sset, grads, vec, cid)
        if grads:
            got["at", l + 1] = r
        g, vec, grads = r["go"], r["vec"], {"gu": r["d_gu"], "dn": r["d_dn"]}
        r = backward_attend(g, at_f[l], hs[l], tabs, at_w[l], vn[l], vh[l], ff_scatter(), grads, vec, cid + 1)
        got["ff", l] = r
        g, vec, grads = r["go"], r["vec"], {"in": r["d_in"], "out": r["d_out"]}
        cid += 2
    got["at", 0] = scatter_last(at_scatter(), grads, vec, cid)
    input_grad = (keep * g)[:rows].reshape(1, rows, width)
    L = range(layers)
    va = jnp.stack([got["at", l]["r_vec"] for l in L])
    vff = jnp.stack([got["ff", l]["r_vec"] for l in L])
    return (
        activations,
        input_grad,
        jnp.stack([got["at", l]["r_in"].reshape(RB, 3, dim) for l in L]),
        jnp.stack([got["at", l]["r_out"] for l in L]),
        jnp.stack([got["ff", l]["r_gu"].reshape(RB, 2, HP)[:, :, :hidden] for l in L]),
        jnp.stack([got["ff", l]["r_dn"][:, :hidden] for l in L]),
        jnp.stack([va[:, 0, :width], vff[:, 0, :width]], axis=1),
        jnp.stack([va[:, 1, :width], vff[:, 1, :width], va[:, 2, :width], vff[:, 2, :width]], axis=1),
        va[:, 3, :dim],
        va[:, 4:7, :dim],
        vff[:, 3, :hidden],
        vff[:, 4:7, :hidden],
    )


def solution(mesh):
    sizes = dict(mesh.shape)
    fits = sizes == {"dp": 8, "ctx": 2, "tp": 2}
    return jax.shard_map(
        fast_device if fits else on_device,
        mesh=mesh,
        in_specs=(
            P("dp", "ctx", None),
            P("dp", "ctx", None),
            P("dp", "ctx"),
            P(None, "dp", "ctx"),
            P("dp"),
            P(None, ("dp", "ctx"), None, "tp"),
            P(None, ("dp", "ctx"), "tp"),
            P(None, ("dp", "ctx"), None, "tp"),
            P(None, ("dp", "ctx"), "tp"),
            P(),
            P(),
            P(None, "tp"),
            P(None, None, "tp"),
            P(None, "tp"),
            P(None, None, "tp"),
        ),
        out_specs=(
            P("dp", "ctx", None),
            P("dp", "ctx", None),
            P(None, ("dp", "ctx"), None, "tp"),
            P(None, ("dp", "ctx"), "tp"),
            P(None, ("dp", "ctx"), None, "tp"),
            P(None, ("dp", "ctx"), "tp"),
            P(),
            P(),
            P(None, "tp"),
            P(None, None, "tp"),
            P(None, "tp"),
            P(None, None, "tp"),
        ),
        check_vma=False,
    )
```

```python
import functools

import jax
import jax.numpy as jnp
from jax import lax
from jax.experimental import pallas as pl
from jax.experimental.pallas import tpu as pltpu
from jax.sharding import PartitionSpec as P

FF = 2730
HEAD_DIM = 64


norm_epsilon = 1e-06
rotary_base = 10000.0
masked_score = -10000.0


def rotary_tables(positions, not_class):
    quarter = HEAD_DIM // 4
    frequency = rotary_base ** (-jnp.arange(quarter, dtype=jnp.float32) / quarter)
    angles = (
        jnp.transpose(positions).astype(jnp.float32)[:, :, None]
        * frequency
        * not_class[:, None, None]
    )
    return (jnp.cos(angles), jnp.sin(angles))


def rotate(values, cosine, sine, direction):
    row_count, head_count, head_dim = values.shape
    paired = values.reshape(row_count, head_count, 2, 2, head_dim // 4)
    first_half = paired[:, :, :, 0]
    second_half = paired[:, :, :, 1]
    cos_rows = cosine[:, None]
    sin_rows = sine[:, None] * direction
    turned = jnp.stack(
        [
            first_half * cos_rows - second_half * sin_rows,
            second_half * cos_rows + first_half * sin_rows,
        ],
        axis=3,
    )
    return turned.reshape(row_count, head_count, head_dim)


def local_norm(values, gain_vec, shift_vec):
    center = values - jnp.mean(values, axis=-1, keepdims=True)
    spread = jnp.mean(center * center, axis=-1, keepdims=True)
    inv_spread = lax.rsqrt(spread + norm_epsilon)
    unit_rows = center * inv_spread
    return (unit_rows * gain_vec + shift_vec, unit_rows, inv_spread)


def local_norm_back(upstream, unit_rows, inv_spread, gain_vec):
    weighted = upstream * gain_vec
    return inv_spread * (
        weighted
        - jnp.mean(weighted, axis=-1, keepdims=True)
        - unit_rows * jnp.mean(weighted * unit_rows, axis=-1, keepdims=True)
    )


def row_totals(first_part, second_part):
    return lax.psum(
        (jnp.sum(first_part, axis=-1, keepdims=True), jnp.sum(second_part, axis=-1, keepdims=True)),
        "tp",
    )


def split_norm(values, gain_vec, shift_vec, full_width):
    sum_first, sum_second = row_totals(values, values * values)
    row_mean = sum_first / full_width
    inv_spread = lax.rsqrt(sum_second / full_width - row_mean * row_mean + norm_epsilon)
    unit_rows = (values - row_mean) * inv_spread
    return (unit_rows * gain_vec + shift_vec, unit_rows, inv_spread)


def split_norm_back(upstream, unit_rows, inv_spread, gain_vec, full_width):
    weighted = upstream * gain_vec
    sum_first, sum_second = row_totals(weighted, weighted * unit_rows)
    return inv_spread * (weighted - sum_first / full_width - unit_rows * (sum_second / full_width))


def tensor_sum(partial_value):
    return lax.psum(partial_value.astype(jnp.bfloat16), "tp").astype(jnp.float32)


def tensor_back(partial_value):
    return lax.psum(partial_value.astype(jnp.bfloat16), "tp").astype(jnp.float32)


def fetch_weights(layer_index, input_weight, output_weight, gate_up_weight, down_weight):
    return (
        lax.all_gather(input_weight[layer_index], ("dp", "ctx"), axis=0, tiled=True),
        lax.all_gather(output_weight[layer_index], ("dp", "ctx"), axis=0, tiled=True),
        lax.all_gather(gate_up_weight[layer_index], ("dp", "ctx"), axis=0, tiled=True),
        lax.all_gather(down_weight[layer_index], ("dp", "ctx"), axis=0, tiled=True),
    )


def masked_scores(queries, key_heads, valid_keys):
    raw_scores = jnp.einsum("qhe,khe->hqk", queries, key_heads, preferred_element_type=jnp.float32)
    return jnp.where(valid_keys[None, None, :] > 0, raw_scores * HEAD_DIM ** (-0.5), masked_score)


def attend_forward(block_items):
    queries, keys_all, values_all, valid_keys = block_items
    key_count = keys_all.shape[0]
    head_count = queries.shape[1]
    key_heads = keys_all.reshape(key_count, head_count, HEAD_DIM)
    value_heads = values_all.reshape(key_count, head_count, HEAD_DIM)
    scores = masked_scores(queries, key_heads, valid_keys)
    row_max = jnp.max(scores, axis=-1, keepdims=True)
    exp_scores = jnp.exp(scores - row_max)
    row_total = jnp.sum(exp_scores, axis=-1, keepdims=True)
    attn_probs = (exp_scores / row_total).astype(jnp.bfloat16)
    attended = jnp.einsum(
        "hqk,khe->qhe", attn_probs, value_heads, preferred_element_type=jnp.float32
    )
    return (
        attended.reshape(queries.shape[0], head_count * HEAD_DIM),
        (row_max + jnp.log(row_total))[:, :, 0],
    )


def attend_backward(block_items):
    queries, keys_all, values_all, valid_keys, log_total, grad_out = block_items
    key_count = keys_all.shape[0]
    head_count = queries.shape[1]
    key_heads = keys_all.reshape(key_count, head_count, HEAD_DIM)
    value_heads = values_all.reshape(key_count, head_count, HEAD_DIM)
    scores = masked_scores(queries, key_heads, valid_keys)
    probs_full = jnp.exp(scores - log_total[:, :, None])
    probs_low = probs_full.astype(jnp.bfloat16)
    grad_probs = jnp.einsum(
        "qhe,khe->hqk", grad_out, value_heads, preferred_element_type=jnp.float32
    )
    row_dot = jnp.sum(probs_full * grad_probs, axis=-1, keepdims=True)
    grad_raw = jnp.where(
        valid_keys[None, None, :] > 0, HEAD_DIM ** (-0.5) * probs_full * (grad_probs - row_dot), 0.0
    ).astype(jnp.bfloat16)
    grad_queries = jnp.einsum(
        "hqk,khe->qhe", grad_raw, key_heads, preferred_element_type=jnp.float32
    )
    grad_keys = jnp.einsum("hqk,qhe->khe", grad_raw, queries, preferred_element_type=jnp.float32)
    grad_values = jnp.einsum(
        "hqk,qhe->khe", probs_low, grad_out, preferred_element_type=jnp.float32
    )
    local_rows = queries.shape[0]
    return (
        grad_queries.reshape(local_rows, head_count * HEAD_DIM),
        grad_keys.reshape(key_count, head_count * HEAD_DIM),
        grad_values.reshape(key_count, head_count * HEAD_DIM),
    )


def contract_rows(left, right):
    return lax.dot_general(
        left, right, (((0,), (0,)), ((), ())), preferred_element_type=jnp.float32
    )


def contract_cols(left, right):
    return lax.dot_general(
        left, right, (((1,), (1,)), ((), ())), preferred_element_type=jnp.float32
    )


def on_device(
    tokens_in,
    cotangent,
    key_mask,
    grid_pos,
    class_index,
    input_weight,
    output_weight,
    gate_up_weight,
    down_weight,
    norm_gains,
    norm_biases,
    head_gains,
    head_biases,
    hidden_gains,
    hidden_biases,
):
    images, rows_dev, model_width = tokens_in.shape
    row_count = images * rows_dev
    dim_local = head_gains.shape[1]
    heads_local = dim_local // HEAD_DIM
    hidden_local = hidden_gains.shape[1]
    layer_count = input_weight.shape[0]
    first_row = lax.axis_index("ctx") * rows_dev
    places = first_row + jnp.arange(rows_dev, dtype=jnp.int32)
    not_class = (places[None, :] != class_index[:, None]).astype(jnp.float32).reshape(row_count)
    cosine, sine = rotary_tables(grid_pos.reshape(2, row_count), not_class)
    row_keep = key_mask.astype(jnp.float32).reshape(row_count, 1)
    key_keep = key_mask.astype(jnp.bfloat16)
    gains_norm = norm_gains.astype(jnp.float32)
    biases_norm = norm_biases.astype(jnp.float32)
    gains_head = head_gains.astype(jnp.float32)
    biases_head = head_biases.astype(jnp.float32)
    gains_hidden = hidden_gains.astype(jnp.float32)
    biases_hidden = hidden_biases.astype(jnp.float32)
    hidden_state = tokens_in.astype(jnp.float32).reshape(row_count, model_width) * row_keep
    saved_layers = []
    for layer_index in range(layer_count):
        layer_mats = fetch_weights(
            layer_index, input_weight, output_weight, gate_up_weight, down_weight
        )
        mat_in, mat_out, mat_gate_up, mat_down = layer_mats
        normed, unit_one, spread_one = local_norm(
            hidden_state, gains_norm[layer_index, 0], biases_norm[layer_index, 0]
        )
        normed_low = normed.astype(jnp.bfloat16)
        projected = jnp.dot(
            normed_low,
            mat_in.reshape(model_width, 3 * dim_local),
            preferred_element_type=jnp.float32,
        ).reshape(row_count, 3, dim_local)
        queries = projected[:, 0] + biases_head[layer_index, 0]
        keys_proj = projected[:, 1]
        values_proj = projected[:, 2] + biases_head[layer_index, 1]
        query_low = rotate(
            queries.reshape(row_count, heads_local, HEAD_DIM), cosine, sine, 1.0
        ).astype(jnp.bfloat16)
        key_low = rotate(
            keys_proj.reshape(row_count, heads_local, HEAD_DIM), cosine, sine, 1.0
        ).astype(jnp.bfloat16)
        value_low = values_proj.astype(jnp.bfloat16)
        keys_all, values_all, valid_all = (
            lax.all_gather(key_low.reshape(images, rows_dev, dim_local), "ctx", axis=1, tiled=True),
            lax.all_gather(
                value_low.reshape(images, rows_dev, dim_local), "ctx", axis=1, tiled=True
            ),
            lax.all_gather(key_keep, "ctx", axis=1, tiled=True),
        )
        query_blocks = query_low.reshape(images, rows_dev, heads_local, HEAD_DIM)
        attended, log_total = lax.map(
            attend_forward, (query_blocks, keys_all, values_all, valid_all)
        )
        attended = attended.reshape(row_count, dim_local)
        head_normed, unit_two, spread_two = split_norm(
            attended, gains_head[layer_index], biases_head[layer_index, 2], model_width
        )
        head_low = head_normed.astype(jnp.bfloat16)
        branch = tensor_sum(contract_cols(head_low, mat_out))
        hidden_mid = hidden_state + row_keep * (branch + biases_norm[layer_index, 2])
        normed_two, unit_three, spread_three = local_norm(
            hidden_mid, gains_norm[layer_index, 1], biases_norm[layer_index, 1]
        )
        normed_two_low = normed_two.astype(jnp.bfloat16)
        gate_up = jnp.dot(
            normed_two_low,
            mat_gate_up.reshape(model_width, 2 * hidden_local),
            preferred_element_type=jnp.float32,
        ).reshape(row_count, 2, hidden_local)
        gate_pre = gate_up[:, 0] + biases_hidden[layer_index, 0]
        up_pre = gate_up[:, 1] + biases_hidden[layer_index, 1]
        inner_act = jax.nn.silu(gate_pre) * up_pre
        inner_normed, unit_four, spread_four = split_norm(
            inner_act, gains_hidden[layer_index], biases_hidden[layer_index, 2], FF
        )
        inner_low = inner_normed.astype(jnp.bfloat16)
        down_out = tensor_sum(contract_cols(inner_low, mat_down))
        hidden_state = hidden_mid + row_keep * (down_out + biases_norm[layer_index, 3])
        held_mats = None
        saved_layers.append(
            (
                held_mats,
                normed_low,
                unit_one,
                spread_one,
                query_blocks,
                keys_all,
                values_all,
                valid_all,
                log_total,
                unit_two,
                spread_two,
                head_low,
                unit_three,
                spread_three,
                normed_two_low,
                gate_pre,
                up_pre,
                unit_four,
                spread_four,
                inner_low,
            )
        )
    activations = hidden_state.reshape(images, rows_dev, model_width).astype(jnp.bfloat16)
    upstream = cotangent.astype(jnp.float32).reshape(row_count, model_width)
    mat_grads = [None] * layer_count
    vector_parts = [None] * layer_count
    for layer_index in reversed(range(layer_count)):
        (
            held_mats,
            normed_low,
            unit_one,
            spread_one,
            query_blocks,
            keys_all,
            values_all,
            valid_all,
            log_total,
            unit_two,
            spread_two,
            head_low,
            unit_three,
            spread_three,
            normed_two_low,
            gate_pre,
            up_pre,
            unit_four,
            spread_four,
            inner_low,
        ) = saved_layers[layer_index]
        mat_in, mat_out, mat_gate_up, mat_down = fetch_weights(
            layer_index, input_weight, output_weight, gate_up_weight, down_weight
        )
        grad_down = row_keep * upstream
        grad_bias_down = jnp.sum(grad_down, axis=0)
        grad_down_low = grad_down.astype(jnp.bfloat16)
        grad_mat_down = contract_rows(grad_down_low, inner_low)
        grad_inner_normed = jnp.dot(grad_down_low, mat_down, preferred_element_type=jnp.float32)
        grad_gain_hidden = jnp.sum(grad_inner_normed * unit_four, axis=0)
        grad_shift_hidden = jnp.sum(grad_inner_normed, axis=0)
        grad_inner = split_norm_back(
            grad_inner_normed, unit_four, spread_four, gains_hidden[layer_index], FF
        )
        sigmoid_gate = jax.nn.sigmoid(gate_pre)
        grad_up = grad_inner * gate_pre * sigmoid_gate
        grad_gate = grad_inner * up_pre * sigmoid_gate * (1.0 + gate_pre * (1.0 - sigmoid_gate))
        grad_gate_up_low = (
            jnp.stack([grad_gate, grad_up], axis=1)
            .astype(jnp.bfloat16)
            .reshape(row_count, 2 * hidden_local)
        )
        grad_mat_gate_up = contract_rows(normed_two_low, grad_gate_up_low).reshape(
            model_width, 2, hidden_local
        )
        grad_normed_two = tensor_back(
            contract_cols(grad_gate_up_low, mat_gate_up.reshape(model_width, 2 * hidden_local))
        )
        grad_gain_two = jnp.sum(grad_normed_two * unit_three, axis=0)
        grad_shift_two = jnp.sum(grad_normed_two, axis=0)
        upstream = upstream + local_norm_back(
            grad_normed_two, unit_three, spread_three, gains_norm[layer_index, 1]
        )
        grad_branch = row_keep * upstream
        grad_bias_out = jnp.sum(grad_branch, axis=0)
        grad_branch_low = grad_branch.astype(jnp.bfloat16)
        grad_mat_out = contract_rows(grad_branch_low, head_low)
        grad_head = jnp.dot(grad_branch_low, mat_out, preferred_element_type=jnp.float32)
        grad_gain_head = jnp.sum(grad_head * unit_two, axis=0)
        grad_shift_head = jnp.sum(grad_head, axis=0)
        grad_attended = split_norm_back(
            grad_head, unit_two, spread_two, gains_head[layer_index], model_width
        )
        grad_att_low = grad_attended.astype(jnp.bfloat16).reshape(
            images, rows_dev, heads_local, HEAD_DIM
        )
        grad_query_rot, grad_keys_all, grad_values_all = lax.map(
            attend_backward,
            (query_blocks, keys_all, values_all, valid_all, log_total, grad_att_low),
        )
        grad_keys_rot, grad_values = (
            lax.psum_scatter(
                grad_keys_all.astype(jnp.bfloat16), "ctx", scatter_dimension=1, tiled=True
            ).astype(jnp.float32),
            lax.psum_scatter(
                grad_values_all.astype(jnp.bfloat16), "ctx", scatter_dimension=1, tiled=True
            ).astype(jnp.float32),
        )
        grad_queries = rotate(
            grad_query_rot.reshape(row_count, heads_local, HEAD_DIM), cosine, sine, -1.0
        ).reshape(row_count, dim_local)
        grad_keys = rotate(
            grad_keys_rot.reshape(row_count, heads_local, HEAD_DIM), cosine, sine, -1.0
        ).reshape(row_count, dim_local)
        grad_values = grad_values.reshape(row_count, dim_local)
        grad_proj_low = (
            jnp.stack([grad_queries, grad_keys, grad_values], axis=1)
            .astype(jnp.bfloat16)
            .reshape(row_count, 3 * dim_local)
        )
        grad_mat_in = contract_rows(normed_low, grad_proj_low).reshape(model_width, 3, dim_local)
        grad_normed_one = tensor_back(
            contract_cols(grad_proj_low, mat_in.reshape(model_width, 3 * dim_local))
        )
        grad_gain_one = jnp.sum(grad_normed_one * unit_one, axis=0)
        grad_shift_one = jnp.sum(grad_normed_one, axis=0)
        upstream = upstream + local_norm_back(
            grad_normed_one, unit_one, spread_one, gains_norm[layer_index, 0]
        )
        mat_grads[layer_index] = (
            lax.psum_scatter(grad_mat_in, ("dp", "ctx"), scatter_dimension=0, tiled=True),
            lax.psum_scatter(grad_mat_out, ("dp", "ctx"), scatter_dimension=0, tiled=True),
            lax.psum_scatter(grad_mat_gate_up, ("dp", "ctx"), scatter_dimension=0, tiled=True),
            lax.psum_scatter(grad_mat_down, ("dp", "ctx"), scatter_dimension=0, tiled=True),
        )
        vector_parts[layer_index] = (
            jnp.stack([grad_gain_one, grad_gain_two]),
            jnp.stack([grad_shift_one, grad_shift_two, grad_bias_out, grad_bias_down]),
            grad_gain_head,
            jnp.stack(
                [jnp.sum(grad_queries, axis=0), jnp.sum(grad_values, axis=0), grad_shift_head]
            ),
            grad_gain_hidden,
            jnp.stack([jnp.sum(grad_gate, axis=0), jnp.sum(grad_up, axis=0), grad_shift_hidden]),
        )
    input_grad = (row_keep * upstream).reshape(images, rows_dev, model_width)
    stacked_vectors = tuple(
        (
            jnp.stack([vector_parts[index][member] for index in range(layer_count)])
            for member in range(6)
        )
    )
    summed_vectors = lax.psum(
        (
            stacked_vectors[0],
            stacked_vectors[1],
            stacked_vectors[2],
            stacked_vectors[3],
            stacked_vectors[4],
            stacked_vectors[5],
        ),
        ("dp", "ctx"),
    )
    grad_input_weight = jnp.stack([mat_grads[index][0] for index in range(layer_count)])
    grad_output_weight = jnp.stack([mat_grads[index][1] for index in range(layer_count)])
    grad_gate_up_weight = jnp.stack([mat_grads[index][2] for index in range(layer_count)])
    grad_down_weight = jnp.stack([mat_grads[index][3] for index in range(layer_count)])
    return (
        activations,
        input_grad,
        grad_input_weight,
        grad_output_weight,
        grad_gate_up_weight,
        grad_down_weight,
        summed_vectors[0],
        summed_vectors[1],
        summed_vectors[2],
        summed_vectors[3],
        summed_vectors[4],
        summed_vectors[5],
    )


MESH = pl.DeviceIdType.MESH

RB=64

class Where:
    def __init__(self):
        self.dp=lax.axis_index("dp"); self.x=lax.axis_index("ctx"); self.c=lax.axis_index("tp")
        self.z=self.dp//2; self.y=self.dp%2
    def nx(self): return (self.dp,1-self.x,self.c)
    def ny(self): return (self.z*2+1-self.y,self.x,self.c)
    def up(self): return ((self.z+1)*2+self.y,self.x,self.c)
    def dn(self): return ((self.z-1)*2+self.y,self.x,self.c)

def greet(w):
    bar=pltpu.get_barrier_semaphore()
    def sig(dev): pl.semaphore_signal(bar,inc=1,device_id=dev,device_id_type=MESH)
    sig(w.nx()); sig(w.ny())
    @pl.when(w.z<3)
    def _(): sig(w.up())
    @pl.when(w.z>0)
    def _(): sig(w.dn())
    pl.semaphore_wait(bar,2+(w.z<3).astype(jnp.int32)+(w.z>0).astype(jnp.int32))

class Gather:
    def __init__(self,w,order,src,out,r0,nr,ssem,rsem,own_sem):
        self.w,self.order,self.src,self.out,self.r0,self.nr=w,order,src,out,r0,nr
        self.ssem,self.rsem=ssem,rsem
        self.pending=[]
    def rows(self,zz,yy,xx):
        return pl.ds(pl.multiple_of(((zz*2+yy)*2+xx)*RB+self.r0,16),self.nr)
    def here(self,zz,yy,xx,own=False):
        return self.src.at[pl.ds(self.r0,self.nr)] if own else self.out.at[self.rows(zz,yy,xx)]
    def copy(self,zz,yy,xx,dev,s,r,own=False):
        return pltpu.make_async_remote_copy(src_ref=self.here(zz,yy,xx,own),dst_ref=self.out.at[self.rows(zz,yy,xx)],
            send_sem=self.ssem.at[s],recv_sem=self.rsem.at[r],device_id=dev,device_id_type=MESH)
    def send(self,cond,*a,**k):
        self.pending.append((cond,a,k))
        if cond is None: self.copy(*a,**k).start()
        else:
            @pl.when(cond)
            def _(): self.copy(*a,**k).start()
    def finish_sends(self):
        for cond,a,k in self.pending:
            if cond is None: self.copy(*a,**k).wait_send()
            else:
                @pl.when(cond)
                def _(a=a,k=k): self.copy(*a,**k).wait_send()
    def arrived(self,zz,yy,xx,r):
        self.copy(zz,yy,xx,self.w.nx(),0,r).wait_recv()

class GatherZ(Gather):
    def pq(self,zz,pself):
        w=self.w
        if self.order=="zyx": return (zz,w.y if pself else 1-w.y,w.x)
        return (zz,w.y,w.x if pself else 1-w.x)
    def pdev(self): return self.w.ny() if self.order=="zyx" else self.w.nx()
    def qdev(self): return self.w.nx() if self.order=="zyx" else self.w.ny()
    def qcoord(self,zz,pself):
        w=self.w
        if self.order=="zyx": return (zz,w.y if pself else 1-w.y,1-w.x)
        return (zz,1-w.y,w.x if pself else 1-w.x)
    def emit(self,cond,zz,k,own=False):
        b=self.pq(zz,True)
        w=self.w
        if k<4:
            c=(w.z<3) if cond is None else jnp.logical_and(cond,w.z<3)
            self.send(c,*b,w.up(),k,zz,own=own)
        if k==0 or k>=4:
            c=(w.z>0) if cond is None else jnp.logical_and(cond,w.z>0)
            self.send(c,*b,w.dn(),7+(k if k==0 else k-3),zz,own=own)
        self.send(cond,*b,self.pdev(),11+k,4+zz,own=own)
        self.send(cond,*b,self.qdev(),18+k,8+zz*2,own=own)
    def rounds(self):
        w=self.w
        self.emit(None,w.z,0,own=True)
        yield
        for k in (1,2,3):
            for kk,zz,cond in ((k,w.z-k,w.z>=k),(k+3,w.z+k,w.z+k<=3)):
                @pl.when(cond)
                def _(zz=zz): self.arrived(*self.pq(zz,True),zz)
                self.emit(cond,zz,kk)
            yield
        for k in (0,1,2,3):
            for kk,zz,cond in (((0,w.z,None),) if k==0 else ((k,w.z-k,w.z>=k),(k+3,w.z+k,w.z+k<=3))):
                b=self.pq(zz,False)
                def go(zz=zz,b=b): self.arrived(*b,4+zz)
                if cond is None: go()
                else: pl.when(cond)(go)
                self.send(cond,*b,self.qdev(),25+kk,8+zz*2+1)
            yield
    def finish(self):
        for zz in range(4):
            for pself in (True,False):
                self.arrived(*self.qcoord(zz,pself),8+zz*2+(0 if pself else 1))
        self.finish_sends()
    NS,NR=32,16

class GatherX(Gather):
    NS,NR=3+4*7,19
    def blk(self,zz,j):
        w=self.w
        return (zz,w.y if j<2 else 1-w.y,w.x if j%2==0 else 1-w.x)
    def vert(self,cond,zz,j,k,own=False):
        w=self.w; b=self.blk(zz,j)
        if k<4:
            c=(w.z<3) if cond is None else jnp.logical_and(cond,w.z<3)
            self.send(c,*b,w.up(),3+j*7+k if k else 3+j*7,3+zz*4+j,own=own)
        if k==0 or k>=4:
            c=(w.z>0) if cond is None else jnp.logical_and(cond,w.z>0)
            self.send(c,*b,w.dn(),3+j*7+(k if k>=4 else 3),3+zz*4+j,own=own)
    def rounds(self):
        w=self.w
        self.send(None,*self.blk(w.z,0),w.nx(),0,0,own=True)
        self.send(None,*self.blk(w.z,0),w.ny(),1,1,own=True)
        self.vert(None,w.z,0,0,own=True)
        yield
        b=self.blk(w.z,1); self.arrived(*b,0)
        self.send(None,*b,w.ny(),2,2)
        yield
        yield
        yield
        self.arrived(*self.blk(w.z,2),1)
        self.arrived(*self.blk(w.z,3),2)
        for j in range(1,4): self.vert(None,w.z,j,0)
        yield
        for k in (1,2,3):
            for j in range(4):
                for kk,zz,cond in ((k,w.z-k,w.z>=k),(k+3,w.z+k,w.z+k<=3)):
                    @pl.when(cond)
                    def _(zz=zz,j=j): self.arrived(*self.blk(zz,j),3+zz*4+j)
                    if k<3: self.vert(cond,zz,j,kk)
                if j%2==1: yield
    def finish(self):
        self.finish_sends()


ZORD=(3,0,2,1)
class Scatter:
    def __init__(self,w,order,src,out,r0,nr,ssem,rsem,lsem,own,bufs):
        self.w,self.order,self.src,self.out,self.r0,self.nr=w,order,src,out,r0,nr
        self.ssem,self.rsem,self.lsem,self.own=ssem,rsem,lsem,own
        self.bufs=bufs
        self.pending=[]
    def rows(self,zz,yy,xx):
        return pl.ds(pl.multiple_of(((zz*2+yy)*2+xx)*RB+self.r0,16),self.nr)
    def send(self,cond,src,dst,dev,s,r):
        mk=lambda: pltpu.make_async_remote_copy(src_ref=src,dst_ref=dst,send_sem=self.ssem.at[s],recv_sem=self.rsem.at[r],device_id=dev,device_id_type=MESH)
        self.pending.append((cond,mk))
        if cond is None: mk().start()
        else: pl.when(cond)(lambda: mk().start())
    def wait(self,cond,dst,r):
        def go(): pltpu.make_async_remote_copy(src_ref=dst,dst_ref=dst,send_sem=self.ssem.at[0],recv_sem=self.rsem.at[r],device_id=self.w.nx(),device_id_type=MESH).wait_recv()
        if cond is None: go()
        else: pl.when(cond)(go)
    def finish(self):
        for cond,mk in self.pending:
            if cond is None: mk().wait_send()
            else: pl.when(cond)(lambda mk=mk: mk().wait_send())
    def total(self,dst,terms,extra=()):
        def strip(i,_):
            s=pl.ds(pl.multiple_of(i*16,16),16)
            t=terms[0][s].astype(jnp.float32)
            for r in terms[1:]: t=t+r[s].astype(jnp.float32)
            dst[s]=t.astype(dst.dtype)
            return 0
        lax.fori_loop(0,self.nr//16,strip,0)

class ScatterZ(Scatter):
    NS,NR=16,17
    def mine(self,zz,pself):
        w=self.w
        if self.order=="zyx": return (zz,w.y if pself else 1-w.y,w.x)
        return (zz,w.y,w.x if pself else 1-w.x)
    def theirs(self,zz,pself):
        w=self.w
        if self.order=="zyx": return (zz,w.y if pself else 1-w.y,1-w.x)
        return (zz,1-w.y,w.x if pself else 1-w.x)
    def rounds(self):
        w=self.w; rq,rp,ru=self.bufs
        pdev=w.ny() if self.order=="zyx" else w.nx()
        qdev=w.nx() if self.order=="zyx" else w.ny()
        loc={}
        for k in (1,0):
            for zz in ZORD:
                c=pltpu.make_async_copy(self.src.at[self.rows(*self.mine(zz,k==0))],self.own.at[zz*2+k],self.lsem.at[zz*2+k]); c.start(); loc[zz*2+k]=c
        for zz in ZORD:
            self.send(None,self.src.at[self.rows(*self.theirs(zz,False))],rq.at[zz*2+1],qdev,zz*2+1,zz*2+1)
        yield
        for zz in ZORD:
            i=zz*2+1
            loc[i].wait(); self.wait(None,rq.at[i],i)
            self.total(rq.at[i],[self.own.at[i],rq.at[i]])
            self.send(None,rq.at[i],rp.at[zz],pdev,8+zz,8+zz)
            self.send(None,self.src.at[self.rows(*self.theirs(zz,True))],rq.at[zz*2],qdev,zz*2,zz*2)
            yield
        def ready(zz):
            loc[zz*2].wait(); self.wait(None,rq.at[zz*2],zz*2); self.wait(None,rp.at[zz],8+zz)
            return [self.own.at[zz*2],rq.at[zz*2],rp.at[zz]]
        for t in (1,2,3):
            for i in range(4):
                for up in (True,False):
                    m=i if up else 3-i
                    if m>=t: continue
                    zz=4-t+m if up else t-1-m
                    @pl.when(w.z==i)
                    def _():
                        terms=ready(zz)
                        if m>0:
                            self.wait(None,ru.at[zz],12+zz); terms.append(ru.at[zz])
                        self.total(rp.at[zz],terms)
                    if up: self.send(w.z==i,rp.at[zz],ru.at[zz],w.up(),12+zz,12+zz)
                    else:
                        to=4 if zz==i-1 else zz
                        self.send(w.z==i,rp.at[zz],ru.at[to],w.dn(),12+zz,12+to)
            yield
        o=self.out.at[pl.ds(self.r0,self.nr)]
        for zz in range(4):
            @pl.when(w.z==zz)
            def _():
                terms=ready(zz)
                if zz>0: self.wait(None,ru.at[zz],12+zz); terms.append(ru.at[zz])
                if zz<3: self.wait(None,ru.at[4],16); terms.append(ru.at[4])
                self.total(o,terms)
        yield

class ScatterX(Scatter):
    NS,NR=19,23
    def blk(self,zz,j):
        w=self.w
        return (zz,w.y if j<2 else 1-w.y,w.x if j%2==0 else 1-w.x)
    def rounds(self):
        w=self.w; ru,ry,rx=self.bufs
        down=lambda zz,j: jnp.where(w.z-1==zz,16+j,zz*4+j)
        loc={}
        for zz in ZORD:
            for j in (3,2,1,0):
                i=zz*4+j
                c=pltpu.make_async_copy(self.src.at[self.rows(*self.blk(zz,j))],self.own.at[i],self.lsem.at[i]); c.start(); loc[i]=c
        J=(3,2,1,0)
        for zz in (3,2,1):
            for j in J: self.send(w.z==0,self.src.at[self.rows(*self.blk(zz,j))],ru.at[zz*4+j],w.up(),zz*4+j,zz*4+j)
        for zz in (0,1,2):
            for j in J:
                to=16+j if zz==2 else zz*4+j
                self.send(w.z==3,self.src.at[self.rows(*self.blk(zz,j))],ru.at[to],w.dn(),zz*4+j,to)
        yield
        for i in loc: loc[i].wait()
        def hop(c,zz,j,up):
            i=zz*4+j
            @pl.when(w.z==c)
            def _():
                self.wait(None,ru.at[i],i)
                self.total(ru.at[i],[self.own.at[i],ru.at[i]])
            if up: self.send(w.z==c,ru.at[i],ru.at[i],w.up(),i,i)
            else:
                to=16+j if zz==c-1 else i
                self.send(w.z==c,ru.at[i],ru.at[to],w.dn(),i,to)
        for j in J:
            hop(1,3,j,True); hop(2,0,j,False)
            if j%2==0: yield
        for j in J:
            hop(1,2,j,True); hop(2,1,j,False)
            hop(2,3,j,True); hop(1,0,j,False)
            if j%2==0: yield
        def zsum(j,dst,extra):
            for zz in range(4):
                i=zz*4+j
                t=[self.own.at[i]]
                if zz>0: t.append(ru.at[i])
                if zz<3: t.append(ru.at[16+j])
                @pl.when(w.z==zz)
                def _():
                    if zz>0: self.wait(None,ru.at[i],i)
                    if zz<3: self.wait(None,ru.at[16+j],16+j)
                    self.total(dst,t+extra)
        sy=self.bufs_stage
        for j in (3,2):
            k=j-2
            zsum(j,sy.at[k],[])
            self.send(None,sy.at[k],ry.at[k],w.ny(),16+k,20+k)
        yield
        self.wait(None,ry.at[1],21)
        zsum(1,sy.at[2],[ry.at[1]])
        self.send(None,sy.at[2],rx.at[0],w.nx(),18,22)
        yield
        self.wait(None,ry.at[0],20)
        self.wait(None,rx.at[0],22)
        zsum(0,self.out.at[pl.ds(self.r0,self.nr)],[ry.at[0],rx.at[0]])
        yield


F32 = jnp.float32
BF = jnp.bfloat16
DMA = pltpu.SemaphoreType.DMA
EPS = 1e-06


def step_all(gens):
    gens = list(gens)
    while gens:
        for g in list(gens):
            try:
                next(g)
            except StopIteration:
                gens.remove(g)
                continue
            yield


def drive(compute, comm, plan, rest):
    for i, _ in enumerate(compute):
        for _ in range(plan[i] if i < len(plan) else rest):
            next(comm, None)
    for _ in comm:
        pass


class GatherSet:
    def __init__(self, parts, names, cut=32):
        self.parts, self.names, self.cut = parts, names, cut

    def scratch(self):
        out = []
        for name, cols, kind in self.parts:
            if kind == "z":
                out += [DMA((GatherZ.NS,)), DMA((GatherZ.NR,))] * 2
            else:
                out += [DMA((GatherX.NS,)), DMA((GatherX.NR,))]
        return out + [DMA((len(self.names),))]

    def start(self, w, srcs, outs, sems):
        sems = list(sems)
        me = pl.multiple_of((w.dp * 2 + w.x) * RB, 16)
        self.locs = []
        for i, name in enumerate(self.names):
            c = pltpu.make_async_copy(srcs[name], outs[name].at[pl.ds(me, RB)], sems[-1].at[i])
            c.start()
            self.locs.append(c)
        self.live = []
        for name, cols, kind in self.parts:
            s, o = srcs[name], outs[name]
            if cols is not None:
                s, o = s.at[:, cols[0] : cols[1]], o.at[:, cols[0] : cols[1]]
            if kind == "z":
                for r0, nr, order in ((0, self.cut, "zyx"), (self.cut, RB - self.cut, "zxy")):
                    self.live.append(GatherZ(w, order, s, o, r0, nr, sems.pop(0), sems.pop(0), None))
            else:
                self.live.append(GatherX(w, "xyz", s, o, 0, 64, sems.pop(0), sems.pop(0), None))
        return step_all([p.rounds() for p in self.live])

    def finish(self):
        for p in self.live:
            p.finish()
        for c in self.locs:
            c.wait()


class VecSum:
    def __init__(self, w, src, out, st, rv, ss, rs):
        self.w, self.src, self.out, self.st, self.rv, self.ss, self.rs = w, src, out, st, rv, ss, rs

    def mk(self, src, k, dev, send):
        return pltpu.make_async_remote_copy(
            src_ref=src, dst_ref=self.rv.at[k], send_sem=self.ss.at[send], recv_sem=self.rs.at[k],
            device_id=dev, device_id_type=MESH)

    def rounds(self):
        w = self.w
        st, rv = self.st, self.rv
        even = w.z % 2 == 0
        odd = w.z % 2 == 1
        mid = jnp.logical_and(w.z > 0, w.z < 3)
        self.mk(self.src, 0, w.nx(), 0).start()
        yield
        yield
        self.mk(self.src, 0, w.nx(), 0).wait_recv()
        st[0] = self.src[...] + rv[0]
        self.mk(st.at[0], 1, w.ny(), 1).start()
        yield
        yield
        self.mk(self.src, 1, w.ny(), 1).wait_recv()
        st[1] = st[0] + rv[1]
        pl.when(even)(lambda: self.mk(st.at[1], 2, w.up(), 2).start())
        pl.when(odd)(lambda: self.mk(st.at[1], 2, w.dn(), 2).start())
        yield
        yield
        self.mk(self.src, 2, w.nx(), 2).wait_recv()
        st[2] = st[1] + rv[2]
        pl.when(w.z == 1)(lambda: self.mk(st.at[2], 3, w.up(), 3).start())
        pl.when(w.z == 2)(lambda: self.mk(st.at[2], 3, w.dn(), 3).start())
        yield
        yield

        @pl.when(mid)
        def _():
            self.mk(self.src, 3, w.nx(), 3).wait_recv()
            st[3] = st[2] + rv[3]
            self.out[...] = st[3]

        pl.when(w.z == 1)(lambda: self.mk(st.at[3], 4, w.dn(), 4).start())
        pl.when(w.z == 2)(lambda: self.mk(st.at[3], 4, w.up(), 4).start())
        yield
        yield

        @pl.when(jnp.logical_not(mid))
        def _():
            self.mk(self.src, 4, w.nx(), 4).wait_recv()
            self.out[...] = rv[4]

        yield
        yield

    def finish(self):
        w = self.w
        self.mk(self.src, 0, w.nx(), 0).wait_send()
        self.mk(self.src, 0, w.nx(), 1).wait_send()
        self.mk(self.src, 0, w.nx(), 2).wait_send()

        @pl.when(jnp.logical_and(w.z > 0, w.z < 3))
        def _():
            self.mk(self.src, 0, w.nx(), 3).wait_send()
            self.mk(self.src, 0, w.nx(), 4).wait_send()


class ScatterSet:
    def __init__(self, parts, names, widths, cut=32, vec=True):
        self.parts, self.names, self.widths, self.cut, self.vec = parts, names, widths, cut, vec

    def scratch(self):
        V = lambda *s: pltpu.VMEM(s, BF)
        sc = []
        for name, cols, kind in self.parts:
            C = self.widths[name] if cols is None else cols[1] - cols[0]
            if kind == "z":
                for nr in (self.cut, RB - self.cut):
                    sc += [DMA((ScatterZ.NS,)), DMA((ScatterZ.NR,)), DMA((8,))]
                    sc += [V(8, nr, C), V(8, nr, C), V(4, nr, C), V(5, nr, C)]
            else:
                sc += [DMA((ScatterX.NS,)), DMA((ScatterX.NR,)), DMA((16,))]
                sc += [V(16, 64, C), V(20, 64, C), V(2, 64, C), V(1, 64, C), V(3, 64, C)]
        if self.vec:
            sc += [pltpu.VMEM((4, 8, HP), F32), pltpu.VMEM((5, 8, HP), F32), DMA((5,)), DMA((5,))]
        return sc

    def start(self, w, srcs, outs, vec, vec_out, sc):
        sc = list(sc)
        self.live = []
        for name, cols, kind in self.parts:
            s, o = srcs[name], outs[name]
            if cols is not None:
                s, o = s.at[:, cols[0] : cols[1]], o.at[:, cols[0] : cols[1]]
            if kind == "z":
                for r0, nr, order in ((0, self.cut, "zyx"), (self.cut, RB - self.cut, "zxy")):
                    ss, rs, ls, own, rq, rp, ru = [sc.pop(0) for _ in range(7)]
                    self.live.append(ScatterZ(w, order, s, o, r0, nr, ss, rs, ls, own, (rq, rp, ru)))
            else:
                ss, rs, ls, own, ru, ry, rx, st = [sc.pop(0) for _ in range(8)]
                p = ScatterX(w, "xyz", s, o, 0, 64, ss, rs, ls, own, (ru, ry, rx))
                p.bufs_stage = st
                self.live.append(p)
        if self.vec:
            st, rv, ss, rs = sc
            self.live.append(VecSum(w, vec, vec_out, st, rv, ss, rs))
        return step_all([p.rounds() for p in self.live])

    def finish(self):
        for p in self.live:
            p.finish()


FF_CUT = 16
AT_G = GatherSet([("in", None, "z"), ("out", None, "x")], ["in", "out"])
FF_G = GatherSet([("gu", None, "z"), ("dn", (0, 512), "z"), ("dn", (512, 1408), "x")], ["gu", "dn"], FF_CUT)


def at_scatter():
    return ScatterSet([("in", None, "z"), ("out", None, "x")], ["in", "out"], {"in": 1536, "out": 512})


def gu_scatter():
    return ScatterSet([("gu", (0, 2176), "z"), ("gu", (2176, 2816), "x")], ["gu"], {"gu": 2816}, FF_CUT)


def dn_scatter():
    return ScatterSet([("dn", (0, 1024), "z"), ("dn", (1024, 1408), "x")], ["dn"], {"dn": 1408}, 32, False)


def rows16(n, fn, step=176):
    def body(i, _):
        fn(pl.ds(pl.multiple_of(i * step, 16), step))
        return 0

    lax.fori_loop(0, n // step, body, 0)


def unit_of(x, width):
    mean = jnp.sum(x, axis=-1, keepdims=True) / width
    c = x - mean
    inv = lax.rsqrt(jnp.sum(c * c, axis=-1, keepdims=True) / width + EPS)
    return c * inv, inv


def dot_nn(a, b):
    return jnp.dot(a, b, preferred_element_type=F32)


def dot_nt(a, b):
    return lax.dot_general(a, b, (((1,), (1,)), ((), ())), preferred_element_type=F32)


def dot_tn(a, b):
    return lax.dot_general(a, b, (((0,), (0,)), ((), ())), preferred_element_type=F32)


def tiles(n, size=256):
    return [(a, min(size, n - a)) for a in range(0, n, size)]


def fold8(x):
    return jnp.sum(x.reshape(x.shape[0] // 8, 8, x.shape[1]), axis=0)


def wide(x, n):
    return jnp.concatenate([x] * (-(-n // 128)), axis=1)[:, :n]


def two_cols(a, b):
    lane = lax.broadcasted_iota(jnp.int32, (a.shape[0], 128), 1)
    return jnp.where(lane == 0, a, jnp.where(lane == 1, b, 0.0))


def turn(x, cos, sin):
    lane = lax.broadcasted_iota(jnp.int32, x.shape, 1)
    other = jnp.where((lane // 16) % 2 == 0, pltpu.roll(x, 112, 1), pltpu.roll(x, 16, 1))
    return x * cos + other * sin


def head_lanes(x, t):
    lane = lax.broadcasted_iota(jnp.int32, x.shape, 1)
    return jnp.where(lane // 64 == t, x, jnp.zeros_like(x))


class Peer:
    def __init__(self, dev, ss, rs):
        self.dev, self.ss, self.rs, self.open = dev, ss, rs, []

    def mk(self, src, dst, k):
        return pltpu.make_async_remote_copy(
            src_ref=src, dst_ref=dst, send_sem=self.ss.at[k], recv_sem=self.rs.at[k], device_id=self.dev, device_id_type=MESH)

    def send(self, src, dst, k):
        c = self.mk(src, dst, k)
        c.start()
        self.open.append(c)

    def recv(self, dst, k):
        self.mk(dst, dst, k).wait_recv()

    def finish(self):
        for c in self.open:
            c.wait_send()


def greet_all(w, links):
    bar = pltpu.get_barrier_semaphore()

    def sig(dev):
        pl.semaphore_signal(bar, inc=1, device_id=dev, device_id_type=MESH)

    sig((w.dp, w.x, 1 - w.c))
    n = jnp.int32(1)
    if links != "core":
        sig(w.nx())
        n = n + 1
    if links == "all":
        sig(w.ny())
        pl.when(w.z < 3)(lambda: sig(w.up()))
        pl.when(w.z > 0)(lambda: sig(w.dn()))
        n = n + 1 + (w.z < 3).astype(jnp.int32) + (w.z > 0).astype(jnp.int32)
    pl.semaphore_wait(bar, n)


class Bag:
    def launch(self):
        self.coming = {n: pltpu.make_async_copy(h, getattr(self, n), self.ld.at[i]) for i, (n, h) in enumerate(self.loads)}
        for c in self.coming.values():
            c.start()
        self.going = []

    def need(self, *names):
        for n in names:
            if n in self.coming:
                self.coming.pop(n).wait()

    def put(self, name, cols=None):
        s, d = getattr(self, name), self.stores[name]
        if cols is not None:
            s, d = s.at[:, cols[0] : cols[1]], d.at[:, cols[0] : cols[1]]
        c = pltpu.make_async_copy(s, d, self.so.at[len(self.going)])
        c.start()
        self.going.append(c)

    def flush(self):
        self.need(*list(self.coming))
        for c in self.going:
            c.wait()


def run_kernel(body, name, cid, ins, outs, scratch, extra=()):
    iname, oname, sname = list(ins), list(outs), list(scratch)
    ld = [n for n in iname if ins[n][1] == "LD"]
    so = [n for n in oname if outs[n][2] == "ST"]
    moved = [pltpu.VMEM(ins[n][0].shape, ins[n][0].dtype) for n in ld] + [pltpu.VMEM(outs[n][0], outs[n][1]) for n in so]
    moved += [DMA((max(len(ld), 1),)), DMA((16,))]

    def kernel(*refs):
        b = Bag()
        ni, no, ns, nm = len(iname), len(oname), len(sname), len(moved)
        for n, r in zip(iname + oname + sname, refs):
            setattr(b, n, r)
        mv = refs[ni + no + ns : ni + no + ns + nm]
        b.loads = [(n, getattr(b, n)) for n in ld]
        b.stores = {n: getattr(b, n) for n in so}
        for n, r in zip(ld + so, mv):
            setattr(b, n, r)
        b.ld, b.so = mv[-2:]
        b.extra = refs[ni + no + ns + nm :]
        b.launch()
        body(b)
        b.flush()

    place = lambda s: pl.BlockSpec(memory_space=pl.ANY if s in ("LD", "ST") else s)
    res = pl.pallas_call(
        kernel,
        out_shape=[jax.ShapeDtypeStruct(outs[n][0], outs[n][1]) for n in oname],
        in_specs=[place(ins[n][1]) for n in iname],
        out_specs=[place(outs[n][2]) for n in oname],
        scratch_shapes=[scratch[n] for n in sname] + moved + list(extra),
        compiler_params=pltpu.CompilerParams(collective_id=cid, has_side_effects=True, vmem_limit_bytes=62 * 2**20),
        name=name,
    )(*[ins[n][0] for n in iname])
    return dict(zip(oname, res))


VM = pltpu.VMEM
ANY = pl.ANY
LD, ST = "LD", "ST"


def gather_first(srcs, gset, cid):
    names = gset.names

    def body(b):
        w = Where()
        greet(w)
        g = gset.start(w, {n: getattr(b, "s_" + n) for n in names}, {n: getattr(b, "w_" + n) for n in names}, b.extra)
        for _ in g:
            pass
        gset.finish()

    return run_kernel(
        body, "gather", cid,
        {"s_" + n: (srcs[n], ANY) for n in names},
        {"w_" + n: ((16 * RB, srcs[n].shape[1]), BF, ANY) for n in names},
        {}, gset.scratch())


def attend_body(b, w, R, core, side):
    hp = b.h.shape[1]
    b.need("h", "vn")
    rows16(R, lambda s: norm_store(b.n, s, b.h[s], b.vn[0:1, :], b.vn[1:2, :]))
    b.need("w_in", "cos", "sin", "keep", "vh")
    D = 512
    for j in range(2):
        kt = dot_nn(b.n[...], b.w_in[:, D + 256 * j : D + 256 * j + 256])
        for hf in range(2):
            l = slice(256 * j + 128 * hf, 256 * j + 128 * hf + 128)
            b.k[0:R, l] = (turn(kt[:, 128 * hf : 128 * hf + 128], b.cos[...], b.sin[...]) * b.keep[...]).astype(BF)
        l = slice(256 * j, 256 * j + 256)
        side.send(b.k.at[pl.ds(0, R), l], b.k.at[pl.ds(R, R), l], 2 * j)
        vt = dot_nn(b.n[...], b.w_in[:, 2 * D + 256 * j : 2 * D + 256 * j + 256]) + b.vh[2:3, l]
        b.v[0:R, l] = vt.astype(BF)
        side.send(b.v.at[pl.ds(0, R), l], b.v.at[pl.ds(R, R), l], 2 * j + 1)
        yield
    for j in range(2):
        qt = dot_nn(b.n[...], b.w_in[:, 256 * j : 256 * j + 256]) + b.vh[1:2, 256 * j : 256 * j + 256]
        for hf in range(2):
            l = slice(256 * j + 128 * hf, 256 * j + 128 * hf + 128)
            b.q[:, l] = (turn(qt[:, 128 * hf : 128 * hf + 128], b.cos[...], b.sin[...]) * 0.125).astype(BF)
    b.put("q")
    b.need("fill")
    yield
    S = 176
    for p in range(4):
        l = slice(128 * p, 128 * p + 128)
        if p % 2 == 0:
            j = p // 2
            lj = slice(256 * j, 256 * j + 256)
            side.recv(b.k.at[pl.ds(R, R), lj], 2 * j)
            side.recv(b.v.at[pl.ds(R, R), lj], 2 * j + 1)
        kp = b.k[:, l]
        vT = b.v[:, l].T
        halves = []
        for t in range(2):
            b.s[...] = dot_nt(kp, head_lanes(b.q[:, l], t))

            def top(i, m):
                r = pl.ds(pl.multiple_of(i * S, 16), S)
                x = b.s[r] + wide(b.fill[r], R)
                return jnp.maximum(m, jnp.max(x.reshape(S // 8, 8, R), axis=0))

            m = lax.fori_loop(0, 2 * R // S, top, jnp.full((8, R), -3.0e38, F32))
            m = jnp.max(m, axis=0, keepdims=True)

            def expo(i, acc):
                r = pl.ds(pl.multiple_of(i * S, 16), S)
                x = jnp.exp(b.s[r] + wide(b.fill[r], R) - m)
                b.p[r] = x.astype(BF)
                return acc + jnp.sum(x.reshape(S // 8, 8, R), axis=0)

            tot = lax.fori_loop(0, 2 * R // S, expo, jnp.zeros((8, R), F32))
            tot = jnp.sum(tot, axis=0, keepdims=True)
            halves.append(dot_nn(vT[64 * t : 64 * t + 64], b.p[...]) / tot)
            b.lse[2 * p + t : 2 * p + t + 1, :] = m + jnp.log(tot)
            yield
        b.o[:, l] = jnp.concatenate(halves, axis=0).T
    for n in ("k", "v", "lse", "o"):
        b.put(n)
    b.need("w_out")

    def stats(s):
        x = b.o[s]
        b.stat[s] = two_cols(jnp.sum(x, axis=-1, keepdims=True), jnp.sum(x * x, axis=-1, keepdims=True))

    rows16(R, stats)
    core.send(b.stat, b.rstat, 0)
    core.recv(b.rstat, 0)

    def unit(s):
        t = b.stat[s] + b.rstat[s]
        mean = t[:, 0:1] / hp
        inv = lax.rsqrt(t[:, 1:2] / hp - mean * mean + EPS)
        b.st[s] = two_cols(mean, inv)
        b.u[s] = ((b.o[s] - mean) * inv * b.vh[0:1, :] + b.vh[3:4, :]).astype(BF)

    rows16(R, unit)
    b.put("st")
    yield
    for d in range(4):
        l = slice(256 * d, 256 * d + 256)
        b.part[:, l] = dot_nt(b.u[...], b.w_out[256 * d : 256 * d + 256, :]).astype(BF)
        core.send(b.part.at[:, l], b.rpart.at[:, l], 1 + d)
        if d % 2 == 1:
            yield
    for d in range(4):
        l = slice(256 * d, 256 * d + 256)
        core.recv(b.rpart.at[:, l], 1 + d)

    def close(s):
        x = b.part[s].astype(F32) + b.rpart[s].astype(F32) + b.vn[4:5, :]
        b.hm[s] = b.h[s] + wide(b.keep[s], x.shape[1]) * x

    rows16(R, close)
    b.put("hm")
    yield


def norm_store(dst, s, x, gain, bias):
    dst[s] = (unit_of(x, x.shape[1])[0] * gain + bias).astype(BF)


def forward_attend(h, tabs, wts, vn, vh, srcs, gset, cid):
    R, D = h.shape

    def body(b):
        w = Where()
        greet_all(w, "all")
        names = gset.names
        comm = gset.start(w, {n: getattr(b, "s_" + n) for n in names}, {n: getattr(b, "g_" + n) for n in names}, b.extra)
        core = Peer((w.dp, w.x, 1 - w.c), b.cs, b.cr)
        side = Peer(w.nx(), b.xs, b.xr)
        for _ in gset.live:
            next(comm)
        n = len(gset.live)
        drive(attend_body(b, w, R, core, side), comm, [0, 0, n, n, n], 3)
        gset.finish()
        core.finish()
        side.finish()

    ins = {"h": (h, LD), "keep": (tabs["keep"], LD), "fill": (tabs["fill"], LD), "cos": (tabs["cos"], LD),
           "sin": (tabs["sin"], LD), "w_in": (wts["in"], LD), "w_out": (wts["out"], LD), "vn": (vn, LD), "vh": (vh, LD)}
    ins.update({"s_" + n: (srcs[n], ANY) for n in gset.names})
    outs = {"hm": ((R, D), F32, ST), "q": ((R, 512), BF, ST), "k": ((2 * R, 512), BF, ST), "v": ((2 * R, 512), BF, ST),
            "lse": ((8, R), F32, ST), "o": ((R, 512), F32, ST), "st": ((R, 128), F32, ST)}
    outs.update({"g_" + n: ((16 * RB, srcs[n].shape[1]), BF, ANY) for n in gset.names})
    scratch = {"n": pltpu.VMEM((R, D), BF), "s": pltpu.VMEM((2 * R, R), F32), "p": pltpu.VMEM((2 * R, R), BF),
               "u": pltpu.VMEM((R, 512), BF), "part": pltpu.VMEM((R, D), BF), "rpart": pltpu.VMEM((R, D), BF),
               "stat": pltpu.VMEM((R, 128), F32), "rstat": pltpu.VMEM((R, 128), F32),
               "cs": DMA((5,)), "cr": DMA((5,)), "xs": DMA((4,)), "xr": DMA((4,))}
    return run_kernel(body, "attend", cid, ins, outs, scratch, gset.scratch())


def hidden_body(b, w, R, core):
    b.need("hm", "vn")
    rows16(R, lambda s: norm_store(b.n, s, b.hm[s], b.vn[2:3, :], b.vn[3:4, :]))
    b.need("w_gu", "vf")
    yield
    for i, (a, n) in enumerate(tiles(HP)):
        b.gate[:, a : a + n] = dot_nn(b.n[...], b.w_gu[:, a : a + n]) + b.vf[1:2, a : a + n]
        b.up[:, a : a + n] = dot_nn(b.n[...], b.w_gu[:, HP + a : HP + a + n]) + b.vf[2:3, a : a + n]
        if i % 2 == 1:
            yield

    b.put("gate")
    b.put("up")

    def stats(s):
        g = b.gate[s]
        z = g * jax.nn.sigmoid(g) * b.up[s]
        b.z[s] = z
        b.stat[s] = two_cols(jnp.sum(z, axis=-1, keepdims=True), jnp.sum(z * z, axis=-1, keepdims=True))

    rows16(R, stats)
    core.send(b.stat, b.rstat, 0)
    core.recv(b.rstat, 0)
    yield

    def unit(s):
        t = b.stat[s] + b.rstat[s]
        mean = t[:, 0:1] / FF
        inv = lax.rsqrt(t[:, 1:2] / FF - mean * mean + EPS)
        b.st[s] = two_cols(mean, inv)
        b.zn[s] = ((b.z[s] - mean) * inv * b.vf[0:1, :] + b.vf[3:4, :]).astype(BF)

    rows16(R, unit)
    b.put("st")
    b.need("w_dn", "keep")
    yield
    for d in range(4):
        l = slice(256 * d, 256 * d + 256)
        b.part[:, l] = dot_nt(b.zn[...], b.w_dn[256 * d : 256 * d + 256, :]).astype(BF)
        core.send(b.part.at[:, l], b.rpart.at[:, l], 1 + d)
        if d % 2 == 1:
            yield
    for d in range(4):
        l = slice(256 * d, 256 * d + 256)
        core.recv(b.rpart.at[:, l], 1 + d)

    def close(s):
        x = b.part[s].astype(F32) + b.rpart[s].astype(F32) + b.vn[5:6, :]
        b.ho[s] = b.hm[s] + wide(b.keep[s], x.shape[1]) * x

    rows16(R, close)
    b.put("ho")
    yield


def forward_hidden(hm, tabs, wts, vn, vf, srcs, gset, cid):
    R, D = hm.shape

    def body(b):
        w = Where()
        greet_all(w, "all" if gset else "core")
        core = Peer((w.dp, w.x, 1 - w.c), b.cs, b.cr)
        comp = hidden_body(b, w, R, core)
        if gset:
            names = gset.names
            comm = gset.start(w, {n: getattr(b, "s_" + n) for n in names}, {n: getattr(b, "g_" + n) for n in names}, b.extra)
            for _ in gset.live:
                next(comm)
            drive(comp, comm, [], 3)
            gset.finish()
        else:
            for _ in comp:
                pass
        core.finish()

    ins = {"hm": (hm, LD), "keep": (tabs["keep"], LD), "w_gu": (wts["gu"], LD), "w_dn": (wts["dn"], LD), "vn": (vn, LD), "vf": (vf, LD)}
    outs = {"ho": ((R, D), F32, ST), "gate": ((R, HP), F32, ST), "up": ((R, HP), F32, ST), "st": ((R, 128), F32, ST)}
    if gset:
        ins.update({"s_" + n: (srcs[n], ANY) for n in gset.names})
        outs.update({"g_" + n: ((16 * RB, srcs[n].shape[1]), BF, ANY) for n in gset.names})
    scratch = {"n": pltpu.VMEM((R, D), BF), "z": pltpu.VMEM((R, HP), F32), "zn": pltpu.VMEM((R, HP), BF),
               "part": pltpu.VMEM((R, D), BF), "rpart": pltpu.VMEM((R, D), BF),
               "stat": pltpu.VMEM((R, 128), F32), "rstat": pltpu.VMEM((R, 128), F32), "cs": DMA((5,)), "cr": DMA((5,))}
    return run_kernel(body, "hidden", cid, ins, outs, scratch, gset.scratch() if gset else ())


def add8(acc, x):
    acc[...] = acc[...] + fold8(x)


def put_vec(b, row, acc, n):
    b.vec[row : row + 1, 0:n] = jnp.sum(acc[...], axis=0, keepdims=True)


def close_back(b, s, x, gain, acc_gain, acc_shift):
    e = b.part[s].astype(F32) + b.rpart[s].astype(F32)
    unit, inv = unit_of(x, x.shape[1])
    add8(acc_gain, e * unit)
    add8(acc_shift, e)
    wt = e * gain
    n = x.shape[1]
    m1 = jnp.sum(wt, axis=-1, keepdims=True) / n
    m2 = jnp.sum(wt * unit, axis=-1, keepdims=True) / n
    b.go[s] = b.g[s] + inv * (wt - m1 - unit * m2)


def hidden_back_body(b, w, R, core):
    D = b.g.shape[1]
    for a in (b.a0, b.a1, b.a2, b.a3, b.a4, b.a5, b.a6, b.vec):
        a[...] = jnp.zeros_like(a)
    b.need("g", "keep", "gate", "up", "st", "vn", "vf")

    def unit4(s):
        g = b.gate[s]
        sg = jax.nn.sigmoid(g)
        return (g * sg * b.up[s] - b.st[s, 0:1]) * b.st[s, 1:2], g, sg

    def first(s):
        e = wide(b.keep[s], D) * b.g[s]
        b.el[s] = e.astype(BF)
        add8(b.a2, e)
        norm_store(b.n, s, b.go[s], b.vn[2:3, :], b.vn[3:4, :])
        b.zn[s] = (unit4(s)[0] * b.vf[0:1, :] + b.vf[3:4, :]).astype(BF)

    rows16(R, first)
    b.need("w_dn")
    yield
    for i, (a, n) in enumerate(tiles(HP)):
        b.ez[:, a : a + n] = dot_nn(b.el[...], b.w_dn[:, a : a + n])
        if i % 3 == 2:
            yield

    def second(s):
        u = unit4(s)[0]
        e = b.ez[s]
        wt = e * b.vf[0:1, :]
        add8(b.a3, e * u)
        add8(b.a6, e)
        b.stat[s] = two_cols(jnp.sum(wt, axis=-1, keepdims=True), jnp.sum(wt * u, axis=-1, keepdims=True))

    rows16(R, second)
    core.send(b.stat, b.rstat, 0)
    b.xT[...] = b.el[...].T
    yield
    for i, (a, n) in enumerate(tiles(HP)):
        b.d_dn[:, a : a + n] = dot_nn(b.xT[...], b.zn[:, a : a + n]).astype(BF)
        if i % 3 == 2:
            yield
    core.recv(b.rstat, 0)

    def third(s):
        u, g, sg = unit4(s)
        t = (b.stat[s] + b.rstat[s]) / FF
        ez = b.st[s, 1:2] * (b.ez[s] * b.vf[0:1, :] - t[:, 0:1] - u * t[:, 1:2])
        eg = ez * b.up[s] * sg * (1.0 + g * (1.0 - sg))
        eu = ez * g * sg
        add8(b.a4, eg)
        add8(b.a5, eu)
        b.egu[s, 0:HP] = eg.astype(BF)
        b.egu[s, HP : 2 * HP] = eu.astype(BF)

    rows16(R, third, 48)
    b.need("w_gu")
    yield
    for d in range(4):
        l = slice(256 * d, 256 * d + 256)
        b.part[:, l] = dot_nt(b.egu[...], b.w_gu[256 * d : 256 * d + 256, :]).astype(BF)
        core.send(b.part.at[:, l], b.rpart.at[:, l], 1 + d)
        yield
    b.xT[...] = b.n[...].T
    for i, (a, n) in enumerate(tiles(2 * HP)):
        b.d_gu[:, a : a + n] = dot_nn(b.xT[...], b.egu[:, a : a + n]).astype(BF)
        if i % 3 == 2 or i == len(tiles(2 * HP)) - 1:
            b.put("d_gu", (a - a % 768, a + n))
            yield
    for d in range(4):
        l = slice(256 * d, 256 * d + 256)
        core.recv(b.rpart.at[:, l], 1 + d)
    rows16(R, lambda s: close_back(b, s, b.go[s], b.vn[2:3, :], b.a0, b.a1))
    b.put("go")
    for row, acc, n in ((0, b.a0, D), (1, b.a1, D), (2, b.a2, D), (3, b.a3, HP), (4, b.a4, HP), (5, b.a5, HP), (6, b.a6, HP)):
        put_vec(b, row, acc, n)
    yield


def attend_back_body(b, w, R, core, side):
    D = b.g.shape[1]
    hp = D
    for a in (b.a0, b.a1, b.a2, b.a3, b.a4, b.a5, b.a6, b.vec):
        a[...] = jnp.zeros_like(a)
    b.need("g", "keep", "o", "st", "vn", "vh")

    def first(s):
        e = wide(b.keep[s], D) * b.g[s]
        b.el[s] = e.astype(BF)
        add8(b.a2, e)
        norm_store(b.n, s, b.go[s], b.vn[0:1, :], b.vn[1:2, :])
        u = (b.o[s] - b.st[s, 0:1]) * b.st[s, 1:2]
        b.u[s] = (u * b.vh[0:1, :] + b.vh[3:4, :]).astype(BF)

    rows16(R, first)
    b.need("w_out")
    yield
    for a, n in tiles(512):
        b.dq[:, a : a + n] = dot_nn(b.el[...], b.w_out[:, a : a + n])

    def second(s):
        u = (b.o[s] - b.st[s, 0:1]) * b.st[s, 1:2]
        e = b.dq[s]
        wt = e * b.vh[0:1, :]
        add8(b.a3, e * u)
        add8(b.a6, e)
        b.stat[s] = two_cols(jnp.sum(wt, axis=-1, keepdims=True), jnp.sum(wt * u, axis=-1, keepdims=True))

    rows16(R, second)
    core.send(b.stat, b.rstat, 0)
    b.xT[...] = b.el[...].T
    yield
    for a, n in tiles(512):
        b.d_out[:, a : a + n] = dot_nn(b.xT[...], b.u[:, a : a + n]).astype(BF)
    b.put("d_out")
    yield
    core.recv(b.rstat, 0)

    def third(s):
        u = (b.o[s] - b.st[s, 0:1]) * b.st[s, 1:2]
        t = (b.stat[s] + b.rstat[s]) / hp
        b.eo[s] = (b.st[s, 1:2] * (b.dq[s] * b.vh[0:1, :] - t[:, 0:1] - u * t[:, 1:2])).astype(BF)

    rows16(R, third, 48)
    b.need("q", "k", "v", "lse", "fill")
    yield
    S = 176
    for p in range(4):
        l = slice(128 * p, 128 * p + 128)
        kp = b.k[:, l]
        vp = b.v[:, l]
        kT = kp.T
        dk, dv, dqs = None, None, []
        for t in range(2):
            qt = head_lanes(b.q[:, l], t)
            ot = head_lanes(b.eo[:, l], t)
            b.s[...] = dot_nt(kp, qt)
            b.dp[...] = dot_nt(vp, ot)
            lse = b.lse[2 * p + t : 2 * p + t + 1, :]

            def expo(i, acc):
                r = pl.ds(pl.multiple_of(i * S, 16), S)
                x = jnp.exp(b.s[r] + wide(b.fill[r], R) - lse)
                b.s[r] = x
                b.p[r] = x.astype(BF)
                return acc + jnp.sum((x * b.dp[r]).reshape(S // 8, 8, R), axis=0)

            tot = lax.fori_loop(0, 2 * R // S, expo, jnp.zeros((8, R), F32))
            tot = jnp.sum(tot, axis=0, keepdims=True)

            def grad(i, _):
                r = pl.ds(pl.multiple_of(i * S, 16), S)
                b.ds[r] = (b.s[r] * (b.dp[r] - tot)).astype(BF)
                return 0

            lax.fori_loop(0, 2 * R // S, grad, 0)
            yield
            v1 = dot_nn(b.p[...], ot)
            k1 = dot_nn(b.ds[...], qt)
            dqs.append(dot_nn(kT[64 * t : 64 * t + 64], b.ds[...]))
            dv = v1 if t == 0 else dv + v1
            dk = k1 if t == 0 else dk + k1
            yield
        dk = jnp.where(b.fill[:, 0:1] == 0.0, dk, 0.0)
        b.dq[:, l] = jnp.concatenate(dqs, axis=0).T * 0.125
        b.dk[:, l] = dk[:R]
        b.dv[:, l] = dv[:R]
        l2 = slice(512 + 128 * p, 640 + 128 * p)
        b.ep[:, l] = dk[R:].astype(BF)
        b.ep[:, l2] = dv[R:].astype(BF)
        side.send(b.ep.at[:, l], b.rk.at[:, l], 2 * p)
        side.send(b.ep.at[:, l2], b.rv.at[:, l], 2 * p + 1)
    b.need("cos", "sin", "w_in")
    yield
    side.finish()
    for p in range(4):
        l = slice(128 * p, 128 * p + 128)
        side.recv(b.rk.at[:, l], 2 * p)
        side.recv(b.rv.at[:, l], 2 * p + 1)

        def last(s):
            cos, sin = b.cos[s], -b.sin[s]
            eq = turn(b.dq[s, l], cos, sin)
            ek = turn(b.dk[s, l] + b.rk[s, l].astype(F32), cos, sin)
            ev = b.dv[s, l] + b.rv[s, l].astype(F32)
            b.a4[:, l] = b.a4[:, l] + fold8(eq)
            b.a5[:, l] = b.a5[:, l] + fold8(ev)
            b.ep[s, l] = eq.astype(BF)
            b.ep[s, 512 + 128 * p : 640 + 128 * p] = ek.astype(BF)
            b.ep[s, 1024 + 128 * p : 1152 + 128 * p] = ev.astype(BF)

        rows16(R, last)
    yield
    for d in range(4):
        l = slice(256 * d, 256 * d + 256)
        b.part[:, l] = dot_nt(b.ep[...], b.w_in[256 * d : 256 * d + 256, :]).astype(BF)
        core.send(b.part.at[:, l], b.rpart.at[:, l], 1 + d)
        if d % 2 == 1:
            yield
    b.xT[...] = b.n[...].T
    for i, (a, n) in enumerate(tiles(1536)):
        b.d_in[:, a : a + n] = dot_nn(b.xT[...], b.ep[:, a : a + n]).astype(BF)
        if i % 3 == 2:
            b.put("d_in", (a - a % 768, a + n))
            yield
    for d in range(4):
        l = slice(256 * d, 256 * d + 256)
        core.recv(b.rpart.at[:, l], 1 + d)
    rows16(R, lambda s: close_back(b, s, b.go[s], b.vn[0:1, :], b.a0, b.a1))
    b.put("go")
    for row, acc, n in ((0, b.a0, D), (1, b.a1, D), (2, b.a2, D), (3, b.a3, 512), (4, b.a4, 512), (5, b.a5, 512), (6, b.a6, 512)):
        put_vec(b, row, acc, n)
    yield


def scatter_args(sset, grads, vec):
    ins = {"s_" + n: (grads[n], ANY) for n in sset.names}
    ins["s_vec"] = (vec, VM)
    outs = {"r_" + n: ((RB, grads[n].shape[1]), F32, VM) for n in sset.names}
    outs["r_vec"] = ((8, HP), F32, VM)
    return ins, outs


def scatter_start(sset, w, b, sc=None):
    n = sset.names
    return sset.start(w, {i: getattr(b, "s_" + i) for i in n}, {i: getattr(b, "r_" + i) for i in n}, b.s_vec, b.r_vec, b.extra if sc is None else sc)


HB_RATE = 2


def backward_hidden(g, fw, hm, tabs, wts, vn, vf, sset, grads, vec, cid):
    R, D = g.shape

    def body(b):
        w = Where()
        greet_all(w, "all")
        core = Peer((w.dp, w.x, 1 - w.c), b.cs, b.cr)
        load = pltpu.make_async_copy(b.hm, b.go, b.ls.at[0])
        load.start()
        comp = hidden_back_body(b, w, R, core)
        if sset:
            comm = scatter_start(sset, w, b, b.extra[:split])
            for _ in sset.live:
                next(comm)
        load.wait()

        def both():
            for _ in range(5):
                if sset:
                    for _ in range(3):
                        next(comm, None)
                yield
            mine = dset.start(w, {"dn": b.d_dn}, {"dn": b.r_dn}, None, None, b.extra[split:])
            for _ in dset.live:
                next(mine)
            yield
            yield from step_all([mine, comm] if sset else [mine])

        drive(comp, both(), [1] * 6, HB_RATE * (2 if sset else 1))
        if sset:
            sset.finish()
        dset.finish()
        core.finish()

    ins = {"g": (g, LD), "keep": (tabs["keep"], LD), "hm": (hm, ANY), "gate": (fw["gate"], LD), "up": (fw["up"], LD), "st": (fw["st"], LD),
           "w_gu": (wts["gu"], LD), "w_dn": (wts["dn"], LD), "vn": (vn, LD), "vf": (vf, LD)}
    outs = {"go": ((R, D), F32, ST), "d_gu": ((D, 2 * HP), BF, ST), "r_dn": ((RB, HP), F32, VM), "vec": ((8, HP), F32, VM)}
    extra = ()
    dset = dn_scatter()
    if sset:
        i2, o2 = scatter_args(sset, grads, vec)
        ins.update(i2)
        outs.update(o2)
        extra = sset.scratch()
    split = len(extra)
    extra = list(extra) + dset.scratch()
    acc = lambda n: pltpu.VMEM((8, n), F32)
    scratch = {"d_dn": pltpu.VMEM((D, HP), BF), "el": pltpu.VMEM((R, D), BF), "xT": pltpu.VMEM((D, R), BF), "n": pltpu.VMEM((R, D), BF), "ez": pltpu.VMEM((R, HP), F32),
               "zn": pltpu.VMEM((R, HP), BF), "egu": pltpu.VMEM((R, 2 * HP), BF), "part": pltpu.VMEM((R, D), BF), "rpart": pltpu.VMEM((R, D), BF),
               "stat": pltpu.VMEM((R, 128), F32), "rstat": pltpu.VMEM((R, 128), F32), "cs": DMA((5,)), "cr": DMA((5,)), "ls": DMA((1,)),
               "a0": acc(D), "a1": acc(D), "a2": acc(D), "a3": acc(HP), "a4": acc(HP), "a5": acc(HP), "a6": acc(HP)}
    return run_kernel(body, "hidden_back", cid, ins, outs, scratch, extra)


def backward_attend(g, fw, h, tabs, wts, vn, vh, sset, grads, vec, cid):
    R, D = g.shape

    def body(b):
        w = Where()
        greet_all(w, "all")
        core = Peer((w.dp, w.x, 1 - w.c), b.cs, b.cr)
        side = Peer(w.nx(), b.xs, b.xr)
        load = pltpu.make_async_copy(b.h, b.go, b.ls.at[0])
        load.start()
        comm = scatter_start(sset, w, b)
        for _ in sset.live:
            next(comm)
        load.wait()
        drive(attend_back_body(b, w, R, core, side), comm, [], 2)
        sset.finish()
        core.finish()

    ins = {"g": (g, LD), "keep": (tabs["keep"], LD), "h": (h, ANY), "fill": (tabs["fill"], LD), "cos": (tabs["cos"], LD), "sin": (tabs["sin"], LD),
           "o": (fw["o"], LD), "st": (fw["st"], LD), "q": (fw["q"], LD), "k": (fw["k"], LD), "v": (fw["v"], LD), "lse": (fw["lse"], LD),
           "w_in": (wts["in"], LD), "w_out": (wts["out"], LD), "vn": (vn, LD), "vh": (vh, LD)}
    outs = {"go": ((R, D), F32, ST), "d_in": ((D, 1536), BF, ST), "d_out": ((D, 512), BF, ST), "vec": ((8, HP), F32, VM)}
    i2, o2 = scatter_args(sset, grads, vec)
    ins.update(i2)
    outs.update(o2)
    acc = lambda n: pltpu.VMEM((8, n), F32)
    B = lambda *s: pltpu.VMEM(s, BF)
    F = lambda *s: pltpu.VMEM(s, F32)
    scratch = {"el": B(R, D), "xT": B(D, R), "n": B(R, D), "u": B(R, 512), "eo": B(R, 512), "s": F(2 * R, R), "dp": F(2 * R, R),
               "p": B(2 * R, R), "ds": B(2 * R, R), "dq": F(R, 512), "dk": F(R, 512), "dv": F(R, 512),
               "rk": B(R, 512), "rv": B(R, 512), "ep": B(R, 1536), "part": B(R, D), "rpart": B(R, D), "stat": F(R, 128), "rstat": F(R, 128),
               "cs": DMA((5,)), "cr": DMA((5,)), "ls": DMA((1,)), "xs": DMA((8,)), "xr": DMA((8,)),
               "a0": acc(D), "a1": acc(D), "a2": acc(D), "a3": acc(512), "a4": acc(512), "a5": acc(512), "a6": acc(512)}
    return run_kernel(body, "attend_back", cid, ins, outs, scratch, sset.scratch())


def scatter_last(sset, grads, vec, cid):
    def body(b):
        w = Where()
        greet(w)
        for _ in scatter_start(sset, w, b):
            pass
        sset.finish()

    ins, outs = scatter_args(sset, grads, vec)
    return run_kernel(body, "scatter", cid, ins, outs, {}, sset.scratch())


HP = 1408


def fast_device(
    tokens_in,
    cotangent,
    key_mask,
    grid_pos,
    class_index,
    input_weight,
    output_weight,
    gate_up_weight,
    down_weight,
    norm_gains,
    norm_biases,
    head_gains,
    head_biases,
    hidden_gains,
    hidden_biases,
):
    _, rows, width = tokens_in.shape
    dim = head_gains.shape[1]
    hidden = hidden_gains.shape[1]
    layers = input_weight.shape[0]
    pad = HP - hidden
    R = -(-rows // 16) * 16
    more = R - rows
    places = lax.axis_index("ctx") * rows + jnp.arange(rows, dtype=jnp.int32)
    not_class = (places != class_index[0]).astype(F32)
    cosine, sine = rotary_tables(grid_pos.reshape(2, rows), not_class)
    c0, c1, s0, s1 = cosine[:, 0], cosine[:, 1], sine[:, 0], sine[:, 1]
    low = lambda a: jnp.pad(a, ((0, more), (0, 0)))
    keep = low(key_mask.astype(F32).reshape(rows, 1))
    fill = jnp.where(jnp.arange(R)[:, None] < rows, (keep - 1.0) * 10000.0, -1.0e30)
    other = lax.ppermute(fill[:, 0], "ctx", [(0, 1), (1, 0)])[:, None]
    tabs = {
        "keep": jnp.broadcast_to(keep, (R, 128)),
        "fill": jnp.broadcast_to(jnp.concatenate([fill, other]), (2 * R, 128)),
        "cos": low(jnp.concatenate([c0, c0, c1, c1] * 2, axis=1)),
        "sin": low(jnp.concatenate([-s0, s0, -s1, s1] * 2, axis=1)),
    }
    gn = norm_gains.astype(F32)
    bn = norm_biases.astype(F32)
    gh = head_gains.astype(F32)[:, None]
    bh = head_biases.astype(F32)
    vh = jnp.pad(jnp.concatenate([gh, bh], axis=1), ((0, 0), (0, 4), (0, 0)))
    vn = jnp.stack([gn[:, 0], bn[:, 0], gn[:, 1], bn[:, 1], bn[:, 2], bn[:, 3]], axis=1)
    vn = jnp.pad(vn, ((0, 0), (0, 2), (0, 0)))
    vf = jnp.concatenate([hidden_gains.astype(F32)[:, None], hidden_biases.astype(F32)], axis=1)
    vf = jnp.pad(vf, ((0, 0), (0, 4), (0, pad)))
    gu = jnp.pad(gate_up_weight, ((0, 0), (0, 0), (0, 0), (0, pad)))
    dn = jnp.pad(down_weight, ((0, 0), (0, 0), (0, pad)))
    at_src = [{"in": input_weight[l].reshape(RB, 3 * dim), "out": output_weight[l]} for l in range(layers)]
    ff_src = [{"gu": gu[l].reshape(RB, 2 * HP), "dn": dn[l]} for l in range(layers)]
    grab = lambda d, names: {n: d["g_" + n] for n in names}
    h = low(tokens_in.astype(F32).reshape(rows, width)) * keep
    first = gather_first(at_src[0], AT_G, 0)
    at_w = {0: {n: first["w_" + n] for n in AT_G.names}}
    ff_w, hs, hms, at_f, ff_f = {}, {}, {}, {}, {}
    for l in range(layers):
        hs[l] = h
        at_f[l] = forward_attend(h, tabs, at_w[l], vn[l], vh[l], ff_src[l], FF_G, 1 + 2 * l)
        ff_w[l] = grab(at_f[l], FF_G.names)
        hms[l] = at_f[l]["hm"]
        nxt = l + 1 < layers
        ff_f[l] = forward_hidden(hms[l], tabs, ff_w[l], vn[l], vf[l], at_src[l + 1] if nxt else None, AT_G if nxt else None, 2 + 2 * l)
        if nxt:
            at_w[l + 1] = grab(ff_f[l], AT_G.names)
        h = ff_f[l]["ho"]
    activations = h[:rows].astype(BF).reshape(1, rows, width)
    g = low(cotangent.astype(F32).reshape(rows, width))
    got = {}
    grads, vec, cid = None, None, 2 * layers + 1
    for l in reversed(range(layers)):
        sset = at_scatter() if grads else None
        r = backward_hidden(g, ff_f[l], hms[l], tabs, ff_w[l], vn[l], vf[l], sset, grads, vec, cid)
        if grads:
            got["at", l + 1] = r
        g, vec, grads, got["dn", l] = r["go"], r["vec"], {"gu": r["d_gu"]}, r["r_dn"]
        r = backward_attend(g, at_f[l], hs[l], tabs, at_w[l], vn[l], vh[l], gu_scatter(), grads, vec, cid + 1)
        got["ff", l] = r
        g, vec, grads = r["go"], r["vec"], {"in": r["d_in"], "out": r["d_out"]}
        cid += 2
    got["at", 0] = scatter_last(at_scatter(), grads, vec, cid)
    input_grad = (keep * g)[:rows].reshape(1, rows, width)
    L = range(layers)
    va = jnp.stack([got["at", l]["r_vec"] for l in L])
    vff = jnp.stack([got["ff", l]["r_vec"] for l in L])
    return (
        activations,
        input_grad,
        jnp.stack([got["at", l]["r_in"].reshape(RB, 3, dim) for l in L]),
        jnp.stack([got["at", l]["r_out"] for l in L]),
        jnp.stack([got["ff", l]["r_gu"].reshape(RB, 2, HP)[:, :, :hidden] for l in L]),
        jnp.stack([got["dn", l][:, :hidden] for l in L]),
        jnp.stack([va[:, 0, :width], vff[:, 0, :width]], axis=1),
        jnp.stack([va[:, 1, :width], vff[:, 1, :width], va[:, 2, :width], vff[:, 2, :width]], axis=1),
        va[:, 3, :dim],
        va[:, 4:7, :dim],
        vff[:, 3, :hidden],
        vff[:, 4:7, :hidden],
    )


def solution(mesh):
    sizes = dict(mesh.shape)
    fits = sizes == {"dp": 8, "ctx": 2, "tp": 2}
    return jax.shard_map(
        fast_device if fits else on_device,
        mesh=mesh,
        in_specs=(
            P("dp", "ctx", None),
            P("dp", "ctx", None),
            P("dp", "ctx"),
            P(None, "dp", "ctx"),
            P("dp"),
            P(None, ("dp", "ctx"), None, "tp"),
            P(None, ("dp", "ctx"), "tp"),
            P(None, ("dp", "ctx"), None, "tp"),
            P(None, ("dp", "ctx"), "tp"),
            P(),
            P(),
            P(None, "tp"),
            P(None, None, "tp"),
            P(None, "tp"),
            P(None, None, "tp"),
        ),
        out_specs=(
            P("dp", "ctx", None),
            P("dp", "ctx", None),
            P(None, ("dp", "ctx"), None, "tp"),
            P(None, ("dp", "ctx"), "tp"),
            P(None, ("dp", "ctx"), None, "tp"),
            P(None, ("dp", "ctx"), "tp"),
            P(),
            P(),
            P(None, "tp"),
            P(None, None, "tp"),
            P(None, "tp"),
            P(None, None, "tp"),
        ),
        check_vma=False,
    )
```

```python
import functools

import jax
import jax.numpy as jnp
from jax import lax
from jax.experimental import pallas as pl
from jax.experimental.pallas import tpu as pltpu
from jax.sharding import PartitionSpec as P

FF = 2730
HEAD_DIM = 64


norm_epsilon = 1e-06
rotary_base = 10000.0
masked_score = -10000.0


def rotary_tables(positions, not_class):
    quarter = HEAD_DIM // 4
    frequency = rotary_base ** (-jnp.arange(quarter, dtype=jnp.float32) / quarter)
    angles = (
        jnp.transpose(positions).astype(jnp.float32)[:, :, None]
        * frequency
        * not_class[:, None, None]
    )
    return (jnp.cos(angles), jnp.sin(angles))


def rotate(values, cosine, sine, direction):
    row_count, head_count, head_dim = values.shape
    paired = values.reshape(row_count, head_count, 2, 2, head_dim // 4)
    first_half = paired[:, :, :, 0]
    second_half = paired[:, :, :, 1]
    cos_rows = cosine[:, None]
    sin_rows = sine[:, None] * direction
    turned = jnp.stack(
        [
            first_half * cos_rows - second_half * sin_rows,
            second_half * cos_rows + first_half * sin_rows,
        ],
        axis=3,
    )
    return turned.reshape(row_count, head_count, head_dim)


def local_norm(values, gain_vec, shift_vec):
    center = values - jnp.mean(values, axis=-1, keepdims=True)
    spread = jnp.mean(center * center, axis=-1, keepdims=True)
    inv_spread = lax.rsqrt(spread + norm_epsilon)
    unit_rows = center * inv_spread
    return (unit_rows * gain_vec + shift_vec, unit_rows, inv_spread)


def local_norm_back(upstream, unit_rows, inv_spread, gain_vec):
    weighted = upstream * gain_vec
    return inv_spread * (
        weighted
        - jnp.mean(weighted, axis=-1, keepdims=True)
        - unit_rows * jnp.mean(weighted * unit_rows, axis=-1, keepdims=True)
    )


def row_totals(first_part, second_part):
    return lax.psum(
        (jnp.sum(first_part, axis=-1, keepdims=True), jnp.sum(second_part, axis=-1, keepdims=True)),
        "tp",
    )


def split_norm(values, gain_vec, shift_vec, full_width):
    sum_first, sum_second = row_totals(values, values * values)
    row_mean = sum_first / full_width
    inv_spread = lax.rsqrt(sum_second / full_width - row_mean * row_mean + norm_epsilon)
    unit_rows = (values - row_mean) * inv_spread
    return (unit_rows * gain_vec + shift_vec, unit_rows, inv_spread)


def split_norm_back(upstream, unit_rows, inv_spread, gain_vec, full_width):
    weighted = upstream * gain_vec
    sum_first, sum_second = row_totals(weighted, weighted * unit_rows)
    return inv_spread * (weighted - sum_first / full_width - unit_rows * (sum_second / full_width))


def tensor_sum(partial_value):
    return lax.psum(partial_value.astype(jnp.bfloat16), "tp").astype(jnp.float32)


def tensor_back(partial_value):
    return lax.psum(partial_value.astype(jnp.bfloat16), "tp").astype(jnp.float32)


def fetch_weights(layer_index, input_weight, output_weight, gate_up_weight, down_weight):
    return (
        lax.all_gather(input_weight[layer_index], ("dp", "ctx"), axis=0, tiled=True),
        lax.all_gather(output_weight[layer_index], ("dp", "ctx"), axis=0, tiled=True),
        lax.all_gather(gate_up_weight[layer_index], ("dp", "ctx"), axis=0, tiled=True),
        lax.all_gather(down_weight[layer_index], ("dp", "ctx"), axis=0, tiled=True),
    )


def masked_scores(queries, key_heads, valid_keys):
    raw_scores = jnp.einsum("qhe,khe->hqk", queries, key_heads, preferred_element_type=jnp.float32)
    return jnp.where(valid_keys[None, None, :] > 0, raw_scores * HEAD_DIM ** (-0.5), masked_score)


def attend_forward(block_items):
    queries, keys_all, values_all, valid_keys = block_items
    key_count = keys_all.shape[0]
    head_count = queries.shape[1]
    key_heads = keys_all.reshape(key_count, head_count, HEAD_DIM)
    value_heads = values_all.reshape(key_count, head_count, HEAD_DIM)
    scores = masked_scores(queries, key_heads, valid_keys)
    row_max = jnp.max(scores, axis=-1, keepdims=True)
    exp_scores = jnp.exp(scores - row_max)
    row_total = jnp.sum(exp_scores, axis=-1, keepdims=True)
    attn_probs = (exp_scores / row_total).astype(jnp.bfloat16)
    attended = jnp.einsum(
        "hqk,khe->qhe", attn_probs, value_heads, preferred_element_type=jnp.float32
    )
    return (
        attended.reshape(queries.shape[0], head_count * HEAD_DIM),
        (row_max + jnp.log(row_total))[:, :, 0],
    )


def attend_backward(block_items):
    queries, keys_all, values_all, valid_keys, log_total, grad_out = block_items
    key_count = keys_all.shape[0]
    head_count = queries.shape[1]
    key_heads = keys_all.reshape(key_count, head_count, HEAD_DIM)
    value_heads = values_all.reshape(key_count, head_count, HEAD_DIM)
    scores = masked_scores(queries, key_heads, valid_keys)
    probs_full = jnp.exp(scores - log_total[:, :, None])
    probs_low = probs_full.astype(jnp.bfloat16)
    grad_probs = jnp.einsum(
        "qhe,khe->hqk", grad_out, value_heads, preferred_element_type=jnp.float32
    )
    row_dot = jnp.sum(probs_full * grad_probs, axis=-1, keepdims=True)
    grad_raw = jnp.where(
        valid_keys[None, None, :] > 0, HEAD_DIM ** (-0.5) * probs_full * (grad_probs - row_dot), 0.0
    ).astype(jnp.bfloat16)
    grad_queries = jnp.einsum(
        "hqk,khe->qhe", grad_raw, key_heads, preferred_element_type=jnp.float32
    )
    grad_keys = jnp.einsum("hqk,qhe->khe", grad_raw, queries, preferred_element_type=jnp.float32)
    grad_values = jnp.einsum(
        "hqk,qhe->khe", probs_low, grad_out, preferred_element_type=jnp.float32
    )
    local_rows = queries.shape[0]
    return (
        grad_queries.reshape(local_rows, head_count * HEAD_DIM),
        grad_keys.reshape(key_count, head_count * HEAD_DIM),
        grad_values.reshape(key_count, head_count * HEAD_DIM),
    )


def contract_rows(left, right):
    return lax.dot_general(
        left, right, (((0,), (0,)), ((), ())), preferred_element_type=jnp.float32
    )


def contract_cols(left, right):
    return lax.dot_general(
        left, right, (((1,), (1,)), ((), ())), preferred_element_type=jnp.float32
    )


def on_device(
    tokens_in,
    cotangent,
    key_mask,
    grid_pos,
    class_index,
    input_weight,
    output_weight,
    gate_up_weight,
    down_weight,
    norm_gains,
    norm_biases,
    head_gains,
    head_biases,
    hidden_gains,
    hidden_biases,
):
    images, rows_dev, model_width = tokens_in.shape
    row_count = images * rows_dev
    dim_local = head_gains.shape[1]
    heads_local = dim_local // HEAD_DIM
    hidden_local = hidden_gains.shape[1]
    layer_count = input_weight.shape[0]
    first_row = lax.axis_index("ctx") * rows_dev
    places = first_row + jnp.arange(rows_dev, dtype=jnp.int32)
    not_class = (places[None, :] != class_index[:, None]).astype(jnp.float32).reshape(row_count)
    cosine, sine = rotary_tables(grid_pos.reshape(2, row_count), not_class)
    row_keep = key_mask.astype(jnp.float32).reshape(row_count, 1)
    key_keep = key_mask.astype(jnp.bfloat16)
    gains_norm = norm_gains.astype(jnp.float32)
    biases_norm = norm_biases.astype(jnp.float32)
    gains_head = head_gains.astype(jnp.float32)
    biases_head = head_biases.astype(jnp.float32)
    gains_hidden = hidden_gains.astype(jnp.float32)
    biases_hidden = hidden_biases.astype(jnp.float32)
    hidden_state = tokens_in.astype(jnp.float32).reshape(row_count, model_width) * row_keep
    saved_layers = []
    for layer_index in range(layer_count):
        layer_mats = fetch_weights(
            layer_index, input_weight, output_weight, gate_up_weight, down_weight
        )
        mat_in, mat_out, mat_gate_up, mat_down = layer_mats
        normed, unit_one, spread_one = local_norm(
            hidden_state, gains_norm[layer_index, 0], biases_norm[layer_index, 0]
        )
        normed_low = normed.astype(jnp.bfloat16)
        projected = jnp.dot(
            normed_low,
            mat_in.reshape(model_width, 3 * dim_local),
            preferred_element_type=jnp.float32,
        ).reshape(row_count, 3, dim_local)
        queries = projected[:, 0] + biases_head[layer_index, 0]
        keys_proj = projected[:, 1]
        values_proj = projected[:, 2] + biases_head[layer_index, 1]
        query_low = rotate(
            queries.reshape(row_count, heads_local, HEAD_DIM), cosine, sine, 1.0
        ).astype(jnp.bfloat16)
        key_low = rotate(
            keys_proj.reshape(row_count, heads_local, HEAD_DIM), cosine, sine, 1.0
        ).astype(jnp.bfloat16)
        value_low = values_proj.astype(jnp.bfloat16)
        keys_all, values_all, valid_all = (
            lax.all_gather(key_low.reshape(images, rows_dev, dim_local), "ctx", axis=1, tiled=True),
            lax.all_gather(
                value_low.reshape(images, rows_dev, dim_local), "ctx", axis=1, tiled=True
            ),
            lax.all_gather(key_keep, "ctx", axis=1, tiled=True),
        )
        query_blocks = query_low.reshape(images, rows_dev, heads_local, HEAD_DIM)
        attended, log_total = lax.map(
            attend_forward, (query_blocks, keys_all, values_all, valid_all)
        )
        attended = attended.reshape(row_count, dim_local)
        head_normed, unit_two, spread_two = split_norm(
            attended, gains_head[layer_index], biases_head[layer_index, 2], model_width
        )
        head_low = head_normed.astype(jnp.bfloat16)
        branch = tensor_sum(contract_cols(head_low, mat_out))
        hidden_mid = hidden_state + row_keep * (branch + biases_norm[layer_index, 2])
        normed_two, unit_three, spread_three = local_norm(
            hidden_mid, gains_norm[layer_index, 1], biases_norm[layer_index, 1]
        )
        normed_two_low = normed_two.astype(jnp.bfloat16)
        gate_up = jnp.dot(
            normed_two_low,
            mat_gate_up.reshape(model_width, 2 * hidden_local),
            preferred_element_type=jnp.float32,
        ).reshape(row_count, 2, hidden_local)
        gate_pre = gate_up[:, 0] + biases_hidden[layer_index, 0]
        up_pre = gate_up[:, 1] + biases_hidden[layer_index, 1]
        inner_act = jax.nn.silu(gate_pre) * up_pre
        inner_normed, unit_four, spread_four = split_norm(
            inner_act, gains_hidden[layer_index], biases_hidden[layer_index, 2], FF
        )
        inner_low = inner_normed.astype(jnp.bfloat16)
        down_out = tensor_sum(contract_cols(inner_low, mat_down))
        hidden_state = hidden_mid + row_keep * (down_out + biases_norm[layer_index, 3])
        held_mats = None
        saved_layers.append(
            (
                held_mats,
                normed_low,
                unit_one,
                spread_one,
                query_blocks,
                keys_all,
                values_all,
                valid_all,
                log_total,
                unit_two,
                spread_two,
                head_low,
                unit_three,
                spread_three,
                normed_two_low,
                gate_pre,
                up_pre,
                unit_four,
                spread_four,
                inner_low,
            )
        )
    activations = hidden_state.reshape(images, rows_dev, model_width).astype(jnp.bfloat16)
    upstream = cotangent.astype(jnp.float32).reshape(row_count, model_width)
    mat_grads = [None] * layer_count
    vector_parts = [None] * layer_count
    for layer_index in reversed(range(layer_count)):
        (
            held_mats,
            normed_low,
            unit_one,
            spread_one,
            query_blocks,
            keys_all,
            values_all,
            valid_all,
            log_total,
            unit_two,
            spread_two,
            head_low,
            unit_three,
            spread_three,
            normed_two_low,
            gate_pre,
            up_pre,
            unit_four,
            spread_four,
            inner_low,
        ) = saved_layers[layer_index]
        mat_in, mat_out, mat_gate_up, mat_down = fetch_weights(
            layer_index, input_weight, output_weight, gate_up_weight, down_weight
        )
        grad_down = row_keep * upstream
        grad_bias_down = jnp.sum(grad_down, axis=0)
        grad_down_low = grad_down.astype(jnp.bfloat16)
        grad_mat_down = contract_rows(grad_down_low, inner_low)
        grad_inner_normed = jnp.dot(grad_down_low, mat_down, preferred_element_type=jnp.float32)
        grad_gain_hidden = jnp.sum(grad_inner_normed * unit_four, axis=0)
        grad_shift_hidden = jnp.sum(grad_inner_normed, axis=0)
        grad_inner = split_norm_back(
            grad_inner_normed, unit_four, spread_four, gains_hidden[layer_index], FF
        )
        sigmoid_gate = jax.nn.sigmoid(gate_pre)
        grad_up = grad_inner * gate_pre * sigmoid_gate
        grad_gate = grad_inner * up_pre * sigmoid_gate * (1.0 + gate_pre * (1.0 - sigmoid_gate))
        grad_gate_up_low = (
            jnp.stack([grad_gate, grad_up], axis=1)
            .astype(jnp.bfloat16)
            .reshape(row_count, 2 * hidden_local)
        )
        grad_mat_gate_up = contract_rows(normed_two_low, grad_gate_up_low).reshape(
            model_width, 2, hidden_local
        )
        grad_normed_two = tensor_back(
            contract_cols(grad_gate_up_low, mat_gate_up.reshape(model_width, 2 * hidden_local))
        )
        grad_gain_two = jnp.sum(grad_normed_two * unit_three, axis=0)
        grad_shift_two = jnp.sum(grad_normed_two, axis=0)
        upstream = upstream + local_norm_back(
            grad_normed_two, unit_three, spread_three, gains_norm[layer_index, 1]
        )
        grad_branch = row_keep * upstream
        grad_bias_out = jnp.sum(grad_branch, axis=0)
        grad_branch_low = grad_branch.astype(jnp.bfloat16)
        grad_mat_out = contract_rows(grad_branch_low, head_low)
        grad_head = jnp.dot(grad_branch_low, mat_out, preferred_element_type=jnp.float32)
        grad_gain_head = jnp.sum(grad_head * unit_two, axis=0)
        grad_shift_head = jnp.sum(grad_head, axis=0)
        grad_attended = split_norm_back(
            grad_head, unit_two, spread_two, gains_head[layer_index], model_width
        )
        grad_att_low = grad_attended.astype(jnp.bfloat16).reshape(
            images, rows_dev, heads_local, HEAD_DIM
        )
        grad_query_rot, grad_keys_all, grad_values_all = lax.map(
            attend_backward,
            (query_blocks, keys_all, values_all, valid_all, log_total, grad_att_low),
        )
        grad_keys_rot, grad_values = (
            lax.psum_scatter(
                grad_keys_all.astype(jnp.bfloat16), "ctx", scatter_dimension=1, tiled=True
            ).astype(jnp.float32),
            lax.psum_scatter(
                grad_values_all.astype(jnp.bfloat16), "ctx", scatter_dimension=1, tiled=True
            ).astype(jnp.float32),
        )
        grad_queries = rotate(
            grad_query_rot.reshape(row_count, heads_local, HEAD_DIM), cosine, sine, -1.0
        ).reshape(row_count, dim_local)
        grad_keys = rotate(
            grad_keys_rot.reshape(row_count, heads_local, HEAD_DIM), cosine, sine, -1.0
        ).reshape(row_count, dim_local)
        grad_values = grad_values.reshape(row_count, dim_local)
        grad_proj_low = (
            jnp.stack([grad_queries, grad_keys, grad_values], axis=1)
            .astype(jnp.bfloat16)
            .reshape(row_count, 3 * dim_local)
        )
        grad_mat_in = contract_rows(normed_low, grad_proj_low).reshape(model_width, 3, dim_local)
        grad_normed_one = tensor_back(
            contract_cols(grad_proj_low, mat_in.reshape(model_width, 3 * dim_local))
        )
        grad_gain_one = jnp.sum(grad_normed_one * unit_one, axis=0)
        grad_shift_one = jnp.sum(grad_normed_one, axis=0)
        upstream = upstream + local_norm_back(
            grad_normed_one, unit_one, spread_one, gains_norm[layer_index, 0]
        )
        mat_grads[layer_index] = (
            lax.psum_scatter(grad_mat_in, ("dp", "ctx"), scatter_dimension=0, tiled=True),
            lax.psum_scatter(grad_mat_out, ("dp", "ctx"), scatter_dimension=0, tiled=True),
            lax.psum_scatter(grad_mat_gate_up, ("dp", "ctx"), scatter_dimension=0, tiled=True),
            lax.psum_scatter(grad_mat_down, ("dp", "ctx"), scatter_dimension=0, tiled=True),
        )
        vector_parts[layer_index] = (
            jnp.stack([grad_gain_one, grad_gain_two]),
            jnp.stack([grad_shift_one, grad_shift_two, grad_bias_out, grad_bias_down]),
            grad_gain_head,
            jnp.stack(
                [jnp.sum(grad_queries, axis=0), jnp.sum(grad_values, axis=0), grad_shift_head]
            ),
            grad_gain_hidden,
            jnp.stack([jnp.sum(grad_gate, axis=0), jnp.sum(grad_up, axis=0), grad_shift_hidden]),
        )
    input_grad = (row_keep * upstream).reshape(images, rows_dev, model_width)
    stacked_vectors = tuple(
        (
            jnp.stack([vector_parts[index][member] for index in range(layer_count)])
            for member in range(6)
        )
    )
    summed_vectors = lax.psum(
        (
            stacked_vectors[0],
            stacked_vectors[1],
            stacked_vectors[2],
            stacked_vectors[3],
            stacked_vectors[4],
            stacked_vectors[5],
        ),
        ("dp", "ctx"),
    )
    grad_input_weight = jnp.stack([mat_grads[index][0] for index in range(layer_count)])
    grad_output_weight = jnp.stack([mat_grads[index][1] for index in range(layer_count)])
    grad_gate_up_weight = jnp.stack([mat_grads[index][2] for index in range(layer_count)])
    grad_down_weight = jnp.stack([mat_grads[index][3] for index in range(layer_count)])
    return (
        activations,
        input_grad,
        grad_input_weight,
        grad_output_weight,
        grad_gate_up_weight,
        grad_down_weight,
        summed_vectors[0],
        summed_vectors[1],
        summed_vectors[2],
        summed_vectors[3],
        summed_vectors[4],
        summed_vectors[5],
    )


MESH = pl.DeviceIdType.MESH

RB=64

class Where:
    def __init__(self):
        self.dp=lax.axis_index("dp"); self.x=lax.axis_index("ctx"); self.c=lax.axis_index("tp")
        self.z=self.dp//2; self.y=self.dp%2
    def nx(self): return (self.dp,1-self.x,self.c)
    def ny(self): return (self.z*2+1-self.y,self.x,self.c)
    def up(self): return ((self.z+1)*2+self.y,self.x,self.c)
    def dn(self): return ((self.z-1)*2+self.y,self.x,self.c)

def greet(w):
    bar=pltpu.get_barrier_semaphore()
    def sig(dev): pl.semaphore_signal(bar,inc=1,device_id=dev,device_id_type=MESH)
    sig(w.nx()); sig(w.ny())
    @pl.when(w.z<3)
    def _(): sig(w.up())
    @pl.when(w.z>0)
    def _(): sig(w.dn())
    pl.semaphore_wait(bar,2+(w.z<3).astype(jnp.int32)+(w.z>0).astype(jnp.int32))

class Gather:
    def __init__(self,w,order,src,out,r0,nr,ssem,rsem,own_sem):
        self.w,self.order,self.src,self.out,self.r0,self.nr=w,order,src,out,r0,nr
        self.ssem,self.rsem=ssem,rsem
        self.pending=[]
    def rows(self,zz,yy,xx):
        return pl.ds(pl.multiple_of(((zz*2+yy)*2+xx)*RB+self.r0,16),self.nr)
    def here(self,zz,yy,xx,own=False):
        return self.src.at[pl.ds(self.r0,self.nr)] if own else self.out.at[self.rows(zz,yy,xx)]
    def copy(self,zz,yy,xx,dev,s,r,own=False):
        return pltpu.make_async_remote_copy(src_ref=self.here(zz,yy,xx,own),dst_ref=self.out.at[self.rows(zz,yy,xx)],
            send_sem=self.ssem.at[s],recv_sem=self.rsem.at[r],device_id=dev,device_id_type=MESH)
    def send(self,cond,*a,**k):
        self.pending.append((cond,a,k))
        if cond is None: self.copy(*a,**k).start()
        else:
            @pl.when(cond)
            def _(): self.copy(*a,**k).start()
    def finish_sends(self):
        for cond,a,k in self.pending:
            if cond is None: self.copy(*a,**k).wait_send()
            else:
                @pl.when(cond)
                def _(a=a,k=k): self.copy(*a,**k).wait_send()
    def arrived(self,zz,yy,xx,r):
        self.copy(zz,yy,xx,self.w.nx(),0,r).wait_recv()

class GatherZ(Gather):
    def pq(self,zz,pself):
        w=self.w
        if self.order=="zyx": return (zz,w.y if pself else 1-w.y,w.x)
        return (zz,w.y,w.x if pself else 1-w.x)
    def pdev(self): return self.w.ny() if self.order=="zyx" else self.w.nx()
    def qdev(self): return self.w.nx() if self.order=="zyx" else self.w.ny()
    def qcoord(self,zz,pself):
        w=self.w
        if self.order=="zyx": return (zz,w.y if pself else 1-w.y,1-w.x)
        return (zz,1-w.y,w.x if pself else 1-w.x)
    def emit(self,cond,zz,k,own=False):
        b=self.pq(zz,True)
        w=self.w
        if k<4:
            c=(w.z<3) if cond is None else jnp.logical_and(cond,w.z<3)
            self.send(c,*b,w.up(),k,zz,own=own)
        if k==0 or k>=4:
            c=(w.z>0) if cond is None else jnp.logical_and(cond,w.z>0)
            self.send(c,*b,w.dn(),7+(k if k==0 else k-3),zz,own=own)
        self.send(cond,*b,self.pdev(),11+k,4+zz,own=own)
        self.send(cond,*b,self.qdev(),18+k,8+zz*2,own=own)
    def rounds(self):
        w=self.w
        self.emit(None,w.z,0,own=True)
        yield
        for k in (1,2,3):
            for kk,zz,cond in ((k,w.z-k,w.z>=k),(k+3,w.z+k,w.z+k<=3)):
                @pl.when(cond)
                def _(zz=zz): self.arrived(*self.pq(zz,True),zz)
                self.emit(cond,zz,kk)
            yield
        for k in (0,1,2,3):
            for kk,zz,cond in (((0,w.z,None),) if k==0 else ((k,w.z-k,w.z>=k),(k+3,w.z+k,w.z+k<=3))):
                b=self.pq(zz,False)
                def go(zz=zz,b=b): self.arrived(*b,4+zz)
                if cond is None: go()
                else: pl.when(cond)(go)
                self.send(cond,*b,self.qdev(),25+kk,8+zz*2+1)
            yield
    def arrive(self):
        for zz in range(4):
            for pself in (True,False):
                self.arrived(*self.qcoord(zz,pself),8+zz*2+(0 if pself else 1))
    NS,NR=32,16

class GatherX(Gather):
    NS,NR=3+4*7,19
    def blk(self,zz,j):
        w=self.w
        return (zz,w.y if j<2 else 1-w.y,w.x if j%2==0 else 1-w.x)
    def vert(self,cond,zz,j,k,own=False):
        w=self.w; b=self.blk(zz,j)
        if k<4:
            c=(w.z<3) if cond is None else jnp.logical_and(cond,w.z<3)
            self.send(c,*b,w.up(),3+j*7+k if k else 3+j*7,3+zz*4+j,own=own)
        if k==0 or k>=4:
            c=(w.z>0) if cond is None else jnp.logical_and(cond,w.z>0)
            self.send(c,*b,w.dn(),3+j*7+(k if k>=4 else 3),3+zz*4+j,own=own)
    def rounds(self):
        w=self.w
        self.send(None,*self.blk(w.z,0),w.nx(),0,0,own=True)
        self.send(None,*self.blk(w.z,0),w.ny(),1,1,own=True)
        self.vert(None,w.z,0,0,own=True)
        yield
        b=self.blk(w.z,1); self.arrived(*b,0)
        self.send(None,*b,w.ny(),2,2)
        yield
        yield
        yield
        self.arrived(*self.blk(w.z,2),1)
        self.arrived(*self.blk(w.z,3),2)
        for j in range(1,4): self.vert(None,w.z,j,0)
        yield
        for k in (1,2,3):
            for j in range(4):
                for kk,zz,cond in ((k,w.z-k,w.z>=k),(k+3,w.z+k,w.z+k<=3)):
                    @pl.when(cond)
                    def _(zz=zz,j=j): self.arrived(*self.blk(zz,j),3+zz*4+j)
                    if k<3: self.vert(cond,zz,j,kk)
                if j%2==1: yield
    def arrive(self):
        pass


ZORD=(3,0,2,1)
class Scatter:
    def __init__(self,w,order,src,out,r0,nr,ssem,rsem,lsem,own,bufs):
        self.w,self.order,self.src,self.out,self.r0,self.nr=w,order,src,out,r0,nr
        self.ssem,self.rsem,self.lsem,self.own=ssem,rsem,lsem,own
        self.bufs=bufs
        self.pending=[]
    def rows(self,zz,yy,xx):
        return pl.ds(pl.multiple_of(((zz*2+yy)*2+xx)*RB+self.r0,16),self.nr)
    def send(self,cond,src,dst,dev,s,r):
        mk=lambda: pltpu.make_async_remote_copy(src_ref=src,dst_ref=dst,send_sem=self.ssem.at[s],recv_sem=self.rsem.at[r],device_id=dev,device_id_type=MESH)
        self.pending.append((cond,mk))
        if cond is None: mk().start()
        else: pl.when(cond)(lambda: mk().start())
    def wait(self,cond,dst,r):
        def go(): pltpu.make_async_remote_copy(src_ref=dst,dst_ref=dst,send_sem=self.ssem.at[0],recv_sem=self.rsem.at[r],device_id=self.w.nx(),device_id_type=MESH).wait_recv()
        if cond is None: go()
        else: pl.when(cond)(go)
    def finish(self):
        for cond,mk in self.pending:
            if cond is None: mk().wait_send()
            else: pl.when(cond)(lambda mk=mk: mk().wait_send())
    def total(self,dst,terms,extra=()):
        def strip(i,_):
            s=pl.ds(pl.multiple_of(i*16,16),16)
            t=terms[0][s].astype(jnp.float32)
            for r in terms[1:]: t=t+r[s].astype(jnp.float32)
            dst[s]=t.astype(dst.dtype)
            return 0
        lax.fori_loop(0,self.nr//16,strip,0)

class ScatterZ(Scatter):
    NS,NR=16,17
    def mine(self,zz,pself):
        w=self.w
        if self.order=="zyx": return (zz,w.y if pself else 1-w.y,w.x)
        return (zz,w.y,w.x if pself else 1-w.x)
    def theirs(self,zz,pself):
        w=self.w
        if self.order=="zyx": return (zz,w.y if pself else 1-w.y,1-w.x)
        return (zz,1-w.y,w.x if pself else 1-w.x)
    def rounds(self):
        w=self.w; rq,rp,ru=self.bufs
        pdev=w.ny() if self.order=="zyx" else w.nx()
        qdev=w.nx() if self.order=="zyx" else w.ny()
        loc={}
        for k in (1,0):
            for zz in ZORD:
                c=pltpu.make_async_copy(self.src.at[self.rows(*self.mine(zz,k==0))],self.own.at[zz*2+k],self.lsem.at[zz*2+k]); c.start(); loc[zz*2+k]=c
        for zz in ZORD:
            self.send(None,self.src.at[self.rows(*self.theirs(zz,False))],rq.at[zz*2+1],qdev,zz*2+1,zz*2+1)
        yield
        for zz in ZORD:
            i=zz*2+1
            loc[i].wait(); self.wait(None,rq.at[i],i)
            self.total(rq.at[i],[self.own.at[i],rq.at[i]])
            self.send(None,rq.at[i],rp.at[zz],pdev,8+zz,8+zz)
            self.send(None,self.src.at[self.rows(*self.theirs(zz,True))],rq.at[zz*2],qdev,zz*2,zz*2)
            yield
        def ready(zz):
            loc[zz*2].wait(); self.wait(None,rq.at[zz*2],zz*2); self.wait(None,rp.at[zz],8+zz)
            return [self.own.at[zz*2],rq.at[zz*2],rp.at[zz]]
        for t in (1,2,3):
            for i in range(4):
                for up in (True,False):
                    m=i if up else 3-i
                    if m>=t: continue
                    zz=4-t+m if up else t-1-m
                    @pl.when(w.z==i)
                    def _():
                        terms=ready(zz)
                        if m>0:
                            self.wait(None,ru.at[zz],12+zz); terms.append(ru.at[zz])
                        self.total(rp.at[zz],terms)
                    if up: self.send(w.z==i,rp.at[zz],ru.at[zz],w.up(),12+zz,12+zz)
                    else:
                        to=4 if zz==i-1 else zz
                        self.send(w.z==i,rp.at[zz],ru.at[to],w.dn(),12+zz,12+to)
            yield
        o=self.out.at[pl.ds(self.r0,self.nr)]
        for zz in range(4):
            @pl.when(w.z==zz)
            def _():
                terms=ready(zz)
                if zz>0: self.wait(None,ru.at[zz],12+zz); terms.append(ru.at[zz])
                if zz<3: self.wait(None,ru.at[4],16); terms.append(ru.at[4])
                self.total(o,terms)
        yield

class ScatterX(Scatter):
    NS,NR=19,23
    def blk(self,zz,j):
        w=self.w
        return (zz,w.y if j<2 else 1-w.y,w.x if j%2==0 else 1-w.x)
    def rounds(self):
        w=self.w; ru,ry,rx=self.bufs
        down=lambda zz,j: jnp.where(w.z-1==zz,16+j,zz*4+j)
        loc={}
        for zz in ZORD:
            for j in (3,2,1,0):
                i=zz*4+j
                c=pltpu.make_async_copy(self.src.at[self.rows(*self.blk(zz,j))],self.own.at[i],self.lsem.at[i]); c.start(); loc[i]=c
        J=(3,2,1,0)
        for zz in (3,2,1):
            for j in J: self.send(w.z==0,self.src.at[self.rows(*self.blk(zz,j))],ru.at[zz*4+j],w.up(),zz*4+j,zz*4+j)
        for zz in (0,1,2):
            for j in J:
                to=16+j if zz==2 else zz*4+j
                self.send(w.z==3,self.src.at[self.rows(*self.blk(zz,j))],ru.at[to],w.dn(),zz*4+j,to)
        yield
        for i in loc: loc[i].wait()
        def hop(c,zz,j,up):
            i=zz*4+j
            @pl.when(w.z==c)
            def _():
                self.wait(None,ru.at[i],i)
                self.total(ru.at[i],[self.own.at[i],ru.at[i]])
            if up: self.send(w.z==c,ru.at[i],ru.at[i],w.up(),i,i)
            else:
                to=16+j if zz==c-1 else i
                self.send(w.z==c,ru.at[i],ru.at[to],w.dn(),i,to)
        for j in J:
            hop(1,3,j,True); hop(2,0,j,False)
            if j%2==0: yield
        for j in J:
            hop(1,2,j,True); hop(2,1,j,False)
            hop(2,3,j,True); hop(1,0,j,False)
            if j%2==0: yield
        def zsum(j,dst,extra):
            for zz in range(4):
                i=zz*4+j
                t=[self.own.at[i]]
                if zz>0: t.append(ru.at[i])
                if zz<3: t.append(ru.at[16+j])
                @pl.when(w.z==zz)
                def _():
                    if zz>0: self.wait(None,ru.at[i],i)
                    if zz<3: self.wait(None,ru.at[16+j],16+j)
                    self.total(dst,t+extra)
        sy=self.bufs_stage
        for j in (3,2):
            k=j-2
            zsum(j,sy.at[k],[])
            self.send(None,sy.at[k],ry.at[k],w.ny(),16+k,20+k)
        yield
        self.wait(None,ry.at[1],21)
        zsum(1,sy.at[2],[ry.at[1]])
        self.send(None,sy.at[2],rx.at[0],w.nx(),18,22)
        yield
        self.wait(None,ry.at[0],20)
        self.wait(None,rx.at[0],22)
        zsum(0,self.out.at[pl.ds(self.r0,self.nr)],[ry.at[0],rx.at[0]])
        yield


F32 = jnp.float32
BF = jnp.bfloat16
DMA = pltpu.SemaphoreType.DMA
EPS = 1e-06


def step_all(gens):
    gens = list(gens)
    while gens:
        for g in list(gens):
            try:
                next(g)
            except StopIteration:
                gens.remove(g)
                continue
            yield


def drive(compute, comm, plan, rest):
    for i, _ in enumerate(compute):
        for _ in range(plan[i] if i < len(plan) else rest):
            next(comm, None)
    for _ in comm:
        pass


class GatherSet:
    def __init__(self, parts, names, cut=32):
        self.parts, self.names, self.cut = parts, names, cut

    def scratch(self):
        out = []
        for name, cols, kind in self.parts:
            if kind == "z":
                out += [DMA((GatherZ.NS,)), DMA((GatherZ.NR,))] * 2
            else:
                out += [DMA((GatherX.NS,)), DMA((GatherX.NR,))]
        return out + [DMA((len(self.names),))]

    def start(self, w, srcs, outs, sems):
        sems = list(sems)
        me = pl.multiple_of((w.dp * 2 + w.x) * RB, 16)
        self.locs = []
        for i, name in enumerate(self.names):
            c = pltpu.make_async_copy(srcs[name], outs[name].at[pl.ds(me, RB)], sems[-1].at[i])
            c.start()
            self.locs.append(c)
        self.live = []
        for name, cols, kind in self.parts:
            s, o = srcs[name], outs[name]
            if cols is not None:
                s, o = s.at[:, cols[0] : cols[1]], o.at[:, cols[0] : cols[1]]
            if kind == "z":
                for r0, nr, order in ((0, self.cut, "zyx"), (self.cut, RB - self.cut, "zxy")):
                    self.live.append(GatherZ(w, order, s, o, r0, nr, sems.pop(0), sems.pop(0), None))
            else:
                self.live.append(GatherX(w, "xyz", s, o, 0, 64, sems.pop(0), sems.pop(0), None))
        return step_all([p.rounds() for p in self.live])

    def arrive(self):
        for p in self.live:
            p.arrive()
        for c in self.locs:
            c.wait()

    def finish_sends(self):
        for p in self.live:
            p.finish_sends()

    def finish(self):
        self.arrive()
        self.finish_sends()


class VecSum:
    def __init__(self, w, src, out, st, rv, ss, rs):
        self.w, self.src, self.out, self.st, self.rv, self.ss, self.rs = w, src, out, st, rv, ss, rs

    def mk(self, src, k, dev, send):
        return pltpu.make_async_remote_copy(
            src_ref=src, dst_ref=self.rv.at[k], send_sem=self.ss.at[send], recv_sem=self.rs.at[k],
            device_id=dev, device_id_type=MESH)

    def rounds(self):
        w = self.w
        st, rv = self.st, self.rv
        even = w.z % 2 == 0
        odd = w.z % 2 == 1
        mid = jnp.logical_and(w.z > 0, w.z < 3)
        self.mk(self.src, 0, w.nx(), 0).start()
        yield
        yield
        self.mk(self.src, 0, w.nx(), 0).wait_recv()
        st[0] = self.src[...] + rv[0]
        self.mk(st.at[0], 1, w.ny(), 1).start()
        yield
        yield
        self.mk(self.src, 1, w.ny(), 1).wait_recv()
        st[1] = st[0] + rv[1]
        pl.when(even)(lambda: self.mk(st.at[1], 2, w.up(), 2).start())
        pl.when(odd)(lambda: self.mk(st.at[1], 2, w.dn(), 2).start())
        yield
        yield
        self.mk(self.src, 2, w.nx(), 2).wait_recv()
        st[2] = st[1] + rv[2]
        pl.when(w.z == 1)(lambda: self.mk(st.at[2], 3, w.up(), 3).start())
        pl.when(w.z == 2)(lambda: self.mk(st.at[2], 3, w.dn(), 3).start())
        yield
        yield

        @pl.when(mid)
        def _():
            self.mk(self.src, 3, w.nx(), 3).wait_recv()
            st[3] = st[2] + rv[3]
            self.out[...] = st[3]

        pl.when(w.z == 1)(lambda: self.mk(st.at[3], 4, w.dn(), 4).start())
        pl.when(w.z == 2)(lambda: self.mk(st.at[3], 4, w.up(), 4).start())
        yield
        yield

        @pl.when(jnp.logical_not(mid))
        def _():
            self.mk(self.src, 4, w.nx(), 4).wait_recv()
            self.out[...] = rv[4]

        yield
        yield

    def finish(self):
        w = self.w
        self.mk(self.src, 0, w.nx(), 0).wait_send()
        self.mk(self.src, 0, w.nx(), 1).wait_send()
        self.mk(self.src, 0, w.nx(), 2).wait_send()

        @pl.when(jnp.logical_and(w.z > 0, w.z < 3))
        def _():
            self.mk(self.src, 0, w.nx(), 3).wait_send()
            self.mk(self.src, 0, w.nx(), 4).wait_send()


class ScatterSet:
    def __init__(self, parts, names, widths, cut=32, vec=True):
        self.parts, self.names, self.widths, self.cut, self.vec = parts, names, widths, cut, vec

    def scratch(self):
        V = lambda *s: pltpu.VMEM(s, BF)
        sc = []
        for name, cols, kind in self.parts:
            C = self.widths[name] if cols is None else cols[1] - cols[0]
            if kind == "z":
                for nr in (self.cut, RB - self.cut):
                    sc += [DMA((ScatterZ.NS,)), DMA((ScatterZ.NR,)), DMA((8,))]
                    sc += [V(8, nr, C), V(8, nr, C), V(4, nr, C), V(5, nr, C)]
            else:
                sc += [DMA((ScatterX.NS,)), DMA((ScatterX.NR,)), DMA((16,))]
                sc += [V(16, 64, C), V(20, 64, C), V(2, 64, C), V(1, 64, C), V(3, 64, C)]
        if self.vec:
            sc += [pltpu.VMEM((4, 8, HP), F32), pltpu.VMEM((5, 8, HP), F32), DMA((5,)), DMA((5,))]
        return sc

    def start(self, w, srcs, outs, vec, vec_out, sc):
        sc = list(sc)
        self.live = []
        for name, cols, kind in self.parts:
            s, o = srcs[name], outs[name]
            if cols is not None:
                s, o = s.at[:, cols[0] : cols[1]], o.at[:, cols[0] : cols[1]]
            if kind == "z":
                for r0, nr, order in ((0, self.cut, "zyx"), (self.cut, RB - self.cut, "zxy")):
                    ss, rs, ls, own, rq, rp, ru = [sc.pop(0) for _ in range(7)]
                    self.live.append(ScatterZ(w, order, s, o, r0, nr, ss, rs, ls, own, (rq, rp, ru)))
            else:
                ss, rs, ls, own, ru, ry, rx, st = [sc.pop(0) for _ in range(8)]
                p = ScatterX(w, "xyz", s, o, 0, 64, ss, rs, ls, own, (ru, ry, rx))
                p.bufs_stage = st
                self.live.append(p)
        if self.vec:
            st, rv, ss, rs = sc
            self.live.append(VecSum(w, vec, vec_out, st, rv, ss, rs))
        return step_all([p.rounds() for p in self.live])

    def finish(self):
        for p in self.live:
            p.finish()


FF_CUT = 16
AT_G = GatherSet([("in", None, "z"), ("out", None, "x")], ["in", "out"])
FF_G = GatherSet([("gu", None, "z"), ("dn", (0, 512), "z"), ("dn", (512, 1408), "x")], ["gu", "dn"], FF_CUT)


def at_scatter():
    return ScatterSet([("in", None, "z"), ("out", None, "x")], ["in", "out"], {"in": 1536, "out": 512})


def gu_scatter():
    return ScatterSet([("gu", (0, 2176), "z"), ("gu", (2176, 2816), "x")], ["gu"], {"gu": 2816}, FF_CUT)


def dn_scatter():
    return ScatterSet([("dn", (0, 1024), "z"), ("dn", (1024, 1408), "x")], ["dn"], {"dn": 1408}, 32, False)


def rows16(n, fn, step=176):
    def body(i, _):
        fn(pl.ds(pl.multiple_of(i * step, 16), step))
        return 0

    lax.fori_loop(0, n // step, body, 0)


def unit_of(x, width):
    mean = jnp.sum(x, axis=-1, keepdims=True) / width
    c = x - mean
    inv = lax.rsqrt(jnp.sum(c * c, axis=-1, keepdims=True) / width + EPS)
    return c * inv, inv


def dot_nn(a, b):
    return jnp.dot(a, b, preferred_element_type=F32)


def dot_nt(a, b):
    return lax.dot_general(a, b, (((1,), (1,)), ((), ())), preferred_element_type=F32)


def dot_tn(a, b):
    return lax.dot_general(a, b, (((0,), (0,)), ((), ())), preferred_element_type=F32)


def tiles(n, size=256):
    return [(a, min(size, n - a)) for a in range(0, n, size)]


def fold8(x):
    return jnp.sum(x.reshape(x.shape[0] // 8, 8, x.shape[1]), axis=0)


def wide(x, n):
    return jnp.concatenate([x] * (-(-n // 128)), axis=1)[:, :n]


def two_cols(a, b):
    lane = lax.broadcasted_iota(jnp.int32, (a.shape[0], 128), 1)
    return jnp.where(lane == 0, a, jnp.where(lane == 1, b, 0.0))


def turn(x, cos, sin):
    lane = lax.broadcasted_iota(jnp.int32, x.shape, 1)
    other = jnp.where((lane // 16) % 2 == 0, pltpu.roll(x, 112, 1), pltpu.roll(x, 16, 1))
    return x * cos + other * sin


def head_lanes(x, t):
    lane = lax.broadcasted_iota(jnp.int32, x.shape, 1)
    return jnp.where(lane // 64 == t, x, jnp.zeros_like(x))


class Peer:
    def __init__(self, dev, ss, rs):
        self.dev, self.ss, self.rs, self.open = dev, ss, rs, []

    def mk(self, src, dst, k):
        return pltpu.make_async_remote_copy(
            src_ref=src, dst_ref=dst, send_sem=self.ss.at[k], recv_sem=self.rs.at[k], device_id=self.dev, device_id_type=MESH)

    def send(self, src, dst, k):
        c = self.mk(src, dst, k)
        c.start()
        self.open.append(c)

    def recv(self, dst, k):
        self.mk(dst, dst, k).wait_recv()

    def finish(self):
        for c in self.open:
            c.wait_send()
        self.open = []


def greet_all(w, links):
    bar = pltpu.get_barrier_semaphore()

    def sig(dev):
        pl.semaphore_signal(bar, inc=1, device_id=dev, device_id_type=MESH)

    sig((w.dp, w.x, 1 - w.c))
    n = jnp.int32(1)
    if links != "core":
        sig(w.nx())
        n = n + 1
    if links == "all":
        sig(w.ny())
        pl.when(w.z < 3)(lambda: sig(w.up()))
        pl.when(w.z > 0)(lambda: sig(w.dn()))
        n = n + 1 + (w.z < 3).astype(jnp.int32) + (w.z > 0).astype(jnp.int32)
    pl.semaphore_wait(bar, n)


class Bag:
    def launch(self):
        self.coming = {n: pltpu.make_async_copy(h, getattr(self, n), self.ld.at[i]) for i, (n, h) in enumerate(self.loads)}
        for n, c in self.coming.items():
            if n not in self.late:
                c.start()
        self.going = []

    def begin(self, *names):
        for n in names:
            self.coming[n].start()

    def need(self, *names):
        for n in names:
            if n in self.coming:
                self.coming.pop(n).wait()

    def put(self, name, cols=None):
        s, d = getattr(self, name), self.stores[name]
        if cols is not None:
            s, d = s.at[:, cols[0] : cols[1]], d.at[:, cols[0] : cols[1]]
        c = pltpu.make_async_copy(s, d, self.so.at[len(self.going)])
        c.start()
        self.going.append(c)

    def flush(self):
        self.need(*list(self.coming))
        for c in self.going:
            c.wait()


def run_kernel(body, name, cid, ins, outs, scratch, extra=()):
    iname, oname, sname = list(ins), list(outs), list(scratch)
    ld = [n for n in iname if ins[n][1] in (LD, LATE)]
    so = [n for n in oname if outs[n][2] == "ST"]
    moved = [pltpu.VMEM(ins[n][0].shape, ins[n][0].dtype) for n in ld] + [pltpu.VMEM(outs[n][0], outs[n][1]) for n in so]
    moved += [DMA((max(len(ld), 1),)), DMA((16,))]

    def kernel(*refs):
        b = Bag()
        ni, no, ns, nm = len(iname), len(oname), len(sname), len(moved)
        for n, r in zip(iname + oname + sname, refs):
            setattr(b, n, r)
        mv = refs[ni + no + ns : ni + no + ns + nm]
        b.loads = [(n, getattr(b, n)) for n in ld]
        b.late = [n for n in ld if ins[n][1] == LATE]
        b.stores = {n: getattr(b, n) for n in so}
        for n, r in zip(ld + so, mv):
            setattr(b, n, r)
        b.ld, b.so = mv[-2:]
        b.extra = refs[ni + no + ns + nm :]
        b.launch()
        body(b)
        b.flush()

    place = lambda s: pl.BlockSpec(memory_space=pl.ANY if s in (LD, ST, LATE) else s)
    res = pl.pallas_call(
        kernel,
        out_shape=[jax.ShapeDtypeStruct(outs[n][0], outs[n][1]) for n in oname],
        in_specs=[place(ins[n][1]) for n in iname],
        out_specs=[place(outs[n][2]) for n in oname],
        scratch_shapes=[scratch[n] for n in sname] + moved + list(extra),
        compiler_params=pltpu.CompilerParams(collective_id=cid, has_side_effects=True, vmem_limit_bytes=62 * 2**20),
        name=name,
    )(*[ins[n][0] for n in iname])
    return dict(zip(oname, res))


VM = pltpu.VMEM
ANY = pl.ANY
LD, ST, LATE = "LD", "ST", "LATE"


def gather_first(srcs, gset, fill, cid):
    names = gset.names
    R = fill.shape[1]

    def body(b):
        w = Where()
        greet(w)
        side = Peer(w.nx(), b.xs, b.xr)
        b.need("fill")
        side.send(b.fill, b.other, 0)
        g = gset.start(w, {n: getattr(b, "s_" + n) for n in names}, {n: getattr(b, "w_" + n) for n in names}, b.extra)
        for _ in g:
            pass
        side.recv(b.other, 0)
        b.both[0:R, :] = jnp.broadcast_to(b.fill[...].T[:, 0:1], (R, 128))
        b.both[R : 2 * R, :] = jnp.broadcast_to(b.other[...].T[:, 0:1], (R, 128))
        b.put("both")
        gset.finish()
        side.finish()

    ins = {"s_" + n: (srcs[n], ANY) for n in names}
    ins["fill"] = (fill, LD)
    outs = {"w_" + n: ((16 * RB, srcs[n].shape[1]), BF, ANY) for n in names}
    outs["both"] = ((2 * R, 128), F32, ST)
    return run_kernel(body, "gather", cid, ins, outs, dict(other=VM((8, R), F32), xs=DMA((1,)), xr=DMA((1,))), gset.scratch())


def attend_body(b, w, R, core, side):
    hp = b.h.shape[1]
    b.need("h", "vn")
    rows16(R, lambda s: norm_store(b.n, s, b.h[s], b.vn[0:1, :], b.vn[1:2, :]))
    b.need("w_in", "cos", "sin", "keep", "vh")
    D = 512
    for j in range(2):
        kt = dot_nn(b.n[...], b.w_in[:, D + 256 * j : D + 256 * j + 256])
        for hf in range(2):
            l = slice(256 * j + 128 * hf, 256 * j + 128 * hf + 128)
            b.k[0:R, l] = (turn(kt[:, 128 * hf : 128 * hf + 128], b.cos[...], b.sin[...]) * b.keep[...]).astype(BF)
        l = slice(256 * j, 256 * j + 256)
        side.send(b.k.at[pl.ds(0, R), l], b.k.at[pl.ds(R, R), l], 2 * j)
        vt = dot_nn(b.n[...], b.w_in[:, 2 * D + 256 * j : 2 * D + 256 * j + 256]) + b.vh[2:3, l]
        b.v[0:R, l] = vt.astype(BF)
        side.send(b.v.at[pl.ds(0, R), l], b.v.at[pl.ds(R, R), l], 2 * j + 1)
        yield
    for j in range(2):
        qt = dot_nn(b.n[...], b.w_in[:, 256 * j : 256 * j + 256]) + b.vh[1:2, 256 * j : 256 * j + 256]
        for hf in range(2):
            l = slice(256 * j + 128 * hf, 256 * j + 128 * hf + 128)
            b.q[:, l] = (turn(qt[:, 128 * hf : 128 * hf + 128], b.cos[...], b.sin[...]) * 0.125).astype(BF)
    b.put("q")
    b.need("fill")
    yield
    S = 176
    for p in range(4):
        l = slice(128 * p, 128 * p + 128)
        if p % 2 == 0:
            j = p // 2
            lj = slice(256 * j, 256 * j + 256)
            side.recv(b.k.at[pl.ds(R, R), lj], 2 * j)
            side.recv(b.v.at[pl.ds(R, R), lj], 2 * j + 1)
        kp = b.k[:, l]
        vT = b.v[:, l].T
        halves = []
        for t in range(2):
            b.s[...] = dot_nt(kp, head_lanes(b.q[:, l], t))

            def top(i, m):
                r = pl.ds(pl.multiple_of(i * S, 16), S)
                x = b.s[r] + wide(b.fill[r], R)
                return jnp.maximum(m, jnp.max(x.reshape(S // 8, 8, R), axis=0))

            m = lax.fori_loop(0, 2 * R // S, top, jnp.full((8, R), -3.0e38, F32))
            m = jnp.max(m, axis=0, keepdims=True)

            def expo(i, acc):
                r = pl.ds(pl.multiple_of(i * S, 16), S)
                x = jnp.exp(b.s[r] + wide(b.fill[r], R) - m)
                b.p[r] = x.astype(BF)
                return acc + jnp.sum(x.reshape(S // 8, 8, R), axis=0)

            tot = lax.fori_loop(0, 2 * R // S, expo, jnp.zeros((8, R), F32))
            tot = jnp.sum(tot, axis=0, keepdims=True)
            halves.append(dot_nn(vT[64 * t : 64 * t + 64], b.p[...]) / tot)
            b.lse[2 * p + t : 2 * p + t + 1, :] = m + jnp.log(tot)
            yield
        b.o[:, l] = jnp.concatenate(halves, axis=0).T
    for n in ("k", "v", "lse", "o"):
        b.put(n)
    b.need("w_out")

    def stats(s):
        x = b.o[s]
        b.stat[s] = two_cols(jnp.sum(x, axis=-1, keepdims=True), jnp.sum(x * x, axis=-1, keepdims=True))

    rows16(R, stats)
    core.send(b.stat, b.rstat, 0)
    core.recv(b.rstat, 0)

    def unit(s):
        t = b.stat[s] + b.rstat[s]
        mean = t[:, 0:1] / hp
        inv = lax.rsqrt(t[:, 1:2] / hp - mean * mean + EPS)
        b.st[s] = two_cols(mean, inv)
        b.u[s] = ((b.o[s] - mean) * inv * b.vh[0:1, :] + b.vh[3:4, :]).astype(BF)

    rows16(R, unit)
    b.put("st")
    yield
    for d in range(4):
        l = slice(256 * d, 256 * d + 256)
        b.part[:, l] = dot_nt(b.u[...], b.w_out[256 * d : 256 * d + 256, :]).astype(BF)
        core.send(b.part.at[:, l], b.rpart.at[:, l], 1 + d)
        if d % 2 == 1:
            yield
    for d in range(4):
        l = slice(256 * d, 256 * d + 256)
        core.recv(b.rpart.at[:, l], 1 + d)

    def close(s):
        x = b.part[s].astype(F32) + b.rpart[s].astype(F32) + b.vn[4:5, :]
        b.hm[s] = b.h[s] + wide(b.keep[s], x.shape[1]) * x

    rows16(R, close)
    b.put("hm")
    yield


def norm_store(dst, s, x, gain, bias):
    dst[s] = (unit_of(x, x.shape[1])[0] * gain + bias).astype(BF)


def hidden_body(b, w, R, core, fetch):
    rows16(R, lambda s: norm_store(b.n, s, b.hm[s], b.vn[2:3, :], b.vn[3:4, :]))
    loads = fetch()
    b.need("vf")
    loads[0].wait()
    yield
    for i, (a, n) in enumerate(tiles(HP)):
        b.gate[:, a : a + n] = dot_nn(b.n[...], b.w_gu[:, a : a + n]) + b.vf[1:2, a : a + n]
        b.up[:, a : a + n] = dot_nn(b.n[...], b.w_gu[:, HP + a : HP + a + n]) + b.vf[2:3, a : a + n]
        if i % 2 == 1:
            yield

    b.put("gate")
    b.put("up")

    def stats(s):
        g = b.gate[s]
        z = g * jax.nn.sigmoid(g) * b.up[s]
        b.z[s] = z
        b.stat[s] = two_cols(jnp.sum(z, axis=-1, keepdims=True), jnp.sum(z * z, axis=-1, keepdims=True))

    rows16(R, stats)
    core.send(b.stat, b.rstat, 0)
    core.recv(b.rstat, 0)
    yield

    def unit(s):
        t = b.stat[s] + b.rstat[s]
        mean = t[:, 0:1] / FF
        inv = lax.rsqrt(t[:, 1:2] / FF - mean * mean + EPS)
        b.zst[s] = two_cols(mean, inv)
        b.zn[s] = ((b.z[s] - mean) * inv * b.vf[0:1, :] + b.vf[3:4, :]).astype(BF)

    rows16(R, unit)
    b.put("zst")
    loads[1].wait()
    yield
    for d in range(4):
        l = slice(256 * d, 256 * d + 256)
        b.part[:, l] = dot_nt(b.zn[...], b.w_dn[256 * d : 256 * d + 256, :]).astype(BF)
        core.send(b.part.at[:, l], b.rpart.at[:, l], 1 + d)
        if d % 2 == 1:
            yield
    for d in range(4):
        l = slice(256 * d, 256 * d + 256)
        core.recv(b.rpart.at[:, l], 1 + d)

    def close(s):
        x = b.part[s].astype(F32) + b.rpart[s].astype(F32) + b.vn[5:6, :]
        b.ho[s] = b.hm[s] + wide(b.keep[s], x.shape[1]) * x

    rows16(R, close)
    b.put("ho")
    yield


def forward_layer(h, tabs, wts, vn, vh, vf, srcs, nxt, cid):
    R, D = h.shape
    fset = FF_G
    aset = AT_G if nxt else None

    def body(b):
        w = Where()
        greet_all(w, "all")
        ends = lambda g: ({n: getattr(b, "s_" + n) for n in g.names}, {n: getattr(b, "g_" + n) for n in g.names})
        ffc = fset.start(w, *ends(fset), b.extra[:split])
        core = Peer((w.dp, w.x, 1 - w.c), b.cs, b.cr)
        side = Peer(w.nx(), b.xs, b.xr)
        n = len(fset.live)
        for _ in range(n):
            next(ffc)

        def comm_all():
            yield from ffc
            if aset:
                yield from aset.start(w, *ends(aset), b.extra[split:])

        comm = comm_all()

        def fetch():
            for _ in ffc:
                pass
            if aset:
                for _ in range(3):
                    next(comm)
            fset.arrive()
            loads = [pltpu.make_async_copy(b.g_gu, b.w_gu, b.ls.at[0]), pltpu.make_async_copy(b.g_dn, b.w_dn, b.ls.at[1])]
            for c in loads:
                c.start()
            return loads

        def comp():
            yield from attend_body(b, w, R, core, side)
            core.finish()
            yield from hidden_body(b, w, R, core, fetch)

        drive(comp(), comm, [0, 0, n, n, n], 3)
        fset.finish_sends()
        if aset:
            aset.finish()
        core.finish()
        side.finish()

    ins = dict(h=(h, LD), keep=(tabs["keep"], LD), fill=(tabs["fill"], LD), cos=(tabs["cos"], LD), sin=(tabs["sin"], LD),
        w_in=(wts["in"], LD), w_out=(wts["out"], LD), vn=(vn, LD), vh=(vh, LD), vf=(vf, LD))
    outs = dict(hm=((R, D), F32, ST), q=((R, 512), BF, ST), k=((2 * R, 512), BF, ST), v=((2 * R, 512), BF, ST),
        lse=((8, R), F32, ST), o=((R, 512), F32, ST), st=((R, 128), F32, ST), ho=((R, D), F32, ST),
        gate=((R, HP), F32, ST), up=((R, HP), F32, ST), zst=((R, 128), F32, ST))
    extra = fset.scratch()
    split = len(extra)
    for g, src in ((fset, srcs), (aset, nxt)):
        if g:
            ins.update({"s_" + n: (src[n], ANY) for n in g.names})
            outs.update({"g_" + n: ((16 * RB, src[n].shape[1]), BF, ANY) for n in g.names})
    if aset:
        extra = extra + aset.scratch()
    B = lambda *s: pltpu.VMEM(s, BF)
    F = lambda *s: pltpu.VMEM(s, F32)
    scratch = dict(n=B(R, D), s=F(2 * R, R), p=B(2 * R, R), u=B(R, 512), part=B(R, D), rpart=B(R, D), stat=F(R, 128),
        rstat=F(R, 128), z=F(R, HP), zn=B(R, HP), w_gu=B(D, 2 * HP), w_dn=B(D, HP), cs=DMA((5,)), cr=DMA((5,)),
        xs=DMA((4,)), xr=DMA((4,)), ls=DMA((2,)))
    return run_kernel(body, "layer", cid, ins, outs, scratch, extra)


def add8(acc, x):
    acc[...] = acc[...] + fold8(x)


def put_vec(b, row, acc, n):
    b.vec[row : row + 1, 0:n] = jnp.sum(acc[...], axis=0, keepdims=True)


def close_back(b, s, x, gain, acc_gain, acc_shift):
    e = b.part[s].astype(F32) + b.rpart[s].astype(F32)
    unit, inv = unit_of(x, x.shape[1])
    add8(acc_gain, e * unit)
    add8(acc_shift, e)
    wt = e * gain
    n = x.shape[1]
    m1 = jnp.sum(wt, axis=-1, keepdims=True) / n
    m2 = jnp.sum(wt * unit, axis=-1, keepdims=True) / n
    b.go[s] = b.g[s] + inv * (wt - m1 - unit * m2)


def hidden_back_body(b, w, R, core):
    D = b.g.shape[1]
    for a in (b.a0, b.a1, b.a2, b.a3, b.a4, b.a5, b.a6, b.vec):
        a[...] = jnp.zeros_like(a)
    b.need("g", "keep")

    def unit4(s):
        g = b.gate[s]
        sg = jax.nn.sigmoid(g)
        return (g * sg * b.up[s] - b.st[s, 0:1]) * b.st[s, 1:2], g, sg

    def first(s):
        e = wide(b.keep[s], D) * b.g[s]
        b.el[s] = e.astype(BF)
        add8(b.a2, e)

    def norms(s):
        norm_store(b.n, s, b.go[s], b.vn[2:3, :], b.vn[3:4, :])
        b.zn[s] = (unit4(s)[0] * b.vf[0:1, :] + b.vf[3:4, :]).astype(BF)

    rows16(R, first)
    b.need("gate", "up", "st", "vn", "vf")
    rows16(R, norms)
    b.need("w_dn")
    b.begin("w_gu")
    yield
    for i, (a, n) in enumerate(tiles(HP)):
        b.ez[:, a : a + n] = dot_nn(b.el[...], b.w_dn[:, a : a + n])
        if i % 3 == 2:
            yield

    def second(s):
        u = unit4(s)[0]
        e = b.ez[s]
        wt = e * b.vf[0:1, :]
        add8(b.a3, e * u)
        add8(b.a6, e)
        b.stat[s] = two_cols(jnp.sum(wt, axis=-1, keepdims=True), jnp.sum(wt * u, axis=-1, keepdims=True))

    rows16(R, second)
    core.send(b.stat, b.rstat, 0)
    b.xT[...] = b.el[...].T
    yield
    for i, (a, n) in enumerate(tiles(HP)):
        b.d_dn[:, a : a + n] = dot_nn(b.xT[...], b.zn[:, a : a + n]).astype(BF)
        if i % 3 == 2:
            yield
    core.recv(b.rstat, 0)

    def third(s):
        u, g, sg = unit4(s)
        t = (b.stat[s] + b.rstat[s]) / FF
        ez = b.st[s, 1:2] * (b.ez[s] * b.vf[0:1, :] - t[:, 0:1] - u * t[:, 1:2])
        eg = ez * b.up[s] * sg * (1.0 + g * (1.0 - sg))
        eu = ez * g * sg
        add8(b.a4, eg)
        add8(b.a5, eu)
        b.egu[s, 0:HP] = eg.astype(BF)
        b.egu[s, HP : 2 * HP] = eu.astype(BF)

    rows16(R, third, 48)
    b.need("w_gu")
    yield
    for d in range(4):
        l = slice(256 * d, 256 * d + 256)
        b.part[:, l] = dot_nt(b.egu[...], b.w_gu[256 * d : 256 * d + 256, :]).astype(BF)
        core.send(b.part.at[:, l], b.rpart.at[:, l], 1 + d)
        yield
    b.xT[...] = b.n[...].T
    for i, (a, n) in enumerate(tiles(2 * HP)):
        b.d_gu[:, a : a + n] = dot_nn(b.xT[...], b.egu[:, a : a + n]).astype(BF)
        if i % 3 == 2 or i == len(tiles(2 * HP)) - 1:
            b.put("d_gu", (a - a % 768, a + n))
            yield
    for d in range(4):
        l = slice(256 * d, 256 * d + 256)
        core.recv(b.rpart.at[:, l], 1 + d)
    rows16(R, lambda s: close_back(b, s, b.go[s], b.vn[2:3, :], b.a0, b.a1))
    b.put("go")
    for row, acc, n in ((0, b.a0, D), (1, b.a1, D), (2, b.a2, D), (3, b.a3, HP), (4, b.a4, HP), (5, b.a5, HP), (6, b.a6, HP)):
        put_vec(b, row, acc, n)
    yield


def attend_back_body(b, w, R, core, side):
    D = b.g.shape[1]
    hp = D
    for a in (b.a0, b.a1, b.a2, b.a3, b.a4, b.a5, b.a6, b.vec):
        a[...] = jnp.zeros_like(a)
    b.need("g", "keep", "o", "st", "vn", "vh")

    def first(s):
        e = wide(b.keep[s], D) * b.g[s]
        b.el[s] = e.astype(BF)
        add8(b.a2, e)
        norm_store(b.n, s, b.go[s], b.vn[0:1, :], b.vn[1:2, :])
        u = (b.o[s] - b.st[s, 0:1]) * b.st[s, 1:2]
        b.u[s] = (u * b.vh[0:1, :] + b.vh[3:4, :]).astype(BF)

    rows16(R, first)
    b.need("w_out")
    b.begin("q", "k", "v", "lse", "fill", "cos", "sin", "w_in")
    yield
    for a, n in tiles(512):
        b.dq[:, a : a + n] = dot_nn(b.el[...], b.w_out[:, a : a + n])

    def second(s):
        u = (b.o[s] - b.st[s, 0:1]) * b.st[s, 1:2]
        e = b.dq[s]
        wt = e * b.vh[0:1, :]
        add8(b.a3, e * u)
        add8(b.a6, e)
        b.stat[s] = two_cols(jnp.sum(wt, axis=-1, keepdims=True), jnp.sum(wt * u, axis=-1, keepdims=True))

    rows16(R, second)
    core.send(b.stat, b.rstat, 0)
    b.xT[...] = b.el[...].T
    yield
    for a, n in tiles(512):
        b.d_out[:, a : a + n] = dot_nn(b.xT[...], b.u[:, a : a + n]).astype(BF)
    b.put("d_out")
    yield
    core.recv(b.rstat, 0)

    def third(s):
        u = (b.o[s] - b.st[s, 0:1]) * b.st[s, 1:2]
        t = (b.stat[s] + b.rstat[s]) / hp
        b.eo[s] = (b.st[s, 1:2] * (b.dq[s] * b.vh[0:1, :] - t[:, 0:1] - u * t[:, 1:2])).astype(BF)

    rows16(R, third, 48)
    b.need("q", "k", "v", "lse", "fill")
    yield
    S = 176
    for p in range(4):
        l = slice(128 * p, 128 * p + 128)
        kp = b.k[:, l]
        vp = b.v[:, l]
        kT = kp.T
        dk, dv, dqs = None, None, []
        for t in range(2):
            qt = head_lanes(b.q[:, l], t)
            ot = head_lanes(b.eo[:, l], t)
            b.s[...] = dot_nt(kp, qt)
            b.dp[...] = dot_nt(vp, ot)
            lse = b.lse[2 * p + t : 2 * p + t + 1, :]

            def expo(i, acc):
                r = pl.ds(pl.multiple_of(i * S, 16), S)
                x = jnp.exp(b.s[r] + wide(b.fill[r], R) - lse)
                b.s[r] = x
                b.p[r] = x.astype(BF)
                return acc + jnp.sum((x * b.dp[r]).reshape(S // 8, 8, R), axis=0)

            tot = lax.fori_loop(0, 2 * R // S, expo, jnp.zeros((8, R), F32))
            tot = jnp.sum(tot, axis=0, keepdims=True)

            def grad(i, _):
                r = pl.ds(pl.multiple_of(i * S, 16), S)
                b.ds[r] = (b.s[r] * (b.dp[r] - tot)).astype(BF)
                return 0

            lax.fori_loop(0, 2 * R // S, grad, 0)
            yield
            v1 = dot_nn(b.p[...], ot)
            k1 = dot_nn(b.ds[...], qt)
            dqs.append(dot_nn(kT[64 * t : 64 * t + 64], b.ds[...]))
            dv = v1 if t == 0 else dv + v1
            dk = k1 if t == 0 else dk + k1
            yield
        dk = jnp.where(b.fill[:, 0:1] == 0.0, dk, 0.0)
        b.dq[:, l] = jnp.concatenate(dqs, axis=0).T * 0.125
        b.dk[:, l] = dk[:R]
        b.dv[:, l] = dv[:R]
        l2 = slice(512 + 128 * p, 640 + 128 * p)
        b.ep[:, l] = dk[R:].astype(BF)
        b.ep[:, l2] = dv[R:].astype(BF)
        side.send(b.ep.at[:, l], b.rk.at[:, l], 2 * p)
        side.send(b.ep.at[:, l2], b.rv.at[:, l], 2 * p + 1)
    b.need("cos", "sin", "w_in")
    yield
    side.finish()
    for p in range(4):
        l = slice(128 * p, 128 * p + 128)
        side.recv(b.rk.at[:, l], 2 * p)
        side.recv(b.rv.at[:, l], 2 * p + 1)

        def last(s):
            cos, sin = b.cos[s], -b.sin[s]
            eq = turn(b.dq[s, l], cos, sin)
            ek = turn(b.dk[s, l] + b.rk[s, l].astype(F32), cos, sin)
            ev = b.dv[s, l] + b.rv[s, l].astype(F32)
            b.a4[:, l] = b.a4[:, l] + fold8(eq)
            b.a5[:, l] = b.a5[:, l] + fold8(ev)
            b.ep[s, l] = eq.astype(BF)
            b.ep[s, 512 + 128 * p : 640 + 128 * p] = ek.astype(BF)
            b.ep[s, 1024 + 128 * p : 1152 + 128 * p] = ev.astype(BF)

        rows16(R, last)
    yield
    for d in range(4):
        l = slice(256 * d, 256 * d + 256)
        b.part[:, l] = dot_nt(b.ep[...], b.w_in[256 * d : 256 * d + 256, :]).astype(BF)
        core.send(b.part.at[:, l], b.rpart.at[:, l], 1 + d)
        if d % 2 == 1:
            yield
    b.xT[...] = b.n[...].T
    for i, (a, n) in enumerate(tiles(1536)):
        b.d_in[:, a : a + n] = dot_nn(b.xT[...], b.ep[:, a : a + n]).astype(BF)
        if i % 3 == 2:
            b.put("d_in", (a - a % 768, a + n))
            yield
    for d in range(4):
        l = slice(256 * d, 256 * d + 256)
        core.recv(b.rpart.at[:, l], 1 + d)
    rows16(R, lambda s: close_back(b, s, b.go[s], b.vn[0:1, :], b.a0, b.a1))
    b.put("go")
    for row, acc, n in ((0, b.a0, D), (1, b.a1, D), (2, b.a2, D), (3, b.a3, 512), (4, b.a4, 512), (5, b.a5, 512), (6, b.a6, 512)):
        put_vec(b, row, acc, n)
    yield


def scatter_args(sset, grads, vec):
    ins = {"s_" + n: (grads[n], ANY) for n in sset.names}
    ins["s_vec"] = (vec, VM)
    outs = {"r_" + n: ((RB, grads[n].shape[1]), F32, VM) for n in sset.names}
    outs["r_vec"] = ((8, HP), F32, VM)
    return ins, outs


def scatter_start(sset, w, b, sc=None):
    n = sset.names
    return sset.start(w, {i: getattr(b, "s_" + i) for i in n}, {i: getattr(b, "r_" + i) for i in n}, b.s_vec, b.r_vec, b.extra if sc is None else sc)


HB_RATE = 2


def backward_hidden(g, fw, hm, tabs, wts, vn, vf, sset, grads, vec, cid):
    R, D = g.shape

    def body(b):
        w = Where()
        greet_all(w, "all")
        core = Peer((w.dp, w.x, 1 - w.c), b.cs, b.cr)
        load = pltpu.make_async_copy(b.hm, b.go, b.ls.at[0])
        load.start()
        comp = hidden_back_body(b, w, R, core)
        if sset:
            comm = scatter_start(sset, w, b, b.extra[:split])
            for _ in sset.live:
                next(comm)
        load.wait()

        def both():
            for _ in range(5):
                if sset:
                    for _ in range(3):
                        next(comm, None)
                yield
            mine = dset.start(w, {"dn": b.d_dn}, {"dn": b.r_dn}, None, None, b.extra[split:])
            for _ in dset.live:
                next(mine)
            yield
            yield from step_all([mine, comm] if sset else [mine])

        drive(comp, both(), [1] * 6, HB_RATE * (2 if sset else 1))
        if sset:
            sset.finish()
        dset.finish()
        core.finish()

    ins = dict(g=(g, LD), keep=(tabs["keep"], LD), hm=(hm, ANY), gate=(fw["gate"], LD), up=(fw["up"], LD),
        st=(fw["zst"], LD), w_gu=(wts["gu"], LATE), w_dn=(wts["dn"], LD), vn=(vn, LD), vf=(vf, LD))
    outs = dict(go=((R, D), F32, ST), d_gu=((D, 2 * HP), BF, ST), r_dn=((RB, HP), F32, VM), vec=((8, HP), F32, VM))
    extra = ()
    dset = dn_scatter()
    if sset:
        i2, o2 = scatter_args(sset, grads, vec)
        ins.update(i2)
        outs.update(o2)
        extra = sset.scratch()
    split = len(extra)
    extra = list(extra) + dset.scratch()
    acc = lambda n: pltpu.VMEM((8, n), F32)
    scratch = dict(d_dn=pltpu.VMEM((D, HP), BF), el=pltpu.VMEM((R, D), BF), xT=pltpu.VMEM((D, R), BF), n=pltpu.VMEM((R, D), BF),
        ez=pltpu.VMEM((R, HP), F32), zn=pltpu.VMEM((R, HP), BF), egu=pltpu.VMEM((R, 2 * HP), BF),
        part=pltpu.VMEM((R, D), BF), rpart=pltpu.VMEM((R, D), BF), stat=pltpu.VMEM((R, 128), F32),
        rstat=pltpu.VMEM((R, 128), F32), cs=DMA((5,)), cr=DMA((5,)), ls=DMA((1,)), a0=acc(D), a1=acc(D), a2=acc(D),
        a3=acc(HP), a4=acc(HP), a5=acc(HP), a6=acc(HP))
    return run_kernel(body, "hidden_back", cid, ins, outs, scratch, extra)


def backward_attend(g, fw, h, tabs, wts, vn, vh, sset, grads, vec, cid):
    R, D = g.shape

    def body(b):
        w = Where()
        greet_all(w, "all")
        core = Peer((w.dp, w.x, 1 - w.c), b.cs, b.cr)
        side = Peer(w.nx(), b.xs, b.xr)
        load = pltpu.make_async_copy(b.h, b.go, b.ls.at[0])
        load.start()
        comm = scatter_start(sset, w, b)
        for _ in sset.live:
            next(comm)
        load.wait()
        drive(attend_back_body(b, w, R, core, side), comm, [1] * 4 + [1, 2] * 8, 2)
        sset.finish()
        core.finish()

    ins = dict(g=(g, LD), keep=(tabs["keep"], LD), h=(h, ANY), fill=(tabs["fill"], LATE), cos=(tabs["cos"], LATE),
        sin=(tabs["sin"], LATE), o=(fw["o"], LD), st=(fw["st"], LD), q=(fw["q"], LATE), k=(fw["k"], LATE),
        v=(fw["v"], LATE), lse=(fw["lse"], LATE), w_in=(wts["in"], LATE), w_out=(wts["out"], LD), vn=(vn, LD),
        vh=(vh, LD))
    outs = dict(go=((R, D), F32, ST), d_in=((D, 1536), BF, ST), d_out=((D, 512), BF, ST), vec=((8, HP), F32, VM))
    i2, o2 = scatter_args(sset, grads, vec)
    ins.update(i2)
    outs.update(o2)
    acc = lambda n: pltpu.VMEM((8, n), F32)
    B = lambda *s: pltpu.VMEM(s, BF)
    F = lambda *s: pltpu.VMEM(s, F32)
    scratch = dict(el=B(R, D), xT=B(D, R), n=B(R, D), u=B(R, 512), eo=B(R, 512), s=F(2 * R, R), dp=F(2 * R, R), p=B(2 * R, R),
        ds=B(2 * R, R), dq=F(R, 512), dk=F(R, 512), dv=F(R, 512), rk=B(R, 512), rv=B(R, 512), ep=B(R, 1536),
        part=B(R, D), rpart=B(R, D), stat=F(R, 128), rstat=F(R, 128), cs=DMA((5,)), cr=DMA((5,)), ls=DMA((1,)),
        xs=DMA((8,)), xr=DMA((8,)), a0=acc(D), a1=acc(D), a2=acc(D), a3=acc(512), a4=acc(512), a5=acc(512),
        a6=acc(512))
    return run_kernel(body, "attend_back", cid, ins, outs, scratch, sset.scratch())


def scatter_last(sset, grads, vec, cid):
    def body(b):
        w = Where()
        greet(w)
        for _ in scatter_start(sset, w, b):
            pass
        sset.finish()

    ins, outs = scatter_args(sset, grads, vec)
    return run_kernel(body, "scatter", cid, ins, outs, {}, sset.scratch())


HP = 1408


def fast_device(
    tokens_in,
    cotangent,
    key_mask,
    grid_pos,
    class_index,
    input_weight,
    output_weight,
    gate_up_weight,
    down_weight,
    norm_gains,
    norm_biases,
    head_gains,
    head_biases,
    hidden_gains,
    hidden_biases,
):
    _, rows, width = tokens_in.shape
    dim = head_gains.shape[1]
    hidden = hidden_gains.shape[1]
    layers = input_weight.shape[0]
    pad = HP - hidden
    R = -(-rows // 16) * 16
    more = R - rows
    places = lax.axis_index("ctx") * rows + jnp.arange(rows, dtype=jnp.int32)
    not_class = (places != class_index[0]).astype(F32)
    cosine, sine = rotary_tables(grid_pos.reshape(2, rows), not_class)
    c0, c1, s0, s1 = cosine[:, 0], cosine[:, 1], sine[:, 0], sine[:, 1]
    low = lambda a: jnp.pad(a, ((0, more), (0, 0)))
    keep = low(key_mask.astype(F32).reshape(rows, 1))
    real = jnp.pad(key_mask.astype(F32).reshape(1, rows), ((0, 0), (0, more)))
    fill = jnp.where(jnp.arange(R)[None] < rows, (real - 1.0) * 10000.0, -1.0e30)
    fill = jnp.broadcast_to(fill, (8, R))
    tabs = dict(keep=jnp.broadcast_to(keep, (R, 128)), cos=low(jnp.concatenate([c0, c0, c1, c1] * 2, axis=1)),
        sin=low(jnp.concatenate([-s0, s0, -s1, s1] * 2, axis=1)))
    gn = norm_gains.astype(F32)
    bn = norm_biases.astype(F32)
    gh = head_gains.astype(F32)[:, None]
    bh = head_biases.astype(F32)
    vh = jnp.pad(jnp.concatenate([gh, bh], axis=1), ((0, 0), (0, 4), (0, 0)))
    vn = jnp.stack([gn[:, 0], bn[:, 0], gn[:, 1], bn[:, 1], bn[:, 2], bn[:, 3]], axis=1)
    vn = jnp.pad(vn, ((0, 0), (0, 2), (0, 0)))
    vf = jnp.concatenate([hidden_gains.astype(F32)[:, None], hidden_biases.astype(F32)], axis=1)
    vf = jnp.pad(vf, ((0, 0), (0, 4), (0, pad)))
    gu = jnp.pad(gate_up_weight, ((0, 0), (0, 0), (0, 0), (0, pad)))
    dn = jnp.pad(down_weight, ((0, 0), (0, 0), (0, pad)))
    at_src = [{"in": input_weight[l].reshape(RB, 3 * dim), "out": output_weight[l]} for l in range(layers)]
    ff_src = [{"gu": gu[l].reshape(RB, 2 * HP), "dn": dn[l]} for l in range(layers)]
    grab = lambda d, names: {n: d["g_" + n] for n in names}
    h = low(tokens_in.astype(F32).reshape(rows, width)) * keep
    first = gather_first(at_src[0], AT_G, fill, 0)
    tabs["fill"] = first["both"]
    at_w = {0: {n: first["w_" + n] for n in AT_G.names}}
    ff_w, hs, fw = {}, {}, {}
    for l in range(layers):
        hs[l] = h
        nxt = l + 1 < layers
        r = forward_layer(h, tabs, at_w[l], vn[l], vh[l], vf[l], ff_src[l], at_src[l + 1] if nxt else None, 1 + l)
        fw[l], h = r, r["ho"]
        ff_w[l] = grab(r, FF_G.names)
        if nxt:
            at_w[l + 1] = grab(r, AT_G.names)
    activations = h[:rows].astype(BF).reshape(1, rows, width)
    g = low(cotangent.astype(F32).reshape(rows, width))
    got = {}
    grads, vec, cid = None, None, layers + 1
    for l in reversed(range(layers)):
        sset = at_scatter() if grads else None
        r = backward_hidden(g, fw[l], fw[l]["hm"], tabs, ff_w[l], vn[l], vf[l], sset, grads, vec, cid)
        if grads:
            got["at", l + 1] = r
        g, vec, grads, got["dn", l] = r["go"], r["vec"], {"gu": r["d_gu"]}, r["r_dn"]
        r = backward_attend(g, fw[l], hs[l], tabs, at_w[l], vn[l], vh[l], gu_scatter(), grads, vec, cid + 1)
        got["ff", l] = r
        g, vec, grads = r["go"], r["vec"], {"in": r["d_in"], "out": r["d_out"]}
        cid += 2
    got["at", 0] = scatter_last(at_scatter(), grads, vec, cid)
    input_grad = (keep * g)[:rows].reshape(1, rows, width)
    L = range(layers)
    va = jnp.stack([got["at", l]["r_vec"] for l in L])
    vff = jnp.stack([got["ff", l]["r_vec"] for l in L])
    return (
        activations,
        input_grad,
        jnp.stack([got["at", l]["r_in"].reshape(RB, 3, dim) for l in L]),
        jnp.stack([got["at", l]["r_out"] for l in L]),
        jnp.stack([got["ff", l]["r_gu"].reshape(RB, 2, HP)[:, :, :hidden] for l in L]),
        jnp.stack([got["dn", l][:, :hidden] for l in L]),
        jnp.stack([va[:, 0, :width], vff[:, 0, :width]], axis=1),
        jnp.stack([va[:, 1, :width], vff[:, 1, :width], va[:, 2, :width], vff[:, 2, :width]], axis=1),
        va[:, 3, :dim],
        va[:, 4:7, :dim],
        vff[:, 3, :hidden],
        vff[:, 4:7, :hidden],
    )


def solution(mesh):
    sizes = dict(mesh.shape)
    fits = sizes == dict(dp=8, ctx=2, tp=2)
    return jax.shard_map(
        fast_device if fits else on_device,
        mesh=mesh,
        in_specs=(
            P("dp", "ctx", None),
            P("dp", "ctx", None),
            P("dp", "ctx"),
            P(None, "dp", "ctx"),
            P("dp"),
            P(None, ("dp", "ctx"), None, "tp"),
            P(None, ("dp", "ctx"), "tp"),
            P(None, ("dp", "ctx"), None, "tp"),
            P(None, ("dp", "ctx"), "tp"),
            P(),
            P(),
            P(None, "tp"),
            P(None, None, "tp"),
            P(None, "tp"),
            P(None, None, "tp"),
        ),
        out_specs=(
            P("dp", "ctx", None),
            P("dp", "ctx", None),
            P(None, ("dp", "ctx"), None, "tp"),
            P(None, ("dp", "ctx"), "tp"),
            P(None, ("dp", "ctx"), None, "tp"),
            P(None, ("dp", "ctx"), "tp"),
            P(),
            P(),
            P(None, "tp"),
            P(None, None, "tp"),
            P(None, "tp"),
            P(None, None, "tp"),
        ),
        check_vma=False,
    )
```

```python
import functools

import jax
import jax.numpy as jnp
from jax import lax
from jax.experimental import pallas as pl
from jax.experimental.pallas import tpu as pltpu
from jax.sharding import PartitionSpec as P

FF = 2730
HEAD_DIM = 64


norm_epsilon = 1e-06
rotary_base = 10000.0
masked_score = -10000.0


def rotary_tables(positions, not_class):
    quarter = HEAD_DIM // 4
    frequency = rotary_base ** (-jnp.arange(quarter, dtype=jnp.float32) / quarter)
    angles = (
        jnp.transpose(positions).astype(jnp.float32)[:, :, None]
        * frequency
        * not_class[:, None, None]
    )
    return (jnp.cos(angles), jnp.sin(angles))


def rotate(values, cosine, sine, direction):
    row_count, head_count, head_dim = values.shape
    paired = values.reshape(row_count, head_count, 2, 2, head_dim // 4)
    first_half = paired[:, :, :, 0]
    second_half = paired[:, :, :, 1]
    cos_rows = cosine[:, None]
    sin_rows = sine[:, None] * direction
    turned = jnp.stack(
        [
            first_half * cos_rows - second_half * sin_rows,
            second_half * cos_rows + first_half * sin_rows,
        ],
        axis=3,
    )
    return turned.reshape(row_count, head_count, head_dim)


def local_norm(values, gain_vec, shift_vec):
    center = values - jnp.mean(values, axis=-1, keepdims=True)
    spread = jnp.mean(center * center, axis=-1, keepdims=True)
    inv_spread = lax.rsqrt(spread + norm_epsilon)
    unit_rows = center * inv_spread
    return (unit_rows * gain_vec + shift_vec, unit_rows, inv_spread)


def local_norm_back(upstream, unit_rows, inv_spread, gain_vec):
    weighted = upstream * gain_vec
    return inv_spread * (
        weighted
        - jnp.mean(weighted, axis=-1, keepdims=True)
        - unit_rows * jnp.mean(weighted * unit_rows, axis=-1, keepdims=True)
    )


def row_totals(first_part, second_part):
    return lax.psum(
        (jnp.sum(first_part, axis=-1, keepdims=True), jnp.sum(second_part, axis=-1, keepdims=True)),
        "tp",
    )


def split_norm(values, gain_vec, shift_vec, full_width):
    sum_first, sum_second = row_totals(values, values * values)
    row_mean = sum_first / full_width
    inv_spread = lax.rsqrt(sum_second / full_width - row_mean * row_mean + norm_epsilon)
    unit_rows = (values - row_mean) * inv_spread
    return (unit_rows * gain_vec + shift_vec, unit_rows, inv_spread)


def split_norm_back(upstream, unit_rows, inv_spread, gain_vec, full_width):
    weighted = upstream * gain_vec
    sum_first, sum_second = row_totals(weighted, weighted * unit_rows)
    return inv_spread * (weighted - sum_first / full_width - unit_rows * (sum_second / full_width))


def tensor_sum(partial_value):
    return lax.psum(partial_value.astype(jnp.bfloat16), "tp").astype(jnp.float32)


def tensor_back(partial_value):
    return lax.psum(partial_value.astype(jnp.bfloat16), "tp").astype(jnp.float32)


def fetch_weights(layer_index, input_weight, output_weight, gate_up_weight, down_weight):
    return (
        lax.all_gather(input_weight[layer_index], ("dp", "ctx"), axis=0, tiled=True),
        lax.all_gather(output_weight[layer_index], ("dp", "ctx"), axis=0, tiled=True),
        lax.all_gather(gate_up_weight[layer_index], ("dp", "ctx"), axis=0, tiled=True),
        lax.all_gather(down_weight[layer_index], ("dp", "ctx"), axis=0, tiled=True),
    )


def masked_scores(queries, key_heads, valid_keys):
    raw_scores = jnp.einsum("qhe,khe->hqk", queries, key_heads, preferred_element_type=jnp.float32)
    return jnp.where(valid_keys[None, None, :] > 0, raw_scores * HEAD_DIM ** (-0.5), masked_score)


def attend_forward(block_items):
    queries, keys_all, values_all, valid_keys = block_items
    key_count = keys_all.shape[0]
    head_count = queries.shape[1]
    key_heads = keys_all.reshape(key_count, head_count, HEAD_DIM)
    value_heads = values_all.reshape(key_count, head_count, HEAD_DIM)
    scores = masked_scores(queries, key_heads, valid_keys)
    row_max = jnp.max(scores, axis=-1, keepdims=True)
    exp_scores = jnp.exp(scores - row_max)
    row_total = jnp.sum(exp_scores, axis=-1, keepdims=True)
    attn_probs = (exp_scores / row_total).astype(jnp.bfloat16)
    attended = jnp.einsum(
        "hqk,khe->qhe", attn_probs, value_heads, preferred_element_type=jnp.float32
    )
    return (
        attended.reshape(queries.shape[0], head_count * HEAD_DIM),
        (row_max + jnp.log(row_total))[:, :, 0],
    )


def attend_backward(block_items):
    queries, keys_all, values_all, valid_keys, log_total, grad_out = block_items
    key_count = keys_all.shape[0]
    head_count = queries.shape[1]
    key_heads = keys_all.reshape(key_count, head_count, HEAD_DIM)
    value_heads = values_all.reshape(key_count, head_count, HEAD_DIM)
    scores = masked_scores(queries, key_heads, valid_keys)
    probs_full = jnp.exp(scores - log_total[:, :, None])
    probs_low = probs_full.astype(jnp.bfloat16)
    grad_probs = jnp.einsum(
        "qhe,khe->hqk", grad_out, value_heads, preferred_element_type=jnp.float32
    )
    row_dot = jnp.sum(probs_full * grad_probs, axis=-1, keepdims=True)
    grad_raw = jnp.where(
        valid_keys[None, None, :] > 0, HEAD_DIM ** (-0.5) * probs_full * (grad_probs - row_dot), 0.0
    ).astype(jnp.bfloat16)
    grad_queries = jnp.einsum(
        "hqk,khe->qhe", grad_raw, key_heads, preferred_element_type=jnp.float32
    )
    grad_keys = jnp.einsum("hqk,qhe->khe", grad_raw, queries, preferred_element_type=jnp.float32)
    grad_values = jnp.einsum(
        "hqk,qhe->khe", probs_low, grad_out, preferred_element_type=jnp.float32
    )
    local_rows = queries.shape[0]
    return (
        grad_queries.reshape(local_rows, head_count * HEAD_DIM),
        grad_keys.reshape(key_count, head_count * HEAD_DIM),
        grad_values.reshape(key_count, head_count * HEAD_DIM),
    )


def contract_rows(left, right):
    return lax.dot_general(
        left, right, (((0,), (0,)), ((), ())), preferred_element_type=jnp.float32
    )


def contract_cols(left, right):
    return lax.dot_general(
        left, right, (((1,), (1,)), ((), ())), preferred_element_type=jnp.float32
    )


def on_device(
    tokens_in,
    cotangent,
    key_mask,
    grid_pos,
    class_index,
    input_weight,
    output_weight,
    gate_up_weight,
    down_weight,
    norm_gains,
    norm_biases,
    head_gains,
    head_biases,
    hidden_gains,
    hidden_biases,
):
    images, rows_dev, model_width = tokens_in.shape
    row_count = images * rows_dev
    dim_local = head_gains.shape[1]
    heads_local = dim_local // HEAD_DIM
    hidden_local = hidden_gains.shape[1]
    layer_count = input_weight.shape[0]
    first_row = lax.axis_index("ctx") * rows_dev
    places = first_row + jnp.arange(rows_dev, dtype=jnp.int32)
    not_class = (places[None, :] != class_index[:, None]).astype(jnp.float32).reshape(row_count)
    cosine, sine = rotary_tables(grid_pos.reshape(2, row_count), not_class)
    row_keep = key_mask.astype(jnp.float32).reshape(row_count, 1)
    key_keep = key_mask.astype(jnp.bfloat16)
    gains_norm = norm_gains.astype(jnp.float32)
    biases_norm = norm_biases.astype(jnp.float32)
    gains_head = head_gains.astype(jnp.float32)
    biases_head = head_biases.astype(jnp.float32)
    gains_hidden = hidden_gains.astype(jnp.float32)
    biases_hidden = hidden_biases.astype(jnp.float32)
    hidden_state = tokens_in.astype(jnp.float32).reshape(row_count, model_width) * row_keep
    saved_layers = []
    for layer_index in range(layer_count):
        layer_mats = fetch_weights(
            layer_index, input_weight, output_weight, gate_up_weight, down_weight
        )
        mat_in, mat_out, mat_gate_up, mat_down = layer_mats
        normed, unit_one, spread_one = local_norm(
            hidden_state, gains_norm[layer_index, 0], biases_norm[layer_index, 0]
        )
        normed_low = normed.astype(jnp.bfloat16)
        projected = jnp.dot(
            normed_low,
            mat_in.reshape(model_width, 3 * dim_local),
            preferred_element_type=jnp.float32,
        ).reshape(row_count, 3, dim_local)
        queries = projected[:, 0] + biases_head[layer_index, 0]
        keys_proj = projected[:, 1]
        values_proj = projected[:, 2] + biases_head[layer_index, 1]
        query_low = rotate(
            queries.reshape(row_count, heads_local, HEAD_DIM), cosine, sine, 1.0
        ).astype(jnp.bfloat16)
        key_low = rotate(
            keys_proj.reshape(row_count, heads_local, HEAD_DIM), cosine, sine, 1.0
        ).astype(jnp.bfloat16)
        value_low = values_proj.astype(jnp.bfloat16)
        keys_all, values_all, valid_all = (
            lax.all_gather(key_low.reshape(images, rows_dev, dim_local), "ctx", axis=1, tiled=True),
            lax.all_gather(
                value_low.reshape(images, rows_dev, dim_local), "ctx", axis=1, tiled=True
            ),
            lax.all_gather(key_keep, "ctx", axis=1, tiled=True),
        )
        query_blocks = query_low.reshape(images, rows_dev, heads_local, HEAD_DIM)
        attended, log_total = lax.map(
            attend_forward, (query_blocks, keys_all, values_all, valid_all)
        )
        attended = attended.reshape(row_count, dim_local)
        head_normed, unit_two, spread_two = split_norm(
            attended, gains_head[layer_index], biases_head[layer_index, 2], model_width
        )
        head_low = head_normed.astype(jnp.bfloat16)
        branch = tensor_sum(contract_cols(head_low, mat_out))
        hidden_mid = hidden_state + row_keep * (branch + biases_norm[layer_index, 2])
        normed_two, unit_three, spread_three = local_norm(
            hidden_mid, gains_norm[layer_index, 1], biases_norm[layer_index, 1]
        )
        normed_two_low = normed_two.astype(jnp.bfloat16)
        gate_up = jnp.dot(
            normed_two_low,
            mat_gate_up.reshape(model_width, 2 * hidden_local),
            preferred_element_type=jnp.float32,
        ).reshape(row_count, 2, hidden_local)
        gate_pre = gate_up[:, 0] + biases_hidden[layer_index, 0]
        up_pre = gate_up[:, 1] + biases_hidden[layer_index, 1]
        inner_act = jax.nn.silu(gate_pre) * up_pre
        inner_normed, unit_four, spread_four = split_norm(
            inner_act, gains_hidden[layer_index], biases_hidden[layer_index, 2], FF
        )
        inner_low = inner_normed.astype(jnp.bfloat16)
        down_out = tensor_sum(contract_cols(inner_low, mat_down))
        hidden_state = hidden_mid + row_keep * (down_out + biases_norm[layer_index, 3])
        held_mats = None
        saved_layers.append(
            (
                held_mats,
                normed_low,
                unit_one,
                spread_one,
                query_blocks,
                keys_all,
                values_all,
                valid_all,
                log_total,
                unit_two,
                spread_two,
                head_low,
                unit_three,
                spread_three,
                normed_two_low,
                gate_pre,
                up_pre,
                unit_four,
                spread_four,
                inner_low,
            )
        )
    activations = hidden_state.reshape(images, rows_dev, model_width).astype(jnp.bfloat16)
    upstream = cotangent.astype(jnp.float32).reshape(row_count, model_width)
    mat_grads = [None] * layer_count
    vector_parts = [None] * layer_count
    for layer_index in reversed(range(layer_count)):
        (
            held_mats,
            normed_low,
            unit_one,
            spread_one,
            query_blocks,
            keys_all,
            values_all,
            valid_all,
            log_total,
            unit_two,
            spread_two,
            head_low,
            unit_three,
            spread_three,
            normed_two_low,
            gate_pre,
            up_pre,
            unit_four,
            spread_four,
            inner_low,
        ) = saved_layers[layer_index]
        mat_in, mat_out, mat_gate_up, mat_down = fetch_weights(
            layer_index, input_weight, output_weight, gate_up_weight, down_weight
        )
        grad_down = row_keep * upstream
        grad_bias_down = jnp.sum(grad_down, axis=0)
        grad_down_low = grad_down.astype(jnp.bfloat16)
        grad_mat_down = contract_rows(grad_down_low, inner_low)
        grad_inner_normed = jnp.dot(grad_down_low, mat_down, preferred_element_type=jnp.float32)
        grad_gain_hidden = jnp.sum(grad_inner_normed * unit_four, axis=0)
        grad_shift_hidden = jnp.sum(grad_inner_normed, axis=0)
        grad_inner = split_norm_back(
            grad_inner_normed, unit_four, spread_four, gains_hidden[layer_index], FF
        )
        sigmoid_gate = jax.nn.sigmoid(gate_pre)
        grad_up = grad_inner * gate_pre * sigmoid_gate
        grad_gate = grad_inner * up_pre * sigmoid_gate * (1.0 + gate_pre * (1.0 - sigmoid_gate))
        grad_gate_up_low = (
            jnp.stack([grad_gate, grad_up], axis=1)
            .astype(jnp.bfloat16)
            .reshape(row_count, 2 * hidden_local)
        )
        grad_mat_gate_up = contract_rows(normed_two_low, grad_gate_up_low).reshape(
            model_width, 2, hidden_local
        )
        grad_normed_two = tensor_back(
            contract_cols(grad_gate_up_low, mat_gate_up.reshape(model_width, 2 * hidden_local))
        )
        grad_gain_two = jnp.sum(grad_normed_two * unit_three, axis=0)
        grad_shift_two = jnp.sum(grad_normed_two, axis=0)
        upstream = upstream + local_norm_back(
            grad_normed_two, unit_three, spread_three, gains_norm[layer_index, 1]
        )
        grad_branch = row_keep * upstream
        grad_bias_out = jnp.sum(grad_branch, axis=0)
        grad_branch_low = grad_branch.astype(jnp.bfloat16)
        grad_mat_out = contract_rows(grad_branch_low, head_low)
        grad_head = jnp.dot(grad_branch_low, mat_out, preferred_element_type=jnp.float32)
        grad_gain_head = jnp.sum(grad_head * unit_two, axis=0)
        grad_shift_head = jnp.sum(grad_head, axis=0)
        grad_attended = split_norm_back(
            grad_head, unit_two, spread_two, gains_head[layer_index], model_width
        )
        grad_att_low = grad_attended.astype(jnp.bfloat16).reshape(
            images, rows_dev, heads_local, HEAD_DIM
        )
        grad_query_rot, grad_keys_all, grad_values_all = lax.map(
            attend_backward,
            (query_blocks, keys_all, values_all, valid_all, log_total, grad_att_low),
        )
        grad_keys_rot, grad_values = (
            lax.psum_scatter(
                grad_keys_all.astype(jnp.bfloat16), "ctx", scatter_dimension=1, tiled=True
            ).astype(jnp.float32),
            lax.psum_scatter(
                grad_values_all.astype(jnp.bfloat16), "ctx", scatter_dimension=1, tiled=True
            ).astype(jnp.float32),
        )
        grad_queries = rotate(
            grad_query_rot.reshape(row_count, heads_local, HEAD_DIM), cosine, sine, -1.0
        ).reshape(row_count, dim_local)
        grad_keys = rotate(
            grad_keys_rot.reshape(row_count, heads_local, HEAD_DIM), cosine, sine, -1.0
        ).reshape(row_count, dim_local)
        grad_values = grad_values.reshape(row_count, dim_local)
        grad_proj_low = (
            jnp.stack([grad_queries, grad_keys, grad_values], axis=1)
            .astype(jnp.bfloat16)
            .reshape(row_count, 3 * dim_local)
        )
        grad_mat_in = contract_rows(normed_low, grad_proj_low).reshape(model_width, 3, dim_local)
        grad_normed_one = tensor_back(
            contract_cols(grad_proj_low, mat_in.reshape(model_width, 3 * dim_local))
        )
        grad_gain_one = jnp.sum(grad_normed_one * unit_one, axis=0)
        grad_shift_one = jnp.sum(grad_normed_one, axis=0)
        upstream = upstream + local_norm_back(
            grad_normed_one, unit_one, spread_one, gains_norm[layer_index, 0]
        )
        mat_grads[layer_index] = (
            lax.psum_scatter(grad_mat_in, ("dp", "ctx"), scatter_dimension=0, tiled=True),
            lax.psum_scatter(grad_mat_out, ("dp", "ctx"), scatter_dimension=0, tiled=True),
            lax.psum_scatter(grad_mat_gate_up, ("dp", "ctx"), scatter_dimension=0, tiled=True),
            lax.psum_scatter(grad_mat_down, ("dp", "ctx"), scatter_dimension=0, tiled=True),
        )
        vector_parts[layer_index] = (
            jnp.stack([grad_gain_one, grad_gain_two]),
            jnp.stack([grad_shift_one, grad_shift_two, grad_bias_out, grad_bias_down]),
            grad_gain_head,
            jnp.stack(
                [jnp.sum(grad_queries, axis=0), jnp.sum(grad_values, axis=0), grad_shift_head]
            ),
            grad_gain_hidden,
            jnp.stack([jnp.sum(grad_gate, axis=0), jnp.sum(grad_up, axis=0), grad_shift_hidden]),
        )
    input_grad = (row_keep * upstream).reshape(images, rows_dev, model_width)
    stacked_vectors = tuple(
        (
            jnp.stack([vector_parts[index][member] for index in range(layer_count)])
            for member in range(6)
        )
    )
    summed_vectors = lax.psum(
        (
            stacked_vectors[0],
            stacked_vectors[1],
            stacked_vectors[2],
            stacked_vectors[3],
            stacked_vectors[4],
            stacked_vectors[5],
        ),
        ("dp", "ctx"),
    )
    grad_input_weight = jnp.stack([mat_grads[index][0] for index in range(layer_count)])
    grad_output_weight = jnp.stack([mat_grads[index][1] for index in range(layer_count)])
    grad_gate_up_weight = jnp.stack([mat_grads[index][2] for index in range(layer_count)])
    grad_down_weight = jnp.stack([mat_grads[index][3] for index in range(layer_count)])
    return (
        activations,
        input_grad,
        grad_input_weight,
        grad_output_weight,
        grad_gate_up_weight,
        grad_down_weight,
        summed_vectors[0],
        summed_vectors[1],
        summed_vectors[2],
        summed_vectors[3],
        summed_vectors[4],
        summed_vectors[5],
    )


MESH = pl.DeviceIdType.MESH

RB=64

class Where:
    def __init__(self):
        self.dp=lax.axis_index("dp"); self.x=lax.axis_index("ctx"); self.c=lax.axis_index("tp")
        self.z=self.dp//2; self.y=self.dp%2
    def nx(self): return (self.dp,1-self.x,self.c)
    def ny(self): return (self.z*2+1-self.y,self.x,self.c)
    def up(self): return ((self.z+1)*2+self.y,self.x,self.c)
    def dn(self): return ((self.z-1)*2+self.y,self.x,self.c)

def greet(w):
    bar=pltpu.get_barrier_semaphore()
    def sig(dev): pl.semaphore_signal(bar,inc=1,device_id=dev,device_id_type=MESH)
    sig(w.nx()); sig(w.ny())
    @pl.when(w.z<3)
    def _(): sig(w.up())
    @pl.when(w.z>0)
    def _(): sig(w.dn())
    pl.semaphore_wait(bar,2+(w.z<3).astype(jnp.int32)+(w.z>0).astype(jnp.int32))

class Gather:
    def __init__(self,w,order,src,out,r0,nr,ssem,rsem,own_sem):
        self.w,self.order,self.src,self.out,self.r0,self.nr=w,order,src,out,r0,nr
        self.ssem,self.rsem=ssem,rsem
        self.pending=[]
    def rows(self,zz,yy,xx):
        return pl.ds(pl.multiple_of(((zz*2+yy)*2+xx)*RB+self.r0,16),self.nr)
    def here(self,zz,yy,xx,own=False):
        return self.src.at[pl.ds(self.r0,self.nr)] if own else self.out.at[self.rows(zz,yy,xx)]
    def copy(self,zz,yy,xx,dev,s,r,own=False):
        return pltpu.make_async_remote_copy(src_ref=self.here(zz,yy,xx,own),dst_ref=self.out.at[self.rows(zz,yy,xx)],
            send_sem=self.ssem.at[s],recv_sem=self.rsem.at[r],device_id=dev,device_id_type=MESH)
    def send(self,cond,*a,**k):
        self.pending.append((cond,a,k))
        if cond is None: self.copy(*a,**k).start()
        else:
            @pl.when(cond)
            def _(): self.copy(*a,**k).start()
    def finish_sends(self):
        for cond,a,k in self.pending:
            if cond is None: self.copy(*a,**k).wait_send()
            else:
                @pl.when(cond)
                def _(a=a,k=k): self.copy(*a,**k).wait_send()
    def arrived(self,zz,yy,xx,r):
        self.copy(zz,yy,xx,self.w.nx(),0,r).wait_recv()

class GatherZ(Gather):
    def pq(self,zz,pself):
        w=self.w
        if self.order=="zyx": return (zz,w.y if pself else 1-w.y,w.x)
        return (zz,w.y,w.x if pself else 1-w.x)
    def pdev(self): return self.w.ny() if self.order=="zyx" else self.w.nx()
    def qdev(self): return self.w.nx() if self.order=="zyx" else self.w.ny()
    def qcoord(self,zz,pself):
        w=self.w
        if self.order=="zyx": return (zz,w.y if pself else 1-w.y,1-w.x)
        return (zz,1-w.y,w.x if pself else 1-w.x)
    def emit(self,cond,zz,k,own=False):
        b=self.pq(zz,True)
        w=self.w
        if k<4:
            c=(w.z<3) if cond is None else jnp.logical_and(cond,w.z<3)
            self.send(c,*b,w.up(),k,zz,own=own)
        if k==0 or k>=4:
            c=(w.z>0) if cond is None else jnp.logical_and(cond,w.z>0)
            self.send(c,*b,w.dn(),7+(k if k==0 else k-3),zz,own=own)
        self.send(cond,*b,self.pdev(),11+k,4+zz,own=own)
        self.send(cond,*b,self.qdev(),18+k,8+zz*2,own=own)
    def rounds(self):
        w=self.w
        self.emit(None,w.z,0,own=True)
        yield
        for k in (1,2,3):
            for kk,zz,cond in ((k,w.z-k,w.z>=k),(k+3,w.z+k,w.z+k<=3)):
                @pl.when(cond)
                def _(zz=zz): self.arrived(*self.pq(zz,True),zz)
                self.emit(cond,zz,kk)
            yield
        for k in (0,1,2,3):
            for kk,zz,cond in (((0,w.z,None),) if k==0 else ((k,w.z-k,w.z>=k),(k+3,w.z+k,w.z+k<=3))):
                b=self.pq(zz,False)
                def go(zz=zz,b=b): self.arrived(*b,4+zz)
                if cond is None: go()
                else: pl.when(cond)(go)
                self.send(cond,*b,self.qdev(),25+kk,8+zz*2+1)
            yield
    def arrive(self):
        for zz in range(4):
            for pself in (True,False):
                self.arrived(*self.qcoord(zz,pself),8+zz*2+(0 if pself else 1))
    NS,NR=32,16

class GatherX(Gather):
    NS,NR=3+4*7,19
    def blk(self,zz,j):
        w=self.w
        return (zz,w.y if j<2 else 1-w.y,w.x if j%2==0 else 1-w.x)
    def vert(self,cond,zz,j,k,own=False):
        w=self.w; b=self.blk(zz,j)
        if k<4:
            c=(w.z<3) if cond is None else jnp.logical_and(cond,w.z<3)
            self.send(c,*b,w.up(),3+j*7+k if k else 3+j*7,3+zz*4+j,own=own)
        if k==0 or k>=4:
            c=(w.z>0) if cond is None else jnp.logical_and(cond,w.z>0)
            self.send(c,*b,w.dn(),3+j*7+(k if k>=4 else 3),3+zz*4+j,own=own)
    def rounds(self):
        w=self.w
        self.send(None,*self.blk(w.z,0),w.nx(),0,0,own=True)
        self.send(None,*self.blk(w.z,0),w.ny(),1,1,own=True)
        self.vert(None,w.z,0,0,own=True)
        yield
        b=self.blk(w.z,1); self.arrived(*b,0)
        self.send(None,*b,w.ny(),2,2)
        yield
        yield
        yield
        self.arrived(*self.blk(w.z,2),1)
        self.arrived(*self.blk(w.z,3),2)
        for j in range(1,4): self.vert(None,w.z,j,0)
        yield
        for k in (1,2,3):
            for j in range(4):
                for kk,zz,cond in ((k,w.z-k,w.z>=k),(k+3,w.z+k,w.z+k<=3)):
                    @pl.when(cond)
                    def _(zz=zz,j=j): self.arrived(*self.blk(zz,j),3+zz*4+j)
                    if k<3: self.vert(cond,zz,j,kk)
                if j%2==1: yield
    def arrive(self):
        pass


ZORD=(3,0,2,1)
class Scatter:
    def __init__(self,w,order,src,out,r0,nr,ssem,rsem,lsem,own,bufs):
        self.w,self.order,self.src,self.out,self.r0,self.nr=w,order,src,out,r0,nr
        self.ssem,self.rsem,self.lsem,self.own=ssem,rsem,lsem,own
        self.bufs=bufs
        self.pending=[]
    def rows(self,zz,yy,xx):
        return pl.ds(pl.multiple_of(((zz*2+yy)*2+xx)*RB+self.r0,16),self.nr)
    def send(self,cond,src,dst,dev,s,r):
        mk=lambda: pltpu.make_async_remote_copy(src_ref=src,dst_ref=dst,send_sem=self.ssem.at[s],recv_sem=self.rsem.at[r],device_id=dev,device_id_type=MESH)
        self.pending.append((cond,mk))
        if cond is None: mk().start()
        else: pl.when(cond)(lambda: mk().start())
    def wait(self,cond,dst,r):
        def go(): pltpu.make_async_remote_copy(src_ref=dst,dst_ref=dst,send_sem=self.ssem.at[0],recv_sem=self.rsem.at[r],device_id=self.w.nx(),device_id_type=MESH).wait_recv()
        if cond is None: go()
        else: pl.when(cond)(go)
    def finish(self):
        for cond,mk in self.pending:
            if cond is None: mk().wait_send()
            else: pl.when(cond)(lambda mk=mk: mk().wait_send())
    def total(self,dst,terms,extra=()):
        def strip(i,_):
            s=pl.ds(pl.multiple_of(i*16,16),16)
            t=terms[0][s].astype(jnp.float32)
            for r in terms[1:]: t=t+r[s].astype(jnp.float32)
            dst[s]=t.astype(dst.dtype)
            return 0
        lax.fori_loop(0,self.nr//16,strip,0)

class ScatterZ(Scatter):
    NS,NR=16,17
    def mine(self,zz,pself):
        w=self.w
        if self.order=="zyx": return (zz,w.y if pself else 1-w.y,w.x)
        return (zz,w.y,w.x if pself else 1-w.x)
    def theirs(self,zz,pself):
        w=self.w
        if self.order=="zyx": return (zz,w.y if pself else 1-w.y,1-w.x)
        return (zz,1-w.y,w.x if pself else 1-w.x)
    def rounds(self):
        w=self.w; rq,rp,ru=self.bufs
        pdev=w.ny() if self.order=="zyx" else w.nx()
        qdev=w.nx() if self.order=="zyx" else w.ny()
        loc={}
        for k in (1,0):
            for zz in ZORD:
                c=pltpu.make_async_copy(self.src.at[self.rows(*self.mine(zz,k==0))],self.own.at[zz*2+k],self.lsem.at[zz*2+k]); c.start(); loc[zz*2+k]=c
        for zz in ZORD:
            self.send(None,self.src.at[self.rows(*self.theirs(zz,False))],rq.at[zz*2+1],qdev,zz*2+1,zz*2+1)
        yield
        for zz in ZORD:
            i=zz*2+1
            loc[i].wait(); self.wait(None,rq.at[i],i)
            self.total(rq.at[i],[self.own.at[i],rq.at[i]])
            self.send(None,rq.at[i],rp.at[zz],pdev,8+zz,8+zz)
            self.send(None,self.src.at[self.rows(*self.theirs(zz,True))],rq.at[zz*2],qdev,zz*2,zz*2)
            yield
        def ready(zz):
            loc[zz*2].wait(); self.wait(None,rq.at[zz*2],zz*2); self.wait(None,rp.at[zz],8+zz)
            return [self.own.at[zz*2],rq.at[zz*2],rp.at[zz]]
        for t in (1,2,3):
            for i in range(4):
                for up in (True,False):
                    m=i if up else 3-i
                    if m>=t: continue
                    zz=4-t+m if up else t-1-m
                    @pl.when(w.z==i)
                    def _():
                        terms=ready(zz)
                        if m>0:
                            self.wait(None,ru.at[zz],12+zz); terms.append(ru.at[zz])
                        self.total(rp.at[zz],terms)
                    if up: self.send(w.z==i,rp.at[zz],ru.at[zz],w.up(),12+zz,12+zz)
                    else:
                        to=4 if zz==i-1 else zz
                        self.send(w.z==i,rp.at[zz],ru.at[to],w.dn(),12+zz,12+to)
            yield
        o=self.out.at[pl.ds(self.r0,self.nr)]
        for zz in range(4):
            @pl.when(w.z==zz)
            def _():
                terms=ready(zz)
                if zz>0: self.wait(None,ru.at[zz],12+zz); terms.append(ru.at[zz])
                if zz<3: self.wait(None,ru.at[4],16); terms.append(ru.at[4])
                self.total(o,terms)
        yield

class ScatterX(Scatter):
    NS,NR=19,23
    def blk(self,zz,j):
        w=self.w
        return (zz,w.y if j<2 else 1-w.y,w.x if j%2==0 else 1-w.x)
    def rounds(self):
        w=self.w; ru,ry,rx=self.bufs
        down=lambda zz,j: jnp.where(w.z-1==zz,16+j,zz*4+j)
        loc={}
        for zz in ZORD:
            for j in (3,2,1,0):
                i=zz*4+j
                c=pltpu.make_async_copy(self.src.at[self.rows(*self.blk(zz,j))],self.own.at[i],self.lsem.at[i]); c.start(); loc[i]=c
        J=(3,2,1,0)
        for zz in (3,2,1):
            for j in J: self.send(w.z==0,self.src.at[self.rows(*self.blk(zz,j))],ru.at[zz*4+j],w.up(),zz*4+j,zz*4+j)
        for zz in (0,1,2):
            for j in J:
                to=16+j if zz==2 else zz*4+j
                self.send(w.z==3,self.src.at[self.rows(*self.blk(zz,j))],ru.at[to],w.dn(),zz*4+j,to)
        yield
        for i in loc: loc[i].wait()
        def hop(c,zz,j,up):
            i=zz*4+j
            @pl.when(w.z==c)
            def _():
                self.wait(None,ru.at[i],i)
                self.total(ru.at[i],[self.own.at[i],ru.at[i]])
            if up: self.send(w.z==c,ru.at[i],ru.at[i],w.up(),i,i)
            else:
                to=16+j if zz==c-1 else i
                self.send(w.z==c,ru.at[i],ru.at[to],w.dn(),i,to)
        for j in J:
            hop(1,3,j,True); hop(2,0,j,False)
            if j%2==0: yield
        for j in J:
            hop(1,2,j,True); hop(2,1,j,False)
            hop(2,3,j,True); hop(1,0,j,False)
            if j%2==0: yield
        def zsum(j,dst,extra):
            for zz in range(4):
                i=zz*4+j
                t=[self.own.at[i]]
                if zz>0: t.append(ru.at[i])
                if zz<3: t.append(ru.at[16+j])
                @pl.when(w.z==zz)
                def _():
                    if zz>0: self.wait(None,ru.at[i],i)
                    if zz<3: self.wait(None,ru.at[16+j],16+j)
                    self.total(dst,t+extra)
        sy=self.bufs_stage
        for j in (3,2):
            k=j-2
            zsum(j,sy.at[k],[])
            self.send(None,sy.at[k],ry.at[k],w.ny(),16+k,20+k)
        yield
        self.wait(None,ry.at[1],21)
        zsum(1,sy.at[2],[ry.at[1]])
        self.send(None,sy.at[2],rx.at[0],w.nx(),18,22)
        yield
        self.wait(None,ry.at[0],20)
        self.wait(None,rx.at[0],22)
        zsum(0,self.out.at[pl.ds(self.r0,self.nr)],[ry.at[0],rx.at[0]])
        yield


F32 = jnp.float32
BF = jnp.bfloat16
DMA = pltpu.SemaphoreType.DMA
EPS = 1e-06


def step_all(gens):
    gens = list(gens)
    while gens:
        for g in list(gens):
            try:
                next(g)
            except StopIteration:
                gens.remove(g)
                continue
            yield


def drive(compute, comm, plan, rest):
    for i, _ in enumerate(compute):
        for _ in range(plan[i] if i < len(plan) else rest):
            next(comm, None)
    for _ in comm:
        pass


class GatherSet:
    def __init__(self, parts, names, cut=32):
        self.parts, self.names, self.cut = parts, names, cut

    def scratch(self):
        out = []
        for name, cols, kind in self.parts:
            if kind == "z":
                out += [DMA((GatherZ.NS,)), DMA((GatherZ.NR,))] * 2
            else:
                out += [DMA((GatherX.NS,)), DMA((GatherX.NR,))]
        return out + [DMA((len(self.names),))]

    def start(self, w, srcs, outs, sems):
        sems = list(sems)
        me = pl.multiple_of((w.dp * 2 + w.x) * RB, 16)
        self.locs = []
        for i, name in enumerate(self.names):
            c = pltpu.make_async_copy(srcs[name], outs[name].at[pl.ds(me, RB)], sems[-1].at[i])
            c.start()
            self.locs.append(c)
        self.live = []
        for name, cols, kind in self.parts:
            s, o = srcs[name], outs[name]
            if cols is not None:
                s, o = s.at[:, cols[0] : cols[1]], o.at[:, cols[0] : cols[1]]
            if kind == "z":
                for r0, nr, order in ((0, self.cut, "zyx"), (self.cut, RB - self.cut, "zxy")):
                    self.live.append(GatherZ(w, order, s, o, r0, nr, sems.pop(0), sems.pop(0), None))
            else:
                self.live.append(GatherX(w, "xyz", s, o, 0, 64, sems.pop(0), sems.pop(0), None))
        return step_all([p.rounds() for p in self.live])

    def arrive(self):
        for p in self.live:
            p.arrive()
        for c in self.locs:
            c.wait()

    def finish_sends(self):
        for p in self.live:
            p.finish_sends()

    def finish(self):
        self.arrive()
        self.finish_sends()


class VecSum:
    def __init__(self, w, src, out, st, rv, ss, rs):
        self.w, self.src, self.out, self.st, self.rv, self.ss, self.rs = w, src, out, st, rv, ss, rs

    def mk(self, src, k, dev, send):
        return pltpu.make_async_remote_copy(
            src_ref=src, dst_ref=self.rv.at[k], send_sem=self.ss.at[send], recv_sem=self.rs.at[k],
            device_id=dev, device_id_type=MESH)

    def rounds(self):
        w = self.w
        st, rv = self.st, self.rv
        even = w.z % 2 == 0
        odd = w.z % 2 == 1
        mid = jnp.logical_and(w.z > 0, w.z < 3)
        self.mk(self.src, 0, w.nx(), 0).start()
        yield
        yield
        self.mk(self.src, 0, w.nx(), 0).wait_recv()
        st[0] = self.src[...] + rv[0]
        self.mk(st.at[0], 1, w.ny(), 1).start()
        yield
        yield
        self.mk(self.src, 1, w.ny(), 1).wait_recv()
        st[1] = st[0] + rv[1]
        pl.when(even)(lambda: self.mk(st.at[1], 2, w.up(), 2).start())
        pl.when(odd)(lambda: self.mk(st.at[1], 2, w.dn(), 2).start())
        yield
        yield
        self.mk(self.src, 2, w.nx(), 2).wait_recv()
        st[2] = st[1] + rv[2]
        pl.when(w.z == 1)(lambda: self.mk(st.at[2], 3, w.up(), 3).start())
        pl.when(w.z == 2)(lambda: self.mk(st.at[2], 3, w.dn(), 3).start())
        yield
        yield

        @pl.when(mid)
        def _():
            self.mk(self.src, 3, w.nx(), 3).wait_recv()
            st[3] = st[2] + rv[3]
            self.out[...] = st[3]

        pl.when(w.z == 1)(lambda: self.mk(st.at[3], 4, w.dn(), 4).start())
        pl.when(w.z == 2)(lambda: self.mk(st.at[3], 4, w.up(), 4).start())
        yield
        yield

        @pl.when(jnp.logical_not(mid))
        def _():
            self.mk(self.src, 4, w.nx(), 4).wait_recv()
            self.out[...] = rv[4]

        yield
        yield

    def finish(self):
        w = self.w
        self.mk(self.src, 0, w.nx(), 0).wait_send()
        self.mk(self.src, 0, w.nx(), 1).wait_send()
        self.mk(self.src, 0, w.nx(), 2).wait_send()

        @pl.when(jnp.logical_and(w.z > 0, w.z < 3))
        def _():
            self.mk(self.src, 0, w.nx(), 3).wait_send()
            self.mk(self.src, 0, w.nx(), 4).wait_send()


class ScatterSet:
    def __init__(self, parts, names, widths, cut=32, vec=True):
        self.parts, self.names, self.widths, self.cut, self.vec = parts, names, widths, cut, vec

    def scratch(self):
        V = lambda *s: pltpu.VMEM(s, BF)
        sc = []
        for name, cols, kind in self.parts:
            C = self.widths[name] if cols is None else cols[1] - cols[0]
            if kind == "z":
                for nr in (self.cut, RB - self.cut):
                    sc += [DMA((ScatterZ.NS,)), DMA((ScatterZ.NR,)), DMA((8,))]
                    sc += [V(8, nr, C), V(8, nr, C), V(4, nr, C), V(5, nr, C)]
            else:
                sc += [DMA((ScatterX.NS,)), DMA((ScatterX.NR,)), DMA((16,))]
                sc += [V(16, 64, C), V(20, 64, C), V(2, 64, C), V(1, 64, C), V(3, 64, C)]
        if self.vec:
            sc += [pltpu.VMEM((4, 8, HP), F32), pltpu.VMEM((5, 8, HP), F32), DMA((5,)), DMA((5,))]
        return sc

    def start(self, w, srcs, outs, vec, vec_out, sc):
        sc = list(sc)
        self.live = []
        for name, cols, kind in self.parts:
            s, o = srcs[name], outs[name]
            if cols is not None:
                s, o = s.at[:, cols[0] : cols[1]], o.at[:, cols[0] : cols[1]]
            if kind == "z":
                for r0, nr, order in ((0, self.cut, "zyx"), (self.cut, RB - self.cut, "zxy")):
                    ss, rs, ls, own, rq, rp, ru = [sc.pop(0) for _ in range(7)]
                    self.live.append(ScatterZ(w, order, s, o, r0, nr, ss, rs, ls, own, (rq, rp, ru)))
            else:
                ss, rs, ls, own, ru, ry, rx, st = [sc.pop(0) for _ in range(8)]
                p = ScatterX(w, "xyz", s, o, 0, 64, ss, rs, ls, own, (ru, ry, rx))
                p.bufs_stage = st
                self.live.append(p)
        if self.vec:
            st, rv, ss, rs = sc
            self.live.append(VecSum(w, vec, vec_out, st, rv, ss, rs))
        return step_all([p.rounds() for p in self.live])

    def finish(self):
        for p in self.live:
            p.finish()


FF_CUT = 16
AT_G = GatherSet([("in", None, "z"), ("out", None, "x")], ["in", "out"])
FF_G = GatherSet([("gu", None, "z"), ("dn", (0, 512), "z"), ("dn", (512, 1408), "x")], ["gu", "dn"], FF_CUT)


def at_scatter():
    return ScatterSet([("in", None, "z"), ("out", None, "x")], ["in", "out"], {"in": 1536, "out": 512})


def gu_scatter():
    return ScatterSet([("gu", (0, 2176), "z"), ("gu", (2176, 2816), "x")], ["gu"], {"gu": 2816}, FF_CUT)


def dn_scatter():
    return ScatterSet([("dn", (0, 1024), "z"), ("dn", (1024, 1408), "x")], ["dn"], {"dn": 1408}, 32, False)


def rows16(n, fn, step=176):
    def body(i, _):
        fn(pl.ds(pl.multiple_of(i * step, 16), step))
        return 0

    lax.fori_loop(0, n // step, body, 0)


def unit_of(x, width):
    mean = jnp.sum(x, axis=-1, keepdims=True) / width
    c = x - mean
    inv = lax.rsqrt(jnp.sum(c * c, axis=-1, keepdims=True) / width + EPS)
    return c * inv, inv


def dot_nn(a, b):
    return jnp.dot(a, b, preferred_element_type=F32)


def dot_nt(a, b):
    return lax.dot_general(a, b, (((1,), (1,)), ((), ())), preferred_element_type=F32)


def dot_tn(a, b):
    return lax.dot_general(a, b, (((0,), (0,)), ((), ())), preferred_element_type=F32)


def tiles(n, size=256):
    return [(a, min(size, n - a)) for a in range(0, n, size)]


def fold8(x):
    return jnp.sum(x.reshape(x.shape[0] // 8, 8, x.shape[1]), axis=0)


def wide(x, n):
    return jnp.concatenate([x] * (-(-n // 128)), axis=1)[:, :n]


def two_cols(a, b):
    lane = lax.broadcasted_iota(jnp.int32, (a.shape[0], 128), 1)
    return jnp.where(lane == 0, a, jnp.where(lane == 1, b, 0.0))


def turn(x, cos, sin):
    lane = lax.broadcasted_iota(jnp.int32, x.shape, 1)
    other = jnp.where((lane // 16) % 2 == 0, pltpu.roll(x, 112, 1), pltpu.roll(x, 16, 1))
    return x * cos + other * sin


def head_lanes(x, t):
    lane = lax.broadcasted_iota(jnp.int32, x.shape, 1)
    return jnp.where(lane // 64 == t, x, jnp.zeros_like(x))


class Peer:
    def __init__(self, dev, ss, rs):
        self.dev, self.ss, self.rs, self.open = dev, ss, rs, []

    def mk(self, src, dst, k):
        return pltpu.make_async_remote_copy(
            src_ref=src, dst_ref=dst, send_sem=self.ss.at[k], recv_sem=self.rs.at[k], device_id=self.dev, device_id_type=MESH)

    def send(self, src, dst, k):
        c = self.mk(src, dst, k)
        c.start()
        self.open.append(c)

    def recv(self, dst, k):
        self.mk(dst, dst, k).wait_recv()

    def finish(self):
        for c in self.open:
            c.wait_send()
        self.open = []


def greet_all(w, links):
    bar = pltpu.get_barrier_semaphore()

    def sig(dev):
        pl.semaphore_signal(bar, inc=1, device_id=dev, device_id_type=MESH)

    sig((w.dp, w.x, 1 - w.c))
    n = jnp.int32(1)
    if links != "core":
        sig(w.nx())
        n = n + 1
    if links == "all":
        sig(w.ny())
        pl.when(w.z < 3)(lambda: sig(w.up()))
        pl.when(w.z > 0)(lambda: sig(w.dn()))
        n = n + 1 + (w.z < 3).astype(jnp.int32) + (w.z > 0).astype(jnp.int32)
    pl.semaphore_wait(bar, n)


class Bag:
    def launch(self):
        self.coming = {n: pltpu.make_async_copy(h, getattr(self, n), self.ld.at[i]) for i, (n, h) in enumerate(self.loads)}
        for n, c in self.coming.items():
            if n not in self.late:
                c.start()
        self.going = []

    def begin(self, *names):
        for n in names:
            self.coming[n].start()

    def need(self, *names):
        for n in names:
            if n in self.coming:
                self.coming.pop(n).wait()

    def put(self, name, cols=None):
        s, d = getattr(self, name), self.stores[name]
        if cols is not None:
            s, d = s.at[:, cols[0] : cols[1]], d.at[:, cols[0] : cols[1]]
        c = pltpu.make_async_copy(s, d, self.so.at[len(self.going)])
        c.start()
        self.going.append(c)

    def flush(self):
        self.need(*list(self.coming))
        for c in self.going:
            c.wait()


def run_kernel(body, name, cid, ins, outs, scratch, extra=()):
    iname, oname, sname = list(ins), list(outs), list(scratch)
    ld = [n for n in iname if ins[n][1] in (LD, LATE)]
    so = [n for n in oname if outs[n][2] == "ST"]
    moved = [pltpu.VMEM(ins[n][0].shape, ins[n][0].dtype) for n in ld] + [pltpu.VMEM(outs[n][0], outs[n][1]) for n in so]
    moved += [DMA((max(len(ld), 1),)), DMA((16,))]

    def kernel(*refs):
        b = Bag()
        ni, no, ns, nm = len(iname), len(oname), len(sname), len(moved)
        for n, r in zip(iname + oname + sname, refs):
            setattr(b, n, r)
        mv = refs[ni + no + ns : ni + no + ns + nm]
        b.loads = [(n, getattr(b, n)) for n in ld]
        b.late = [n for n in ld if ins[n][1] == LATE]
        b.stores = {n: getattr(b, n) for n in so}
        for n, r in zip(ld + so, mv):
            setattr(b, n, r)
        b.ld, b.so = mv[-2:]
        b.extra = refs[ni + no + ns + nm :]
        b.launch()
        body(b)
        b.flush()

    place = lambda s: pl.BlockSpec(memory_space=pl.ANY if s in (LD, ST, LATE) else s)
    res = pl.pallas_call(
        kernel,
        out_shape=[jax.ShapeDtypeStruct(outs[n][0], outs[n][1]) for n in oname],
        in_specs=[place(ins[n][1]) for n in iname],
        out_specs=[place(outs[n][2]) for n in oname],
        scratch_shapes=[scratch[n] for n in sname] + moved + list(extra),
        compiler_params=pltpu.CompilerParams(collective_id=cid, has_side_effects=True, vmem_limit_bytes=62 * 2**20),
        name=name,
    )(*[ins[n][0] for n in iname])
    return dict(zip(oname, res))


VM = pltpu.VMEM
ANY = pl.ANY
LD, ST, LATE = "LD", "ST", "LATE"


def gather_first(srcs, gset, fill, cid):
    names = gset.names
    R = fill.shape[1]

    def body(b):
        w = Where()
        greet(w)
        side = Peer(w.nx(), b.xs, b.xr)
        b.need("fill")
        side.send(b.fill, b.other, 0)
        g = gset.start(w, {n: getattr(b, "s_" + n) for n in names}, {n: getattr(b, "w_" + n) for n in names}, b.extra)
        for _ in g:
            pass
        side.recv(b.other, 0)
        b.both[0:R, :] = jnp.broadcast_to(b.fill[...].T[:, 0:1], (R, 128))
        b.both[R : 2 * R, :] = jnp.broadcast_to(b.other[...].T[:, 0:1], (R, 128))
        b.put("both")
        gset.finish()
        side.finish()

    ins = {"s_" + n: (srcs[n], ANY) for n in names}
    ins["fill"] = (fill, LD)
    outs = {"w_" + n: ((16 * RB, srcs[n].shape[1]), BF, ANY) for n in names}
    outs["both"] = ((2 * R, 128), F32, ST)
    return run_kernel(body, "gather", cid, ins, outs, dict(other=VM((8, R), F32), xs=DMA((1,)), xr=DMA((1,))), gset.scratch())


def attend_body(b, w, R, core, side):
    hp = b.h.shape[1]
    b.need("h", "vn")
    rows16(R, lambda s: norm_store(b.n, s, b.h[s], b.vn[0:1, :], b.vn[1:2, :]))
    b.need("w_in", "cos", "sin", "keep", "vh")
    D = 512
    for j in range(2):
        kt = dot_nn(b.n[...], b.w_in[:, D + 256 * j : D + 256 * j + 256])
        for hf in range(2):
            l = slice(256 * j + 128 * hf, 256 * j + 128 * hf + 128)
            b.k[0:R, l] = (turn(kt[:, 128 * hf : 128 * hf + 128], b.cos[...], b.sin[...]) * b.keep[...]).astype(BF)
        l = slice(256 * j, 256 * j + 256)
        side.send(b.k.at[pl.ds(0, R), l], b.k.at[pl.ds(R, R), l], 2 * j)
        vt = dot_nn(b.n[...], b.w_in[:, 2 * D + 256 * j : 2 * D + 256 * j + 256]) + b.vh[2:3, l]
        b.v[0:R, l] = vt.astype(BF)
        side.send(b.v.at[pl.ds(0, R), l], b.v.at[pl.ds(R, R), l], 2 * j + 1)
        yield
    for j in range(2):
        qt = dot_nn(b.n[...], b.w_in[:, 256 * j : 256 * j + 256]) + b.vh[1:2, 256 * j : 256 * j + 256]
        for hf in range(2):
            l = slice(256 * j + 128 * hf, 256 * j + 128 * hf + 128)
            b.q[:, l] = (turn(qt[:, 128 * hf : 128 * hf + 128], b.cos[...], b.sin[...]) * 0.125).astype(BF)
    b.put("q")
    b.need("fill")
    yield
    S = 176
    for p in range(4):
        l = slice(128 * p, 128 * p + 128)
        if p % 2 == 0:
            j = p // 2
            lj = slice(256 * j, 256 * j + 256)
            side.recv(b.k.at[pl.ds(R, R), lj], 2 * j)
            side.recv(b.v.at[pl.ds(R, R), lj], 2 * j + 1)
        kp = b.k[:, l]
        vT = b.v[:, l].T
        halves = []
        for t in range(2):
            b.s[...] = dot_nt(kp, head_lanes(b.q[:, l], t))

            def top(i, m):
                r = pl.ds(pl.multiple_of(i * S, 16), S)
                x = b.s[r] + wide(b.fill[r], R)
                return jnp.maximum(m, jnp.max(x.reshape(S // 8, 8, R), axis=0))

            m = lax.fori_loop(0, 2 * R // S, top, jnp.full((8, R), -3.0e38, F32))
            m = jnp.max(m, axis=0, keepdims=True)

            def expo(i, acc):
                r = pl.ds(pl.multiple_of(i * S, 16), S)
                x = jnp.exp(b.s[r] + wide(b.fill[r], R) - m)
                b.p[r] = x.astype(BF)
                return acc + jnp.sum(x.reshape(S // 8, 8, R), axis=0)

            tot = lax.fori_loop(0, 2 * R // S, expo, jnp.zeros((8, R), F32))
            tot = jnp.sum(tot, axis=0, keepdims=True)
            halves.append(dot_nn(vT[64 * t : 64 * t + 64], b.p[...]) / tot)
            b.lse[2 * p + t : 2 * p + t + 1, :] = m + jnp.log(tot)
            yield
        b.o[:, l] = jnp.concatenate(halves, axis=0).T
    for n in ("k", "v", "lse", "o"):
        b.put(n)
    b.need("w_out")

    def stats(s):
        x = b.o[s]
        b.stat[s] = two_cols(jnp.sum(x, axis=-1, keepdims=True), jnp.sum(x * x, axis=-1, keepdims=True))

    rows16(R, stats)
    core.send(b.stat, b.rstat, 0)
    core.recv(b.rstat, 0)

    def unit(s):
        t = b.stat[s] + b.rstat[s]
        mean = t[:, 0:1] / hp
        inv = lax.rsqrt(t[:, 1:2] / hp - mean * mean + EPS)
        b.st[s] = two_cols(mean, inv)
        b.u[s] = ((b.o[s] - mean) * inv * b.vh[0:1, :] + b.vh[3:4, :]).astype(BF)

    rows16(R, unit)
    b.put("st")
    yield
    for d in range(4):
        l = slice(256 * d, 256 * d + 256)
        b.part[:, l] = dot_nt(b.u[...], b.w_out[256 * d : 256 * d + 256, :]).astype(BF)
        core.send(b.part.at[:, l], b.rpart.at[:, l], 1 + d)
        if d % 2 == 1:
            yield
    for d in range(4):
        l = slice(256 * d, 256 * d + 256)
        core.recv(b.rpart.at[:, l], 1 + d)

    def close(s):
        x = b.part[s].astype(F32) + b.rpart[s].astype(F32) + b.vn[4:5, :]
        b.hm[s] = b.h[s] + wide(b.keep[s], x.shape[1]) * x

    rows16(R, close)
    b.put("hm")
    yield


def norm_store(dst, s, x, gain, bias):
    dst[s] = (unit_of(x, x.shape[1])[0] * gain + bias).astype(BF)


def hidden_body(b, w, R, core, fetch):
    rows16(R, lambda s: norm_store(b.n, s, b.hm[s], b.vn[2:3, :], b.vn[3:4, :]))
    loads = fetch()
    b.need("vf")
    loads[0].wait()
    yield
    for i, (a, n) in enumerate(tiles(HP)):
        b.gate[:, a : a + n] = dot_nn(b.n[...], b.w_gu[:, a : a + n]) + b.vf[1:2, a : a + n]
        b.up[:, a : a + n] = dot_nn(b.n[...], b.w_gu[:, HP + a : HP + a + n]) + b.vf[2:3, a : a + n]
        if i % 2 == 1:
            yield

    b.put("gate")
    b.put("up")

    def stats(s):
        g = b.gate[s]
        z = g * jax.nn.sigmoid(g) * b.up[s]
        b.z[s] = z
        b.stat[s] = two_cols(jnp.sum(z, axis=-1, keepdims=True), jnp.sum(z * z, axis=-1, keepdims=True))

    rows16(R, stats)
    core.send(b.stat, b.rstat, 0)
    core.recv(b.rstat, 0)
    yield

    def unit(s):
        t = b.stat[s] + b.rstat[s]
        mean = t[:, 0:1] / FF
        inv = lax.rsqrt(t[:, 1:2] / FF - mean * mean + EPS)
        b.zst[s] = two_cols(mean, inv)
        b.zn[s] = ((b.z[s] - mean) * inv * b.vf[0:1, :] + b.vf[3:4, :]).astype(BF)

    rows16(R, unit)
    b.put("zst")
    loads[1].wait()
    yield
    for d in range(4):
        l = slice(256 * d, 256 * d + 256)
        b.part[:, l] = dot_nt(b.zn[...], b.w_dn[256 * d : 256 * d + 256, :]).astype(BF)
        core.send(b.part.at[:, l], b.rpart.at[:, l], 1 + d)
        if d % 2 == 1:
            yield
    for d in range(4):
        l = slice(256 * d, 256 * d + 256)
        core.recv(b.rpart.at[:, l], 1 + d)

    def close(s):
        x = b.part[s].astype(F32) + b.rpart[s].astype(F32) + b.vn[5:6, :]
        b.ho[s] = b.hm[s] + wide(b.keep[s], x.shape[1]) * x

    rows16(R, close)
    b.put("ho")
    yield


def forward_layer(h, tabs, wts, vn, vh, vf, srcs, nxt, cid):
    R, D = h.shape
    fset = FF_G
    aset = AT_G if nxt else None

    def body(b):
        w = Where()
        greet_all(w, "all")
        ends = lambda g: ({n: getattr(b, "s_" + n) for n in g.names}, {n: getattr(b, "g_" + n) for n in g.names})
        ffc = fset.start(w, *ends(fset), b.extra[:split])
        core = Peer((w.dp, w.x, 1 - w.c), b.cs, b.cr)
        side = Peer(w.nx(), b.xs, b.xr)
        n = len(fset.live)
        for _ in range(n):
            next(ffc)

        def comm_all():
            yield from ffc
            if aset:
                yield from aset.start(w, *ends(aset), b.extra[split:])

        comm = comm_all()

        def fetch():
            for _ in ffc:
                pass
            if aset:
                for _ in range(3):
                    next(comm)
            fset.arrive()
            loads = [pltpu.make_async_copy(b.g_gu, b.w_gu, b.ls.at[0]), pltpu.make_async_copy(b.g_dn, b.w_dn, b.ls.at[1])]
            for c in loads:
                c.start()
            return loads

        def comp():
            yield from attend_body(b, w, R, core, side)
            core.finish()
            yield from hidden_body(b, w, R, core, fetch)

        drive(comp(), comm, [0, 0, n, 0, n, 0, n], 2)
        fset.finish_sends()
        if aset:
            aset.finish()
        core.finish()
        side.finish()

    ins = dict(h=(h, LD), keep=(tabs["keep"], LD), fill=(tabs["fill"], LD), cos=(tabs["cos"], LD), sin=(tabs["sin"], LD),
        w_in=(wts["in"], LD), w_out=(wts["out"], LD), vn=(vn, LD), vh=(vh, LD), vf=(vf, LD))
    outs = dict(hm=((R, D), F32, ST), q=((R, 512), BF, ST), k=((2 * R, 512), BF, ST), v=((2 * R, 512), BF, ST),
        lse=((8, R), F32, ST), o=((R, 512), F32, ST), st=((R, 128), F32, ST), ho=((R, D), F32, ST),
        gate=((R, HP), F32, ST), up=((R, HP), F32, ST), zst=((R, 128), F32, ST))
    extra = fset.scratch()
    split = len(extra)
    for g, src in ((fset, srcs), (aset, nxt)):
        if g:
            ins.update({"s_" + n: (src[n], ANY) for n in g.names})
            outs.update({"g_" + n: ((16 * RB, src[n].shape[1]), BF, ANY) for n in g.names})
    if aset:
        extra = extra + aset.scratch()
    B = lambda *s: pltpu.VMEM(s, BF)
    F = lambda *s: pltpu.VMEM(s, F32)
    scratch = dict(n=B(R, D), s=F(2 * R, R), p=B(2 * R, R), u=B(R, 512), part=B(R, D), rpart=B(R, D), stat=F(R, 128),
        rstat=F(R, 128), z=F(R, HP), zn=B(R, HP), w_gu=B(D, 2 * HP), w_dn=B(D, HP), cs=DMA((5,)), cr=DMA((5,)),
        xs=DMA((4,)), xr=DMA((4,)), ls=DMA((2,)))
    return run_kernel(body, "layer", cid, ins, outs, scratch, extra)


def add8(acc, x):
    acc[...] = acc[...] + fold8(x)


def put_vec(b, row, acc, n):
    b.vec[row : row + 1, 0:n] = jnp.sum(acc[...], axis=0, keepdims=True)


def close_back(b, s, x, gain, acc_gain, acc_shift):
    e = b.part[s].astype(F32) + b.rpart[s].astype(F32)
    unit, inv = unit_of(x, x.shape[1])
    add8(acc_gain, e * unit)
    add8(acc_shift, e)
    wt = e * gain
    n = x.shape[1]
    m1 = jnp.sum(wt, axis=-1, keepdims=True) / n
    m2 = jnp.sum(wt * unit, axis=-1, keepdims=True) / n
    b.go[s] = b.g[s] + inv * (wt - m1 - unit * m2)


def hidden_back_body(b, w, R, core):
    D = b.g.shape[1]
    for a in (b.a0, b.a1, b.a2, b.a3, b.a4, b.a5, b.a6, b.vec):
        a[...] = jnp.zeros_like(a)
    b.need("g", "keep")

    def unit4(s):
        g = b.gate[s]
        sg = jax.nn.sigmoid(g)
        return (g * sg * b.up[s] - b.st[s, 0:1]) * b.st[s, 1:2], g, sg

    def first(s):
        e = wide(b.keep[s], D) * b.g[s]
        b.el[s] = e.astype(BF)
        add8(b.a2, e)

    def norms(s):
        norm_store(b.n, s, b.go[s], b.vn[2:3, :], b.vn[3:4, :])
        b.zn[s] = (unit4(s)[0] * b.vf[0:1, :] + b.vf[3:4, :]).astype(BF)

    rows16(R, first)
    b.need("gate", "up", "st", "vn", "vf")
    rows16(R, norms)
    b.need("w_dn")
    b.begin("w_gu")
    yield
    for i, (a, n) in enumerate(tiles(HP)):
        b.ez[:, a : a + n] = dot_nn(b.el[...], b.w_dn[:, a : a + n])
        if i % 3 == 2:
            yield

    def second(s):
        u = unit4(s)[0]
        e = b.ez[s]
        wt = e * b.vf[0:1, :]
        add8(b.a3, e * u)
        add8(b.a6, e)
        b.stat[s] = two_cols(jnp.sum(wt, axis=-1, keepdims=True), jnp.sum(wt * u, axis=-1, keepdims=True))

    rows16(R, second)
    core.send(b.stat, b.rstat, 0)
    b.xT[...] = b.el[...].T
    yield
    for i, (a, n) in enumerate(tiles(HP)):
        b.d_dn[:, a : a + n] = dot_nn(b.xT[...], b.zn[:, a : a + n]).astype(BF)
        if i % 3 == 2:
            yield
    core.recv(b.rstat, 0)

    def third(s):
        u, g, sg = unit4(s)
        t = (b.stat[s] + b.rstat[s]) / FF
        ez = b.st[s, 1:2] * (b.ez[s] * b.vf[0:1, :] - t[:, 0:1] - u * t[:, 1:2])
        eg = ez * b.up[s] * sg * (1.0 + g * (1.0 - sg))
        eu = ez * g * sg
        add8(b.a4, eg)
        add8(b.a5, eu)
        b.egu[s, 0:HP] = eg.astype(BF)
        b.egu[s, HP : 2 * HP] = eu.astype(BF)

    rows16(R, third, 48)
    b.need("w_gu")
    yield
    for d in range(4):
        l = slice(256 * d, 256 * d + 256)
        b.part[:, l] = dot_nt(b.egu[...], b.w_gu[256 * d : 256 * d + 256, :]).astype(BF)
        core.send(b.part.at[:, l], b.rpart.at[:, l], 1 + d)
        yield
    b.xT[...] = b.n[...].T
    for i, (a, n) in enumerate(tiles(2 * HP)):
        b.d_gu[:, a : a + n] = dot_nn(b.xT[...], b.egu[:, a : a + n]).astype(BF)
        if i % 3 == 2 or i == len(tiles(2 * HP)) - 1:
            b.put("d_gu", (a - a % 768, a + n))
            yield
    for d in range(4):
        l = slice(256 * d, 256 * d + 256)
        core.recv(b.rpart.at[:, l], 1 + d)
    rows16(R, lambda s: close_back(b, s, b.go[s], b.vn[2:3, :], b.a0, b.a1))
    b.put("go")
    for row, acc, n in ((0, b.a0, D), (1, b.a1, D), (2, b.a2, D), (3, b.a3, HP), (4, b.a4, HP), (5, b.a5, HP), (6, b.a6, HP)):
        put_vec(b, row, acc, n)
    yield


def attend_back_body(b, w, R, core, side):
    D = b.g.shape[1]
    hp = D
    for a in (b.a0, b.a1, b.a2, b.a3, b.a4, b.a5, b.a6, b.vec):
        a[...] = jnp.zeros_like(a)
    b.need("g", "keep", "o", "st", "vn", "vh")

    def first(s):
        e = wide(b.keep[s], D) * b.g[s]
        b.el[s] = e.astype(BF)
        add8(b.a2, e)
        norm_store(b.n, s, b.go[s], b.vn[0:1, :], b.vn[1:2, :])
        u = (b.o[s] - b.st[s, 0:1]) * b.st[s, 1:2]
        b.u[s] = (u * b.vh[0:1, :] + b.vh[3:4, :]).astype(BF)

    rows16(R, first)
    b.need("w_out")
    b.begin("q", "k", "v", "lse", "fill", "cos", "sin", "w_in")
    yield
    for a, n in tiles(512):
        b.dq[:, a : a + n] = dot_nn(b.el[...], b.w_out[:, a : a + n])

    def second(s):
        u = (b.o[s] - b.st[s, 0:1]) * b.st[s, 1:2]
        e = b.dq[s]
        wt = e * b.vh[0:1, :]
        add8(b.a3, e * u)
        add8(b.a6, e)
        b.stat[s] = two_cols(jnp.sum(wt, axis=-1, keepdims=True), jnp.sum(wt * u, axis=-1, keepdims=True))

    rows16(R, second)
    core.send(b.stat, b.rstat, 0)
    b.xT[...] = b.el[...].T
    yield
    for a, n in tiles(512):
        b.d_out[:, a : a + n] = dot_nn(b.xT[...], b.u[:, a : a + n]).astype(BF)
    b.put("d_out")
    yield
    core.recv(b.rstat, 0)

    def third(s):
        u = (b.o[s] - b.st[s, 0:1]) * b.st[s, 1:2]
        t = (b.stat[s] + b.rstat[s]) / hp
        b.eo[s] = (b.st[s, 1:2] * (b.dq[s] * b.vh[0:1, :] - t[:, 0:1] - u * t[:, 1:2])).astype(BF)

    rows16(R, third, 48)
    b.need("q", "k", "v", "lse", "fill")
    yield
    S = 176
    for p in range(4):
        l = slice(128 * p, 128 * p + 128)
        kp = b.k[:, l]
        vp = b.v[:, l]
        kT = kp.T
        dk, dv, dqs = None, None, []
        for t in range(2):
            qt = head_lanes(b.q[:, l], t)
            ot = head_lanes(b.eo[:, l], t)
            b.s[...] = dot_nt(kp, qt)
            b.dp[...] = dot_nt(vp, ot)
            lse = b.lse[2 * p + t : 2 * p + t + 1, :]

            def expo(i, acc):
                r = pl.ds(pl.multiple_of(i * S, 16), S)
                x = jnp.exp(b.s[r] + wide(b.fill[r], R) - lse)
                b.s[r] = x
                b.p[r] = x.astype(BF)
                return acc + jnp.sum((x * b.dp[r]).reshape(S // 8, 8, R), axis=0)

            tot = lax.fori_loop(0, 2 * R // S, expo, jnp.zeros((8, R), F32))
            tot = jnp.sum(tot, axis=0, keepdims=True)

            def grad(i, _):
                r = pl.ds(pl.multiple_of(i * S, 16), S)
                b.ds[r] = (b.s[r] * (b.dp[r] - tot)).astype(BF)
                return 0

            lax.fori_loop(0, 2 * R // S, grad, 0)
            yield
            v1 = dot_nn(b.p[...], ot)
            k1 = dot_nn(b.ds[...], qt)
            dqs.append(dot_nn(kT[64 * t : 64 * t + 64], b.ds[...]))
            dv = v1 if t == 0 else dv + v1
            dk = k1 if t == 0 else dk + k1
            yield
        dk = jnp.where(b.fill[:, 0:1] == 0.0, dk, 0.0)
        b.dq[:, l] = jnp.concatenate(dqs, axis=0).T * 0.125
        b.dk[:, l] = dk[:R]
        b.dv[:, l] = dv[:R]
        l2 = slice(512 + 128 * p, 640 + 128 * p)
        b.ep[:, l] = dk[R:].astype(BF)
        b.ep[:, l2] = dv[R:].astype(BF)
        side.send(b.ep.at[:, l], b.rk.at[:, l], 2 * p)
        side.send(b.ep.at[:, l2], b.rv.at[:, l], 2 * p + 1)
    b.need("cos", "sin", "w_in")
    yield
    side.finish()
    for p in range(4):
        l = slice(128 * p, 128 * p + 128)
        side.recv(b.rk.at[:, l], 2 * p)
        side.recv(b.rv.at[:, l], 2 * p + 1)

        def last(s):
            cos, sin = b.cos[s], -b.sin[s]
            eq = turn(b.dq[s, l], cos, sin)
            ek = turn(b.dk[s, l] + b.rk[s, l].astype(F32), cos, sin)
            ev = b.dv[s, l] + b.rv[s, l].astype(F32)
            b.a4[:, l] = b.a4[:, l] + fold8(eq)
            b.a5[:, l] = b.a5[:, l] + fold8(ev)
            b.ep[s, l] = eq.astype(BF)
            b.ep[s, 512 + 128 * p : 640 + 128 * p] = ek.astype(BF)
            b.ep[s, 1024 + 128 * p : 1152 + 128 * p] = ev.astype(BF)

        rows16(R, last)
    yield
    for d in range(4):
        l = slice(256 * d, 256 * d + 256)
        b.part[:, l] = dot_nt(b.ep[...], b.w_in[256 * d : 256 * d + 256, :]).astype(BF)
        core.send(b.part.at[:, l], b.rpart.at[:, l], 1 + d)
        if d % 2 == 1:
            yield
    b.xT[...] = b.n[...].T
    for i, (a, n) in enumerate(tiles(1536)):
        b.d_in[:, a : a + n] = dot_nn(b.xT[...], b.ep[:, a : a + n]).astype(BF)
        if i % 3 == 2:
            b.put("d_in", (a - a % 768, a + n))
            yield
    for d in range(4):
        l = slice(256 * d, 256 * d + 256)
        core.recv(b.rpart.at[:, l], 1 + d)
    rows16(R, lambda s: close_back(b, s, b.go[s], b.vn[0:1, :], b.a0, b.a1))
    b.put("go")
    for row, acc, n in ((0, b.a0, D), (1, b.a1, D), (2, b.a2, D), (3, b.a3, 512), (4, b.a4, 512), (5, b.a5, 512), (6, b.a6, 512)):
        put_vec(b, row, acc, n)
    yield


def scatter_args(sset, grads, vec):
    ins = {"s_" + n: (grads[n], ANY) for n in sset.names}
    ins["s_vec"] = (vec, VM)
    outs = {"r_" + n: ((RB, grads[n].shape[1]), F32, VM) for n in sset.names}
    outs["r_vec"] = ((8, HP), F32, VM)
    return ins, outs


def scatter_start(sset, w, b, sc=None):
    n = sset.names
    return sset.start(w, {i: getattr(b, "s_" + i) for i in n}, {i: getattr(b, "r_" + i) for i in n}, b.s_vec, b.r_vec, b.extra if sc is None else sc)


HB_RATE = 2


def backward_hidden(g, fw, hm, tabs, wts, vn, vf, sset, grads, vec, cid):
    R, D = g.shape

    def body(b):
        w = Where()
        greet_all(w, "all")
        core = Peer((w.dp, w.x, 1 - w.c), b.cs, b.cr)
        load = pltpu.make_async_copy(b.hm, b.go, b.ls.at[0])
        load.start()
        comp = hidden_back_body(b, w, R, core)
        if sset:
            comm = scatter_start(sset, w, b, b.extra[:split])
            for _ in sset.live:
                next(comm)
        load.wait()

        def both():
            for _ in range(5):
                if sset:
                    for _ in range(3):
                        next(comm, None)
                yield
            mine = dset.start(w, {"dn": b.d_dn}, {"dn": b.r_dn}, None, None, b.extra[split:])
            for _ in dset.live:
                next(mine)
            yield
            yield from step_all([mine, comm] if sset else [mine])

        drive(comp, both(), [1] * 6, HB_RATE * (2 if sset else 1))
        if sset:
            sset.finish()
        dset.finish()
        core.finish()

    ins = dict(g=(g, LD), keep=(tabs["keep"], LD), hm=(hm, ANY), gate=(fw["gate"], LD), up=(fw["up"], LD),
        st=(fw["zst"], LD), w_gu=(wts["gu"], LATE), w_dn=(wts["dn"], LD), vn=(vn, LD), vf=(vf, LD))
    outs = dict(go=((R, D), F32, ST), d_gu=((D, 2 * HP), BF, ST), r_dn=((RB, HP), F32, VM), vec=((8, HP), F32, VM))
    extra = ()
    dset = dn_scatter()
    if sset:
        i2, o2 = scatter_args(sset, grads, vec)
        ins.update(i2)
        outs.update(o2)
        extra = sset.scratch()
    split = len(extra)
    extra = list(extra) + dset.scratch()
    acc = lambda n: pltpu.VMEM((8, n), F32)
    scratch = dict(d_dn=pltpu.VMEM((D, HP), BF), el=pltpu.VMEM((R, D), BF), xT=pltpu.VMEM((D, R), BF), n=pltpu.VMEM((R, D), BF),
        ez=pltpu.VMEM((R, HP), F32), zn=pltpu.VMEM((R, HP), BF), egu=pltpu.VMEM((R, 2 * HP), BF),
        part=pltpu.VMEM((R, D), BF), rpart=pltpu.VMEM((R, D), BF), stat=pltpu.VMEM((R, 128), F32),
        rstat=pltpu.VMEM((R, 128), F32), cs=DMA((5,)), cr=DMA((5,)), ls=DMA((1,)), a0=acc(D), a1=acc(D), a2=acc(D),
        a3=acc(HP), a4=acc(HP), a5=acc(HP), a6=acc(HP))
    return run_kernel(body, "hidden_back", cid, ins, outs, scratch, extra)


def backward_attend(g, fw, h, tabs, wts, vn, vh, sset, grads, vec, cid):
    R, D = g.shape

    def body(b):
        w = Where()
        greet_all(w, "all")
        core = Peer((w.dp, w.x, 1 - w.c), b.cs, b.cr)
        side = Peer(w.nx(), b.xs, b.xr)
        load = pltpu.make_async_copy(b.h, b.go, b.ls.at[0])
        load.start()
        comm = scatter_start(sset, w, b)
        for _ in sset.live:
            next(comm)
        load.wait()
        drive(attend_back_body(b, w, R, core, side), comm, [1] * 4 + [1, 2] * 8, 2)
        sset.finish()
        core.finish()

    ins = dict(g=(g, LD), keep=(tabs["keep"], LD), h=(h, ANY), fill=(tabs["fill"], LATE), cos=(tabs["cos"], LATE),
        sin=(tabs["sin"], LATE), o=(fw["o"], LD), st=(fw["st"], LD), q=(fw["q"], LATE), k=(fw["k"], LATE),
        v=(fw["v"], LATE), lse=(fw["lse"], LATE), w_in=(wts["in"], LATE), w_out=(wts["out"], LD), vn=(vn, LD),
        vh=(vh, LD))
    outs = dict(go=((R, D), F32, ST), d_in=((D, 1536), BF, ST), d_out=((D, 512), BF, ST), vec=((8, HP), F32, VM))
    i2, o2 = scatter_args(sset, grads, vec)
    ins.update(i2)
    outs.update(o2)
    acc = lambda n: pltpu.VMEM((8, n), F32)
    B = lambda *s: pltpu.VMEM(s, BF)
    F = lambda *s: pltpu.VMEM(s, F32)
    scratch = dict(el=B(R, D), xT=B(D, R), n=B(R, D), u=B(R, 512), eo=B(R, 512), s=F(2 * R, R), dp=F(2 * R, R), p=B(2 * R, R),
        ds=B(2 * R, R), dq=F(R, 512), dk=F(R, 512), dv=F(R, 512), rk=B(R, 512), rv=B(R, 512), ep=B(R, 1536),
        part=B(R, D), rpart=B(R, D), stat=F(R, 128), rstat=F(R, 128), cs=DMA((5,)), cr=DMA((5,)), ls=DMA((1,)),
        xs=DMA((8,)), xr=DMA((8,)), a0=acc(D), a1=acc(D), a2=acc(D), a3=acc(512), a4=acc(512), a5=acc(512),
        a6=acc(512))
    return run_kernel(body, "attend_back", cid, ins, outs, scratch, sset.scratch())


def scatter_last(sset, grads, vec, cid):
    def body(b):
        w = Where()
        greet(w)
        for _ in scatter_start(sset, w, b):
            pass
        sset.finish()

    ins, outs = scatter_args(sset, grads, vec)
    return run_kernel(body, "scatter", cid, ins, outs, {}, sset.scratch())


HP = 1408


def fast_device(
    tokens_in,
    cotangent,
    key_mask,
    grid_pos,
    class_index,
    input_weight,
    output_weight,
    gate_up_weight,
    down_weight,
    norm_gains,
    norm_biases,
    head_gains,
    head_biases,
    hidden_gains,
    hidden_biases,
):
    _, rows, width = tokens_in.shape
    dim = head_gains.shape[1]
    hidden = hidden_gains.shape[1]
    layers = input_weight.shape[0]
    pad = HP - hidden
    R = -(-rows // 16) * 16
    more = R - rows
    places = lax.axis_index("ctx") * rows + jnp.arange(rows, dtype=jnp.int32)
    not_class = (places != class_index[0]).astype(F32)
    cosine, sine = rotary_tables(grid_pos.reshape(2, rows), not_class)
    c0, c1, s0, s1 = cosine[:, 0], cosine[:, 1], sine[:, 0], sine[:, 1]
    low = lambda a: jnp.pad(a, ((0, more), (0, 0)))
    keep = low(key_mask.astype(F32).reshape(rows, 1))
    real = jnp.pad(key_mask.astype(F32).reshape(1, rows), ((0, 0), (0, more)))
    fill = jnp.where(jnp.arange(R)[None] < rows, (real - 1.0) * 10000.0, -1.0e30)
    fill = jnp.broadcast_to(fill, (8, R))
    tabs = dict(keep=jnp.broadcast_to(keep, (R, 128)), cos=low(jnp.concatenate([c0, c0, c1, c1] * 2, axis=1)),
        sin=low(jnp.concatenate([-s0, s0, -s1, s1] * 2, axis=1)))
    gn = norm_gains.astype(F32)
    bn = norm_biases.astype(F32)
    gh = head_gains.astype(F32)[:, None]
    bh = head_biases.astype(F32)
    vh = jnp.pad(jnp.concatenate([gh, bh], axis=1), ((0, 0), (0, 4), (0, 0)))
    vn = jnp.stack([gn[:, 0], bn[:, 0], gn[:, 1], bn[:, 1], bn[:, 2], bn[:, 3]], axis=1)
    vn = jnp.pad(vn, ((0, 0), (0, 2), (0, 0)))
    vf = jnp.concatenate([hidden_gains.astype(F32)[:, None], hidden_biases.astype(F32)], axis=1)
    vf = jnp.pad(vf, ((0, 0), (0, 4), (0, pad)))
    gu = jnp.pad(gate_up_weight, ((0, 0), (0, 0), (0, 0), (0, pad)))
    dn = jnp.pad(down_weight, ((0, 0), (0, 0), (0, pad)))
    at_src = [{"in": input_weight[l].reshape(RB, 3 * dim), "out": output_weight[l]} for l in range(layers)]
    ff_src = [{"gu": gu[l].reshape(RB, 2 * HP), "dn": dn[l]} for l in range(layers)]
    grab = lambda d, names: {n: d["g_" + n] for n in names}
    h = low(tokens_in.astype(F32).reshape(rows, width)) * keep
    first = gather_first(at_src[0], AT_G, fill, 0)
    tabs["fill"] = first["both"]
    at_w = {0: {n: first["w_" + n] for n in AT_G.names}}
    ff_w, hs, fw = {}, {}, {}
    for l in range(layers):
        hs[l] = h
        nxt = l + 1 < layers
        r = forward_layer(h, tabs, at_w[l], vn[l], vh[l], vf[l], ff_src[l], at_src[l + 1] if nxt else None, 1 + l)
        fw[l], h = r, r["ho"]
        ff_w[l] = grab(r, FF_G.names)
        if nxt:
            at_w[l + 1] = grab(r, AT_G.names)
    activations = h[:rows].astype(BF).reshape(1, rows, width)
    g = low(cotangent.astype(F32).reshape(rows, width))
    got = {}
    grads, vec, cid = None, None, layers + 1
    for l in reversed(range(layers)):
        sset = at_scatter() if grads else None
        r = backward_hidden(g, fw[l], fw[l]["hm"], tabs, ff_w[l], vn[l], vf[l], sset, grads, vec, cid)
        if grads:
            got["at", l + 1] = r
        g, vec, grads, got["dn", l] = r["go"], r["vec"], {"gu": r["d_gu"]}, r["r_dn"]
        r = backward_attend(g, fw[l], hs[l], tabs, at_w[l], vn[l], vh[l], gu_scatter(), grads, vec, cid + 1)
        got["ff", l] = r
        g, vec, grads = r["go"], r["vec"], {"in": r["d_in"], "out": r["d_out"]}
        cid += 2
    got["at", 0] = scatter_last(at_scatter(), grads, vec, cid)
    input_grad = (keep * g)[:rows].reshape(1, rows, width)
    L = range(layers)
    va = jnp.stack([got["at", l]["r_vec"] for l in L])
    vff = jnp.stack([got["ff", l]["r_vec"] for l in L])
    return (
        activations,
        input_grad,
        jnp.stack([got["at", l]["r_in"].reshape(RB, 3, dim) for l in L]),
        jnp.stack([got["at", l]["r_out"] for l in L]),
        jnp.stack([got["ff", l]["r_gu"].reshape(RB, 2, HP)[:, :, :hidden] for l in L]),
        jnp.stack([got["dn", l][:, :hidden] for l in L]),
        jnp.stack([va[:, 0, :width], vff[:, 0, :width]], axis=1),
        jnp.stack([va[:, 1, :width], vff[:, 1, :width], va[:, 2, :width], vff[:, 2, :width]], axis=1),
        va[:, 3, :dim],
        va[:, 4:7, :dim],
        vff[:, 3, :hidden],
        vff[:, 4:7, :hidden],
    )


def solution(mesh):
    sizes = dict(mesh.shape)
    fits = sizes == dict(dp=8, ctx=2, tp=2)
    return jax.shard_map(
        fast_device if fits else on_device,
        mesh=mesh,
        in_specs=(
            P("dp", "ctx", None),
            P("dp", "ctx", None),
            P("dp", "ctx"),
            P(None, "dp", "ctx"),
            P("dp"),
            P(None, ("dp", "ctx"), None, "tp"),
            P(None, ("dp", "ctx"), "tp"),
            P(None, ("dp", "ctx"), None, "tp"),
            P(None, ("dp", "ctx"), "tp"),
            P(),
            P(),
            P(None, "tp"),
            P(None, None, "tp"),
            P(None, "tp"),
            P(None, None, "tp"),
        ),
        out_specs=(
            P("dp", "ctx", None),
            P("dp", "ctx", None),
            P(None, ("dp", "ctx"), None, "tp"),
            P(None, ("dp", "ctx"), "tp"),
            P(None, ("dp", "ctx"), None, "tp"),
            P(None, ("dp", "ctx"), "tp"),
            P(),
            P(),
            P(None, "tp"),
            P(None, None, "tp"),
            P(None, "tp"),
            P(None, None, "tp"),
        ),
        check_vma=False,
    )
```

```python
import functools

import jax
import jax.numpy as jnp
from jax import lax
from jax.experimental import pallas as pl
from jax.experimental.pallas import tpu as pltpu
from jax.sharding import PartitionSpec as P

FF = 2730
HEAD_DIM = 64


norm_epsilon = 1e-06
rotary_base = 10000.0
masked_score = -10000.0


def rotary_tables(positions, not_class):
    quarter = HEAD_DIM // 4
    frequency = rotary_base ** (-jnp.arange(quarter, dtype=jnp.float32) / quarter)
    angles = (
        jnp.transpose(positions).astype(jnp.float32)[:, :, None]
        * frequency
        * not_class[:, None, None]
    )
    return (jnp.cos(angles), jnp.sin(angles))


def rotate(values, cosine, sine, direction):
    row_count, head_count, head_dim = values.shape
    paired = values.reshape(row_count, head_count, 2, 2, head_dim // 4)
    first_half = paired[:, :, :, 0]
    second_half = paired[:, :, :, 1]
    cos_rows = cosine[:, None]
    sin_rows = sine[:, None] * direction
    turned = jnp.stack(
        [
            first_half * cos_rows - second_half * sin_rows,
            second_half * cos_rows + first_half * sin_rows,
        ],
        axis=3,
    )
    return turned.reshape(row_count, head_count, head_dim)


def local_norm(values, gain_vec, shift_vec):
    center = values - jnp.mean(values, axis=-1, keepdims=True)
    spread = jnp.mean(center * center, axis=-1, keepdims=True)
    inv_spread = lax.rsqrt(spread + norm_epsilon)
    unit_rows = center * inv_spread
    return (unit_rows * gain_vec + shift_vec, unit_rows, inv_spread)


def local_norm_back(upstream, unit_rows, inv_spread, gain_vec):
    weighted = upstream * gain_vec
    return inv_spread * (
        weighted
        - jnp.mean(weighted, axis=-1, keepdims=True)
        - unit_rows * jnp.mean(weighted * unit_rows, axis=-1, keepdims=True)
    )


def row_totals(first_part, second_part):
    return lax.psum(
        (jnp.sum(first_part, axis=-1, keepdims=True), jnp.sum(second_part, axis=-1, keepdims=True)),
        "tp",
    )


def split_norm(values, gain_vec, shift_vec, full_width):
    sum_first, sum_second = row_totals(values, values * values)
    row_mean = sum_first / full_width
    inv_spread = lax.rsqrt(sum_second / full_width - row_mean * row_mean + norm_epsilon)
    unit_rows = (values - row_mean) * inv_spread
    return (unit_rows * gain_vec + shift_vec, unit_rows, inv_spread)


def split_norm_back(upstream, unit_rows, inv_spread, gain_vec, full_width):
    weighted = upstream * gain_vec
    sum_first, sum_second = row_totals(weighted, weighted * unit_rows)
    return inv_spread * (weighted - sum_first / full_width - unit_rows * (sum_second / full_width))


def tensor_sum(partial_value):
    return lax.psum(partial_value.astype(jnp.bfloat16), "tp").astype(jnp.float32)


def tensor_back(partial_value):
    return lax.psum(partial_value.astype(jnp.bfloat16), "tp").astype(jnp.float32)


def fetch_weights(layer_index, input_weight, output_weight, gate_up_weight, down_weight):
    return (
        lax.all_gather(input_weight[layer_index], ("dp", "ctx"), axis=0, tiled=True),
        lax.all_gather(output_weight[layer_index], ("dp", "ctx"), axis=0, tiled=True),
        lax.all_gather(gate_up_weight[layer_index], ("dp", "ctx"), axis=0, tiled=True),
        lax.all_gather(down_weight[layer_index], ("dp", "ctx"), axis=0, tiled=True),
    )


def masked_scores(queries, key_heads, valid_keys):
    raw_scores = jnp.einsum("qhe,khe->hqk", queries, key_heads, preferred_element_type=jnp.float32)
    return jnp.where(valid_keys[None, None, :] > 0, raw_scores * HEAD_DIM ** (-0.5), masked_score)


def attend_forward(block_items):
    queries, keys_all, values_all, valid_keys = block_items
    key_count = keys_all.shape[0]
    head_count = queries.shape[1]
    key_heads = keys_all.reshape(key_count, head_count, HEAD_DIM)
    value_heads = values_all.reshape(key_count, head_count, HEAD_DIM)
    scores = masked_scores(queries, key_heads, valid_keys)
    row_max = jnp.max(scores, axis=-1, keepdims=True)
    exp_scores = jnp.exp(scores - row_max)
    row_total = jnp.sum(exp_scores, axis=-1, keepdims=True)
    attn_probs = (exp_scores / row_total).astype(jnp.bfloat16)
    attended = jnp.einsum(
        "hqk,khe->qhe", attn_probs, value_heads, preferred_element_type=jnp.float32
    )
    return (
        attended.reshape(queries.shape[0], head_count * HEAD_DIM),
        (row_max + jnp.log(row_total))[:, :, 0],
    )


def attend_backward(block_items):
    queries, keys_all, values_all, valid_keys, log_total, grad_out = block_items
    key_count = keys_all.shape[0]
    head_count = queries.shape[1]
    key_heads = keys_all.reshape(key_count, head_count, HEAD_DIM)
    value_heads = values_all.reshape(key_count, head_count, HEAD_DIM)
    scores = masked_scores(queries, key_heads, valid_keys)
    probs_full = jnp.exp(scores - log_total[:, :, None])
    probs_low = probs_full.astype(jnp.bfloat16)
    grad_probs = jnp.einsum(
        "qhe,khe->hqk", grad_out, value_heads, preferred_element_type=jnp.float32
    )
    row_dot = jnp.sum(probs_full * grad_probs, axis=-1, keepdims=True)
    grad_raw = jnp.where(
        valid_keys[None, None, :] > 0, HEAD_DIM ** (-0.5) * probs_full * (grad_probs - row_dot), 0.0
    ).astype(jnp.bfloat16)
    grad_queries = jnp.einsum(
        "hqk,khe->qhe", grad_raw, key_heads, preferred_element_type=jnp.float32
    )
    grad_keys = jnp.einsum("hqk,qhe->khe", grad_raw, queries, preferred_element_type=jnp.float32)
    grad_values = jnp.einsum(
        "hqk,qhe->khe", probs_low, grad_out, preferred_element_type=jnp.float32
    )
    local_rows = queries.shape[0]
    return (
        grad_queries.reshape(local_rows, head_count * HEAD_DIM),
        grad_keys.reshape(key_count, head_count * HEAD_DIM),
        grad_values.reshape(key_count, head_count * HEAD_DIM),
    )


def contract_rows(left, right):
    return lax.dot_general(
        left, right, (((0,), (0,)), ((), ())), preferred_element_type=jnp.float32
    )


def contract_cols(left, right):
    return lax.dot_general(
        left, right, (((1,), (1,)), ((), ())), preferred_element_type=jnp.float32
    )


def on_device(
    tokens_in,
    cotangent,
    key_mask,
    grid_pos,
    class_index,
    input_weight,
    output_weight,
    gate_up_weight,
    down_weight,
    norm_gains,
    norm_biases,
    head_gains,
    head_biases,
    hidden_gains,
    hidden_biases,
):
    images, rows_dev, model_width = tokens_in.shape
    row_count = images * rows_dev
    dim_local = head_gains.shape[1]
    heads_local = dim_local // HEAD_DIM
    hidden_local = hidden_gains.shape[1]
    layer_count = input_weight.shape[0]
    first_row = lax.axis_index("ctx") * rows_dev
    places = first_row + jnp.arange(rows_dev, dtype=jnp.int32)
    not_class = (places[None, :] != class_index[:, None]).astype(jnp.float32).reshape(row_count)
    cosine, sine = rotary_tables(grid_pos.reshape(2, row_count), not_class)
    row_keep = key_mask.astype(jnp.float32).reshape(row_count, 1)
    key_keep = key_mask.astype(jnp.bfloat16)
    gains_norm = norm_gains.astype(jnp.float32)
    biases_norm = norm_biases.astype(jnp.float32)
    gains_head = head_gains.astype(jnp.float32)
    biases_head = head_biases.astype(jnp.float32)
    gains_hidden = hidden_gains.astype(jnp.float32)
    biases_hidden = hidden_biases.astype(jnp.float32)
    hidden_state = tokens_in.astype(jnp.float32).reshape(row_count, model_width) * row_keep
    saved_layers = []
    for layer_index in range(layer_count):
        layer_mats = fetch_weights(
            layer_index, input_weight, output_weight, gate_up_weight, down_weight
        )
        mat_in, mat_out, mat_gate_up, mat_down = layer_mats
        normed, unit_one, spread_one = local_norm(
            hidden_state, gains_norm[layer_index, 0], biases_norm[layer_index, 0]
        )
        normed_low = normed.astype(jnp.bfloat16)
        projected = jnp.dot(
            normed_low,
            mat_in.reshape(model_width, 3 * dim_local),
            preferred_element_type=jnp.float32,
        ).reshape(row_count, 3, dim_local)
        queries = projected[:, 0] + biases_head[layer_index, 0]
        keys_proj = projected[:, 1]
        values_proj = projected[:, 2] + biases_head[layer_index, 1]
        query_low = rotate(
            queries.reshape(row_count, heads_local, HEAD_DIM), cosine, sine, 1.0
        ).astype(jnp.bfloat16)
        key_low = rotate(
            keys_proj.reshape(row_count, heads_local, HEAD_DIM), cosine, sine, 1.0
        ).astype(jnp.bfloat16)
        value_low = values_proj.astype(jnp.bfloat16)
        keys_all, values_all, valid_all = (
            lax.all_gather(key_low.reshape(images, rows_dev, dim_local), "ctx", axis=1, tiled=True),
            lax.all_gather(
                value_low.reshape(images, rows_dev, dim_local), "ctx", axis=1, tiled=True
            ),
            lax.all_gather(key_keep, "ctx", axis=1, tiled=True),
        )
        query_blocks = query_low.reshape(images, rows_dev, heads_local, HEAD_DIM)
        attended, log_total = lax.map(
            attend_forward, (query_blocks, keys_all, values_all, valid_all)
        )
        attended = attended.reshape(row_count, dim_local)
        head_normed, unit_two, spread_two = split_norm(
            attended, gains_head[layer_index], biases_head[layer_index, 2], model_width
        )
        head_low = head_normed.astype(jnp.bfloat16)
        branch = tensor_sum(contract_cols(head_low, mat_out))
        hidden_mid = hidden_state + row_keep * (branch + biases_norm[layer_index, 2])
        normed_two, unit_three, spread_three = local_norm(
            hidden_mid, gains_norm[layer_index, 1], biases_norm[layer_index, 1]
        )
        normed_two_low = normed_two.astype(jnp.bfloat16)
        gate_up = jnp.dot(
            normed_two_low,
            mat_gate_up.reshape(model_width, 2 * hidden_local),
            preferred_element_type=jnp.float32,
        ).reshape(row_count, 2, hidden_local)
        gate_pre = gate_up[:, 0] + biases_hidden[layer_index, 0]
        up_pre = gate_up[:, 1] + biases_hidden[layer_index, 1]
        inner_act = jax.nn.silu(gate_pre) * up_pre
        inner_normed, unit_four, spread_four = split_norm(
            inner_act, gains_hidden[layer_index], biases_hidden[layer_index, 2], FF
        )
        inner_low = inner_normed.astype(jnp.bfloat16)
        down_out = tensor_sum(contract_cols(inner_low, mat_down))
        hidden_state = hidden_mid + row_keep * (down_out + biases_norm[layer_index, 3])
        held_mats = None
        saved_layers.append(
            (
                held_mats,
                normed_low,
                unit_one,
                spread_one,
                query_blocks,
                keys_all,
                values_all,
                valid_all,
                log_total,
                unit_two,
                spread_two,
                head_low,
                unit_three,
                spread_three,
                normed_two_low,
                gate_pre,
                up_pre,
                unit_four,
                spread_four,
                inner_low,
            )
        )
    activations = hidden_state.reshape(images, rows_dev, model_width).astype(jnp.bfloat16)
    upstream = cotangent.astype(jnp.float32).reshape(row_count, model_width)
    mat_grads = [None] * layer_count
    vector_parts = [None] * layer_count
    for layer_index in reversed(range(layer_count)):
        (
            held_mats,
            normed_low,
            unit_one,
            spread_one,
            query_blocks,
            keys_all,
            values_all,
            valid_all,
            log_total,
            unit_two,
            spread_two,
            head_low,
            unit_three,
            spread_three,
            normed_two_low,
            gate_pre,
            up_pre,
            unit_four,
            spread_four,
            inner_low,
        ) = saved_layers[layer_index]
        mat_in, mat_out, mat_gate_up, mat_down = fetch_weights(
            layer_index, input_weight, output_weight, gate_up_weight, down_weight
        )
        grad_down = row_keep * upstream
        grad_bias_down = jnp.sum(grad_down, axis=0)
        grad_down_low = grad_down.astype(jnp.bfloat16)
        grad_mat_down = contract_rows(grad_down_low, inner_low)
        grad_inner_normed = jnp.dot(grad_down_low, mat_down, preferred_element_type=jnp.float32)
        grad_gain_hidden = jnp.sum(grad_inner_normed * unit_four, axis=0)
        grad_shift_hidden = jnp.sum(grad_inner_normed, axis=0)
        grad_inner = split_norm_back(
            grad_inner_normed, unit_four, spread_four, gains_hidden[layer_index], FF
        )
        sigmoid_gate = jax.nn.sigmoid(gate_pre)
        grad_up = grad_inner * gate_pre * sigmoid_gate
        grad_gate = grad_inner * up_pre * sigmoid_gate * (1.0 + gate_pre * (1.0 - sigmoid_gate))
        grad_gate_up_low = (
            jnp.stack([grad_gate, grad_up], axis=1)
            .astype(jnp.bfloat16)
            .reshape(row_count, 2 * hidden_local)
        )
        grad_mat_gate_up = contract_rows(normed_two_low, grad_gate_up_low).reshape(
            model_width, 2, hidden_local
        )
        grad_normed_two = tensor_back(
            contract_cols(grad_gate_up_low, mat_gate_up.reshape(model_width, 2 * hidden_local))
        )
        grad_gain_two = jnp.sum(grad_normed_two * unit_three, axis=0)
        grad_shift_two = jnp.sum(grad_normed_two, axis=0)
        upstream = upstream + local_norm_back(
            grad_normed_two, unit_three, spread_three, gains_norm[layer_index, 1]
        )
        grad_branch = row_keep * upstream
        grad_bias_out = jnp.sum(grad_branch, axis=0)
        grad_branch_low = grad_branch.astype(jnp.bfloat16)
        grad_mat_out = contract_rows(grad_branch_low, head_low)
        grad_head = jnp.dot(grad_branch_low, mat_out, preferred_element_type=jnp.float32)
        grad_gain_head = jnp.sum(grad_head * unit_two, axis=0)
        grad_shift_head = jnp.sum(grad_head, axis=0)
        grad_attended = split_norm_back(
            grad_head, unit_two, spread_two, gains_head[layer_index], model_width
        )
        grad_att_low = grad_attended.astype(jnp.bfloat16).reshape(
            images, rows_dev, heads_local, HEAD_DIM
        )
        grad_query_rot, grad_keys_all, grad_values_all = lax.map(
            attend_backward,
            (query_blocks, keys_all, values_all, valid_all, log_total, grad_att_low),
        )
        grad_keys_rot, grad_values = (
            lax.psum_scatter(
                grad_keys_all.astype(jnp.bfloat16), "ctx", scatter_dimension=1, tiled=True
            ).astype(jnp.float32),
            lax.psum_scatter(
                grad_values_all.astype(jnp.bfloat16), "ctx", scatter_dimension=1, tiled=True
            ).astype(jnp.float32),
        )
        grad_queries = rotate(
            grad_query_rot.reshape(row_count, heads_local, HEAD_DIM), cosine, sine, -1.0
        ).reshape(row_count, dim_local)
        grad_keys = rotate(
            grad_keys_rot.reshape(row_count, heads_local, HEAD_DIM), cosine, sine, -1.0
        ).reshape(row_count, dim_local)
        grad_values = grad_values.reshape(row_count, dim_local)
        grad_proj_low = (
            jnp.stack([grad_queries, grad_keys, grad_values], axis=1)
            .astype(jnp.bfloat16)
            .reshape(row_count, 3 * dim_local)
        )
        grad_mat_in = contract_rows(normed_low, grad_proj_low).reshape(model_width, 3, dim_local)
        grad_normed_one = tensor_back(
            contract_cols(grad_proj_low, mat_in.reshape(model_width, 3 * dim_local))
        )
        grad_gain_one = jnp.sum(grad_normed_one * unit_one, axis=0)
        grad_shift_one = jnp.sum(grad_normed_one, axis=0)
        upstream = upstream + local_norm_back(
            grad_normed_one, unit_one, spread_one, gains_norm[layer_index, 0]
        )
        mat_grads[layer_index] = (
            lax.psum_scatter(grad_mat_in, ("dp", "ctx"), scatter_dimension=0, tiled=True),
            lax.psum_scatter(grad_mat_out, ("dp", "ctx"), scatter_dimension=0, tiled=True),
            lax.psum_scatter(grad_mat_gate_up, ("dp", "ctx"), scatter_dimension=0, tiled=True),
            lax.psum_scatter(grad_mat_down, ("dp", "ctx"), scatter_dimension=0, tiled=True),
        )
        vector_parts[layer_index] = (
            jnp.stack([grad_gain_one, grad_gain_two]),
            jnp.stack([grad_shift_one, grad_shift_two, grad_bias_out, grad_bias_down]),
            grad_gain_head,
            jnp.stack(
                [jnp.sum(grad_queries, axis=0), jnp.sum(grad_values, axis=0), grad_shift_head]
            ),
            grad_gain_hidden,
            jnp.stack([jnp.sum(grad_gate, axis=0), jnp.sum(grad_up, axis=0), grad_shift_hidden]),
        )
    input_grad = (row_keep * upstream).reshape(images, rows_dev, model_width)
    stacked_vectors = tuple(
        (
            jnp.stack([vector_parts[index][member] for index in range(layer_count)])
            for member in range(6)
        )
    )
    summed_vectors = lax.psum(
        (
            stacked_vectors[0],
            stacked_vectors[1],
            stacked_vectors[2],
            stacked_vectors[3],
            stacked_vectors[4],
            stacked_vectors[5],
        ),
        ("dp", "ctx"),
    )
    grad_input_weight = jnp.stack([mat_grads[index][0] for index in range(layer_count)])
    grad_output_weight = jnp.stack([mat_grads[index][1] for index in range(layer_count)])
    grad_gate_up_weight = jnp.stack([mat_grads[index][2] for index in range(layer_count)])
    grad_down_weight = jnp.stack([mat_grads[index][3] for index in range(layer_count)])
    return (
        activations,
        input_grad,
        grad_input_weight,
        grad_output_weight,
        grad_gate_up_weight,
        grad_down_weight,
        summed_vectors[0],
        summed_vectors[1],
        summed_vectors[2],
        summed_vectors[3],
        summed_vectors[4],
        summed_vectors[5],
    )


MESH = pl.DeviceIdType.MESH

RB=64

class Where:
    def __init__(self):
        self.dp=lax.axis_index("dp"); self.x=lax.axis_index("ctx"); self.c=lax.axis_index("tp")
        self.z=self.dp//2; self.y=self.dp%2
    def nx(self): return (self.dp,1-self.x,self.c)
    def ny(self): return (self.z*2+1-self.y,self.x,self.c)
    def up(self): return ((self.z+1)*2+self.y,self.x,self.c)
    def dn(self): return ((self.z-1)*2+self.y,self.x,self.c)

def greet(w):
    bar=pltpu.get_barrier_semaphore()
    def sig(dev): pl.semaphore_signal(bar,inc=1,device_id=dev,device_id_type=MESH)
    sig(w.nx()); sig(w.ny())
    @pl.when(w.z<3)
    def _(): sig(w.up())
    @pl.when(w.z>0)
    def _(): sig(w.dn())
    pl.semaphore_wait(bar,2+(w.z<3).astype(jnp.int32)+(w.z>0).astype(jnp.int32))

class Gather:
    def __init__(self,w,order,src,out,r0,nr,ssem,rsem,own_sem):
        self.w,self.order,self.src,self.out,self.r0,self.nr=w,order,src,out,r0,nr
        self.ssem,self.rsem=ssem,rsem
        self.pending=[]
    def rows(self,zz,yy,xx):
        return pl.ds(pl.multiple_of(((zz*2+yy)*2+xx)*RB+self.r0,16),self.nr)
    def here(self,zz,yy,xx,own=False):
        return self.src.at[pl.ds(self.r0,self.nr)] if own else self.out.at[self.rows(zz,yy,xx)]
    def copy(self,zz,yy,xx,dev,s,r,own=False):
        return pltpu.make_async_remote_copy(src_ref=self.here(zz,yy,xx,own),dst_ref=self.out.at[self.rows(zz,yy,xx)],
            send_sem=self.ssem.at[s],recv_sem=self.rsem.at[r],device_id=dev,device_id_type=MESH)
    def send(self,cond,*a,**k):
        self.pending.append((cond,a,k))
        if cond is None: self.copy(*a,**k).start()
        else:
            @pl.when(cond)
            def _(): self.copy(*a,**k).start()
    def finish_sends(self):
        for cond,a,k in self.pending:
            if cond is None: self.copy(*a,**k).wait_send()
            else:
                @pl.when(cond)
                def _(a=a,k=k): self.copy(*a,**k).wait_send()
    def arrived(self,zz,yy,xx,r):
        self.copy(zz,yy,xx,self.w.nx(),0,r).wait_recv()

class GatherZ(Gather):
    def pq(self,zz,pself):
        w=self.w
        if self.order=="zyx": return (zz,w.y if pself else 1-w.y,w.x)
        return (zz,w.y,w.x if pself else 1-w.x)
    def pdev(self): return self.w.ny() if self.order=="zyx" else self.w.nx()
    def qdev(self): return self.w.nx() if self.order=="zyx" else self.w.ny()
    def qcoord(self,zz,pself):
        w=self.w
        if self.order=="zyx": return (zz,w.y if pself else 1-w.y,1-w.x)
        return (zz,1-w.y,w.x if pself else 1-w.x)
    def emit(self,cond,zz,k,own=False):
        b=self.pq(zz,True)
        w=self.w
        if k<4:
            c=(w.z<3) if cond is None else jnp.logical_and(cond,w.z<3)
            self.send(c,*b,w.up(),k,zz,own=own)
        if k==0 or k>=4:
            c=(w.z>0) if cond is None else jnp.logical_and(cond,w.z>0)
            self.send(c,*b,w.dn(),7+(k if k==0 else k-3),zz,own=own)
        self.send(cond,*b,self.pdev(),11+k,4+zz,own=own)
        self.send(cond,*b,self.qdev(),18+k,8+zz*2,own=own)
    def rounds(self):
        w=self.w
        self.emit(None,w.z,0,own=True)
        yield
        for k in (1,2,3):
            for kk,zz,cond in ((k,w.z-k,w.z>=k),(k+3,w.z+k,w.z+k<=3)):
                @pl.when(cond)
                def _(zz=zz): self.arrived(*self.pq(zz,True),zz)
                self.emit(cond,zz,kk)
            yield
        for k in (0,1,2,3):
            for kk,zz,cond in (((0,w.z,None),) if k==0 else ((k,w.z-k,w.z>=k),(k+3,w.z+k,w.z+k<=3))):
                b=self.pq(zz,False)
                def go(zz=zz,b=b): self.arrived(*b,4+zz)
                if cond is None: go()
                else: pl.when(cond)(go)
                self.send(cond,*b,self.qdev(),25+kk,8+zz*2+1)
            yield
    def arrive(self):
        for zz in range(4):
            for pself in (True,False):
                self.arrived(*self.qcoord(zz,pself),8+zz*2+(0 if pself else 1))
    NS,NR=32,16

class GatherX(Gather):
    NS,NR=3+4*7,19
    def blk(self,zz,j):
        w=self.w
        return (zz,w.y if j<2 else 1-w.y,w.x if j%2==0 else 1-w.x)
    def vert(self,cond,zz,j,k,own=False):
        w=self.w; b=self.blk(zz,j)
        if k<4:
            c=(w.z<3) if cond is None else jnp.logical_and(cond,w.z<3)
            self.send(c,*b,w.up(),3+j*7+k if k else 3+j*7,3+zz*4+j,own=own)
        if k==0 or k>=4:
            c=(w.z>0) if cond is None else jnp.logical_and(cond,w.z>0)
            self.send(c,*b,w.dn(),3+j*7+(k if k>=4 else 3),3+zz*4+j,own=own)
    def rounds(self):
        w=self.w
        self.send(None,*self.blk(w.z,0),w.nx(),0,0,own=True)
        self.send(None,*self.blk(w.z,0),w.ny(),1,1,own=True)
        self.vert(None,w.z,0,0,own=True)
        yield
        b=self.blk(w.z,1); self.arrived(*b,0)
        self.send(None,*b,w.ny(),2,2)
        yield
        yield
        yield
        self.arrived(*self.blk(w.z,2),1)
        self.arrived(*self.blk(w.z,3),2)
        for j in range(1,4): self.vert(None,w.z,j,0)
        yield
        for k in (1,2,3):
            for j in range(4):
                for kk,zz,cond in ((k,w.z-k,w.z>=k),(k+3,w.z+k,w.z+k<=3)):
                    @pl.when(cond)
                    def _(zz=zz,j=j): self.arrived(*self.blk(zz,j),3+zz*4+j)
                    if k<3: self.vert(cond,zz,j,kk)
                if j%2==1: yield
    def arrive(self):
        pass


ZORD=(3,0,2,1)
class Scatter:
    def __init__(self,w,order,src,out,r0,nr,ssem,rsem,lsem,own,bufs):
        self.w,self.order,self.src,self.out,self.r0,self.nr=w,order,src,out,r0,nr
        self.ssem,self.rsem,self.lsem,self.own=ssem,rsem,lsem,own
        self.bufs=bufs
        self.pending=[]
    def rows(self,zz,yy,xx):
        return pl.ds(pl.multiple_of(((zz*2+yy)*2+xx)*RB+self.r0,16),self.nr)
    def send(self,cond,src,dst,dev,s,r):
        mk=lambda: pltpu.make_async_remote_copy(src_ref=src,dst_ref=dst,send_sem=self.ssem.at[s],recv_sem=self.rsem.at[r],device_id=dev,device_id_type=MESH)
        self.pending.append((cond,mk))
        if cond is None: mk().start()
        else: pl.when(cond)(lambda: mk().start())
    def wait(self,cond,dst,r):
        def go(): pltpu.make_async_remote_copy(src_ref=dst,dst_ref=dst,send_sem=self.ssem.at[0],recv_sem=self.rsem.at[r],device_id=self.w.nx(),device_id_type=MESH).wait_recv()
        if cond is None: go()
        else: pl.when(cond)(go)
    def finish(self):
        for cond,mk in self.pending:
            if cond is None: mk().wait_send()
            else: pl.when(cond)(lambda mk=mk: mk().wait_send())
    def total(self,dst,terms,extra=()):
        def strip(i,_):
            s=pl.ds(pl.multiple_of(i*16,16),16)
            t=terms[0][s].astype(jnp.float32)
            for r in terms[1:]: t=t+r[s].astype(jnp.float32)
            dst[s]=t.astype(dst.dtype)
            return 0
        lax.fori_loop(0,self.nr//16,strip,0)

class ScatterZ(Scatter):
    NS,NR=16,17
    def mine(self,zz,pself):
        w=self.w
        if self.order=="zyx": return (zz,w.y if pself else 1-w.y,w.x)
        return (zz,w.y,w.x if pself else 1-w.x)
    def theirs(self,zz,pself):
        w=self.w
        if self.order=="zyx": return (zz,w.y if pself else 1-w.y,1-w.x)
        return (zz,1-w.y,w.x if pself else 1-w.x)
    def rounds(self):
        w=self.w; rq,rp,ru=self.bufs
        pdev=w.ny() if self.order=="zyx" else w.nx()
        qdev=w.nx() if self.order=="zyx" else w.ny()
        loc={}
        for k in (1,0):
            for zz in ZORD:
                c=pltpu.make_async_copy(self.src.at[self.rows(*self.mine(zz,k==0))],self.own.at[zz*2+k],self.lsem.at[zz*2+k]); c.start(); loc[zz*2+k]=c
        for zz in ZORD:
            self.send(None,self.src.at[self.rows(*self.theirs(zz,False))],rq.at[zz*2+1],qdev,zz*2+1,zz*2+1)
        yield
        for zz in ZORD:
            i=zz*2+1
            loc[i].wait(); self.wait(None,rq.at[i],i)
            self.total(rq.at[i],[self.own.at[i],rq.at[i]])
            self.send(None,rq.at[i],rp.at[zz],pdev,8+zz,8+zz)
            self.send(None,self.src.at[self.rows(*self.theirs(zz,True))],rq.at[zz*2],qdev,zz*2,zz*2)
            yield
        def ready(zz):
            loc[zz*2].wait(); self.wait(None,rq.at[zz*2],zz*2); self.wait(None,rp.at[zz],8+zz)
            return [self.own.at[zz*2],rq.at[zz*2],rp.at[zz]]
        for t in (1,2,3):
            for i in range(4):
                for up in (True,False):
                    m=i if up else 3-i
                    if m>=t: continue
                    zz=4-t+m if up else t-1-m
                    @pl.when(w.z==i)
                    def _():
                        terms=ready(zz)
                        if m>0:
                            self.wait(None,ru.at[zz],12+zz); terms.append(ru.at[zz])
                        self.total(rp.at[zz],terms)
                    if up: self.send(w.z==i,rp.at[zz],ru.at[zz],w.up(),12+zz,12+zz)
                    else:
                        to=4 if zz==i-1 else zz
                        self.send(w.z==i,rp.at[zz],ru.at[to],w.dn(),12+zz,12+to)
            yield
        o=self.out.at[pl.ds(self.r0,self.nr)]
        for zz in range(4):
            @pl.when(w.z==zz)
            def _():
                terms=ready(zz)
                if zz>0: self.wait(None,ru.at[zz],12+zz); terms.append(ru.at[zz])
                if zz<3: self.wait(None,ru.at[4],16); terms.append(ru.at[4])
                self.total(o,terms)
        yield

class ScatterX(Scatter):
    NS,NR=19,23
    def blk(self,zz,j):
        w=self.w
        return (zz,w.y if j<2 else 1-w.y,w.x if j%2==0 else 1-w.x)
    def rounds(self):
        w=self.w; ru,ry,rx=self.bufs
        down=lambda zz,j: jnp.where(w.z-1==zz,16+j,zz*4+j)
        loc={}
        for zz in ZORD:
            for j in (3,2,1,0):
                i=zz*4+j
                c=pltpu.make_async_copy(self.src.at[self.rows(*self.blk(zz,j))],self.own.at[i],self.lsem.at[i]); c.start(); loc[i]=c
        J=(3,2,1,0)
        for zz in (3,2,1):
            for j in J: self.send(w.z==0,self.src.at[self.rows(*self.blk(zz,j))],ru.at[zz*4+j],w.up(),zz*4+j,zz*4+j)
        for zz in (0,1,2):
            for j in J:
                to=16+j if zz==2 else zz*4+j
                self.send(w.z==3,self.src.at[self.rows(*self.blk(zz,j))],ru.at[to],w.dn(),zz*4+j,to)
        yield
        for i in loc: loc[i].wait()
        def hop(c,zz,j,up):
            i=zz*4+j
            @pl.when(w.z==c)
            def _():
                self.wait(None,ru.at[i],i)
                self.total(ru.at[i],[self.own.at[i],ru.at[i]])
            if up: self.send(w.z==c,ru.at[i],ru.at[i],w.up(),i,i)
            else:
                to=16+j if zz==c-1 else i
                self.send(w.z==c,ru.at[i],ru.at[to],w.dn(),i,to)
        for j in J:
            hop(1,3,j,True); hop(2,0,j,False)
            if j%2==0: yield
        for j in J:
            hop(1,2,j,True); hop(2,1,j,False)
            hop(2,3,j,True); hop(1,0,j,False)
            if j%2==0: yield
        def zsum(j,dst,extra):
            for zz in range(4):
                i=zz*4+j
                t=[self.own.at[i]]
                if zz>0: t.append(ru.at[i])
                if zz<3: t.append(ru.at[16+j])
                @pl.when(w.z==zz)
                def _():
                    if zz>0: self.wait(None,ru.at[i],i)
                    if zz<3: self.wait(None,ru.at[16+j],16+j)
                    self.total(dst,t+extra)
        sy=self.bufs_stage
        for j in (3,2):
            k=j-2
            zsum(j,sy.at[k],[])
            self.send(None,sy.at[k],ry.at[k],w.ny(),16+k,20+k)
        yield
        self.wait(None,ry.at[1],21)
        zsum(1,sy.at[2],[ry.at[1]])
        self.send(None,sy.at[2],rx.at[0],w.nx(),18,22)
        yield
        self.wait(None,ry.at[0],20)
        self.wait(None,rx.at[0],22)
        zsum(0,self.out.at[pl.ds(self.r0,self.nr)],[ry.at[0],rx.at[0]])
        yield


F32 = jnp.float32
BF = jnp.bfloat16
DMA = pltpu.SemaphoreType.DMA
EPS = 1e-06


def step_all(gens):
    gens = list(gens)
    while gens:
        for g in list(gens):
            try:
                next(g)
            except StopIteration:
                gens.remove(g)
                continue
            yield


def drive(compute, comm, plan, rest):
    for i, _ in enumerate(compute):
        for _ in range(plan[i] if i < len(plan) else rest):
            next(comm, None)
    for _ in comm:
        pass


class GatherSet:
    def __init__(self, parts, names, cut=32):
        self.parts, self.names, self.cut = parts, names, cut

    def scratch(self):
        out = []
        for name, cols, kind in self.parts:
            if kind == "z":
                out += [DMA((GatherZ.NS,)), DMA((GatherZ.NR,))] * 2
            else:
                out += [DMA((GatherX.NS,)), DMA((GatherX.NR,))]
        return out + [DMA((len(self.names),))]

    def start(self, w, srcs, outs, sems):
        sems = list(sems)
        me = pl.multiple_of((w.dp * 2 + w.x) * RB, 16)
        self.locs = []
        for i, name in enumerate(self.names):
            c = pltpu.make_async_copy(srcs[name], outs[name].at[pl.ds(me, RB)], sems[-1].at[i])
            c.start()
            self.locs.append(c)
        self.live = []
        for name, cols, kind in self.parts:
            s, o = srcs[name], outs[name]
            if cols is not None:
                s, o = s.at[:, cols[0] : cols[1]], o.at[:, cols[0] : cols[1]]
            if kind == "z":
                for r0, nr, order in ((0, self.cut, "zyx"), (self.cut, RB - self.cut, "zxy")):
                    self.live.append(GatherZ(w, order, s, o, r0, nr, sems.pop(0), sems.pop(0), None))
            else:
                self.live.append(GatherX(w, "xyz", s, o, 0, 64, sems.pop(0), sems.pop(0), None))
        return step_all([p.rounds() for p in self.live])

    def arrive(self):
        for p in self.live:
            p.arrive()
        for c in self.locs:
            c.wait()

    def finish_sends(self):
        for p in self.live:
            p.finish_sends()

    def finish(self):
        self.arrive()
        self.finish_sends()


class VecSum:
    def __init__(self, w, src, out, st, rv, ss, rs):
        self.w, self.src, self.out, self.st, self.rv, self.ss, self.rs = w, src, out, st, rv, ss, rs

    def mk(self, src, k, dev, send):
        return pltpu.make_async_remote_copy(
            src_ref=src, dst_ref=self.rv.at[k], send_sem=self.ss.at[send], recv_sem=self.rs.at[k],
            device_id=dev, device_id_type=MESH)

    def rounds(self):
        w = self.w
        st, rv = self.st, self.rv
        even = w.z % 2 == 0
        odd = w.z % 2 == 1
        mid = jnp.logical_and(w.z > 0, w.z < 3)
        self.mk(self.src, 0, w.nx(), 0).start()
        yield
        yield
        self.mk(self.src, 0, w.nx(), 0).wait_recv()
        st[0] = self.src[...] + rv[0]
        self.mk(st.at[0], 1, w.ny(), 1).start()
        yield
        yield
        self.mk(self.src, 1, w.ny(), 1).wait_recv()
        st[1] = st[0] + rv[1]
        pl.when(even)(lambda: self.mk(st.at[1], 2, w.up(), 2).start())
        pl.when(odd)(lambda: self.mk(st.at[1], 2, w.dn(), 2).start())
        yield
        yield
        self.mk(self.src, 2, w.nx(), 2).wait_recv()
        st[2] = st[1] + rv[2]
        pl.when(w.z == 1)(lambda: self.mk(st.at[2], 3, w.up(), 3).start())
        pl.when(w.z == 2)(lambda: self.mk(st.at[2], 3, w.dn(), 3).start())
        yield
        yield

        @pl.when(mid)
        def _():
            self.mk(self.src, 3, w.nx(), 3).wait_recv()
            st[3] = st[2] + rv[3]
            self.out[...] = st[3]

        pl.when(w.z == 1)(lambda: self.mk(st.at[3], 4, w.dn(), 4).start())
        pl.when(w.z == 2)(lambda: self.mk(st.at[3], 4, w.up(), 4).start())
        yield
        yield

        @pl.when(jnp.logical_not(mid))
        def _():
            self.mk(self.src, 4, w.nx(), 4).wait_recv()
            self.out[...] = rv[4]

        yield
        yield

    def finish(self):
        w = self.w
        self.mk(self.src, 0, w.nx(), 0).wait_send()
        self.mk(self.src, 0, w.nx(), 1).wait_send()
        self.mk(self.src, 0, w.nx(), 2).wait_send()

        @pl.when(jnp.logical_and(w.z > 0, w.z < 3))
        def _():
            self.mk(self.src, 0, w.nx(), 3).wait_send()
            self.mk(self.src, 0, w.nx(), 4).wait_send()


class ScatterSet:
    def __init__(self, parts, names, widths, cut=32, vec=True):
        self.parts, self.names, self.widths, self.cut, self.vec = parts, names, widths, cut, vec

    def scratch(self):
        V = lambda *s: pltpu.VMEM(s, BF)
        sc = []
        for name, cols, kind in self.parts:
            C = self.widths[name] if cols is None else cols[1] - cols[0]
            if kind == "z":
                for nr in (self.cut, RB - self.cut):
                    sc += [DMA((ScatterZ.NS,)), DMA((ScatterZ.NR,)), DMA((8,))]
                    sc += [V(8, nr, C), V(8, nr, C), V(4, nr, C), V(5, nr, C)]
            else:
                sc += [DMA((ScatterX.NS,)), DMA((ScatterX.NR,)), DMA((16,))]
                sc += [V(16, 64, C), V(20, 64, C), V(2, 64, C), V(1, 64, C), V(3, 64, C)]
        if self.vec:
            sc += [pltpu.VMEM((4, 8, HP), F32), pltpu.VMEM((5, 8, HP), F32), DMA((5,)), DMA((5,))]
        return sc

    def start(self, w, srcs, outs, vec, vec_out, sc):
        sc = list(sc)
        self.live = []
        for name, cols, kind in self.parts:
            s, o = srcs[name], outs[name]
            if cols is not None:
                s, o = s.at[:, cols[0] : cols[1]], o.at[:, cols[0] : cols[1]]
            if kind == "z":
                for r0, nr, order in ((0, self.cut, "zyx"), (self.cut, RB - self.cut, "zxy")):
                    ss, rs, ls, own, rq, rp, ru = [sc.pop(0) for _ in range(7)]
                    self.live.append(ScatterZ(w, order, s, o, r0, nr, ss, rs, ls, own, (rq, rp, ru)))
            else:
                ss, rs, ls, own, ru, ry, rx, st = [sc.pop(0) for _ in range(8)]
                p = ScatterX(w, "xyz", s, o, 0, 64, ss, rs, ls, own, (ru, ry, rx))
                p.bufs_stage = st
                self.live.append(p)
        if self.vec:
            st, rv, ss, rs = sc
            self.live.append(VecSum(w, vec, vec_out, st, rv, ss, rs))
        return step_all([p.rounds() for p in self.live])

    def finish(self):
        for p in self.live:
            p.finish()


FF_CUT = 16
AT_G = GatherSet([("in", None, "z"), ("out", None, "x")], ["in", "out"])
FF_G = GatherSet([("gu", None, "z"), ("dn", (0, 512), "z"), ("dn", (512, 1408), "x")], ["gu", "dn"], FF_CUT)


def at_scatter():
    return ScatterSet([("in", None, "z"), ("out", None, "x")], ["in", "out"], {"in": 1536, "out": 512})


def gu_scatter():
    return ScatterSet([("gu", (0, 2176), "z"), ("gu", (2176, 2816), "x")], ["gu"], {"gu": 2816}, FF_CUT)


def dn_scatter():
    return ScatterSet([("dn", (0, 1024), "z"), ("dn", (1024, 1408), "x")], ["dn"], {"dn": 1408}, 32, False)


def rows16(n, fn, step=176):
    def body(i, _):
        fn(pl.ds(pl.multiple_of(i * step, 16), step))
        return 0

    lax.fori_loop(0, n // step, body, 0)


def unit_of(x, width):
    mean = jnp.sum(x, axis=-1, keepdims=True) / width
    c = x - mean
    inv = lax.rsqrt(jnp.sum(c * c, axis=-1, keepdims=True) / width + EPS)
    return c * inv, inv


def dot_nn(a, b):
    return jnp.dot(a, b, preferred_element_type=F32)


def dot_nt(a, b):
    return lax.dot_general(a, b, (((1,), (1,)), ((), ())), preferred_element_type=F32)


def dot_tn(a, b):
    return lax.dot_general(a, b, (((0,), (0,)), ((), ())), preferred_element_type=F32)


def tiles(n, size=256):
    return [(a, min(size, n - a)) for a in range(0, n, size)]


def fold8(x):
    return jnp.sum(x.reshape(x.shape[0] // 8, 8, x.shape[1]), axis=0)


def wide(x, n):
    return jnp.concatenate([x] * (-(-n // 128)), axis=1)[:, :n]


def two_cols(a, b):
    lane = lax.broadcasted_iota(jnp.int32, (a.shape[0], 128), 1)
    return jnp.where(lane == 0, a, jnp.where(lane == 1, b, 0.0))


def turn(x, cos, sin):
    lane = lax.broadcasted_iota(jnp.int32, x.shape, 1)
    other = jnp.where((lane // 16) % 2 == 0, pltpu.roll(x, 112, 1), pltpu.roll(x, 16, 1))
    return x * cos + other * sin


def head_lanes(x, t):
    lane = lax.broadcasted_iota(jnp.int32, x.shape, 1)
    return jnp.where(lane // 64 == t, x, jnp.zeros_like(x))


class Peer:
    def __init__(self, dev, ss, rs):
        self.dev, self.ss, self.rs, self.open = dev, ss, rs, []

    def mk(self, src, dst, k):
        return pltpu.make_async_remote_copy(
            src_ref=src, dst_ref=dst, send_sem=self.ss.at[k], recv_sem=self.rs.at[k], device_id=self.dev, device_id_type=MESH)

    def send(self, src, dst, k):
        c = self.mk(src, dst, k)
        c.start()
        self.open.append(c)

    def recv(self, dst, k):
        self.mk(dst, dst, k).wait_recv()

    def finish(self):
        for c in self.open:
            c.wait_send()
        self.open = []


def greet_all(w, links):
    bar = pltpu.get_barrier_semaphore()

    def sig(dev):
        pl.semaphore_signal(bar, inc=1, device_id=dev, device_id_type=MESH)

    sig((w.dp, w.x, 1 - w.c))
    n = jnp.int32(1)
    if links != "core":
        sig(w.nx())
        n = n + 1
    if links == "all":
        sig(w.ny())
        pl.when(w.z < 3)(lambda: sig(w.up()))
        pl.when(w.z > 0)(lambda: sig(w.dn()))
        n = n + 1 + (w.z < 3).astype(jnp.int32) + (w.z > 0).astype(jnp.int32)
    pl.semaphore_wait(bar, n)


class Bag:
    def launch(self):
        self.coming = {n: pltpu.make_async_copy(h, getattr(self, n), self.ld.at[i]) for i, (n, h) in enumerate(self.loads)}
        for n, c in self.coming.items():
            if n not in self.late:
                c.start()
        self.going = []

    def begin(self, *names):
        for n in names:
            self.coming[n].start()

    def need(self, *names):
        for n in names:
            if n in self.coming:
                self.coming.pop(n).wait()

    def put(self, name, cols=None):
        s, d = getattr(self, name), self.stores[name]
        if cols is not None:
            s, d = s.at[:, cols[0] : cols[1]], d.at[:, cols[0] : cols[1]]
        c = pltpu.make_async_copy(s, d, self.so.at[len(self.going)])
        c.start()
        self.going.append(c)

    def flush(self):
        self.need(*list(self.coming))
        for c in self.going:
            c.wait()


def run_kernel(body, name, cid, ins, outs, scratch, extra=()):
    iname, oname, sname = list(ins), list(outs), list(scratch)
    ld = [n for n in iname if ins[n][1] in (LD, LATE)]
    so = [n for n in oname if outs[n][2] == "ST"]
    moved = [pltpu.VMEM(ins[n][0].shape, ins[n][0].dtype) for n in ld] + [pltpu.VMEM(outs[n][0], outs[n][1]) for n in so]
    moved += [DMA((max(len(ld), 1),)), DMA((16,))]

    def kernel(*refs):
        b = Bag()
        ni, no, ns, nm = len(iname), len(oname), len(sname), len(moved)
        for n, r in zip(iname + oname + sname, refs):
            setattr(b, n, r)
        mv = refs[ni + no + ns : ni + no + ns + nm]
        b.loads = [(n, getattr(b, n)) for n in ld]
        b.late = [n for n in ld if ins[n][1] == LATE]
        b.stores = {n: getattr(b, n) for n in so}
        for n, r in zip(ld + so, mv):
            setattr(b, n, r)
        b.ld, b.so = mv[-2:]
        b.extra = refs[ni + no + ns + nm :]
        b.launch()
        body(b)
        b.flush()

    place = lambda s: pl.BlockSpec(memory_space=pl.ANY if s in (LD, ST, LATE) else s)
    res = pl.pallas_call(
        kernel,
        out_shape=[jax.ShapeDtypeStruct(outs[n][0], outs[n][1]) for n in oname],
        in_specs=[place(ins[n][1]) for n in iname],
        out_specs=[place(outs[n][2]) for n in oname],
        scratch_shapes=[scratch[n] for n in sname] + moved + list(extra),
        compiler_params=pltpu.CompilerParams(collective_id=cid, has_side_effects=True, vmem_limit_bytes=62 * 2**20),
        name=name,
    )(*[ins[n][0] for n in iname])
    return dict(zip(oname, res))


VM = pltpu.VMEM
ANY = pl.ANY
LD, ST, LATE = "LD", "ST", "LATE"


def gather_first(srcs, gset, fill, cid):
    names = gset.names
    R = fill.shape[1]

    def body(b):
        w = Where()
        greet(w)
        side = Peer(w.nx(), b.xs, b.xr)
        b.need("fill")
        side.send(b.fill, b.other, 0)
        g = gset.start(w, {n: getattr(b, "s_" + n) for n in names}, {n: getattr(b, "w_" + n) for n in names}, b.extra)
        for _ in g:
            pass
        side.recv(b.other, 0)
        b.both[0:R, :] = jnp.broadcast_to(b.fill[...].T[:, 0:1], (R, 128))
        b.both[R : 2 * R, :] = jnp.broadcast_to(b.other[...].T[:, 0:1], (R, 128))
        b.put("both")
        gset.finish()
        side.finish()

    ins = {"s_" + n: (srcs[n], ANY) for n in names}
    ins["fill"] = (fill, LD)
    outs = {"w_" + n: ((16 * RB, srcs[n].shape[1]), BF, ANY) for n in names}
    outs["both"] = ((2 * R, 128), F32, ST)
    return run_kernel(body, "gather", cid, ins, outs, dict(other=VM((8, R), F32), xs=DMA((1,)), xr=DMA((1,))), gset.scratch())


def attend_body(b, w, R, core, side):
    hp = b.h.shape[1]
    b.need("h", "vn")
    rows16(R, lambda s: norm_store(b.n, s, b.h[s], b.vn[0:1, :], b.vn[1:2, :]))
    b.need("w_in", "cos", "sin", "keep", "vh")
    D = 512
    for j in range(2):
        kt = dot_nn(b.n[...], b.w_in[:, D + 256 * j : D + 256 * j + 256])
        for hf in range(2):
            l = slice(256 * j + 128 * hf, 256 * j + 128 * hf + 128)
            b.k[0:R, l] = (turn(kt[:, 128 * hf : 128 * hf + 128], b.cos[...], b.sin[...]) * b.keep[...]).astype(BF)
        l = slice(256 * j, 256 * j + 256)
        side.send(b.k.at[pl.ds(0, R), l], b.k.at[pl.ds(R, R), l], 2 * j)
        vt = dot_nn(b.n[...], b.w_in[:, 2 * D + 256 * j : 2 * D + 256 * j + 256]) + b.vh[2:3, l]
        b.v[0:R, l] = vt.astype(BF)
        side.send(b.v.at[pl.ds(0, R), l], b.v.at[pl.ds(R, R), l], 2 * j + 1)
        yield
    for j in range(2):
        qt = dot_nn(b.n[...], b.w_in[:, 256 * j : 256 * j + 256]) + b.vh[1:2, 256 * j : 256 * j + 256]
        for hf in range(2):
            l = slice(256 * j + 128 * hf, 256 * j + 128 * hf + 128)
            b.q[:, l] = (turn(qt[:, 128 * hf : 128 * hf + 128], b.cos[...], b.sin[...]) * 0.125).astype(BF)
    b.put("q")
    b.need("fill")
    yield
    S = 176
    for p in range(4):
        l = slice(128 * p, 128 * p + 128)
        if p % 2 == 0:
            j = p // 2
            lj = slice(256 * j, 256 * j + 256)
            side.recv(b.k.at[pl.ds(R, R), lj], 2 * j)
            side.recv(b.v.at[pl.ds(R, R), lj], 2 * j + 1)
        kp = b.k[:, l]
        vT = b.v[:, l].T
        halves = []
        for t in range(2):
            b.s[...] = dot_nt(kp, head_lanes(b.q[:, l], t))

            def top(i, m):
                r = pl.ds(pl.multiple_of(i * S, 16), S)
                x = b.s[r] + wide(b.fill[r], R)
                return jnp.maximum(m, jnp.max(x.reshape(S // 8, 8, R), axis=0))

            m = lax.fori_loop(0, 2 * R // S, top, jnp.full((8, R), -3.0e38, F32))
            m = jnp.max(m, axis=0, keepdims=True)

            def expo(i, acc):
                r = pl.ds(pl.multiple_of(i * S, 16), S)
                x = jnp.exp(b.s[r] + wide(b.fill[r], R) - m)
                b.p[r] = x.astype(BF)
                return acc + jnp.sum(x.reshape(S // 8, 8, R), axis=0)

            tot = lax.fori_loop(0, 2 * R // S, expo, jnp.zeros((8, R), F32))
            tot = jnp.sum(tot, axis=0, keepdims=True)
            halves.append(dot_nn(vT[64 * t : 64 * t + 64], b.p[...]) / tot)
            b.lse[2 * p + t : 2 * p + t + 1, :] = m + jnp.log(tot)
            yield
        b.o[:, l] = jnp.concatenate(halves, axis=0).T
    for n in ("k", "v", "lse", "o"):
        b.put(n)
    b.need("w_out")

    def stats(s):
        x = b.o[s]
        b.stat[s] = two_cols(jnp.sum(x, axis=-1, keepdims=True), jnp.sum(x * x, axis=-1, keepdims=True))

    rows16(R, stats)
    core.send(b.stat, b.rstat, 0)
    core.recv(b.rstat, 0)

    def unit(s):
        t = b.stat[s] + b.rstat[s]
        mean = t[:, 0:1] / hp
        inv = lax.rsqrt(t[:, 1:2] / hp - mean * mean + EPS)
        b.st[s] = two_cols(mean, inv)
        b.u[s] = ((b.o[s] - mean) * inv * b.vh[0:1, :] + b.vh[3:4, :]).astype(BF)

    rows16(R, unit)
    b.put("st")
    yield
    for d in range(4):
        l = slice(256 * d, 256 * d + 256)
        b.part[:, l] = dot_nt(b.u[...], b.w_out[256 * d : 256 * d + 256, :]).astype(BF)
        core.send(b.part.at[:, l], b.rpart.at[:, l], 1 + d)
        if d % 2 == 1:
            yield
    for d in range(4):
        l = slice(256 * d, 256 * d + 256)
        core.recv(b.rpart.at[:, l], 1 + d)

    def close(s):
        x = b.part[s].astype(F32) + b.rpart[s].astype(F32) + b.vn[4:5, :]
        b.hm[s] = b.h[s] + wide(b.keep[s], x.shape[1]) * x

    rows16(R, close)
    b.put("hm")
    yield


def norm_store(dst, s, x, gain, bias):
    dst[s] = (unit_of(x, x.shape[1])[0] * gain + bias).astype(BF)


def hidden_body(b, w, R, core, fetch):
    rows16(R, lambda s: norm_store(b.n, s, b.hm[s], b.vn[2:3, :], b.vn[3:4, :]))
    loads = fetch()
    b.need("vf")
    loads[0].wait()
    yield
    for i, (a, n) in enumerate(tiles(HP)):
        b.gate[:, a : a + n] = dot_nn(b.n[...], b.w_gu[:, a : a + n]) + b.vf[1:2, a : a + n]
        b.up[:, a : a + n] = dot_nn(b.n[...], b.w_gu[:, HP + a : HP + a + n]) + b.vf[2:3, a : a + n]
        if i % 2 == 1:
            yield

    b.put("gate")
    b.put("up")

    def stats(s):
        g = b.gate[s]
        z = g * jax.nn.sigmoid(g) * b.up[s]
        b.z[s] = z
        b.stat[s] = two_cols(jnp.sum(z, axis=-1, keepdims=True), jnp.sum(z * z, axis=-1, keepdims=True))

    rows16(R, stats)
    core.send(b.stat, b.rstat, 0)
    core.recv(b.rstat, 0)
    yield

    def unit(s):
        t = b.stat[s] + b.rstat[s]
        mean = t[:, 0:1] / FF
        inv = lax.rsqrt(t[:, 1:2] / FF - mean * mean + EPS)
        b.zst[s] = two_cols(mean, inv)
        b.zn[s] = ((b.z[s] - mean) * inv * b.vf[0:1, :] + b.vf[3:4, :]).astype(BF)

    rows16(R, unit)
    b.put("zst")
    loads[1].wait()
    yield
    for d in range(4):
        l = slice(256 * d, 256 * d + 256)
        b.part[:, l] = dot_nt(b.zn[...], b.w_dn[256 * d : 256 * d + 256, :]).astype(BF)
        core.send(b.part.at[:, l], b.rpart.at[:, l], 1 + d)
        if d % 2 == 1:
            yield
    for d in range(4):
        l = slice(256 * d, 256 * d + 256)
        core.recv(b.rpart.at[:, l], 1 + d)

    def close(s):
        x = b.part[s].astype(F32) + b.rpart[s].astype(F32) + b.vn[5:6, :]
        b.ho[s] = b.hm[s] + wide(b.keep[s], x.shape[1]) * x

    rows16(R, close)
    b.put("ho")
    yield


def forward_layer(h, tabs, wts, vn, vh, vf, srcs, nxt, cid):
    R, D = h.shape
    fset = FF_G
    aset = AT_G if nxt else None

    def body(b):
        w = Where()
        greet_all(w, "all")
        ends = lambda g: ({n: getattr(b, "s_" + n) for n in g.names}, {n: getattr(b, "g_" + n) for n in g.names})
        ffc = fset.start(w, *ends(fset), b.extra[:split])
        core = Peer((w.dp, w.x, 1 - w.c), b.cs, b.cr)
        side = Peer(w.nx(), b.xs, b.xr)
        n = len(fset.live)
        for _ in range(n):
            next(ffc)

        def comm_all():
            yield from ffc
            if aset:
                yield from aset.start(w, *ends(aset), b.extra[split:])

        comm = comm_all()

        def fetch():
            for _ in ffc:
                pass
            if aset:
                for _ in range(3):
                    next(comm)
            fset.arrive()
            loads = [pltpu.make_async_copy(b.g_gu, b.w_gu, b.ls.at[0]), pltpu.make_async_copy(b.g_dn, b.w_dn, b.ls.at[1])]
            for c in loads:
                c.start()
            return loads

        def comp():
            yield from attend_body(b, w, R, core, side)
            core.finish()
            yield from hidden_body(b, w, R, core, fetch)

        drive(comp(), comm, [0, 0, n, 0, n, 0, n] + [1] * 4, 3)
        fset.finish_sends()
        if aset:
            aset.finish()
        core.finish()
        side.finish()

    ins = dict(h=(h, LD), keep=(tabs["keep"], LD), fill=(tabs["fill"], LD), cos=(tabs["cos"], LD), sin=(tabs["sin"], LD),
        w_in=(wts["in"], LD), w_out=(wts["out"], LD), vn=(vn, LD), vh=(vh, LD), vf=(vf, LD))
    outs = dict(hm=((R, D), F32, ST), q=((R, 512), BF, ST), k=((2 * R, 512), BF, ST), v=((2 * R, 512), BF, ST),
        lse=((8, R), F32, ST), o=((R, 512), F32, ST), st=((R, 128), F32, ST), ho=((R, D), F32, ST),
        gate=((R, HP), F32, ST), up=((R, HP), F32, ST), zst=((R, 128), F32, ST))
    extra = fset.scratch()
    split = len(extra)
    for g, src in ((fset, srcs), (aset, nxt)):
        if g:
            ins.update({"s_" + n: (src[n], ANY) for n in g.names})
            outs.update({"g_" + n: ((16 * RB, src[n].shape[1]), BF, ANY) for n in g.names})
    if aset:
        extra = extra + aset.scratch()
    B = lambda *s: pltpu.VMEM(s, BF)
    F = lambda *s: pltpu.VMEM(s, F32)
    scratch = dict(n=B(R, D), s=F(2 * R, R), p=B(2 * R, R), u=B(R, 512), part=B(R, D), rpart=B(R, D), stat=F(R, 128),
        rstat=F(R, 128), z=F(R, HP), zn=B(R, HP), w_gu=B(D, 2 * HP), w_dn=B(D, HP), cs=DMA((5,)), cr=DMA((5,)),
        xs=DMA((4,)), xr=DMA((4,)), ls=DMA((2,)))
    return run_kernel(body, "layer", cid, ins, outs, scratch, extra)


def add8(acc, x):
    acc[...] = acc[...] + fold8(x)


def put_vec(b, row, acc, n):
    b.vec[row : row + 1, 0:n] = jnp.sum(acc[...], axis=0, keepdims=True)


def close_back(b, s, x, gain, acc_gain, acc_shift):
    e = b.part[s].astype(F32) + b.rpart[s].astype(F32)
    unit, inv = unit_of(x, x.shape[1])
    add8(acc_gain, e * unit)
    add8(acc_shift, e)
    wt = e * gain
    n = x.shape[1]
    m1 = jnp.sum(wt, axis=-1, keepdims=True) / n
    m2 = jnp.sum(wt * unit, axis=-1, keepdims=True) / n
    b.go[s] = b.g[s] + inv * (wt - m1 - unit * m2)


def hidden_back_body(b, w, R, core):
    D = b.g.shape[1]
    for a in (b.a0, b.a1, b.a2, b.a3, b.a4, b.a5, b.a6, b.vec):
        a[...] = jnp.zeros_like(a)
    b.need("g", "keep")

    def unit4(s):
        g = b.gate[s]
        sg = jax.nn.sigmoid(g)
        return (g * sg * b.up[s] - b.st[s, 0:1]) * b.st[s, 1:2], g, sg

    def first(s):
        e = wide(b.keep[s], D) * b.g[s]
        b.el[s] = e.astype(BF)
        add8(b.a2, e)

    def norms(s):
        norm_store(b.n, s, b.go[s], b.vn[2:3, :], b.vn[3:4, :])
        b.zn[s] = (unit4(s)[0] * b.vf[0:1, :] + b.vf[3:4, :]).astype(BF)

    rows16(R, first)
    b.need("gate", "up", "st", "vn", "vf")
    rows16(R, norms)
    b.need("w_dn")
    b.begin("w_gu")
    yield
    for i, (a, n) in enumerate(tiles(HP)):
        b.ez[:, a : a + n] = dot_nn(b.el[...], b.w_dn[:, a : a + n])
        if i % 3 == 2:
            yield

    def second(s):
        u = unit4(s)[0]
        e = b.ez[s]
        wt = e * b.vf[0:1, :]
        add8(b.a3, e * u)
        add8(b.a6, e)
        b.stat[s] = two_cols(jnp.sum(wt, axis=-1, keepdims=True), jnp.sum(wt * u, axis=-1, keepdims=True))

    rows16(R, second)
    core.send(b.stat, b.rstat, 0)
    b.xT[...] = b.el[...].T
    yield
    for i, (a, n) in enumerate(tiles(HP)):
        b.d_dn[:, a : a + n] = dot_nn(b.xT[...], b.zn[:, a : a + n]).astype(BF)
        if i % 3 == 2:
            yield
    core.recv(b.rstat, 0)

    def third(s):
        u, g, sg = unit4(s)
        t = (b.stat[s] + b.rstat[s]) / FF
        ez = b.st[s, 1:2] * (b.ez[s] * b.vf[0:1, :] - t[:, 0:1] - u * t[:, 1:2])
        eg = ez * b.up[s] * sg * (1.0 + g * (1.0 - sg))
        eu = ez * g * sg
        add8(b.a4, eg)
        add8(b.a5, eu)
        b.egu[s, 0:HP] = eg.astype(BF)
        b.egu[s, HP : 2 * HP] = eu.astype(BF)

    rows16(R, third, 48)
    b.need("w_gu")
    yield
    for d in range(4):
        l = slice(256 * d, 256 * d + 256)
        b.part[:, l] = dot_nt(b.egu[...], b.w_gu[256 * d : 256 * d + 256, :]).astype(BF)
        core.send(b.part.at[:, l], b.rpart.at[:, l], 1 + d)
        yield
    b.xT[...] = b.n[...].T
    for i, (a, n) in enumerate(tiles(2 * HP)):
        b.d_gu[:, a : a + n] = dot_nn(b.xT[...], b.egu[:, a : a + n]).astype(BF)
        if i % 3 == 2 or i == len(tiles(2 * HP)) - 1:
            b.put("d_gu", (a - a % 768, a + n))
            yield
    for d in range(4):
        l = slice(256 * d, 256 * d + 256)
        core.recv(b.rpart.at[:, l], 1 + d)
    rows16(R, lambda s: close_back(b, s, b.go[s], b.vn[2:3, :], b.a0, b.a1))
    b.put("go")
    for row, acc, n in ((0, b.a0, D), (1, b.a1, D), (2, b.a2, D), (3, b.a3, HP), (4, b.a4, HP), (5, b.a5, HP), (6, b.a6, HP)):
        put_vec(b, row, acc, n)
    yield


def attend_back_body(b, w, R, core, side):
    D = b.g.shape[1]
    hp = D
    for a in (b.a0, b.a1, b.a2, b.a3, b.a4, b.a5, b.a6, b.vec):
        a[...] = jnp.zeros_like(a)
    b.need("g", "keep", "o", "st", "vn", "vh")

    def first(s):
        e = wide(b.keep[s], D) * b.g[s]
        b.el[s] = e.astype(BF)
        add8(b.a2, e)
        norm_store(b.n, s, b.go[s], b.vn[0:1, :], b.vn[1:2, :])
        u = (b.o[s] - b.st[s, 0:1]) * b.st[s, 1:2]
        b.u[s] = (u * b.vh[0:1, :] + b.vh[3:4, :]).astype(BF)

    rows16(R, first)
    b.need("w_out")
    b.begin("q", "k", "v", "lse", "fill", "cos", "sin", "w_in")
    yield
    for a, n in tiles(512):
        b.dq[:, a : a + n] = dot_nn(b.el[...], b.w_out[:, a : a + n])

    def second(s):
        u = (b.o[s] - b.st[s, 0:1]) * b.st[s, 1:2]
        e = b.dq[s]
        wt = e * b.vh[0:1, :]
        add8(b.a3, e * u)
        add8(b.a6, e)
        b.stat[s] = two_cols(jnp.sum(wt, axis=-1, keepdims=True), jnp.sum(wt * u, axis=-1, keepdims=True))

    rows16(R, second)
    core.send(b.stat, b.rstat, 0)
    b.xT[...] = b.el[...].T
    yield
    for a, n in tiles(512):
        b.d_out[:, a : a + n] = dot_nn(b.xT[...], b.u[:, a : a + n]).astype(BF)
    b.put("d_out")
    yield
    core.recv(b.rstat, 0)

    def third(s):
        u = (b.o[s] - b.st[s, 0:1]) * b.st[s, 1:2]
        t = (b.stat[s] + b.rstat[s]) / hp
        b.eo[s] = (b.st[s, 1:2] * (b.dq[s] * b.vh[0:1, :] - t[:, 0:1] - u * t[:, 1:2])).astype(BF)

    rows16(R, third, 48)
    b.need("q", "k", "v", "lse", "fill")
    yield
    S = 176
    for p in range(4):
        l = slice(128 * p, 128 * p + 128)
        kp = b.k[:, l]
        vp = b.v[:, l]
        kT = kp.T
        dk, dv, dqs = None, None, []
        for t in range(2):
            qt = head_lanes(b.q[:, l], t)
            ot = head_lanes(b.eo[:, l], t)
            b.s[...] = dot_nt(kp, qt)
            b.dp[...] = dot_nt(vp, ot)
            lse = b.lse[2 * p + t : 2 * p + t + 1, :]

            def expo(i, acc):
                r = pl.ds(pl.multiple_of(i * S, 16), S)
                x = jnp.exp(b.s[r] + wide(b.fill[r], R) - lse)
                b.s[r] = x
                b.p[r] = x.astype(BF)
                return acc + jnp.sum((x * b.dp[r]).reshape(S // 8, 8, R), axis=0)

            tot = lax.fori_loop(0, 2 * R // S, expo, jnp.zeros((8, R), F32))
            tot = jnp.sum(tot, axis=0, keepdims=True)

            def grad(i, _):
                r = pl.ds(pl.multiple_of(i * S, 16), S)
                b.ds[r] = (b.s[r] * (b.dp[r] - tot)).astype(BF)
                return 0

            lax.fori_loop(0, 2 * R // S, grad, 0)
            yield
            v1 = dot_nn(b.p[...], ot)
            k1 = dot_nn(b.ds[...], qt)
            dqs.append(dot_nn(kT[64 * t : 64 * t + 64], b.ds[...]))
            dv = v1 if t == 0 else dv + v1
            dk = k1 if t == 0 else dk + k1
            yield
        dk = jnp.where(b.fill[:, 0:1] == 0.0, dk, 0.0)
        b.dq[:, l] = jnp.concatenate(dqs, axis=0).T * 0.125
        b.dk[:, l] = dk[:R]
        b.dv[:, l] = dv[:R]
        l2 = slice(512 + 128 * p, 640 + 128 * p)
        b.ep[:, l] = dk[R:].astype(BF)
        b.ep[:, l2] = dv[R:].astype(BF)
        side.send(b.ep.at[:, l], b.rk.at[:, l], 2 * p)
        side.send(b.ep.at[:, l2], b.rv.at[:, l], 2 * p + 1)
    b.need("cos", "sin", "w_in")
    yield
    side.finish()
    for p in range(4):
        l = slice(128 * p, 128 * p + 128)
        side.recv(b.rk.at[:, l], 2 * p)
        side.recv(b.rv.at[:, l], 2 * p + 1)

        def last(s):
            cos, sin = b.cos[s], -b.sin[s]
            eq = turn(b.dq[s, l], cos, sin)
            ek = turn(b.dk[s, l] + b.rk[s, l].astype(F32), cos, sin)
            ev = b.dv[s, l] + b.rv[s, l].astype(F32)
            b.a4[:, l] = b.a4[:, l] + fold8(eq)
            b.a5[:, l] = b.a5[:, l] + fold8(ev)
            b.ep[s, l] = eq.astype(BF)
            b.ep[s, 512 + 128 * p : 640 + 128 * p] = ek.astype(BF)
            b.ep[s, 1024 + 128 * p : 1152 + 128 * p] = ev.astype(BF)

        rows16(R, last)
    yield
    for d in range(4):
        l = slice(256 * d, 256 * d + 256)
        b.part[:, l] = dot_nt(b.ep[...], b.w_in[256 * d : 256 * d + 256, :]).astype(BF)
        core.send(b.part.at[:, l], b.rpart.at[:, l], 1 + d)
        if d % 2 == 1:
            yield
    b.xT[...] = b.n[...].T
    for i, (a, n) in enumerate(tiles(1536)):
        b.d_in[:, a : a + n] = dot_nn(b.xT[...], b.ep[:, a : a + n]).astype(BF)
        if i % 3 == 2:
            b.put("d_in", (a - a % 768, a + n))
            yield
    for d in range(4):
        l = slice(256 * d, 256 * d + 256)
        core.recv(b.rpart.at[:, l], 1 + d)
    rows16(R, lambda s: close_back(b, s, b.go[s], b.vn[0:1, :], b.a0, b.a1))
    b.put("go")
    for row, acc, n in ((0, b.a0, D), (1, b.a1, D), (2, b.a2, D), (3, b.a3, 512), (4, b.a4, 512), (5, b.a5, 512), (6, b.a6, 512)):
        put_vec(b, row, acc, n)
    yield


def scatter_args(sset, grads, vec):
    ins = {"s_" + n: (grads[n], ANY) for n in sset.names}
    ins["s_vec"] = (vec, VM)
    outs = {"r_" + n: ((RB, grads[n].shape[1]), F32, VM) for n in sset.names}
    outs["r_vec"] = ((8, HP), F32, VM)
    return ins, outs


def scatter_start(sset, w, b, sc=None):
    n = sset.names
    return sset.start(w, {i: getattr(b, "s_" + i) for i in n}, {i: getattr(b, "r_" + i) for i in n}, b.s_vec, b.r_vec, b.extra if sc is None else sc)


HB_RATE = 2


def backward_hidden(g, fw, hm, tabs, wts, vn, vf, sset, grads, vec, cid):
    R, D = g.shape

    def body(b):
        w = Where()
        greet_all(w, "all")
        core = Peer((w.dp, w.x, 1 - w.c), b.cs, b.cr)
        load = pltpu.make_async_copy(b.hm, b.go, b.ls.at[0])
        load.start()
        comp = hidden_back_body(b, w, R, core)
        if sset:
            comm = scatter_start(sset, w, b, b.extra[:split])
            for _ in sset.live:
                next(comm)
        load.wait()

        def both():
            for _ in range(5):
                if sset:
                    for _ in range(3):
                        next(comm, None)
                yield
            mine = dset.start(w, {"dn": b.d_dn}, {"dn": b.r_dn}, None, None, b.extra[split:])
            for _ in dset.live:
                next(mine)
            yield
            yield from step_all([mine, comm] if sset else [mine])

        drive(comp, both(), [1] * 6, HB_RATE * (2 if sset else 1))
        if sset:
            sset.finish()
        dset.finish()
        core.finish()

    ins = dict(g=(g, LD), keep=(tabs["keep"], LD), hm=(hm, ANY), gate=(fw["gate"], LD), up=(fw["up"], LD),
        st=(fw["zst"], LD), w_gu=(wts["gu"], LATE), w_dn=(wts["dn"], LD), vn=(vn, LD), vf=(vf, LD))
    outs = dict(go=((R, D), F32, ST), d_gu=((D, 2 * HP), BF, ST), r_dn=((RB, HP), F32, VM), vec=((8, HP), F32, VM))
    extra = ()
    dset = dn_scatter()
    if sset:
        i2, o2 = scatter_args(sset, grads, vec)
        ins.update(i2)
        outs.update(o2)
        extra = sset.scratch()
    split = len(extra)
    extra = list(extra) + dset.scratch()
    acc = lambda n: pltpu.VMEM((8, n), F32)
    scratch = dict(d_dn=pltpu.VMEM((D, HP), BF), el=pltpu.VMEM((R, D), BF), xT=pltpu.VMEM((D, R), BF), n=pltpu.VMEM((R, D), BF),
        ez=pltpu.VMEM((R, HP), F32), zn=pltpu.VMEM((R, HP), BF), egu=pltpu.VMEM((R, 2 * HP), BF),
        part=pltpu.VMEM((R, D), BF), rpart=pltpu.VMEM((R, D), BF), stat=pltpu.VMEM((R, 128), F32),
        rstat=pltpu.VMEM((R, 128), F32), cs=DMA((5,)), cr=DMA((5,)), ls=DMA((1,)), a0=acc(D), a1=acc(D), a2=acc(D),
        a3=acc(HP), a4=acc(HP), a5=acc(HP), a6=acc(HP))
    return run_kernel(body, "hidden_back", cid, ins, outs, scratch, extra)


def backward_attend(g, fw, h, tabs, wts, vn, vh, sset, grads, vec, cid):
    R, D = g.shape

    def body(b):
        w = Where()
        greet_all(w, "all")
        core = Peer((w.dp, w.x, 1 - w.c), b.cs, b.cr)
        side = Peer(w.nx(), b.xs, b.xr)
        load = pltpu.make_async_copy(b.h, b.go, b.ls.at[0])
        load.start()
        comm = scatter_start(sset, w, b)
        for _ in sset.live:
            next(comm)
        load.wait()
        drive(attend_back_body(b, w, R, core, side), comm, [1] * 4 + [1, 2] * 8, 2)
        sset.finish()
        core.finish()

    ins = dict(g=(g, LD), keep=(tabs["keep"], LD), h=(h, ANY), fill=(tabs["fill"], LATE), cos=(tabs["cos"], LATE),
        sin=(tabs["sin"], LATE), o=(fw["o"], LD), st=(fw["st"], LD), q=(fw["q"], LATE), k=(fw["k"], LATE),
        v=(fw["v"], LATE), lse=(fw["lse"], LATE), w_in=(wts["in"], LATE), w_out=(wts["out"], LD), vn=(vn, LD),
        vh=(vh, LD))
    outs = dict(go=((R, D), F32, ST), d_in=((D, 1536), BF, ST), d_out=((D, 512), BF, ST), vec=((8, HP), F32, VM))
    i2, o2 = scatter_args(sset, grads, vec)
    ins.update(i2)
    outs.update(o2)
    acc = lambda n: pltpu.VMEM((8, n), F32)
    B = lambda *s: pltpu.VMEM(s, BF)
    F = lambda *s: pltpu.VMEM(s, F32)
    scratch = dict(el=B(R, D), xT=B(D, R), n=B(R, D), u=B(R, 512), eo=B(R, 512), s=F(2 * R, R), dp=F(2 * R, R), p=B(2 * R, R),
        ds=B(2 * R, R), dq=F(R, 512), dk=F(R, 512), dv=F(R, 512), rk=B(R, 512), rv=B(R, 512), ep=B(R, 1536),
        part=B(R, D), rpart=B(R, D), stat=F(R, 128), rstat=F(R, 128), cs=DMA((5,)), cr=DMA((5,)), ls=DMA((1,)),
        xs=DMA((8,)), xr=DMA((8,)), a0=acc(D), a1=acc(D), a2=acc(D), a3=acc(512), a4=acc(512), a5=acc(512),
        a6=acc(512))
    return run_kernel(body, "attend_back", cid, ins, outs, scratch, sset.scratch())


def scatter_last(sset, grads, vec, cid):
    def body(b):
        w = Where()
        greet(w)
        for _ in scatter_start(sset, w, b):
            pass
        sset.finish()

    ins, outs = scatter_args(sset, grads, vec)
    return run_kernel(body, "scatter", cid, ins, outs, {}, sset.scratch())


HP = 1408


def fast_device(
    tokens_in,
    cotangent,
    key_mask,
    grid_pos,
    class_index,
    input_weight,
    output_weight,
    gate_up_weight,
    down_weight,
    norm_gains,
    norm_biases,
    head_gains,
    head_biases,
    hidden_gains,
    hidden_biases,
):
    _, rows, width = tokens_in.shape
    dim = head_gains.shape[1]
    hidden = hidden_gains.shape[1]
    layers = input_weight.shape[0]
    pad = HP - hidden
    R = -(-rows // 16) * 16
    more = R - rows
    places = lax.axis_index("ctx") * rows + jnp.arange(rows, dtype=jnp.int32)
    not_class = (places != class_index[0]).astype(F32)
    cosine, sine = rotary_tables(grid_pos.reshape(2, rows), not_class)
    c0, c1, s0, s1 = cosine[:, 0], cosine[:, 1], sine[:, 0], sine[:, 1]
    low = lambda a: jnp.pad(a, ((0, more), (0, 0)))
    keep = low(key_mask.astype(F32).reshape(rows, 1))
    real = jnp.pad(key_mask.astype(F32).reshape(1, rows), ((0, 0), (0, more)))
    fill = jnp.where(jnp.arange(R)[None] < rows, (real - 1.0) * 10000.0, -1.0e30)
    fill = jnp.broadcast_to(fill, (8, R))
    tabs = dict(keep=jnp.broadcast_to(keep, (R, 128)), cos=low(jnp.concatenate([c0, c0, c1, c1] * 2, axis=1)),
        sin=low(jnp.concatenate([-s0, s0, -s1, s1] * 2, axis=1)))
    gn = norm_gains.astype(F32)
    bn = norm_biases.astype(F32)
    gh = head_gains.astype(F32)[:, None]
    bh = head_biases.astype(F32)
    vh = jnp.pad(jnp.concatenate([gh, bh], axis=1), ((0, 0), (0, 4), (0, 0)))
    vn = jnp.stack([gn[:, 0], bn[:, 0], gn[:, 1], bn[:, 1], bn[:, 2], bn[:, 3]], axis=1)
    vn = jnp.pad(vn, ((0, 0), (0, 2), (0, 0)))
    vf = jnp.concatenate([hidden_gains.astype(F32)[:, None], hidden_biases.astype(F32)], axis=1)
    vf = jnp.pad(vf, ((0, 0), (0, 4), (0, pad)))
    gu = jnp.pad(gate_up_weight, ((0, 0), (0, 0), (0, 0), (0, pad)))
    dn = jnp.pad(down_weight, ((0, 0), (0, 0), (0, pad)))
    at_src = [{"in": input_weight[l].reshape(RB, 3 * dim), "out": output_weight[l]} for l in range(layers)]
    ff_src = [{"gu": gu[l].reshape(RB, 2 * HP), "dn": dn[l]} for l in range(layers)]
    grab = lambda d, names: {n: d["g_" + n] for n in names}
    h = low(tokens_in.astype(F32).reshape(rows, width)) * keep
    first = gather_first(at_src[0], AT_G, fill, 0)
    tabs["fill"] = first["both"]
    at_w = {0: {n: first["w_" + n] for n in AT_G.names}}
    ff_w, hs, fw = {}, {}, {}
    for l in range(layers):
        hs[l] = h
        nxt = l + 1 < layers
        r = forward_layer(h, tabs, at_w[l], vn[l], vh[l], vf[l], ff_src[l], at_src[l + 1] if nxt else None, 1 + l)
        fw[l], h = r, r["ho"]
        ff_w[l] = grab(r, FF_G.names)
        if nxt:
            at_w[l + 1] = grab(r, AT_G.names)
    activations = h[:rows].astype(BF).reshape(1, rows, width)
    g = low(cotangent.astype(F32).reshape(rows, width))
    got = {}
    grads, vec, cid = None, None, layers + 1
    for l in reversed(range(layers)):
        sset = at_scatter() if grads else None
        r = backward_hidden(g, fw[l], fw[l]["hm"], tabs, ff_w[l], vn[l], vf[l], sset, grads, vec, cid)
        if grads:
            got["at", l + 1] = r
        g, vec, grads, got["dn", l] = r["go"], r["vec"], {"gu": r["d_gu"]}, r["r_dn"]
        r = backward_attend(g, fw[l], hs[l], tabs, at_w[l], vn[l], vh[l], gu_scatter(), grads, vec, cid + 1)
        got["ff", l] = r
        g, vec, grads = r["go"], r["vec"], {"in": r["d_in"], "out": r["d_out"]}
        cid += 2
    got["at", 0] = scatter_last(at_scatter(), grads, vec, cid)
    input_grad = (keep * g)[:rows].reshape(1, rows, width)
    L = range(layers)
    va = jnp.stack([got["at", l]["r_vec"] for l in L])
    vff = jnp.stack([got["ff", l]["r_vec"] for l in L])
    return (
        activations,
        input_grad,
        jnp.stack([got["at", l]["r_in"].reshape(RB, 3, dim) for l in L]),
        jnp.stack([got["at", l]["r_out"] for l in L]),
        jnp.stack([got["ff", l]["r_gu"].reshape(RB, 2, HP)[:, :, :hidden] for l in L]),
        jnp.stack([got["dn", l][:, :hidden] for l in L]),
        jnp.stack([va[:, 0, :width], vff[:, 0, :width]], axis=1),
        jnp.stack([va[:, 1, :width], vff[:, 1, :width], va[:, 2, :width], vff[:, 2, :width]], axis=1),
        va[:, 3, :dim],
        va[:, 4:7, :dim],
        vff[:, 3, :hidden],
        vff[:, 4:7, :hidden],
    )


def solution(mesh):
    sizes = dict(mesh.shape)
    fits = sizes == dict(dp=8, ctx=2, tp=2)
    return jax.shard_map(
        fast_device if fits else on_device,
        mesh=mesh,
        in_specs=(
            P("dp", "ctx", None),
            P("dp", "ctx", None),
            P("dp", "ctx"),
            P(None, "dp", "ctx"),
            P("dp"),
            P(None, ("dp", "ctx"), None, "tp"),
            P(None, ("dp", "ctx"), "tp"),
            P(None, ("dp", "ctx"), None, "tp"),
            P(None, ("dp", "ctx"), "tp"),
            P(),
            P(),
            P(None, "tp"),
            P(None, None, "tp"),
            P(None, "tp"),
            P(None, None, "tp"),
        ),
        out_specs=(
            P("dp", "ctx", None),
            P("dp", "ctx", None),
            P(None, ("dp", "ctx"), None, "tp"),
            P(None, ("dp", "ctx"), "tp"),
            P(None, ("dp", "ctx"), None, "tp"),
            P(None, ("dp", "ctx"), "tp"),
            P(),
            P(),
            P(None, "tp"),
            P(None, None, "tp"),
            P(None, "tp"),
            P(None, None, "tp"),
        ),
        check_vma=False,
    )
```
